32 devices in a mesh: brick: 8 (over y, x, core), slab: 4 (over z).
Axes of the slice: x: 2, y: 2, z: 4, core: 2. Of those that a mesh axis runs over, the one named last changes fastest.
Arguments:
- positions: float32 [3, 4, 1536], P(None, 'slab', 'brick'), may hold values from -3 to 3
- types: int32 [4, 1536], P('slab', 'brick'), may hold values from 0 to 1, as said below
- neighbours: int32 [4, 1536, 64], P('slab', 'brick'), may hold values from 0 to 383
- neighbour_count: int32 [4, 1536], P('slab', 'brick'), may hold values from 32 to 64, as said below
- send_index: int32 [4, 1536], P('slab', 'brick'), may hold values from 0 to 191
- cell_x: int32 [4, 1536], P('slab', 'brick'), may hold values from 0 to 31, as said below
- cell_y: int32 [4, 1536], P('slab', 'brick'), may hold values from 0 to 63, as said below
- cell_z: int32 [4, 1536], P('slab', 'brick'), may hold values from 0 to 255, as said below
- spline_fraction: float32 [3, 4, 1536], P(None, 'slab', 'brick'), may hold values from 0 to 1
- embed_first: float32 [2, 25], replicated, may hold values from -4 to 4
- embed_second: float32 [25, 50], replicated, may hold values from -1.25 to 1.25
- embed_third: float32 [50, 100], replicated, may hold values from -0.875 to 0.875
- energy_in: float32 [1600, 240], replicated, may hold values from -0.3125 to 0.3125
- energy_hidden: float32 [2, 240, 240], replicated, may hold values from -0.375 to 0.375
- energy_out: float32 [240], replicated, may hold values from -0.375 to 0.375
- wannier_in: float32 [1600, 240], replicated, may hold values from -0.3125 to 0.3125
- wannier_hidden: float32 [2, 240, 240], replicated, may hold values from -0.375 to 0.375
- wannier_out: float32 [240], replicated, may hold values from -0.01953125 to 0.01953125
- charge_base: float32 [2], replicated, may hold values from -2 to 1
Outputs:
- atom_energy: float32 [4, 1536], P('slab', 'brick')
- potential: float32 [256, 256, 256], P('brick', 'slab')
The draws below stay inside these ranges and needn't reach their ends.
Inputs may be any that keep to these rules, and one draw needn't show every extreme that they name: The first neighbour_count entries of an atom's neighbour row are live, the rest are padding; the first atom of every block has all 64 slots live. `types`: atoms 3k, 3k + 1 and 3k + 2 of a row form one water molecule: one oxygen and two hydrogens. `cell_x`: each hydrogen's first grid point along the first dimension is that of its molecule's oxygen or one further. `cell_y`: each hydrogen's first grid point along the second dimension is that of its molecule's oxygen or one further. `cell_z`: each hydrogen's first grid point along the third dimension is that of its molecule's oxygen or one further.
All inputs are finite; a program needn't handle non-finite values.
Results may differ from the reference program's by a relative error of at most 0.0003.
Values sent between devices are 32-bit elements; how exact they have to be, the bound alone decides.
No kernel may reach another device: no remote copies, remote signals or barrier semaphores. Data moves between devices by JAX's collectives and lax.ppermute only.
A program may use at most 128 MiB of HBM per device.

```python
import math
import jax
import jax.numpy as jnp
from jax import lax

NG = 256
A_DEV = 192
NB = 64
EMB1 = 25
EMB2 = 50
EMB3 = 100
AXIS = 16
FIT = 240
FIT_LAYERS = 2
GHOST = 96
CX = 32
CY = 64
ATOMS_B = 1536
DESC = 1600
N_BRICK = 8
N_SLAB = 4


def oxygen_flags(key):
    oxygen_slot = jax.random.randint(key, (N_SLAB, ATOMS_B // 3), 0, 3)
    slot_atom = jnp.repeat(oxygen_slot, 3, axis=1)
    position_in = (jnp.arange(ATOMS_B, dtype=jnp.int32) % 3)[None, :]
    return slot_atom == position_in


def place_cells(key, span, salt):
    oxygen = oxygen_flags(key)
    key = jax.random.fold_in(key, salt)
    anchor_key = jax.random.fold_in(key, 1)
    offset_key = jax.random.fold_in(key, 2)
    anchor = jax.random.randint(anchor_key, (N_SLAB, ATOMS_B // 3), 0, span - 1)
    offset = jax.random.randint(offset_key, (N_SLAB, ATOMS_B), 0, 2)
    column = jnp.arange(ATOMS_B, dtype=jnp.int32)[None, :]
    leading = column % A_DEV < 3
    anchor_atom = jnp.repeat(anchor, 3, axis=1)
    anchor_atom = jnp.where(leading, span - 2, anchor_atom)
    offset = jnp.where(leading, 1, offset)
    return (anchor_atom + jnp.where(oxygen, 0, offset)).astype(jnp.int32)


def draw_types(key, part):
    oxygen = oxygen_flags(key)
    return jnp.where(oxygen, 0, 1).astype(jnp.int32)


def draw_cell_x(key, part):
    return place_cells(key, CX, 11)


def draw_cell_y(key, part):
    return place_cells(key, CY, 13)


def draw_cell_z(key, part):
    return place_cells(key, NG, 17)


def draw_charge_base(key, part):
    key = jax.random.fold_in(key, 21)
    magnitude = jax.random.uniform(key, (), jnp.float32, 1.0, 1.6)
    return jnp.stack([-magnitude, 0.5 * magnitude]).astype(jnp.float32)


def draw_neighbour_count(key, part):
    key = jax.random.fold_in(key, 5)
    counts = jax.random.randint(key, (N_SLAB, ATOMS_B), NB // 2, NB + 1)
    column = jnp.arange(ATOMS_B, dtype=jnp.int32)
    return jnp.where((column % A_DEV == 0)[None, :], NB, counts).astype(jnp.int32)


def touch_ends(drawn, rng, smallest, largest):
    longest = drawn.shape.index(max(drawn.shape))
    spots = []
    for shift in (0, 1):
        where = [jax.random.randint(jax.random.fold_in(rng, axis), (), 0, length) for axis, length in enumerate(drawn.shape)]
        where[longest] = (where[longest] + shift) % drawn.shape[longest]
        spots.append(tuple(where))
    return drawn.at[spots[0]].set(smallest).at[spots[1]].set(largest)


def block_levels(rng, shape, cuts, low, top_value):
    gain, own = 1.0, jax.random.fold_in(rng, 6)
    for position, blocks in cuts:
        steps = jnp.exp(jax.random.uniform(jax.random.fold_in(own, position), (blocks,), jnp.float32, low / len(cuts), top_value / len(cuts)))
        gain = gain * jnp.repeat(steps, shape[position] // blocks).reshape([-1 if axis == position else 1 for axis in range(len(shape))])
    return gain


def noise(key, shape, deviation, most, split=(), held_as=jnp.bfloat16):
    factor_of = block_levels(key, shape, split, -0.22, 0.18) if split else 1.0
    drawn = jax.random.normal(key, shape, jnp.float32) * deviation * factor_of
    return jnp.minimum(jnp.maximum(drawn, -most), most).astype(held_as)


def setup_inputs(seed: int = 0) -> dict:
    streams_of = jax.random.split(jax.random.key(seed), 20)
    return {
        "positions": noise(streams_of[0], (3, N_SLAB, ATOMS_B), 0.5, 3.0, ((1, 4), (2, 8)), jnp.float32),
        "types": draw_types(jax.random.fold_in(streams_of[19], 71), 0),
        "neighbours": touch_ends(jax.random.randint(streams_of[2], (N_SLAB, ATOMS_B, NB), 0, A_DEV + 2 * GHOST), jax.random.fold_in(streams_of[2], 1), 0, (A_DEV + 2 * GHOST) - 1).astype(jnp.int32),
        "neighbour_count": draw_neighbour_count(jax.random.fold_in(streams_of[19], 71), 0),
        "send_index": touch_ends(jax.random.randint(streams_of[4], (N_SLAB, 2 * GHOST * N_BRICK), 0, A_DEV), jax.random.fold_in(streams_of[4], 1), 0, A_DEV - 1).astype(jnp.int32),
        "cell_x": draw_cell_x(jax.random.fold_in(streams_of[19], 71), 0),
        "cell_y": draw_cell_y(jax.random.fold_in(streams_of[19], 71), 0),
        "cell_z": draw_cell_z(jax.random.fold_in(streams_of[19], 71), 0),
        "spline_fraction": jnp.clip(1.0 * jax.random.uniform(streams_of[8], (3, N_SLAB, ATOMS_B), jnp.float32) ** block_levels(streams_of[8], (3, N_SLAB, ATOMS_B), ((1, 4), (2, 8)), -0.2, 0.2), 0.0, 1.0),
        "embed_first": noise(streams_of[9], (2, EMB1), 1.0, 4.0, (), jnp.float32),
        "embed_second": noise(streams_of[10], (EMB1, EMB2), EMB1 ** -0.5, 1.25, (), jnp.float32),
        "embed_third": noise(streams_of[11], (EMB2, EMB3), EMB2 ** -0.5, 0.875, (), jnp.float32),
        "energy_in": noise(streams_of[12], (DESC, FIT), (DESC // 4) ** -0.5, 0.3125, (), jnp.float32),
        "energy_hidden": noise(streams_of[13], (FIT_LAYERS, FIT, FIT), FIT ** -0.5, 0.375, (), jnp.float32),
        "energy_out": noise(streams_of[14], (FIT,), FIT ** -0.5, 0.375, (), jnp.float32),
        "wannier_in": noise(streams_of[15], (DESC, FIT), (DESC // 4) ** -0.5, 0.3125, (), jnp.float32),
        "wannier_hidden": noise(streams_of[16], (FIT_LAYERS, FIT, FIT), FIT ** -0.5, 0.375, (), jnp.float32),
        "wannier_out": noise(streams_of[17], (FIT,), (400 * FIT) ** -0.5, 0.01953125, (), jnp.float32),
        "charge_base": draw_charge_base(jax.random.fold_in(streams_of[19], 71), 0),
    }


HIGH = lax.Precision.HIGHEST


def spline_weights(fraction):
    cubed = fraction * fraction * fraction
    square = fraction * fraction
    return jnp.stack([(1.0 - fraction) * (1.0 - fraction) * (1.0 - fraction) / 6.0,
                      (3.0 * cubed - 6.0 * square + 4.0) / 6.0,
                      (-3.0 * cubed + 3.0 * square + 3.0 * fraction + 1.0) / 6.0,
                      cubed / 6.0])


def fitting(descriptor, weight_in, weight_hidden, weight_out):
    hidden = jnp.tanh(jnp.dot(descriptor, weight_in, precision=HIGH))
    for depth_index in range(weight_hidden.shape[0]):
        hidden = jnp.tanh(jnp.dot(hidden, weight_hidden[depth_index], precision=HIGH)) + hidden
    return jnp.dot(hidden, weight_out, precision=HIGH)


def atom_terms(extended, neighbour_rows, neighbour_total, embed_first, embed_second, embed_third,
               energy_in, energy_hidden, energy_out, wannier_in, wannier_hidden, wannier_out):
    atom_count, slots = neighbour_rows.shape
    ghost_rows = (extended.shape[1] - atom_count) // 2
    block_size = 64 if atom_count % 64 == 0 else atom_count
    blocks = atom_count // block_size
    present = (jnp.arange(slots, dtype=jnp.int32)[None, :] < neighbour_total[:, None]).astype(jnp.float32)
    centre_ids = (ghost_rows + jnp.arange(atom_count, dtype=jnp.int32)).reshape(blocks, block_size)

    def one_block(pieces):
        centre_rows, rows_block, present_block = pieces
        centre_block = extended[:3, centre_rows]
        gathered = extended[:, rows_block]
        offsets = gathered[:3] - centre_block[:, :, None]
        smooth = present_block / (1.0 + jnp.sum(offsets * offsets, axis=0))
        environment = jnp.stack([smooth, smooth * offsets[0], smooth * offsets[1], smooth * offsets[2]], axis=-1)
        kind = gathered[3][:, :, None]
        first = jnp.tanh(smooth[:, :, None] * ((1.0 - kind) * embed_first[0] + kind * embed_first[1]))
        second = jnp.tanh(jnp.einsum('anm,mk->ank', first, embed_second, precision=HIGH)) + jnp.concatenate([first, first], axis=-1)
        third = jnp.tanh(jnp.einsum('anm,mk->ank', second, embed_third, precision=HIGH)) + jnp.concatenate([second, second], axis=-1)
        moments = jnp.einsum('anm,anc->amc', third, environment, precision=HIGH) / slots
        descriptor = jnp.einsum('amc,akc->amk', moments, moments[:, :AXIS], precision=HIGH).reshape(block_size, -1)
        return (fitting(descriptor, energy_in, energy_hidden, energy_out),
                fitting(descriptor, wannier_in, wannier_hidden, wannier_out))

    energy_short, charge_shift = lax.map(one_block, (centre_ids, neighbour_rows.reshape(blocks, block_size, slots),
                                                     present.reshape(blocks, block_size, slots)))
    return energy_short.reshape(atom_count), charge_shift.reshape(atom_count)


def green_table(first, second, third, size):
    def folded(index):
        return jnp.where(index < size // 2, index, index - size).astype(jnp.float32) * (2.0 * math.pi / size)
    kappa_x = folded(first)[:, None, None]
    kappa_y = folded(second)[None, :, None]
    kappa_z = folded(third)[None, None, :]
    squared = kappa_x * kappa_x + kappa_y * kappa_y + kappa_z * kappa_z
    root = ((first[:, None, None] == 0) & (second[None, :, None] == 0) & (third[None, None, :] == 0)).astype(jnp.float32)
    return (1.0 - root) * jnp.exp(-0.5 * squared) / (squared + root)


def reference(positions, types, neighbours, neighbour_count, send_index, cell_x, cell_y, cell_z, spline_fraction,
              embed_first, embed_second, embed_third, energy_in, energy_hidden, energy_out,
              wannier_in, wannier_hidden, wannier_out, charge_base):
    kind_float = types.astype(jnp.float32)
    own_atoms = jnp.concatenate([positions, kind_float[None]], axis=0).reshape(4, N_SLAB, N_BRICK, A_DEV)
    send_rows = send_index.reshape(N_SLAB, N_BRICK, 2 * GHOST)
    outgoing = jnp.take_along_axis(own_atoms, jnp.broadcast_to(send_rows[None], (4,) + send_rows.shape), axis=3)
    lower_ghosts = jnp.roll(outgoing[..., GHOST:], 1, axis=2)
    upper_ghosts = jnp.roll(outgoing[..., :GHOST], -1, axis=2)
    extended = jnp.concatenate([lower_ghosts, own_atoms, upper_ghosts], axis=3)
    total_blocks = N_SLAB * N_BRICK
    extended_blocks = jnp.moveaxis(extended, 0, 2).reshape(total_blocks, 4, A_DEV + 2 * GHOST)
    neighbour_blocks = neighbours.reshape(total_blocks, A_DEV, NB)
    count_blocks = neighbour_count.reshape(total_blocks, A_DEV)

    def per_block(pieces):
        return atom_terms(pieces[0], pieces[1], pieces[2], embed_first, embed_second, embed_third,
                          energy_in, energy_hidden, energy_out, wannier_in, wannier_hidden, wannier_out)

    energy_short, charge_shift = lax.map(per_block, (extended_blocks, neighbour_blocks, count_blocks))
    energy_short = energy_short.reshape(N_SLAB, ATOMS_B)
    charge = (1.0 - kind_float) * charge_base[0] + kind_float * charge_base[1] + charge_shift.reshape(N_SLAB, ATOMS_B)

    brick_column = (jnp.arange(ATOMS_B, dtype=jnp.int32) // A_DEV)[None, :]
    slab_row = jnp.arange(N_SLAB, dtype=jnp.int32)[:, None]
    steps_four = jnp.arange(4, dtype=jnp.int32)[:, None, None]
    index_x = (brick_column * CX + cell_x + steps_four) % NG
    index_y = (slab_row * CY + cell_y + steps_four) % NG
    index_z = (cell_z + steps_four) % NG
    weight_x = spline_weights(spline_fraction[0])
    weight_y = spline_weights(spline_fraction[1])
    weight_z = spline_weights(spline_fraction[2])
    shape_all = (4, 4, 4, N_SLAB, ATOMS_B)
    point_x = jnp.broadcast_to(index_x[:, None, None], shape_all)
    point_y = jnp.broadcast_to(index_y[None, :, None], shape_all)
    point_z = jnp.broadcast_to(index_z[None, None, :], shape_all)
    product = weight_x[:, None, None] * weight_y[None, :, None] * weight_z[None, None, :]
    charge_grid = jnp.zeros((NG, NG, NG), jnp.float32).at[point_x, point_y, point_z].add(product * charge)
    spectrum = jnp.fft.fftn(charge_grid)
    grid_index = jnp.arange(NG, dtype=jnp.int32)
    factor = green_table(grid_index, grid_index, grid_index, NG)
    potential = jnp.real(jnp.fft.ifftn(spectrum * factor)).astype(jnp.float32)
    potential_at = jnp.sum(potential[point_x, point_y, point_z] * product, axis=(0, 1, 2))
    atom_energy = energy_short + 0.5 * charge * potential_at
    return atom_energy, potential
```

```python
import functools
import math

import jax
import jax.numpy as jnp
import ml_dtypes
import numpy as np
from jax import lax
from jax.experimental import pallas as pl
from jax.experimental.pallas import tpu as pltpu
from jax.sharding import PartitionSpec as P

NG = 256
AXIS = 16


HIGH = lax.Precision.HIGHEST


def with_halo(cells, sides, width):
    for axis, dim in sides:
        count = lax.axis_size(axis)
        head = lax.slice_in_dim(cells, 0, width, axis=dim)
        tail = lax.slice_in_dim(cells, cells.shape[dim] - width, cells.shape[dim], axis=dim)
        cells = jnp.concatenate(
            [
                lax.ppermute(tail, axis, [(i, (i + 1) % count) for i in range(count)]),
                cells,
                lax.ppermute(head, axis, [((i + 1) % count, i) for i in range(count)]),
            ],
            axis=dim,
        )
    return cells


def spline_weights(fraction):
    cubed = fraction * fraction * fraction
    square = fraction * fraction
    return jnp.stack(
        [
            (1.0 - fraction) * (1.0 - fraction) * (1.0 - fraction) / 6.0,
            (3.0 * cubed - 6.0 * square + 4.0) / 6.0,
            (-3.0 * cubed + 3.0 * square + 3.0 * fraction + 1.0) / 6.0,
            cubed / 6.0,
        ]
    )


def fitting(descriptor, weight_in, weight_hidden, weight_out):
    hidden = jnp.tanh(jnp.dot(descriptor, weight_in, precision=HIGH))
    for depth_index in range(weight_hidden.shape[0]):
        hidden = jnp.tanh(jnp.dot(hidden, weight_hidden[depth_index], precision=HIGH)) + hidden
    return jnp.dot(hidden, weight_out, precision=HIGH)


def atom_terms(
    extended,
    neighbour_rows,
    neighbour_total,
    embed_first,
    embed_second,
    embed_third,
    energy_in,
    energy_hidden,
    energy_out,
    wannier_in,
    wannier_hidden,
    wannier_out,
):
    atom_count, slots = neighbour_rows.shape
    ghost_rows = (extended.shape[1] - atom_count) // 2
    block_size = 64
    blocks = atom_count // block_size
    present = (jnp.arange(slots, dtype=jnp.int32)[None, :] < neighbour_total[:, None]).astype(
        jnp.float32
    )
    centre_ids = (ghost_rows + jnp.arange(atom_count, dtype=jnp.int32)).reshape(blocks, block_size)
    second_weight = embed_second.T
    third_weight = embed_third.T

    def one_block(pieces):
        centre_rows, rows_block, present_block = pieces
        centre_block = extended[:3, centre_rows]
        gathered = extended[:, rows_block]
        offsets = gathered[:3] - centre_block[:, :, None]
        smooth = present_block / (1.0 + jnp.sum(offsets * offsets, axis=0))
        environment = jnp.stack(
            [smooth, smooth * offsets[0], smooth * offsets[1], smooth * offsets[2]], axis=0
        )
        kind = gathered[3][None]
        mixing = (1.0 - kind) * embed_first[0][:, None, None] + kind * embed_first[1][:, None, None]
        first = jnp.tanh(smooth[None] * mixing).reshape(embed_first.shape[1], block_size * slots)
        second = jnp.tanh(jnp.dot(second_weight, first, precision=HIGH)) + jnp.concatenate(
            [first, first], axis=0
        )
        third = jnp.tanh(jnp.dot(third_weight, second, precision=HIGH)) + jnp.concatenate(
            [second, second], axis=0
        )
        third_blocks = third.reshape(third.shape[0], block_size, slots)
        moments = jnp.einsum("kan,can->akc", third_blocks, environment, precision=HIGH) / slots
        descriptor = jnp.einsum("amc,akc->amk", moments, moments[:, :AXIS], precision=HIGH).reshape(
            block_size, -1
        )
        return (
            fitting(descriptor, energy_in, energy_hidden, energy_out),
            fitting(descriptor, wannier_in, wannier_hidden, wannier_out),
        )

    energy_short, charge_shift = lax.map(
        one_block,
        (
            centre_ids,
            neighbour_rows.reshape(blocks, block_size, slots),
            present.reshape(blocks, block_size, slots),
        ),
    )
    return (energy_short.reshape(atom_count), charge_shift.reshape(atom_count))


def green_table(first, second, third, size):

    def folded(index):
        return jnp.where(index < size // 2, index, index - size).astype(jnp.float32) * (
            2.0 * math.pi / size
        )

    kappa_x = folded(first)[:, None, None]
    kappa_y = folded(second)[None, :, None]
    kappa_z = folded(third)[None, None, :]
    squared = kappa_x * kappa_x + kappa_y * kappa_y + kappa_z * kappa_z
    root = (
        (first[:, None, None] == 0) & (second[None, :, None] == 0) & (third[None, None, :] == 0)
    ).astype(jnp.float32)
    return (1.0 - root) * jnp.exp(-0.5 * squared) / (squared + root)


def dft_tables(size):
    index = jnp.arange(size, dtype=jnp.int32)
    phase = (index[:, None] * index[None, :] % size).astype(jnp.float32) * (2.0 * math.pi / size)
    return (jnp.cos(phase), jnp.sin(phase))


def along(values, table, axis_index):
    result = jnp.tensordot(values, table, axes=([axis_index], [0]), precision=HIGH)
    return jnp.moveaxis(result, -1, axis_index)


def complex_transform(paired, axis_index, cosine, sine, inverse):
    real_part = paired[0]
    imag_part = paired[1]
    inner = axis_index - 1
    real_cos = along(real_part, cosine, inner)
    real_sin = along(real_part, sine, inner)
    imag_cos = along(imag_part, cosine, inner)
    imag_sin = along(imag_part, sine, inner)
    if inverse:
        return jnp.stack([real_cos - imag_sin, imag_cos + real_sin])
    return jnp.stack([real_cos + imag_sin, imag_cos - real_sin])


def fold_windows(values, axis_index, block, count):
    front = jnp.moveaxis(values, axis_index, 0)
    rest = front.shape[1:]
    windows = front.reshape((count, block + 3) + rest)
    main_part = windows[:, :block]
    carried = jnp.roll(windows[:, block:], 1, axis=0)
    main_part = main_part.at[:, :3].add(carried)
    return jnp.moveaxis(main_part.reshape((count * block,) + rest), 0, axis_index)


def make_windows(values, axis_index, block, count):
    front = jnp.moveaxis(values, axis_index, 0)
    rest = front.shape[1:]
    pieces = front.reshape((count, block) + rest)
    trailing = jnp.roll(pieces, -1, axis=0)[:, :3]
    windows = jnp.concatenate([pieces, trailing], axis=1)
    return jnp.moveaxis(windows.reshape((count * (block + 3),) + rest), 0, axis_index)


def spread_matrix(start, weights, width, wrap_size):
    offsets = jnp.arange(4, dtype=jnp.int32)[:, None, None]
    target = start[None, :, None] + offsets
    if wrap_size > 0:
        target = target % wrap_size
    hits = (target == jnp.arange(width, dtype=jnp.int32)[None, None, :]).astype(jnp.float32)
    return jnp.sum(weights[:, :, None] * hits, axis=0)


def per_device_general(
    positions,
    types,
    neighbours,
    neighbour_count,
    send_index,
    cell_x,
    cell_y,
    cell_z,
    spline_fraction,
    embed_first,
    embed_second,
    embed_third,
    energy_in,
    energy_hidden,
    energy_out,
    wannier_in,
    wannier_hidden,
    wannier_out,
    charge_base,
):
    atom_count = types.shape[1]
    ghost_rows = send_index.shape[1] // 2
    kind_float = types[0].astype(jnp.float32)
    own_atoms = jnp.concatenate([positions[:, 0], kind_float[None]], axis=0)
    outgoing = own_atoms[:, send_index[0]]
    padded_ghosts = with_halo(outgoing, (("brick", 1),), ghost_rows)
    extended = jnp.concatenate(
        [padded_ghosts[:, :ghost_rows], own_atoms, padded_ghosts[:, 3 * ghost_rows :]], axis=1
    )
    energy_short, charge_shift = atom_terms(
        extended,
        neighbours[0],
        neighbour_count[0],
        embed_first,
        embed_second,
        embed_third,
        energy_in,
        energy_hidden,
        energy_out,
        wannier_in,
        wannier_hidden,
        wannier_out,
    )
    charge = (1.0 - kind_float) * charge_base[0] + kind_float * charge_base[1] + charge_shift
    count_x = lax.axis_size("brick")
    count_y = lax.axis_size("slab")
    block_x = NG // count_x
    block_y = NG // count_y
    wide_x = block_x + 3
    wide_y = block_y + 3
    spread_x = spread_matrix(cell_x[0], spline_weights(spline_fraction[0, 0]), wide_x, 0)
    spread_y = spread_matrix(cell_y[0], spline_weights(spline_fraction[1, 0]), wide_y, 0)
    spread_z = spread_matrix(cell_z[0], spline_weights(spline_fraction[2, 0]), NG, NG)
    spread_xy = (spread_x[:, :, None] * spread_y[:, None, :]).reshape(atom_count, wide_x * wide_y)
    charge_grid = jnp.einsum(
        "ap,az->pz", spread_xy, charge[:, None] * spread_z, precision=HIGH
    ).reshape(wide_x, wide_y, NG)
    cosine, sine = dft_tables(NG)
    scale = 1.0 / (NG * NG * NG)
    full_index = jnp.arange(NG, dtype=jnp.int32)
    paired = jnp.stack([along(charge_grid, cosine, 2), -along(charge_grid, sine, 2)])
    moved = lax.all_to_all(paired, "slab", split_axis=3, concat_axis=2, tiled=True)
    moved = complex_transform(fold_windows(moved, 2, block_y, count_y), 2, cosine, sine, False)
    moved = lax.all_to_all(moved, "brick", split_axis=2, concat_axis=1, tiled=True)
    moved = complex_transform(fold_windows(moved, 1, block_x, count_x), 1, cosine, sine, False)
    part_y = NG // count_x
    part_z = NG // count_y
    index_y = lax.axis_index("brick") * part_y + jnp.arange(part_y, dtype=jnp.int32)
    index_z = lax.axis_index("slab") * part_z + jnp.arange(part_z, dtype=jnp.int32)
    moved = moved * (green_table(full_index, index_y, index_z, NG) * scale)[None]
    moved = make_windows(complex_transform(moved, 1, cosine, sine, True), 1, block_x, count_x)
    moved = lax.all_to_all(moved, "brick", split_axis=1, concat_axis=2, tiled=True)
    moved = make_windows(complex_transform(moved, 2, cosine, sine, True), 2, block_y, count_y)
    moved = lax.all_to_all(moved, "slab", split_axis=2, concat_axis=3, tiled=True)
    potential_wide = along(moved[0], cosine, 2) - along(moved[1], sine, 2)
    sampled = jnp.einsum(
        "ap,pz->az", spread_xy, potential_wide.reshape(wide_x * wide_y, NG), precision=HIGH
    )
    potential_at = jnp.sum(sampled * spread_z, axis=1)
    atom_energy = energy_short + 0.5 * charge * potential_at
    return (atom_energy[None, :], potential_wide[:block_x, :block_y])


def split(values):
    high = values.astype(jnp.bfloat16)
    low = (values - high.astype(jnp.float32)).astype(jnp.bfloat16)
    return high, low


def multiply(left, right, dims):
    return lax.dot_general(left, right, (dims, ((), ())), preferred_element_type=jnp.float32)


def triple(left, right, dims=((1,), (0,))):
    return (
        multiply(left[0], right[0], dims)
        + multiply(left[0], right[1], dims)
        + multiply(left[1], right[0], dims)
    )


LANES = ((1,), (1,))


def lane_pick(table, index):
    return jnp.take_along_axis(table, index, axis=1, mode="promise_in_bounds")


def full_spec(count):
    return [pl.BlockSpec(memory_space=pltpu.VMEM)] * count


def collect_kernel(
    base_ref,
    positions_ref,
    types_ref,
    count_ref,
    send_ref,
    cell_x_ref,
    cell_y_ref,
    cell_z_ref,
    fraction_ref,
    own_ref,
    outgoing_ref,
    static_ref,
):
    atoms = types_ref.shape[1]
    own_ref[...] = jnp.zeros_like(own_ref)
    static = jnp.concatenate(
        [
            (cell_x_ref[...] + base_ref[0]).astype(jnp.float32),
            cell_y_ref[...].astype(jnp.float32),
            cell_z_ref[...].astype(jnp.float32),
        ]
        + [fraction_ref[axis] for axis in range(3)]
        + [jnp.zeros((2, atoms), jnp.float32)],
        axis=0,
    )
    for copy in range(static_ref.shape[0]):
        static_ref[copy] = static
    for axis in range(3):
        own_ref[axis : axis + 1, 0:atoms] = positions_ref[axis]
    own_ref[3:4, 0:atoms] = types_ref[...].astype(jnp.float32)
    own_ref[4:5, 0:atoms] = count_ref[...].astype(jnp.float32)
    own_ref[5:6, 0:atoms] = send_ref[...].astype(jnp.float32)
    for chunk in range(2):
        lanes = slice(128 * chunk, 128 * chunk + 128)
        wanted = jnp.broadcast_to(own_ref[5:6, lanes], (8, 128)).astype(jnp.int32)
        within = wanted & 127
        outgoing_ref[:, lanes] = jnp.where(
            wanted < 128,
            lane_pick(own_ref[:, 0:128], within),
            lane_pick(own_ref[:, 128:256], within),
        )


def collect(
    copies, base, positions, types, counts, send_index, cell_x, cell_y, cell_z, fraction
):
    atoms = types.shape[1]
    return pl.pallas_call(
        collect_kernel,
        out_shape=[
            jax.ShapeDtypeStruct((8, 256), jnp.float32),
            jax.ShapeDtypeStruct((8, 256), jnp.float32),
            jax.ShapeDtypeStruct((copies, 8, atoms), jnp.float32),
        ],
        in_specs=[pl.BlockSpec(memory_space=pltpu.SMEM)] + full_spec(8),
        out_specs=full_spec(3),
        name="collect_atoms",
    )(base, positions, types, counts, send_index, cell_x, cell_y, cell_z, fraction)


def fitting_rows(descriptor_ref, weight_in_ref, weight_hidden_ref, weight_out_ref):
    depth = weight_in_ref.shape[1]
    first = depth // 256 * 256
    hidden = triple(
        split(descriptor_ref[:, 0:first]), split(weight_in_ref[:, 0:first]), LANES
    )
    if first < depth:
        hidden = hidden + triple(
            split(descriptor_ref[:, first:depth]), split(weight_in_ref[:, first:depth]), LANES
        )
    hidden = jnp.tanh(hidden)
    for layer in range(weight_hidden_ref.shape[0]):
        hidden = jnp.tanh(triple(split(hidden), split(weight_hidden_ref[layer]))) + hidden
    width = hidden.shape[1]
    out_weight = jnp.broadcast_to(weight_out_ref[...], (8, width))
    return triple(split(out_weight), split(hidden), LANES)


def natural_order(rows):
    atoms = rows.shape[1]
    padded = jnp.concatenate([rows, jnp.zeros((8, 256 - atoms), jnp.float32)], axis=1)
    pieces = []
    for chunk in range(2):
        atom = 128 * chunk + lax.broadcasted_iota(jnp.int32, (8, 128), 1)
        late = atom >= atoms // 2
        within = jnp.where(late, atom - atoms // 2, atom)
        place = 8 * (within >> 2) + (within & 3) + jnp.where(late, 4, 0)
        place = jnp.minimum(place, 255)
        pieces.append(
            jnp.where(
                place < 128,
                lane_pick(padded[:, 0:128], place & 127),
                lane_pick(padded[:, 128:256], place & 127),
            )
        )
    return jnp.concatenate(pieces, axis=1)[0:1, 0:atoms]


def network_kernel(
    ghosts,
    base_ref,
    own_ref,
    lower_ref,
    upper_ref,
    slots_ref,
    types_ref,
    first_ref,
    second_ref,
    third_ref,
    spot_ref,
    weight_in_hbm,
    weight_hidden_hbm,
    weight_out_ref,
    descriptor_ref,
    charge_ref,
    copies_ref,
    environment_ref,
    kind_ref,
    moments_ref,
    padded_ref,
    weight_in_ref,
    weight_hidden_ref,
    semaphores,
):
    fetches = [
        pltpu.make_async_copy(weight_in_hbm, weight_in_ref, semaphores.at[0]),
        pltpu.make_async_copy(weight_hidden_hbm, weight_hidden_ref, semaphores.at[1]),
    ]
    for fetch in fetches:
        fetch.start()
    slots, atoms = slots_ref.shape
    rows = atoms // 2
    lane = lax.broadcasted_iota(jnp.int32, (8, 128), 1)
    sub = lax.broadcasted_iota(jnp.int32, (8, 128), 0)

    width = first_ref.shape[1]
    padded_ref[...] = jnp.zeros_like(padded_ref)
    padded_ref[0, 0:2, 0:width] = first_ref[...]
    for column in range(2):
        padded_ref[1, 0:width, 32 * column : 32 * column + width] = second_ref[
            :, width * column : width * (column + 1)
        ]
    for row in range(2):
        for column in range(4):
            padded_ref[2, 32 * row : 32 * row + width, 32 * column : 32 * column + width] = (
                third_ref[
                    width * row : width * (row + 1), width * column : width * (column + 1)
                ]
            )
    first_table = padded_ref[0].T
    embed_zero = jnp.broadcast_to(first_table[0:32, 0:1], (32, 128))
    embed_one = jnp.broadcast_to(first_table[0:32, 1:2], (32, 128))
    second_high, second_low = split(padded_ref[1].T[0:64, 0:32])
    second_weight = jnp.concatenate([second_high, second_high, second_low], axis=1)
    third_high, third_low = split(padded_ref[2].T[:, 0:64])
    third_weight = jnp.concatenate([third_high, third_high, third_low], axis=1)

    def spread(ref, field, chunk):
        return jnp.broadcast_to(ref[field : field + 1, 128 * chunk : 128 * chunk + 128], (8, 128))

    own = [[spread(own_ref, field, chunk) for chunk in range(2)] for field in range(5)]
    lower = [[spread(lower_ref, field, chunk) for chunk in range(2)] for field in range(4)]
    upper = [spread(upper_ref, field, 0) for field in range(4)]

    def pick_two(tables, index):
        within = index & 127
        return jnp.where(index < 128, lane_pick(tables[0], within), lane_pick(tables[1], within))

    pairs = jnp.concatenate([slots_ref[:, 0:rows], slots_ref[:, rows:atoms]], axis=0).T
    for tile in range(rows // 8):
        band = slice(8 * tile, 8 * tile + 8)
        index = pairs[band, :]
        centre = 8 * tile + sub + jnp.where(lane < 64, 0, rows)
        from_own = jnp.clip(index - ghosts, 0, atoms - 1)
        from_lower = jnp.minimum(index + (atoms - ghosts), 255)
        from_upper = jnp.clip(index - (ghosts + atoms), 0, 127)

        def neighbour(field):
            below = pick_two(lower[field], from_lower)
            inside = pick_two(own[field], from_own)
            above = lane_pick(upper[field], from_upper)
            return jnp.where(
                index < ghosts, below, jnp.where(index < ghosts + atoms, inside, above)
            )

        offsets = [neighbour(field) - pick_two(own[field], centre) for field in range(3)]
        live = pick_two(own[4], centre)
        present = jnp.where((lane & 63).astype(jnp.float32) < live, 1.0, 0.0)
        smooth = present / (
            1.0 + (offsets[0] * offsets[0] + offsets[1] * offsets[1] + offsets[2] * offsets[2])
        )
        environment_ref[0, band, :] = smooth
        for field in range(3):
            environment_ref[1 + field, band, :] = smooth * offsets[field]
        kind_ref[band, :] = neighbour(3)

    group = 8

    def stacked(values):
        high, low = split(values)
        return jnp.concatenate([high, low, high], axis=0)

    def one_group(start):
        pieces = []
        for row in range(group):
            smooth = jnp.broadcast_to(environment_ref[0, pl.ds(start + row, 1), :], (32, 128))
            kind = jnp.broadcast_to(kind_ref[pl.ds(start + row, 1), :], (32, 128))
            pieces.append(
                jnp.tanh(smooth * ((1.0 - kind) * embed_zero + kind * embed_one))
            )
        first = jnp.concatenate(pieces, axis=1)
        second = jnp.tanh(multiply(second_weight, stacked(first), ((1,), (0,))))
        second = second + jnp.concatenate([first, first], axis=0)
        third = jnp.tanh(multiply(third_weight, stacked(second), ((1,), (0,))))
        third = third + jnp.concatenate([second, second], axis=0)
        third_pair = split(third)
        for half in range(group // 4):
            columns = slice(512 * half, 512 * half + 512)
            bands = []
            for part in range(4):
                bands.append(
                    jnp.concatenate(
                        [
                            jnp.where(
                                sub == row + jnp.where(lane < 64, 0, 4),
                                jnp.broadcast_to(
                                    environment_ref[part, pl.ds(start + 4 * half + row, 1), :],
                                    (8, 128),
                                ),
                                0.0,
                            )
                            for row in range(4)
                        ],
                        axis=1,
                    )
                )
            environment = split(jnp.concatenate(bands, axis=0))
            both = multiply(
                jnp.concatenate(environment, axis=0), third_pair[0][:, columns], LANES
            )
            sums = both[0:32] + both[32:64]
            sums = sums + multiply(environment[0], third_pair[1][:, columns], LANES)
            sums = sums * (1.0 / slots)
            for part in range(4):
                moments_ref[part, pl.ds(2 * start + 8 * half, 8), :] = sums[
                    8 * part : 8 * part + 8
                ]

    def body(step, carry):
        one_group(pl.multiple_of(step * 2 * group, 2 * group))
        one_group(pl.multiple_of(step * 2 * group + group, group))
        return carry

    lax.fori_loop(0, rows // (2 * group), body, 0)

    chunks = (descriptor_ref.shape[1] + 127) // 128
    last = descriptor_ref.shape[1] - 128 * (chunks - 1)

    def describe(step, carry):
        band = pl.ds(pl.multiple_of(step * 8, 8), 8)
        moments = [moments_ref[part, band, :] for part in range(4)]
        axis_part = [lane_pick(moments[part], lane & 15) for part in range(4)]
        for chunk in range(chunks):
            spot = jnp.broadcast_to(spot_ref[chunk : chunk + 1, :], (8, 128))
            total = lane_pick(moments[0], spot) * axis_part[0]
            for part in range(1, 4):
                total = total + lane_pick(moments[part], spot) * axis_part[part]
            if chunk < chunks - 1:
                descriptor_ref[band, 128 * chunk : 128 * chunk + 128] = total
            else:
                descriptor_ref[band, 128 * chunk : 128 * chunk + last] = total[:, 0:last]
        return carry

    lax.fori_loop(0, atoms // 8, describe, 0)

    for fetch in fetches:
        fetch.wait()
    shift = fitting_rows(descriptor_ref, weight_in_ref, weight_hidden_ref, weight_out_ref)
    kind = types_ref[...].astype(jnp.float32)
    charge = (1.0 - kind) * base_ref[0] + kind * base_ref[1] + natural_order(shift)
    charge_ref[...] = charge
    for copy in range(copies_ref.shape[0]):
        copies_ref[copy] = charge


def spot_table(embed, desc):
    column = np.arange(desc) // AXIS
    quarter = embed // 4
    place = 32 * (column // quarter) + column % quarter
    chunks = (desc + 127) // 128
    table = np.zeros((chunks * 128,), np.int32)
    table[:desc] = place
    padded = np.zeros(((chunks + 7) // 8 * 8, 128), np.int32)
    padded[:chunks] = table.reshape(chunks, 128)
    return padded


def networks(
    copies,
    ghosts,
    charge_base,
    own,
    lower,
    upper,
    neighbours,
    types,
    embed_first,
    embed_second,
    embed_third,
    weight_in,
    weight_hidden,
    weight_out,
):
    atoms = types.shape[1]
    desc, width = weight_in.shape
    spots = jnp.asarray(spot_table(embed_third.shape[1], desc))
    anywhere = pl.BlockSpec(memory_space=pl.ANY)
    return pl.pallas_call(
        functools.partial(network_kernel, ghosts),
        out_shape=[
            jax.ShapeDtypeStruct((atoms, desc), jnp.float32),
            jax.ShapeDtypeStruct((1, atoms), jnp.float32),
            jax.ShapeDtypeStruct((copies, 1, atoms), jnp.float32),
        ],
        in_specs=[pl.BlockSpec(memory_space=pltpu.SMEM)]
        + full_spec(9)
        + [anywhere, anywhere]
        + full_spec(1),
        out_specs=full_spec(3),
        scratch_shapes=[
            pltpu.VMEM((4, atoms // 2, 128), jnp.float32),
            pltpu.VMEM((atoms // 2, 128), jnp.float32),
            pltpu.VMEM((4, atoms, 128), jnp.float32),
            pltpu.VMEM((3, 128, 128), jnp.float32),
            pltpu.VMEM((width, desc), jnp.float32),
            pltpu.VMEM(weight_hidden.shape, jnp.float32),
            pltpu.SemaphoreType.DMA((2,)),
        ],
        compiler_params=pltpu.CompilerParams(vmem_limit_bytes=32 * 2**20),
        name="networks",
    )(
        charge_base,
        own,
        lower,
        upper,
        neighbours[0].T,
        types,
        embed_first,
        embed_second,
        embed_third,
        spots,
        weight_in.T,
        weight_hidden,
        weight_out.reshape(1, -1),
    )


def energy_kernel(descriptor_ref, weight_in_ref, weight_hidden_ref, weight_out_ref, energy_ref):
    energy_ref[...] = natural_order(
        fitting_rows(descriptor_ref, weight_in_ref, weight_hidden_ref, weight_out_ref)
    )


def energies(descriptor, weight_in, weight_hidden, weight_out):
    atoms, desc = descriptor.shape
    width = weight_in.shape[1]
    return pl.pallas_call(
        energy_kernel,
        out_shape=jax.ShapeDtypeStruct((1, atoms), jnp.float32),
        in_specs=full_spec(4),
        out_specs=pl.BlockSpec(memory_space=pltpu.VMEM),
        compiler_params=pltpu.CompilerParams(vmem_limit_bytes=32 * 2**20),
        cost_estimate=pl.CostEstimate(
            flops=6 * atoms * desc * width, bytes_accessed=4 * desc * width, transcendentals=0
        ),
        name="energies",
    )(descriptor, weight_in.T, weight_hidden, weight_out.reshape(1, -1))


def weight_rows(fraction):
    square = fraction * fraction
    cubed = square * fraction
    rest = 1.0 - fraction
    return [
        rest * rest * rest / 6.0,
        (3.0 * cubed - 6.0 * square + 4.0) / 6.0,
        (-3.0 * cubed + 3.0 * square + 3.0 * fraction + 1.0) / 6.0,
        cubed / 6.0,
    ]


def placed_weights(distance, weights):
    shape = distance.shape
    result = jnp.zeros(shape, jnp.float32)
    for step in range(4):
        result = jnp.where(
            distance == step, jnp.broadcast_to(weights[step], shape), result
        )
    return result


def atom_factors(fields, waves_ref, cosine_ref, window, scale):
    row = lambda field: fields[field : field + 1, :]
    atoms = fields.shape[1]
    start_x = row(0).astype(jnp.int32)
    start_y = row(1).astype(jnp.int32)
    start_z = row(2).astype(jnp.int32)
    along_x = weight_rows(row(3))
    along_y = weight_rows(row(4))
    along_z = weight_rows(row(5))
    if scale is not None:
        along_x = [weight * scale for weight in along_x]
    rows_x = lax.broadcasted_iota(jnp.int32, (NG, atoms), 0)
    table_x = placed_weights((rows_x - start_x) & (NG - 1), along_x)
    rows_y = lax.broadcasted_iota(jnp.int32, (window, atoms), 0)
    table_y = placed_weights(rows_y - start_y, along_y)
    parts = waves_ref.shape[0]
    cosine = jnp.broadcast_to(cosine_ref[...], (parts, 128))
    wave = jnp.broadcast_to(waves_ref[:, 0:1], (parts, 128))
    shift = jnp.broadcast_to(waves_ref[:, 1:2], (parts, 128))
    pieces = []
    for chunk in range(atoms // 128):
        lanes = slice(128 * chunk, 128 * chunk + 128)
        total = jnp.zeros((parts, 128), jnp.float32)
        for step in range(4):
            place = jnp.broadcast_to(start_z[:, lanes] + step, (parts, 128))
            phase = (wave * place + shift) & (NG - 1)
            value = lane_pick(cosine, phase & 127)
            value = jnp.where(phase < 128, value, -value)
            total = total + value * jnp.broadcast_to(along_z[step][:, lanes], (parts, 128))
        pieces.append(total)
    table_z = jnp.concatenate(pieces, axis=1)
    table_yz = jnp.concatenate(
        [table_y * table_z[part : part + 1, :] for part in range(parts)], axis=0
    )
    return table_x, table_yz


def wave_of(index):
    return jnp.where(index <= NG // 2, index, index - NG // 2)


def solve_kernel(
    block_x,
    block_y,
    window,
    kappa_ref,
    static_ref,
    charge_ref,
    waves_ref,
    cosine_ref,
    tables_hbm,
    sent_ref,
    half_ref,
    atoms_ref,
    grid_ref,
    tables_ref,
    semaphore,
):
    slabs = atoms_ref.shape[0]
    parts = waves_ref.shape[0]
    bricks = NG // block_x
    block = static_ref.shape[2]
    step = pl.program_id(0)

    @pl.when(step == 0)
    def _():
        fetch = pltpu.make_async_copy(tables_hbm, tables_ref, semaphore)
        fetch.start()
        for slab in range(slabs):
            for brick in range(bricks):
                lanes = slice(block * brick, block * (brick + 1))
                atoms_ref[slab, :, lanes] = static_ref[slab * bricks + brick]
                atoms_ref[slab, 6:7, lanes] = charge_ref[slab * bricks + brick]
        grid_ref[...] = jnp.zeros_like(grid_ref)
        for slab in range(slabs):
            fields = atoms_ref[slab]
            table_x, table_yz = atom_factors(
                fields, waves_ref, cosine_ref, window, fields[6:7, :]
            )
            spread = triple(split(table_yz), split(table_x), LANES)
            rows = slice(slab * block_y, slab * block_y + window)
            for part in range(parts):
                grid_ref[part, rows, :] += spread[part * window : part * window + window]
        extra = window - block_y
        for part in range(parts):
            grid_ref[part, 0:extra, :] += grid_ref[part, NG : NG + extra, :]
        fetch.wait()

    basis = (tables_ref[0], tables_ref[1])
    turned = (tables_ref[2], tables_ref[3])
    swapped = (tables_ref[4], tables_ref[5])
    index_x = lax.broadcasted_iota(jnp.int32, (NG, 1), 0)
    index_y = lax.broadcasted_iota(jnp.int32, (1, NG), 1)

    def factors(index):
        kappa = wave_of(index).astype(jnp.float32) * (2.0 * math.pi / NG)
        squared = kappa * kappa
        ends = (index == 0) | (index == NG // 2)
        return squared, jnp.exp(-0.5 * squared) * jnp.where(ends, 1.0 / NG, 2.0 / NG)

    square_x, damp_x = factors(index_x)
    square_y, damp_y = factors(index_y)
    square_xy = square_x + square_y
    damp_xy = damp_x * damp_y

    first = jnp.concatenate(
        [
            triple(basis, split(grid_ref[2 * step + part, 0:NG, :]), LANES)
            for part in range(2)
        ],
        axis=0,
    )
    both = triple(split(first), turned)
    scaled = []
    for part in range(2):
        squared = square_xy + kappa_ref[2 * step + part, 0]
        root = jnp.where(squared == 0.0, 1.0, 0.0)
        green = (1.0 - root) * (damp_xy * kappa_ref[2 * step + part, 1]) / (squared + root)
        scaled.append(both[NG * part : NG * (part + 1)] * green)
    back = triple(turned, split(jnp.concatenate(scaled, axis=1)))
    halves = [back[:, 0:NG], back[:, NG:]]
    for part in range(2):
        half_ref[part] = halves[part]
    full = [triple(split(halves[0]), basis), triple(split(halves[1]), swapped)]
    low_lanes = lax.broadcasted_iota(jnp.int32, (block_x, 128), 1) < block_y
    for brick in range(bricks):
        rows = slice(block_x * brick, block_x * (brick + 1))
        for slab in range(0, slabs, 2):
            lanes = slice(block_y * slab, block_y * slab + 128)
            here = [values[rows, lanes] for values in full]
            sent_ref[brick * slabs + slab, 0] = jnp.where(low_lanes, here[0], here[1])
            sent_ref[brick * slabs + slab + 1, 0] = jnp.where(low_lanes, here[1], here[0])


def solve(block_x, block_y, window, kappa, static, charge, waves, cosine_row, tables):
    devices, _, atoms = static.shape
    slabs = NG // block_y
    bricks = NG // block_x
    parts = waves.shape[0]
    whole = lambda shape: pl.BlockSpec(shape, lambda step: (0,) * len(shape))
    return pl.pallas_call(
        functools.partial(solve_kernel, block_x, block_y, window),
        grid=(parts // 2,),
        out_shape=[
            jax.ShapeDtypeStruct((devices, parts // 2, block_x, 128), jnp.float32),
            jax.ShapeDtypeStruct((parts, NG, NG), jnp.float32),
            jax.ShapeDtypeStruct((slabs, 8, bricks * atoms), jnp.float32),
        ],
        in_specs=[
            pl.BlockSpec(memory_space=pltpu.SMEM),
            whole(static.shape),
            whole(charge.shape),
            whole(waves.shape),
            whole(cosine_row.shape),
            pl.BlockSpec(memory_space=pl.ANY),
        ],
        out_specs=[
            pl.BlockSpec((devices, 1, block_x, 128), lambda step: (0, step, 0, 0)),
            pl.BlockSpec((2, NG, NG), lambda step: (step, 0, 0)),
            whole((slabs, 8, bricks * atoms)),
        ],
        scratch_shapes=[
            pltpu.VMEM((parts, NG + window - block_y, NG), jnp.float32),
            pltpu.VMEM(tables.shape, tables.dtype),
            pltpu.SemaphoreType.DMA,
        ],
        compiler_params=pltpu.CompilerParams(vmem_limit_bytes=48 * 2**20),
        name="solve",
    )(kappa, static, charge, waves, cosine_row, tables)


def sample_kernel(window, atoms_ref, waves_ref, cosine_ref, half_ref, table_ref, out_ref):
    slabs = atoms_ref.shape[0]
    parts = waves_ref.shape[0]
    bricks = out_ref.shape[0] // slabs
    block = out_ref.shape[2]
    table = (table_ref[0], table_ref[1])
    planes = [triple(table, split(half_ref[part]), LANES) for part in range(parts)]
    for slab in range(slabs):
        table_x, table_yz = atom_factors(
            atoms_ref[slab], waves_ref, cosine_ref, window, None
        )
        rows = slice(window * slab, window * (slab + 1))
        values = jnp.concatenate([plane[rows] for plane in planes], axis=0)
        along = triple(split(values), split(table_x))
        sums = jnp.sum(along * table_yz, axis=0, keepdims=True)
        for brick in range(bricks):
            out_ref[slab * bricks + brick] = sums[:, block * brick : block * (brick + 1)]


def sample(block, window, atoms, waves, cosine_row, half, table):
    slabs, _, row_atoms = atoms.shape
    parts = waves.shape[0]
    return pl.pallas_call(
        functools.partial(sample_kernel, window),
        out_shape=jax.ShapeDtypeStruct((slabs * row_atoms // block, 1, block), jnp.float32),
        in_specs=full_spec(5),
        out_specs=pl.BlockSpec(memory_space=pltpu.VMEM),
        compiler_params=pltpu.CompilerParams(vmem_limit_bytes=48 * 2**20),
        cost_estimate=pl.CostEstimate(
            flops=6 * slabs * row_atoms * parts * window * NG,
            bytes_accessed=4 * half.size,
            transcendentals=0,
        ),
        name="sample",
    )(atoms, waves, cosine_row, half, table)


def finish_kernel(block_y, got_ref, table_ref, out_ref):
    table = (table_ref[0], table_ref[1])
    rows = []
    for line in range(got_ref.shape[1]):
        turned = got_ref[:, line, :].T
        rows.append(jnp.concatenate([turned[0:block_y], turned[block_y:]], axis=1))
    result = triple(split(jnp.concatenate(rows, axis=0)), table)
    for line in range(got_ref.shape[1]):
        out_ref[line] = result[block_y * line : block_y * (line + 1)]


def finish(block_x, block_y, got, table):
    step = 8
    return pl.pallas_call(
        functools.partial(finish_kernel, block_y),
        grid=(block_x // step,),
        out_shape=jax.ShapeDtypeStruct((block_x, block_y, NG), jnp.float32),
        in_specs=[
            pl.BlockSpec((NG // 2, step, 128), lambda index: (0, index, 0)),
            pl.BlockSpec((2, NG, NG), lambda index: (0, 0, 0)),
        ],
        out_specs=pl.BlockSpec((step, block_y, NG), lambda index: (index, 0, 0)),
        compiler_params=pltpu.CompilerParams(vmem_limit_bytes=32 * 2**20),
        name="finish",
    )(got, table)


def two_parts(table):
    table = np.asarray(table, np.float32)
    high = table.astype(ml_dtypes.bfloat16)
    low = (table - high.astype(np.float32)).astype(ml_dtypes.bfloat16)
    return np.stack([high, low])


def real_basis():
    index = np.arange(NG)
    wave = np.where(index <= NG // 2, index, index - NG // 2)
    angle = (wave[:, None] * index[None, :] % NG) * (2.0 * math.pi / NG)
    return np.where((index <= NG // 2)[:, None], np.cos(angle), np.sin(angle))


def per_device(
    positions,
    types,
    neighbours,
    neighbour_count,
    send_index,
    cell_x,
    cell_y,
    cell_z,
    spline_fraction,
    embed_first,
    embed_second,
    embed_third,
    energy_in,
    energy_hidden,
    energy_out,
    wannier_in,
    wannier_hidden,
    wannier_out,
    charge_base,
):
    atoms = types.shape[1]
    ghosts = send_index.shape[1] // 2
    count_x = lax.axis_size("brick")
    count_y = lax.axis_size("slab")
    devices = count_x * count_y
    block_x = NG // count_x
    block_y = NG // count_y
    window = block_y + 8
    parts = NG // devices
    brick = lax.axis_index("brick")
    slab = lax.axis_index("slab")

    def exchange(values, axes):
        return lax.all_to_all(values, axes, split_axis=0, concat_axis=0, tiled=True)

    own, outgoing, static = collect(
        devices,
        (brick * block_x).astype(jnp.int32).reshape(1),
        positions,
        types,
        neighbour_count,
        send_index,
        cell_x,
        cell_y,
        cell_z,
        spline_fraction,
    )
    up = [(i, (i + 1) % count_x) for i in range(count_x)]
    down = [((i + 1) % count_x, i) for i in range(count_x)]
    lower = lax.ppermute(outgoing, "brick", up)
    upper = lax.ppermute(outgoing, "brick", down)
    static = exchange(static, ("slab", "brick"))

    descriptor, charge, charge_copies = networks(
        devices,
        ghosts,
        charge_base,
        own,
        lower,
        upper,
        neighbours,
        types,
        embed_first,
        embed_second,
        embed_third,
        wannier_in,
        wannier_hidden,
        wannier_out,
    )
    every_charge = exchange(charge_copies, ("slab", "brick"))

    part = (brick * count_y + slab) * parts + jnp.arange(parts, dtype=jnp.int32)
    wave = wave_of(part)
    waves = jnp.stack([wave, jnp.where(part <= NG // 2, 0, 3 * NG // 4)], axis=1)
    kappa = wave.astype(jnp.float32) * (2.0 * math.pi / NG)
    squared = kappa * kappa
    ends = (part == 0) | (part == NG // 2)
    kappa = jnp.stack(
        [squared, jnp.exp(-0.5 * squared) * jnp.where(ends, 1.0 / NG, 2.0 / NG)], axis=1
    )
    basis = real_basis()
    swapped = basis.reshape(NG, -1, 2, block_y)[:, :, ::-1].reshape(NG, NG)
    tables = np.concatenate([two_parts(basis), two_parts(basis.T), two_parts(swapped)])
    cosine_row = np.cos(np.arange(128) * (2.0 * math.pi / NG)).astype(np.float32)[None]
    sent, half, every_atom = solve(
        block_x,
        block_y,
        window,
        kappa,
        static,
        every_charge,
        waves,
        jnp.asarray(cosine_row),
        jnp.asarray(tables),
    )
    got = exchange(sent.reshape(devices, -1, 128), ("brick", "slab"))
    points = (np.arange(count_y)[:, None] * block_y + np.arange(window)[None, :]) % NG
    partial = sample(
        atoms,
        window,
        every_atom,
        waves,
        jnp.asarray(cosine_row),
        half,
        jnp.asarray(two_parts(basis.T[points.reshape(-1)])),
    )
    energy_short = energies(descriptor, energy_in, energy_hidden, energy_out)
    potential_at = jnp.sum(exchange(partial, ("slab", "brick")), axis=0)
    atom_energy = energy_short + 0.5 * charge * potential_at
    pairs = basis.reshape(-1, 2, NG).transpose(1, 0, 2)
    ordered = np.stack([two_parts(pairs.reshape(NG, NG)), two_parts(pairs[::-1].reshape(NG, NG))])
    potential = finish(
        block_x,
        block_y,
        got.reshape(NG // 2, block_x, 128),
        lax.dynamic_index_in_dim(jnp.asarray(ordered), slab % 2, 0, keepdims=False),
    )
    return atom_energy, potential


def solution(mesh):
    placed = (
        P(None, "slab", "brick"),
        P("slab", "brick"),
        P("slab", "brick", None),
        P("slab", "brick"),
        P("slab", "brick"),
        P("slab", "brick"),
        P("slab", "brick"),
        P("slab", "brick"),
        P(None, "slab", "brick"),
    ) + (P(),) * 10
    fits = 2 * (NG // mesh.shape["slab"]) == 128 and (NG // 2) % mesh.size == 0
    return jax.shard_map(
        per_device if fits else per_device_general,
        mesh=mesh,
        in_specs=placed,
        out_specs=(P("slab", "brick"), P("brick", "slab", None)),
        check_vma=False,
    )
```

```python
import functools
import math

import jax
import jax.numpy as jnp
import ml_dtypes
import numpy as np
from jax import lax
from jax.experimental import pallas as pl
from jax.experimental.pallas import tpu as pltpu
from jax.sharding import PartitionSpec as P

NG = 256
AXIS = 16


HIGH = lax.Precision.HIGHEST


def with_halo(cells, sides, width):
    for axis, dim in sides:
        count = lax.axis_size(axis)
        head = lax.slice_in_dim(cells, 0, width, axis=dim)
        tail = lax.slice_in_dim(cells, cells.shape[dim] - width, cells.shape[dim], axis=dim)
        cells = jnp.concatenate(
            [
                lax.ppermute(tail, axis, [(i, (i + 1) % count) for i in range(count)]),
                cells,
                lax.ppermute(head, axis, [((i + 1) % count, i) for i in range(count)]),
            ],
            axis=dim,
        )
    return cells


def spline_weights(fraction):
    cubed = fraction * fraction * fraction
    square = fraction * fraction
    return jnp.stack(
        [
            (1.0 - fraction) * (1.0 - fraction) * (1.0 - fraction) / 6.0,
            (3.0 * cubed - 6.0 * square + 4.0) / 6.0,
            (-3.0 * cubed + 3.0 * square + 3.0 * fraction + 1.0) / 6.0,
            cubed / 6.0,
        ]
    )


def fitting(descriptor, weight_in, weight_hidden, weight_out):
    hidden = jnp.tanh(jnp.dot(descriptor, weight_in, precision=HIGH))
    for depth_index in range(weight_hidden.shape[0]):
        hidden = jnp.tanh(jnp.dot(hidden, weight_hidden[depth_index], precision=HIGH)) + hidden
    return jnp.dot(hidden, weight_out, precision=HIGH)


def atom_terms(
    extended,
    neighbour_rows,
    neighbour_total,
    embed_first,
    embed_second,
    embed_third,
    energy_in,
    energy_hidden,
    energy_out,
    wannier_in,
    wannier_hidden,
    wannier_out,
):
    atom_count, slots = neighbour_rows.shape
    ghost_rows = (extended.shape[1] - atom_count) // 2
    block_size = 64
    blocks = atom_count // block_size
    present = (jnp.arange(slots, dtype=jnp.int32)[None, :] < neighbour_total[:, None]).astype(
        jnp.float32
    )
    centre_ids = (ghost_rows + jnp.arange(atom_count, dtype=jnp.int32)).reshape(blocks, block_size)
    second_weight = embed_second.T
    third_weight = embed_third.T

    def one_block(pieces):
        centre_rows, rows_block, present_block = pieces
        centre_block = extended[:3, centre_rows]
        gathered = extended[:, rows_block]
        offsets = gathered[:3] - centre_block[:, :, None]
        smooth = present_block / (1.0 + jnp.sum(offsets * offsets, axis=0))
        environment = jnp.stack(
            [smooth, smooth * offsets[0], smooth * offsets[1], smooth * offsets[2]], axis=0
        )
        kind = gathered[3][None]
        mixing = (1.0 - kind) * embed_first[0][:, None, None] + kind * embed_first[1][:, None, None]
        first = jnp.tanh(smooth[None] * mixing).reshape(embed_first.shape[1], block_size * slots)
        second = jnp.tanh(jnp.dot(second_weight, first, precision=HIGH)) + jnp.concatenate(
            [first, first], axis=0
        )
        third = jnp.tanh(jnp.dot(third_weight, second, precision=HIGH)) + jnp.concatenate(
            [second, second], axis=0
        )
        third_blocks = third.reshape(third.shape[0], block_size, slots)
        moments = jnp.einsum("kan,can->akc", third_blocks, environment, precision=HIGH) / slots
        descriptor = jnp.einsum("amc,akc->amk", moments, moments[:, :AXIS], precision=HIGH).reshape(
            block_size, -1
        )
        return (
            fitting(descriptor, energy_in, energy_hidden, energy_out),
            fitting(descriptor, wannier_in, wannier_hidden, wannier_out),
        )

    energy_short, charge_shift = lax.map(
        one_block,
        (
            centre_ids,
            neighbour_rows.reshape(blocks, block_size, slots),
            present.reshape(blocks, block_size, slots),
        ),
    )
    return (energy_short.reshape(atom_count), charge_shift.reshape(atom_count))


def green_table(first, second, third, size):

    def folded(index):
        return jnp.where(index < size // 2, index, index - size).astype(jnp.float32) * (
            2.0 * math.pi / size
        )

    kappa_x = folded(first)[:, None, None]
    kappa_y = folded(second)[None, :, None]
    kappa_z = folded(third)[None, None, :]
    squared = kappa_x * kappa_x + kappa_y * kappa_y + kappa_z * kappa_z
    root = (
        (first[:, None, None] == 0) & (second[None, :, None] == 0) & (third[None, None, :] == 0)
    ).astype(jnp.float32)
    return (1.0 - root) * jnp.exp(-0.5 * squared) / (squared + root)


def dft_tables(size):
    index = jnp.arange(size, dtype=jnp.int32)
    phase = (index[:, None] * index[None, :] % size).astype(jnp.float32) * (2.0 * math.pi / size)
    return (jnp.cos(phase), jnp.sin(phase))


def along(values, table, axis_index):
    result = jnp.tensordot(values, table, axes=([axis_index], [0]), precision=HIGH)
    return jnp.moveaxis(result, -1, axis_index)


def complex_transform(paired, axis_index, cosine, sine, inverse):
    real_part = paired[0]
    imag_part = paired[1]
    inner = axis_index - 1
    real_cos = along(real_part, cosine, inner)
    real_sin = along(real_part, sine, inner)
    imag_cos = along(imag_part, cosine, inner)
    imag_sin = along(imag_part, sine, inner)
    if inverse:
        return jnp.stack([real_cos - imag_sin, imag_cos + real_sin])
    return jnp.stack([real_cos + imag_sin, imag_cos - real_sin])


def fold_windows(values, axis_index, block, count):
    front = jnp.moveaxis(values, axis_index, 0)
    rest = front.shape[1:]
    windows = front.reshape((count, block + 3) + rest)
    main_part = windows[:, :block]
    carried = jnp.roll(windows[:, block:], 1, axis=0)
    main_part = main_part.at[:, :3].add(carried)
    return jnp.moveaxis(main_part.reshape((count * block,) + rest), 0, axis_index)


def make_windows(values, axis_index, block, count):
    front = jnp.moveaxis(values, axis_index, 0)
    rest = front.shape[1:]
    pieces = front.reshape((count, block) + rest)
    trailing = jnp.roll(pieces, -1, axis=0)[:, :3]
    windows = jnp.concatenate([pieces, trailing], axis=1)
    return jnp.moveaxis(windows.reshape((count * (block + 3),) + rest), 0, axis_index)


def spread_matrix(start, weights, width, wrap_size):
    offsets = jnp.arange(4, dtype=jnp.int32)[:, None, None]
    target = start[None, :, None] + offsets
    if wrap_size > 0:
        target = target % wrap_size
    hits = (target == jnp.arange(width, dtype=jnp.int32)[None, None, :]).astype(jnp.float32)
    return jnp.sum(weights[:, :, None] * hits, axis=0)


def per_device_general(
    positions,
    types,
    neighbours,
    neighbour_count,
    send_index,
    cell_x,
    cell_y,
    cell_z,
    spline_fraction,
    embed_first,
    embed_second,
    embed_third,
    energy_in,
    energy_hidden,
    energy_out,
    wannier_in,
    wannier_hidden,
    wannier_out,
    charge_base,
):
    atom_count = types.shape[1]
    ghost_rows = send_index.shape[1] // 2
    kind_float = types[0].astype(jnp.float32)
    own_atoms = jnp.concatenate([positions[:, 0], kind_float[None]], axis=0)
    outgoing = own_atoms[:, send_index[0]]
    padded_ghosts = with_halo(outgoing, (("brick", 1),), ghost_rows)
    extended = jnp.concatenate(
        [padded_ghosts[:, :ghost_rows], own_atoms, padded_ghosts[:, 3 * ghost_rows :]], axis=1
    )
    energy_short, charge_shift = atom_terms(
        extended,
        neighbours[0],
        neighbour_count[0],
        embed_first,
        embed_second,
        embed_third,
        energy_in,
        energy_hidden,
        energy_out,
        wannier_in,
        wannier_hidden,
        wannier_out,
    )
    charge = (1.0 - kind_float) * charge_base[0] + kind_float * charge_base[1] + charge_shift
    count_x = lax.axis_size("brick")
    count_y = lax.axis_size("slab")
    block_x = NG // count_x
    block_y = NG // count_y
    wide_x = block_x + 3
    wide_y = block_y + 3
    spread_x = spread_matrix(cell_x[0], spline_weights(spline_fraction[0, 0]), wide_x, 0)
    spread_y = spread_matrix(cell_y[0], spline_weights(spline_fraction[1, 0]), wide_y, 0)
    spread_z = spread_matrix(cell_z[0], spline_weights(spline_fraction[2, 0]), NG, NG)
    spread_xy = (spread_x[:, :, None] * spread_y[:, None, :]).reshape(atom_count, wide_x * wide_y)
    charge_grid = jnp.einsum(
        "ap,az->pz", spread_xy, charge[:, None] * spread_z, precision=HIGH
    ).reshape(wide_x, wide_y, NG)
    cosine, sine = dft_tables(NG)
    scale = 1.0 / (NG * NG * NG)
    full_index = jnp.arange(NG, dtype=jnp.int32)
    paired = jnp.stack([along(charge_grid, cosine, 2), -along(charge_grid, sine, 2)])
    moved = lax.all_to_all(paired, "slab", split_axis=3, concat_axis=2, tiled=True)
    moved = complex_transform(fold_windows(moved, 2, block_y, count_y), 2, cosine, sine, False)
    moved = lax.all_to_all(moved, "brick", split_axis=2, concat_axis=1, tiled=True)
    moved = complex_transform(fold_windows(moved, 1, block_x, count_x), 1, cosine, sine, False)
    part_y = NG // count_x
    part_z = NG // count_y
    index_y = lax.axis_index("brick") * part_y + jnp.arange(part_y, dtype=jnp.int32)
    index_z = lax.axis_index("slab") * part_z + jnp.arange(part_z, dtype=jnp.int32)
    moved = moved * (green_table(full_index, index_y, index_z, NG) * scale)[None]
    moved = make_windows(complex_transform(moved, 1, cosine, sine, True), 1, block_x, count_x)
    moved = lax.all_to_all(moved, "brick", split_axis=1, concat_axis=2, tiled=True)
    moved = make_windows(complex_transform(moved, 2, cosine, sine, True), 2, block_y, count_y)
    moved = lax.all_to_all(moved, "slab", split_axis=2, concat_axis=3, tiled=True)
    potential_wide = along(moved[0], cosine, 2) - along(moved[1], sine, 2)
    sampled = jnp.einsum(
        "ap,pz->az", spread_xy, potential_wide.reshape(wide_x * wide_y, NG), precision=HIGH
    )
    potential_at = jnp.sum(sampled * spread_z, axis=1)
    atom_energy = energy_short + 0.5 * charge * potential_at
    return (atom_energy[None, :], potential_wide[:block_x, :block_y])


def split(values):
    high = values.astype(jnp.bfloat16)
    low = (values - high.astype(jnp.float32)).astype(jnp.bfloat16)
    return high, low


def multiply(left, right, dims):
    return lax.dot_general(left, right, (dims, ((), ())), preferred_element_type=jnp.float32)


def triple(left, right, dims=((1,), (0,))):
    return (
        multiply(left[0], right[0], dims)
        + multiply(left[0], right[1], dims)
        + multiply(left[1], right[0], dims)
    )


LANES = ((1,), (1,))


def lane_pick(table, index):
    return jnp.take_along_axis(table, index, axis=1, mode="promise_in_bounds")


def whole(shape):
    return pl.BlockSpec(tuple(shape), lambda step: (0,) * len(shape))


def whole_specs(*arrays):
    return [whole(array.shape) for array in arrays]


def collect_kernel(
    positions_ref, types_ref, count_ref, send_ref, own_ref, outgoing_ref
):
    atoms = types_ref.shape[1]
    own_ref[...] = jnp.zeros_like(own_ref)
    for axis in range(3):
        own_ref[axis : axis + 1, 0:atoms] = positions_ref[axis]
    own_ref[3:4, 0:atoms] = types_ref[...].astype(jnp.float32)
    own_ref[4:5, 0:atoms] = count_ref[...].astype(jnp.float32)
    own_ref[5:6, 0:atoms] = send_ref[...].astype(jnp.float32)
    for chunk in range(2):
        lanes = slice(128 * chunk, 128 * chunk + 128)
        wanted = jnp.broadcast_to(own_ref[5:6, lanes], (8, 128)).astype(jnp.int32)
        within = wanted & 127
        outgoing_ref[:, lanes] = jnp.where(
            wanted < 128,
            lane_pick(own_ref[:, 0:128], within),
            lane_pick(own_ref[:, 128:256], within),
        )


def collect(positions, types, counts, send_index):
    arrays = (positions, types, counts, send_index)
    result = jax.ShapeDtypeStruct((8, 256), jnp.float32)
    return pl.pallas_call(
        collect_kernel,
        grid=(1,),
        out_shape=[result, result],
        in_specs=whole_specs(*arrays),
        out_specs=whole_specs(result, result),
        name="collect_atoms",
    )(*arrays)


def fitting_rows(descriptor_ref, weight_in_ref, weight_hidden_ref, weight_out_ref):
    depth = weight_in_ref.shape[1]
    first = depth // 256 * 256
    hidden = triple(
        split(descriptor_ref[:, 0:first]), split(weight_in_ref[:, 0:first]), LANES
    )
    if first < depth:
        hidden = hidden + triple(
            split(descriptor_ref[:, first:depth]), split(weight_in_ref[:, first:depth]), LANES
        )
    hidden = jnp.tanh(hidden)
    for layer in range(weight_hidden_ref.shape[0]):
        hidden = jnp.tanh(triple(split(hidden), split(weight_hidden_ref[layer]))) + hidden
    width = hidden.shape[1]
    out_weight = jnp.broadcast_to(weight_out_ref[...], (8, width))
    return triple(split(out_weight), split(hidden), LANES)


def natural_order(rows):
    atoms = rows.shape[1]
    padded = jnp.concatenate([rows, jnp.zeros((8, 256 - atoms), jnp.float32)], axis=1)
    pieces = []
    for chunk in range(2):
        atom = 128 * chunk + lax.broadcasted_iota(jnp.int32, (8, 128), 1)
        late = atom >= atoms // 2
        within = jnp.where(late, atom - atoms // 2, atom)
        place = 8 * (within >> 2) + (within & 3) + jnp.where(late, 4, 0)
        place = jnp.minimum(place, 255)
        pieces.append(
            jnp.where(
                place < 128,
                lane_pick(padded[:, 0:128], place & 127),
                lane_pick(padded[:, 128:256], place & 127),
            )
        )
    return jnp.concatenate(pieces, axis=1)[0:1, 0:atoms]


def network_kernel(
    ghosts,
    base_ref,
    charges_ref,
    own_ref,
    lower_ref,
    upper_ref,
    slots_ref,
    types_ref,
    cell_x_ref,
    cell_y_ref,
    cell_z_ref,
    fraction_ref,
    first_ref,
    second_ref,
    third_ref,
    spot_ref,
    weight_in_hbm,
    weight_hidden_hbm,
    weight_out_ref,
    descriptor_hbm,
    charge_ref,
    copies_ref,
    descriptor_ref,
    environment_ref,
    kind_ref,
    moments_ref,
    padded_ref,
    weight_in_ref,
    weight_hidden_ref,
    semaphores,
):
    fetches = [
        pltpu.make_async_copy(weight_in_hbm, weight_in_ref, semaphores.at[0]),
        pltpu.make_async_copy(weight_hidden_hbm, weight_hidden_ref, semaphores.at[1]),
    ]
    for fetch in fetches:
        fetch.start()
    slots, atoms = slots_ref.shape
    rows = atoms // 2
    lane = lax.broadcasted_iota(jnp.int32, (8, 128), 1)
    sub = lax.broadcasted_iota(jnp.int32, (8, 128), 0)

    width = first_ref.shape[1]
    padded_ref[...] = jnp.zeros_like(padded_ref)
    padded_ref[0, 0:2, 0:width] = first_ref[...]
    for column in range(2):
        padded_ref[1, 0:width, 32 * column : 32 * column + width] = second_ref[
            :, width * column : width * (column + 1)
        ]
    for row in range(2):
        for column in range(4):
            padded_ref[2, 32 * row : 32 * row + width, 32 * column : 32 * column + width] = (
                third_ref[
                    width * row : width * (row + 1), width * column : width * (column + 1)
                ]
            )
    first_table = padded_ref[0].T
    embed_zero = jnp.broadcast_to(first_table[0:32, 0:1], (32, 128))
    embed_one = jnp.broadcast_to(first_table[0:32, 1:2], (32, 128))
    second_high, second_low = split(padded_ref[1].T[0:64, 0:32])
    second_weight = jnp.concatenate([second_high, second_high, second_low], axis=1)
    third_high, third_low = split(padded_ref[2].T[:, 0:64])
    third_weight = jnp.concatenate([third_high, third_high, third_low], axis=1)

    def spread(ref, field, chunk):
        return jnp.broadcast_to(ref[field : field + 1, 128 * chunk : 128 * chunk + 128], (8, 128))

    own = [[spread(own_ref, field, chunk) for chunk in range(2)] for field in range(5)]
    lower = [[spread(lower_ref, field, chunk) for chunk in range(2)] for field in range(4)]
    upper = [spread(upper_ref, field, 0) for field in range(4)]

    def pick_two(tables, index):
        within = index & 127
        return jnp.where(index < 128, lane_pick(tables[0], within), lane_pick(tables[1], within))

    pairs = jnp.concatenate([slots_ref[:, 0:rows], slots_ref[:, rows:atoms]], axis=0).T
    for tile in range(rows // 8):
        band = slice(8 * tile, 8 * tile + 8)
        index = pairs[band, :]
        centre = 8 * tile + sub + jnp.where(lane < 64, 0, rows)
        from_own = jnp.clip(index - ghosts, 0, atoms - 1)
        from_lower = jnp.minimum(index + (atoms - ghosts), 255)
        from_upper = jnp.clip(index - (ghosts + atoms), 0, 127)

        def neighbour(field):
            below = pick_two(lower[field], from_lower)
            inside = pick_two(own[field], from_own)
            above = lane_pick(upper[field], from_upper)
            return jnp.where(
                index < ghosts, below, jnp.where(index < ghosts + atoms, inside, above)
            )

        offsets = [neighbour(field) - pick_two(own[field], centre) for field in range(3)]
        live = pick_two(own[4], centre)
        present = jnp.where((lane & 63).astype(jnp.float32) < live, 1.0, 0.0)
        smooth = present / (
            1.0 + (offsets[0] * offsets[0] + offsets[1] * offsets[1] + offsets[2] * offsets[2])
        )
        environment_ref[0, band, :] = smooth
        for field in range(3):
            environment_ref[1 + field, band, :] = smooth * offsets[field]
        kind_ref[band, :] = neighbour(3)

    group = 8

    def stacked(values):
        high, low = split(values)
        return jnp.concatenate([high, low, high], axis=0)

    def one_group(start):
        pieces = []
        for row in range(group):
            smooth = jnp.broadcast_to(environment_ref[0, pl.ds(start + row, 1), :], (32, 128))
            kind = jnp.broadcast_to(kind_ref[pl.ds(start + row, 1), :], (32, 128))
            pieces.append(
                jnp.tanh(smooth * ((1.0 - kind) * embed_zero + kind * embed_one))
            )
        first = jnp.concatenate(pieces, axis=1)
        second = jnp.tanh(multiply(second_weight, stacked(first), ((1,), (0,))))
        second = second + jnp.concatenate([first, first], axis=0)
        third = jnp.tanh(multiply(third_weight, stacked(second), ((1,), (0,))))
        third = third + jnp.concatenate([second, second], axis=0)
        third_pair = split(third)
        for half in range(group // 4):
            columns = slice(512 * half, 512 * half + 512)
            bands = []
            for part in range(4):
                bands.append(
                    jnp.concatenate(
                        [
                            jnp.where(
                                sub == row + jnp.where(lane < 64, 0, 4),
                                jnp.broadcast_to(
                                    environment_ref[part, pl.ds(start + 4 * half + row, 1), :],
                                    (8, 128),
                                ),
                                0.0,
                            )
                            for row in range(4)
                        ],
                        axis=1,
                    )
                )
            environment = split(jnp.concatenate(bands, axis=0))
            both = multiply(
                jnp.concatenate(environment, axis=0), third_pair[0][:, columns], LANES
            )
            sums = both[0:32] + both[32:64]
            sums = sums + multiply(environment[0], third_pair[1][:, columns], LANES)
            sums = sums * (1.0 / slots)
            for part in range(4):
                moments_ref[part, pl.ds(2 * start + 8 * half, 8), :] = sums[
                    8 * part : 8 * part + 8
                ]

    def body(step, carry):
        one_group(pl.multiple_of(step * 2 * group, 2 * group))
        one_group(pl.multiple_of(step * 2 * group + group, group))
        return carry

    lax.fori_loop(0, rows // (2 * group), body, 0)

    chunks = (descriptor_ref.shape[1] + 127) // 128
    last = descriptor_ref.shape[1] - 128 * (chunks - 1)

    def describe(step, carry):
        band = pl.ds(pl.multiple_of(step * 8, 8), 8)
        moments = [moments_ref[part, band, :] for part in range(4)]
        axis_part = [lane_pick(moments[part], lane & 15) for part in range(4)]
        for chunk in range(chunks):
            spot = jnp.broadcast_to(spot_ref[chunk : chunk + 1, :], (8, 128))
            total = lane_pick(moments[0], spot) * axis_part[0]
            for part in range(1, 4):
                total = total + lane_pick(moments[part], spot) * axis_part[part]
            if chunk < chunks - 1:
                descriptor_ref[band, 128 * chunk : 128 * chunk + 128] = total
            else:
                descriptor_ref[band, 128 * chunk : 128 * chunk + last] = total[:, 0:last]
        return carry

    lax.fori_loop(0, atoms // 8, describe, 0)

    store = pltpu.make_async_copy(descriptor_ref, descriptor_hbm, semaphores.at[2])
    store.start()
    for fetch in fetches:
        fetch.wait()
    shift = fitting_rows(descriptor_ref, weight_in_ref, weight_hidden_ref, weight_out_ref)
    kind = types_ref[...].astype(jnp.float32)
    charge = (1.0 - kind) * charges_ref[0] + kind * charges_ref[1] + natural_order(shift)
    charge_ref[...] = charge
    fields = jnp.concatenate(
        [
            cell_x_ref[...].astype(jnp.float32),
            (cell_y_ref[...] + base_ref[0]).astype(jnp.float32),
            cell_z_ref[...].astype(jnp.float32),
        ]
        + [fraction_ref[axis] for axis in range(3)]
        + [charge, jnp.zeros((1, atoms), jnp.float32)],
        axis=0,
    )
    for copy in range(copies_ref.shape[0]):
        copies_ref[copy] = fields
    store.wait()


def spot_table(embed, desc):
    column = np.arange(desc) // AXIS
    quarter = embed // 4
    place = 32 * (column // quarter) + column % quarter
    chunks = (desc + 127) // 128
    table = np.zeros((chunks * 128,), np.int32)
    table[:desc] = place
    padded = np.zeros(((chunks + 7) // 8 * 8, 128), np.int32)
    padded[:chunks] = table.reshape(chunks, 128)
    return padded


def networks(
    copies,
    ghosts,
    base,
    charge_base,
    own,
    lower,
    upper,
    neighbours,
    types,
    cells,
    fraction,
    embed,
    weight_in,
    weight_hidden,
    weight_out,
):
    atoms = types.shape[1]
    desc, width = weight_in.shape
    spots = jnp.asarray(spot_table(embed[2].shape[1], desc))
    anywhere = pl.BlockSpec(memory_space=pl.ANY)
    scalars = pl.BlockSpec(memory_space=pltpu.SMEM)
    blocks = (own, lower, upper, neighbours[0].T, types, *cells, fraction, *embed, spots)
    weight_out = weight_out.reshape(1, -1)
    results = [
        jax.ShapeDtypeStruct((atoms, desc), jnp.float32),
        jax.ShapeDtypeStruct((1, atoms), jnp.float32),
        jax.ShapeDtypeStruct((copies, 8, atoms), jnp.float32),
    ]
    return pl.pallas_call(
        functools.partial(network_kernel, ghosts),
        grid=(1,),
        out_shape=results,
        in_specs=[scalars, scalars]
        + whole_specs(*blocks)
        + [anywhere, anywhere]
        + whole_specs(weight_out),
        out_specs=[anywhere] + whole_specs(*results[1:]),
        scratch_shapes=[
            pltpu.VMEM((atoms, desc), jnp.float32),
            pltpu.VMEM((4, atoms // 2, 128), jnp.float32),
            pltpu.VMEM((atoms // 2, 128), jnp.float32),
            pltpu.VMEM((4, atoms, 128), jnp.float32),
            pltpu.VMEM((3, 128, 128), jnp.float32),
            pltpu.VMEM((width, desc), jnp.float32),
            pltpu.VMEM(weight_hidden.shape, jnp.float32),
            pltpu.SemaphoreType.DMA((3,)),
        ],
        compiler_params=pltpu.CompilerParams(vmem_limit_bytes=32 * 2**20),
        name="networks",
    )(base, charge_base, *blocks, weight_in.T, weight_hidden, weight_out)


def energy_kernel(descriptor_ref, weight_in_ref, weight_hidden_ref, weight_out_ref, energy_ref):
    energy_ref[...] = natural_order(
        fitting_rows(descriptor_ref, weight_in_ref, weight_hidden_ref, weight_out_ref)
    )


def energies(descriptor, weight_in, weight_hidden, weight_out):
    atoms, desc = descriptor.shape
    width = weight_in.shape[1]
    arrays = (descriptor, weight_in.T, weight_hidden, weight_out.reshape(1, -1))
    result = jax.ShapeDtypeStruct((1, atoms), jnp.float32)
    return pl.pallas_call(
        energy_kernel,
        grid=(1,),
        out_shape=result,
        in_specs=whole_specs(*arrays),
        out_specs=whole(result.shape),
        compiler_params=pltpu.CompilerParams(vmem_limit_bytes=32 * 2**20),
        cost_estimate=pl.CostEstimate(
            flops=6 * atoms * desc * width, bytes_accessed=4 * desc * width, transcendentals=0
        ),
        name="energies",
    )(*arrays)


def weight_rows(fraction):
    square = fraction * fraction
    cubed = square * fraction
    rest = 1.0 - fraction
    return [
        rest * rest * rest / 6.0,
        (3.0 * cubed - 6.0 * square + 4.0) / 6.0,
        (-3.0 * cubed + 3.0 * square + 3.0 * fraction + 1.0) / 6.0,
        cubed / 6.0,
    ]


def placed_weights(distance, weights):
    shape = distance.shape
    result = jnp.zeros(shape, jnp.float32)
    for step in range(4):
        result = jnp.where(
            distance == step, jnp.broadcast_to(weights[step], shape), result
        )
    return result


def third_factors(fields, waves_ref, cosine_ref):
    atoms = fields.shape[1]
    start = fields[2:3, :].astype(jnp.int32)
    along = weight_rows(fields[5:6, :])
    parts = waves_ref.shape[0]
    cosine = jnp.broadcast_to(cosine_ref[...], (parts, 128))
    wave = jnp.broadcast_to(waves_ref[:, 0:1], (parts, 128))
    shift = jnp.broadcast_to(waves_ref[:, 1:2], (parts, 128))
    pieces = []
    for chunk in range(atoms // 128):
        lanes = slice(128 * chunk, 128 * chunk + 128)
        total = jnp.zeros((parts, 128), jnp.float32)
        for step in range(4):
            place = jnp.broadcast_to(start[:, lanes] + step, (parts, 128))
            phase = (wave * place + shift) & (NG - 1)
            value = lane_pick(cosine, phase & 127)
            value = jnp.where(phase < 128, value, -value)
            total = total + value * jnp.broadcast_to(along[step][:, lanes], (parts, 128))
        pieces.append(total)
    return jnp.concatenate(pieces, axis=1)


def first_third(fields, waves_ref, cosine_ref, window, scale):
    atoms = fields.shape[1]
    third = third_factors(fields, waves_ref, cosine_ref)
    if scale is not None:
        third = third * scale
    rows = lax.broadcasted_iota(jnp.int32, (window, atoms), 0)
    first = placed_weights(
        rows - fields[0:1, :].astype(jnp.int32), weight_rows(fields[3:4, :])
    )
    return jnp.concatenate(
        [first * third[part : part + 1, :] for part in range(third.shape[0])], axis=0
    )


def second_factors(fields, base):
    rows = lax.broadcasted_iota(jnp.int32, (NG, fields.shape[1]), 0)
    start = fields[1:2, :].astype(jnp.int32) - base
    return placed_weights((rows - start) & (NG - 1), weight_rows(fields[4:5, :]))


def wave_of(index):
    return jnp.where(index <= NG // 2, index, index - NG // 2)


def solve_kernel(
    block_x,
    block_y,
    window,
    kappa_ref,
    pair_ref,
    static_ref,
    waves_ref,
    cosine_ref,
    tables_hbm,
    last_hbm,
    sent_ref,
    full_ref,
    atoms_ref,
    grid_ref,
    tables_ref,
    last_ref,
    semaphores,
):
    slabs = NG // block_y
    bricks = NG // block_x
    parts = waves_ref.shape[0]
    block = static_ref.shape[2]
    step = pl.program_id(0)

    @pl.when(step == 0)
    def _():
        fetches = [
            pltpu.make_async_copy(tables_hbm, tables_ref, semaphores.at[0]),
            pltpu.make_async_copy(last_hbm.at[pair_ref[0]], last_ref, semaphores.at[1]),
        ]
        for fetch in fetches:
            fetch.start()
        for slab in range(slabs):
            lanes = slice(block * slab, block * (slab + 1))
            for brick in range(bricks):
                atoms_ref[brick, :, lanes] = static_ref[slab * bricks + brick]
        grid_ref[...] = jnp.zeros_like(grid_ref)
        for brick in range(bricks):
            fields = atoms_ref[brick]
            table = split(first_third(fields, waves_ref, cosine_ref, window, fields[6:7, :]))
            spread = triple(table, split(second_factors(fields, 0)), LANES)
            rows = slice(block_x * brick, block_x * brick + window)
            for part in range(parts):
                grid_ref[part, rows, :] += spread[part * window : part * window + window]
        extra = window - block_x
        for part in range(parts):
            grid_ref[part, 0:extra, :] += grid_ref[part, NG : NG + extra, :]
        for fetch in fetches:
            fetch.wait()

    basis = (tables_ref[0], tables_ref[1])
    turned = (tables_ref[2], tables_ref[3])
    last = (last_ref[0], last_ref[1])
    index_x = lax.broadcasted_iota(jnp.int32, (NG, 1), 0)
    index_y = lax.broadcasted_iota(jnp.int32, (1, NG), 1)

    def factors(index):
        kappa = wave_of(index).astype(jnp.float32) * (2.0 * math.pi / NG)
        squared = kappa * kappa
        ends = (index == 0) | (index == NG // 2)
        return squared, jnp.exp(-0.5 * squared) * jnp.where(ends, 1.0 / NG, 2.0 / NG)

    square_x, damp_x = factors(index_x)
    square_y, damp_y = factors(index_y)
    square_xy = square_x + square_y
    damp_xy = damp_x * damp_y

    planes = jnp.concatenate([grid_ref[2 * step + part, 0:NG, :] for part in range(2)], axis=1)
    first = triple(basis, split(planes))
    first = jnp.concatenate([first[:, 0:NG], first[:, NG:]], axis=0)
    both = triple(split(first), turned)
    scaled = []
    for part in range(2):
        squared = square_xy + kappa_ref[2 * step + part, 0]
        root = jnp.where(squared == 0.0, 1.0, 0.0)
        green = (1.0 - root) * (damp_xy * kappa_ref[2 * step + part, 1]) / (squared + root)
        scaled.append(both[NG * part : NG * (part + 1)] * green)
    back = triple(turned, split(jnp.concatenate(scaled, axis=1)))
    back = jnp.concatenate([back[:, 0:NG], back[:, NG:]], axis=0)
    full = triple(split(back), last)
    full_ref[0] = full[0:NG]
    full_ref[1] = full[NG:]
    low_lanes = lax.broadcasted_iota(jnp.int32, (NG, 128), 1) < block_y
    even = full[0:NG, 0:128]
    odd = full[NG:, 0:128]
    blocks = [
        jnp.where(low_lanes, even, pltpu.roll(odd, block_y, 1)),
        jnp.where(low_lanes, pltpu.roll(even, block_y, 1), odd),
    ]
    for brick in range(bricks):
        rows = slice(block_x * brick, block_x * (brick + 1))
        for side in range(2):
            sent_ref[2 * brick + side, 0] = blocks[side][rows]


def solve(block_x, block_y, window, kappa, pair, static, waves, cosine_row, tables, last):
    devices, _, atoms = static.shape
    slabs = NG // block_y
    bricks = NG // block_x
    parts = waves.shape[0]
    anywhere = pl.BlockSpec(memory_space=pl.ANY)
    scalars = pl.BlockSpec(memory_space=pltpu.SMEM)
    return pl.pallas_call(
        functools.partial(solve_kernel, block_x, block_y, window),
        grid=(parts // 2,),
        out_shape=[
            jax.ShapeDtypeStruct((2 * bricks, parts // 2, block_x, 128), jnp.float32),
            jax.ShapeDtypeStruct((parts, NG, NG), jnp.float32),
            jax.ShapeDtypeStruct((bricks, 8, slabs * atoms), jnp.float32),
        ],
        in_specs=[scalars, scalars]
        + whole_specs(static, waves, cosine_row)
        + [anywhere, anywhere],
        out_specs=[
            pl.BlockSpec((2 * bricks, 1, block_x, 128), lambda step: (0, step, 0, 0)),
            pl.BlockSpec((2, NG, NG), lambda step: (step, 0, 0)),
            whole((bricks, 8, slabs * atoms)),
        ],
        scratch_shapes=[
            pltpu.VMEM((parts, NG + window - block_x, NG), jnp.float32),
            pltpu.VMEM(tables.shape, tables.dtype),
            pltpu.VMEM(last.shape[1:], last.dtype),
            pltpu.SemaphoreType.DMA((2,)),
        ],
        compiler_params=pltpu.CompilerParams(vmem_limit_bytes=48 * 2**20),
        name="solve",
    )(kappa, pair, static, waves, cosine_row, tables, last)


def sample_kernel(
    block_x, block_y, window, pair_ref, atoms_ref, waves_ref, cosine_ref, full_ref, out_ref
):
    bricks = atoms_ref.shape[0]
    parts = waves_ref.shape[0]
    block = out_ref.shape[2]
    base = 2 * block_y * pair_ref[0]
    lanes = pl.ds(pl.multiple_of(2 * block * pair_ref[0], 128), 2 * block)
    for brick in range(bricks):
        fields = atoms_ref[brick, :, lanes]
        weights = first_third(fields, waves_ref, cosine_ref, window, None)
        start = block_x * brick
        inside = min(window, NG - start)
        values = []
        for part in range(parts):
            values.append(full_ref[part, start : start + inside, :])
            if inside < window:
                values.append(full_ref[part, 0 : window - inside, :])
        values = split(jnp.concatenate(values, axis=0))
        along = triple(values, split(second_factors(fields, base)))
        sums = jnp.sum(along * weights, axis=0, keepdims=True)
        for side in range(2):
            out_ref[2 * brick + side] = sums[:, block * side : block * (side + 1)]


def sample(block, block_x, block_y, window, pair, atoms, waves, cosine_row, full):
    bricks = atoms.shape[0]
    parts = waves.shape[0]
    result = jax.ShapeDtypeStruct((2 * bricks, 1, block), jnp.float32)
    return pl.pallas_call(
        functools.partial(sample_kernel, block_x, block_y, window),
        grid=(1,),
        out_shape=result,
        in_specs=[pl.BlockSpec(memory_space=pltpu.SMEM)]
        + whole_specs(atoms, waves, cosine_row, full),
        out_specs=whole(result.shape),
        compiler_params=pltpu.CompilerParams(vmem_limit_bytes=48 * 2**20),
        cost_estimate=pl.CostEstimate(
            flops=12 * bricks * block * parts * window * NG,
            bytes_accessed=4 * full.size,
            transcendentals=0,
        ),
        name="sample",
    )(pair, atoms, waves, cosine_row, full)


def finish_kernel(block_y, got_ref, table_ref, out_ref):
    table = (table_ref[0], table_ref[1])
    rows = []
    for line in range(got_ref.shape[1]):
        turned = got_ref[:, line, :].T
        rows.append(jnp.concatenate([turned[0:block_y], turned[block_y:]], axis=1))
    result = triple(split(jnp.concatenate(rows, axis=0)), table)
    for line in range(got_ref.shape[1]):
        out_ref[line] = result[block_y * line : block_y * (line + 1)]


def finish(block_x, block_y, got, table):
    step = 8
    return pl.pallas_call(
        functools.partial(finish_kernel, block_y),
        grid=(block_x // step,),
        out_shape=jax.ShapeDtypeStruct((block_x, block_y, NG), jnp.float32),
        in_specs=[
            pl.BlockSpec((NG // 2, step, 128), lambda index: (0, index, 0)),
            pl.BlockSpec((2, NG, NG), lambda index: (0, 0, 0)),
        ],
        out_specs=pl.BlockSpec((step, block_y, NG), lambda index: (index, 0, 0)),
        compiler_params=pltpu.CompilerParams(vmem_limit_bytes=32 * 2**20),
        name="finish",
    )(got, table)


def two_parts(table):
    table = np.asarray(table, np.float32)
    high = table.astype(ml_dtypes.bfloat16)
    low = (table - high.astype(np.float32)).astype(ml_dtypes.bfloat16)
    return np.stack([high, low])


def real_basis():
    index = np.arange(NG)
    wave = np.where(index <= NG // 2, index, index - NG // 2)
    angle = (wave[:, None] * index[None, :] % NG) * (2.0 * math.pi / NG)
    return np.where((index <= NG // 2)[:, None], np.cos(angle), np.sin(angle))


def per_device(
    positions,
    types,
    neighbours,
    neighbour_count,
    send_index,
    cell_x,
    cell_y,
    cell_z,
    spline_fraction,
    embed_first,
    embed_second,
    embed_third,
    energy_in,
    energy_hidden,
    energy_out,
    wannier_in,
    wannier_hidden,
    wannier_out,
    charge_base,
):
    atoms = types.shape[1]
    ghosts = send_index.shape[1] // 2
    count_x = lax.axis_size("brick")
    count_y = lax.axis_size("slab")
    block_x = NG // count_x
    block_y = NG // count_y
    window = block_x + 8
    parts = NG // (2 * count_x)
    brick = lax.axis_index("brick")
    slab = lax.axis_index("slab")
    pair = (slab // 2).astype(jnp.int32).reshape(1)
    halves = [
        [b * count_y + 2 * p + side for b in range(count_x) for side in range(2)]
        for p in range(count_y // 2)
    ]

    def exchange(values, axes, groups=None):
        return lax.all_to_all(
            values, axes, split_axis=0, concat_axis=0, tiled=True, axis_index_groups=groups
        )

    own, outgoing = collect(positions, types, neighbour_count, send_index)
    up = [(i, (i + 1) % count_x) for i in range(count_x)]
    down = [((i + 1) % count_x, i) for i in range(count_x)]
    lower = lax.ppermute(outgoing, "brick", up)
    upper = lax.ppermute(outgoing, "brick", down)
    descriptor, charge, fields = networks(
        count_x * count_y,
        ghosts,
        (slab * block_y).astype(jnp.int32).reshape(1),
        charge_base,
        own,
        lower,
        upper,
        neighbours,
        types,
        (cell_x, cell_y, cell_z),
        spline_fraction,
        (embed_first, embed_second, embed_third),
        wannier_in,
        wannier_hidden,
        wannier_out,
    )
    every_field = exchange(fields, ("slab", "brick"))

    part = (2 * brick + slab % 2) * parts + jnp.arange(parts, dtype=jnp.int32)
    wave = wave_of(part)
    waves = jnp.stack([wave, jnp.where(part <= NG // 2, 0, 3 * NG // 4)], axis=1)
    kappa = wave.astype(jnp.float32) * (2.0 * math.pi / NG)
    squared = kappa * kappa
    ends = (part == 0) | (part == NG // 2)
    kappa = jnp.stack(
        [squared, jnp.exp(-0.5 * squared) * jnp.where(ends, 1.0 / NG, 2.0 / NG)], axis=1
    )
    basis = real_basis()
    tables = np.concatenate([two_parts(basis), two_parts(basis.T)])
    last = []
    for p in range(count_y // 2):
        points = (2 * block_y * p + np.arange(2 * block_y + 8)) % NG
        columns = np.zeros((NG, NG))
        columns[:, : points.size] = basis[:, points]
        last.append(two_parts(columns))
    cosine_row = np.cos(np.arange(128) * (2.0 * math.pi / NG)).astype(np.float32)[None]
    cosine_row = jnp.asarray(cosine_row)
    sent, full, every_atom = solve(
        block_x,
        block_y,
        window,
        kappa,
        pair,
        every_field,
        waves,
        cosine_row,
        jnp.asarray(tables),
        jnp.asarray(np.stack(last)),
    )
    got = exchange(sent.reshape(2 * count_x, -1, 128), ("brick", "slab"), halves)
    partial = sample(
        atoms, block_x, block_y, window, pair, every_atom, waves, cosine_row, full
    )
    energy_short = energies(descriptor, energy_in, energy_hidden, energy_out)
    partial, got = lax.optimization_barrier((partial, got))
    potential_at = jnp.sum(exchange(partial, ("brick", "slab"), halves), axis=0)
    atom_energy = energy_short + 0.5 * charge * potential_at
    pairs = basis.reshape(-1, 2, NG).transpose(1, 0, 2).reshape(NG, NG)
    potential = finish(
        block_x, block_y, got.reshape(NG // 2, block_x, 128), jnp.asarray(two_parts(pairs))
    )
    return atom_energy, potential


def solution(mesh):
    placed = (
        P(None, "slab", "brick"),
        P("slab", "brick"),
        P("slab", "brick", None),
        P("slab", "brick"),
        P("slab", "brick"),
        P("slab", "brick"),
        P("slab", "brick"),
        P("slab", "brick"),
        P(None, "slab", "brick"),
    ) + (P(),) * 10
    bricks, slabs = mesh.shape["brick"], mesh.shape["slab"]
    fits = 2 * NG == 128 * slabs and slabs % 2 == 0 and NG % (4 * bricks) == 0
    return jax.shard_map(
        per_device if fits else per_device_general,
        mesh=mesh,
        in_specs=placed,
        out_specs=(P("slab", "brick"), P("brick", "slab", None)),
        check_vma=False,
    )
```

```python
import functools
import math

import jax
import jax.numpy as jnp
import ml_dtypes
import numpy as np
from jax import lax
from jax.experimental import pallas as pl
from jax.experimental.pallas import tpu as pltpu
from jax.sharding import PartitionSpec as P

NG = 256
AXIS = 16
VMEM_BYTES = 60 * 2**20


HIGH = lax.Precision.HIGHEST


def with_halo(cells, sides, width):
    for axis, dim in sides:
        count = lax.axis_size(axis)
        head = lax.slice_in_dim(cells, 0, width, axis=dim)
        tail = lax.slice_in_dim(cells, cells.shape[dim] - width, cells.shape[dim], axis=dim)
        cells = jnp.concatenate(
            [
                lax.ppermute(tail, axis, [(i, (i + 1) % count) for i in range(count)]),
                cells,
                lax.ppermute(head, axis, [((i + 1) % count, i) for i in range(count)]),
            ],
            axis=dim,
        )
    return cells


def spline_weights(fraction):
    cubed = fraction * fraction * fraction
    square = fraction * fraction
    return jnp.stack(
        [
            (1.0 - fraction) * (1.0 - fraction) * (1.0 - fraction) / 6.0,
            (3.0 * cubed - 6.0 * square + 4.0) / 6.0,
            (-3.0 * cubed + 3.0 * square + 3.0 * fraction + 1.0) / 6.0,
            cubed / 6.0,
        ]
    )


def fitting(descriptor, weight_in, weight_hidden, weight_out):
    hidden = jnp.tanh(jnp.dot(descriptor, weight_in, precision=HIGH))
    for depth_index in range(weight_hidden.shape[0]):
        hidden = jnp.tanh(jnp.dot(hidden, weight_hidden[depth_index], precision=HIGH)) + hidden
    return jnp.dot(hidden, weight_out, precision=HIGH)


def atom_terms(
    extended,
    neighbour_rows,
    neighbour_total,
    embed_first,
    embed_second,
    embed_third,
    energy_in,
    energy_hidden,
    energy_out,
    wannier_in,
    wannier_hidden,
    wannier_out,
):
    atom_count, slots = neighbour_rows.shape
    ghost_rows = (extended.shape[1] - atom_count) // 2
    block_size = 64
    blocks = atom_count // block_size
    present = (jnp.arange(slots, dtype=jnp.int32)[None, :] < neighbour_total[:, None]).astype(
        jnp.float32
    )
    centre_ids = (ghost_rows + jnp.arange(atom_count, dtype=jnp.int32)).reshape(blocks, block_size)
    second_weight = embed_second.T
    third_weight = embed_third.T

    def one_block(pieces):
        centre_rows, rows_block, present_block = pieces
        centre_block = extended[:3, centre_rows]
        gathered = extended[:, rows_block]
        offsets = gathered[:3] - centre_block[:, :, None]
        smooth = present_block / (1.0 + jnp.sum(offsets * offsets, axis=0))
        environment = jnp.stack(
            [smooth, smooth * offsets[0], smooth * offsets[1], smooth * offsets[2]], axis=0
        )
        kind = gathered[3][None]
        mixing = (1.0 - kind) * embed_first[0][:, None, None] + kind * embed_first[1][:, None, None]
        first = jnp.tanh(smooth[None] * mixing).reshape(embed_first.shape[1], block_size * slots)
        second = jnp.tanh(jnp.dot(second_weight, first, precision=HIGH)) + jnp.concatenate(
            [first, first], axis=0
        )
        third = jnp.tanh(jnp.dot(third_weight, second, precision=HIGH)) + jnp.concatenate(
            [second, second], axis=0
        )
        third_blocks = third.reshape(third.shape[0], block_size, slots)
        moments = jnp.einsum("kan,can->akc", third_blocks, environment, precision=HIGH) / slots
        descriptor = jnp.einsum("amc,akc->amk", moments, moments[:, :AXIS], precision=HIGH).reshape(
            block_size, -1
        )
        return (
            fitting(descriptor, energy_in, energy_hidden, energy_out),
            fitting(descriptor, wannier_in, wannier_hidden, wannier_out),
        )

    energy_short, charge_shift = lax.map(
        one_block,
        (
            centre_ids,
            neighbour_rows.reshape(blocks, block_size, slots),
            present.reshape(blocks, block_size, slots),
        ),
    )
    return (energy_short.reshape(atom_count), charge_shift.reshape(atom_count))


def green_table(first, second, third, size):

    def folded(index):
        return jnp.where(index < size // 2, index, index - size).astype(jnp.float32) * (
            2.0 * math.pi / size
        )

    kappa_x = folded(first)[:, None, None]
    kappa_y = folded(second)[None, :, None]
    kappa_z = folded(third)[None, None, :]
    squared = kappa_x * kappa_x + kappa_y * kappa_y + kappa_z * kappa_z
    root = (
        (first[:, None, None] == 0) & (second[None, :, None] == 0) & (third[None, None, :] == 0)
    ).astype(jnp.float32)
    return (1.0 - root) * jnp.exp(-0.5 * squared) / (squared + root)


def dft_tables(size):
    index = jnp.arange(size, dtype=jnp.int32)
    phase = (index[:, None] * index[None, :] % size).astype(jnp.float32) * (2.0 * math.pi / size)
    return (jnp.cos(phase), jnp.sin(phase))


def along(values, table, axis_index):
    result = jnp.tensordot(values, table, axes=([axis_index], [0]), precision=HIGH)
    return jnp.moveaxis(result, -1, axis_index)


def complex_transform(paired, axis_index, cosine, sine, inverse):
    real_part = paired[0]
    imag_part = paired[1]
    inner = axis_index - 1
    real_cos = along(real_part, cosine, inner)
    real_sin = along(real_part, sine, inner)
    imag_cos = along(imag_part, cosine, inner)
    imag_sin = along(imag_part, sine, inner)
    if inverse:
        return jnp.stack([real_cos - imag_sin, imag_cos + real_sin])
    return jnp.stack([real_cos + imag_sin, imag_cos - real_sin])


def fold_windows(values, axis_index, block, count):
    front = jnp.moveaxis(values, axis_index, 0)
    rest = front.shape[1:]
    windows = front.reshape((count, block + 3) + rest)
    main_part = windows[:, :block]
    carried = jnp.roll(windows[:, block:], 1, axis=0)
    main_part = main_part.at[:, :3].add(carried)
    return jnp.moveaxis(main_part.reshape((count * block,) + rest), 0, axis_index)


def make_windows(values, axis_index, block, count):
    front = jnp.moveaxis(values, axis_index, 0)
    rest = front.shape[1:]
    pieces = front.reshape((count, block) + rest)
    trailing = jnp.roll(pieces, -1, axis=0)[:, :3]
    windows = jnp.concatenate([pieces, trailing], axis=1)
    return jnp.moveaxis(windows.reshape((count * (block + 3),) + rest), 0, axis_index)


def spread_matrix(start, weights, width, wrap_size):
    offsets = jnp.arange(4, dtype=jnp.int32)[:, None, None]
    target = start[None, :, None] + offsets
    if wrap_size > 0:
        target = target % wrap_size
    hits = (target == jnp.arange(width, dtype=jnp.int32)[None, None, :]).astype(jnp.float32)
    return jnp.sum(weights[:, :, None] * hits, axis=0)


def per_device_general(
    positions,
    types,
    neighbours,
    neighbour_count,
    send_index,
    cell_x,
    cell_y,
    cell_z,
    spline_fraction,
    embed_first,
    embed_second,
    embed_third,
    energy_in,
    energy_hidden,
    energy_out,
    wannier_in,
    wannier_hidden,
    wannier_out,
    charge_base,
):
    atom_count = types.shape[1]
    ghost_rows = send_index.shape[1] // 2
    kind_float = types[0].astype(jnp.float32)
    own_atoms = jnp.concatenate([positions[:, 0], kind_float[None]], axis=0)
    outgoing = own_atoms[:, send_index[0]]
    padded_ghosts = with_halo(outgoing, (("brick", 1),), ghost_rows)
    extended = jnp.concatenate(
        [padded_ghosts[:, :ghost_rows], own_atoms, padded_ghosts[:, 3 * ghost_rows :]], axis=1
    )
    energy_short, charge_shift = atom_terms(
        extended,
        neighbours[0],
        neighbour_count[0],
        embed_first,
        embed_second,
        embed_third,
        energy_in,
        energy_hidden,
        energy_out,
        wannier_in,
        wannier_hidden,
        wannier_out,
    )
    charge = (1.0 - kind_float) * charge_base[0] + kind_float * charge_base[1] + charge_shift
    count_x = lax.axis_size("brick")
    count_y = lax.axis_size("slab")
    block_x = NG // count_x
    block_y = NG // count_y
    wide_x = block_x + 3
    wide_y = block_y + 3
    spread_x = spread_matrix(cell_x[0], spline_weights(spline_fraction[0, 0]), wide_x, 0)
    spread_y = spread_matrix(cell_y[0], spline_weights(spline_fraction[1, 0]), wide_y, 0)
    spread_z = spread_matrix(cell_z[0], spline_weights(spline_fraction[2, 0]), NG, NG)
    spread_xy = (spread_x[:, :, None] * spread_y[:, None, :]).reshape(atom_count, wide_x * wide_y)
    charge_grid = jnp.einsum(
        "ap,az->pz", spread_xy, charge[:, None] * spread_z, precision=HIGH
    ).reshape(wide_x, wide_y, NG)
    cosine, sine = dft_tables(NG)
    scale = 1.0 / (NG * NG * NG)
    full_index = jnp.arange(NG, dtype=jnp.int32)
    paired = jnp.stack([along(charge_grid, cosine, 2), -along(charge_grid, sine, 2)])
    moved = lax.all_to_all(paired, "slab", split_axis=3, concat_axis=2, tiled=True)
    moved = complex_transform(fold_windows(moved, 2, block_y, count_y), 2, cosine, sine, False)
    moved = lax.all_to_all(moved, "brick", split_axis=2, concat_axis=1, tiled=True)
    moved = complex_transform(fold_windows(moved, 1, block_x, count_x), 1, cosine, sine, False)
    part_y = NG // count_x
    part_z = NG // count_y
    index_y = lax.axis_index("brick") * part_y + jnp.arange(part_y, dtype=jnp.int32)
    index_z = lax.axis_index("slab") * part_z + jnp.arange(part_z, dtype=jnp.int32)
    moved = moved * (green_table(full_index, index_y, index_z, NG) * scale)[None]
    moved = make_windows(complex_transform(moved, 1, cosine, sine, True), 1, block_x, count_x)
    moved = lax.all_to_all(moved, "brick", split_axis=1, concat_axis=2, tiled=True)
    moved = make_windows(complex_transform(moved, 2, cosine, sine, True), 2, block_y, count_y)
    moved = lax.all_to_all(moved, "slab", split_axis=2, concat_axis=3, tiled=True)
    potential_wide = along(moved[0], cosine, 2) - along(moved[1], sine, 2)
    sampled = jnp.einsum(
        "ap,pz->az", spread_xy, potential_wide.reshape(wide_x * wide_y, NG), precision=HIGH
    )
    potential_at = jnp.sum(sampled * spread_z, axis=1)
    atom_energy = energy_short + 0.5 * charge * potential_at
    return (atom_energy[None, :], potential_wide[:block_x, :block_y])


def split(values):
    high = values.astype(jnp.bfloat16)
    low = (values - high.astype(jnp.float32)).astype(jnp.bfloat16)
    return high, low


def multiply(left, right, dims):
    return lax.dot_general(left, right, (dims, ((), ())), preferred_element_type=jnp.float32)


def triple(left, right, dims=((1,), (0,))):
    return (
        multiply(left[0], right[0], dims)
        + multiply(left[0], right[1], dims)
        + multiply(left[1], right[0], dims)
    )


LANES = ((1,), (1,))


def lane_pick(table, index):
    return jnp.take_along_axis(table, index, axis=1, mode="promise_in_bounds")


def whole(shape):
    return pl.BlockSpec(tuple(shape), lambda step: (0,) * len(shape))


def whole_specs(*arrays):
    return [whole(array.shape) for array in arrays]


def collect_kernel(
    positions_ref, types_ref, count_ref, send_ref, own_ref, outgoing_ref
):
    atoms = types_ref.shape[1]
    own_ref[...] = jnp.zeros_like(own_ref)
    for axis in range(3):
        own_ref[axis : axis + 1, 0:atoms] = positions_ref[axis]
    own_ref[3:4, 0:atoms] = types_ref[...].astype(jnp.float32)
    own_ref[4:5, 0:atoms] = count_ref[...].astype(jnp.float32)
    own_ref[5:6, 0:atoms] = send_ref[...].astype(jnp.float32)
    for chunk in range(2):
        lanes = slice(128 * chunk, 128 * chunk + 128)
        wanted = jnp.broadcast_to(own_ref[5:6, lanes], (8, 128)).astype(jnp.int32)
        within = wanted & 127
        outgoing_ref[:, lanes] = jnp.where(
            wanted < 128,
            lane_pick(own_ref[:, 0:128], within),
            lane_pick(own_ref[:, 128:256], within),
        )


def collect(positions, types, counts, send_index):
    arrays = (positions, types, counts, send_index)
    result = jax.ShapeDtypeStruct((8, 256), jnp.float32)
    return pl.pallas_call(
        collect_kernel,
        grid=(1,),
        out_shape=[result, result],
        in_specs=whole_specs(*arrays),
        out_specs=whole_specs(result, result),
        compiler_params=pltpu.CompilerParams(vmem_limit_bytes=VMEM_BYTES),
        name="collect_atoms",
    )(*arrays)


def fitting_rows(descriptor_ref, weight_in_ref, weight_hidden_ref, weight_out_ref):
    depth = weight_in_ref.shape[1]
    first = depth // 256 * 256
    hidden = triple(
        split(descriptor_ref[:, 0:first]), split(weight_in_ref[:, 0:first]), LANES
    )
    if first < depth:
        hidden = hidden + triple(
            split(descriptor_ref[:, first:depth]), split(weight_in_ref[:, first:depth]), LANES
        )
    hidden = jnp.tanh(hidden)
    for layer in range(weight_hidden_ref.shape[0]):
        hidden = jnp.tanh(triple(split(hidden), split(weight_hidden_ref[layer]))) + hidden
    width = hidden.shape[1]
    out_weight = jnp.broadcast_to(weight_out_ref[...], (8, width))
    return triple(split(out_weight), split(hidden), LANES)


def natural_order(rows):
    atoms = rows.shape[1]
    padded = jnp.concatenate([rows, jnp.zeros((8, 256 - atoms), jnp.float32)], axis=1)
    pieces = []
    for chunk in range(2):
        atom = 128 * chunk + lax.broadcasted_iota(jnp.int32, (8, 128), 1)
        late = atom >= atoms // 2
        within = jnp.where(late, atom - atoms // 2, atom)
        place = 8 * (within >> 2) + (within & 3) + jnp.where(late, 4, 0)
        place = jnp.minimum(place, 255)
        pieces.append(
            jnp.where(
                place < 128,
                lane_pick(padded[:, 0:128], place & 127),
                lane_pick(padded[:, 128:256], place & 127),
            )
        )
    return jnp.concatenate(pieces, axis=1)[0:1, 0:atoms]


def network_kernel(
    ghosts,
    base_ref,
    charges_ref,
    own_ref,
    lower_ref,
    upper_ref,
    slots_ref,
    types_ref,
    cell_x_ref,
    cell_y_ref,
    cell_z_ref,
    fraction_ref,
    first_ref,
    second_ref,
    third_ref,
    spot_ref,
    weight_in_hbm,
    weight_hidden_hbm,
    weight_out_ref,
    descriptor_hbm,
    charge_ref,
    copies_ref,
    descriptor_ref,
    environment_ref,
    kind_ref,
    moments_ref,
    padded_ref,
    weight_in_ref,
    weight_hidden_ref,
    semaphores,
):
    fetches = [
        pltpu.make_async_copy(weight_in_hbm, weight_in_ref, semaphores.at[0]),
        pltpu.make_async_copy(weight_hidden_hbm, weight_hidden_ref, semaphores.at[1]),
    ]
    for fetch in fetches:
        fetch.start()
    slots, atoms = slots_ref.shape
    rows = atoms // 2
    lane = lax.broadcasted_iota(jnp.int32, (8, 128), 1)
    sub = lax.broadcasted_iota(jnp.int32, (8, 128), 0)

    width = first_ref.shape[1]
    padded_ref[...] = jnp.zeros_like(padded_ref)
    padded_ref[0, 0:2, 0:width] = first_ref[...]
    for column in range(2):
        padded_ref[1, 0:width, 32 * column : 32 * column + width] = second_ref[
            :, width * column : width * (column + 1)
        ]
    for row in range(2):
        for column in range(4):
            padded_ref[2, 32 * row : 32 * row + width, 32 * column : 32 * column + width] = (
                third_ref[
                    width * row : width * (row + 1), width * column : width * (column + 1)
                ]
            )
    first_table = padded_ref[0].T
    embed_zero = jnp.broadcast_to(first_table[0:32, 0:1], (32, 128))
    embed_one = jnp.broadcast_to(first_table[0:32, 1:2], (32, 128))
    second_high, second_low = split(padded_ref[1].T[0:64, 0:32])
    second_weight = jnp.concatenate([second_high, second_high, second_low], axis=1)
    third_high, third_low = split(padded_ref[2].T[:, 0:64])
    third_weight = jnp.concatenate([third_high, third_high, third_low], axis=1)

    def spread(ref, field, chunk):
        return jnp.broadcast_to(ref[field : field + 1, 128 * chunk : 128 * chunk + 128], (8, 128))

    own = [[spread(own_ref, field, chunk) for chunk in range(2)] for field in range(5)]
    lower = [[spread(lower_ref, field, chunk) for chunk in range(2)] for field in range(4)]
    upper = [spread(upper_ref, field, 0) for field in range(4)]

    def pick_two(tables, index):
        within = index & 127
        return jnp.where(index < 128, lane_pick(tables[0], within), lane_pick(tables[1], within))

    pairs = jnp.concatenate([slots_ref[:, 0:rows], slots_ref[:, rows:atoms]], axis=0).T
    for tile in range(rows // 8):
        band = slice(8 * tile, 8 * tile + 8)
        index = pairs[band, :]
        centre = 8 * tile + sub + jnp.where(lane < 64, 0, rows)
        from_own = jnp.clip(index - ghosts, 0, atoms - 1)
        from_lower = jnp.minimum(index + (atoms - ghosts), 255)
        from_upper = jnp.clip(index - (ghosts + atoms), 0, 127)

        def neighbour(field):
            below = pick_two(lower[field], from_lower)
            inside = pick_two(own[field], from_own)
            above = lane_pick(upper[field], from_upper)
            return jnp.where(
                index < ghosts, below, jnp.where(index < ghosts + atoms, inside, above)
            )

        offsets = [neighbour(field) - pick_two(own[field], centre) for field in range(3)]
        live = pick_two(own[4], centre)
        present = jnp.where((lane & 63).astype(jnp.float32) < live, 1.0, 0.0)
        smooth = present / (
            1.0 + (offsets[0] * offsets[0] + offsets[1] * offsets[1] + offsets[2] * offsets[2])
        )
        environment_ref[0, band, :] = smooth
        for field in range(3):
            environment_ref[1 + field, band, :] = smooth * offsets[field]
        kind_ref[band, :] = neighbour(3)

    group = 8

    def stacked(values):
        high, low = split(values)
        return jnp.concatenate([high, low, high], axis=0)

    def one_group(start):
        pieces = []
        for row in range(group):
            smooth = jnp.broadcast_to(environment_ref[0, pl.ds(start + row, 1), :], (32, 128))
            kind = jnp.broadcast_to(kind_ref[pl.ds(start + row, 1), :], (32, 128))
            pieces.append(
                jnp.tanh(smooth * ((1.0 - kind) * embed_zero + kind * embed_one))
            )
        first = jnp.concatenate(pieces, axis=1)
        second = jnp.tanh(multiply(second_weight, stacked(first), ((1,), (0,))))
        second = second + jnp.concatenate([first, first], axis=0)
        third = jnp.tanh(multiply(third_weight, stacked(second), ((1,), (0,))))
        third = third + jnp.concatenate([second, second], axis=0)
        third_pair = split(third)
        for half in range(group // 4):
            columns = slice(512 * half, 512 * half + 512)
            bands = []
            for part in range(4):
                bands.append(
                    jnp.concatenate(
                        [
                            jnp.where(
                                sub == row + jnp.where(lane < 64, 0, 4),
                                jnp.broadcast_to(
                                    environment_ref[part, pl.ds(start + 4 * half + row, 1), :],
                                    (8, 128),
                                ),
                                0.0,
                            )
                            for row in range(4)
                        ],
                        axis=1,
                    )
                )
            environment = split(jnp.concatenate(bands, axis=0))
            both = multiply(
                jnp.concatenate(environment, axis=0), third_pair[0][:, columns], LANES
            )
            sums = both[0:32] + both[32:64]
            sums = sums + multiply(environment[0], third_pair[1][:, columns], LANES)
            sums = sums * (1.0 / slots)
            for part in range(4):
                moments_ref[part, pl.ds(2 * start + 8 * half, 8), :] = sums[
                    8 * part : 8 * part + 8
                ]

    def body(step, carry):
        one_group(pl.multiple_of(step * 2 * group, 2 * group))
        one_group(pl.multiple_of(step * 2 * group + group, group))
        return carry

    lax.fori_loop(0, rows // (2 * group), body, 0)

    chunks = (descriptor_ref.shape[1] + 127) // 128
    last = descriptor_ref.shape[1] - 128 * (chunks - 1)

    def describe(step, carry):
        band = pl.ds(pl.multiple_of(step * 8, 8), 8)
        moments = [moments_ref[part, band, :] for part in range(4)]
        axis_part = [lane_pick(moments[part], lane & 15) for part in range(4)]
        for chunk in range(chunks):
            spot = jnp.broadcast_to(spot_ref[chunk : chunk + 1, :], (8, 128))
            total = lane_pick(moments[0], spot) * axis_part[0]
            for part in range(1, 4):
                total = total + lane_pick(moments[part], spot) * axis_part[part]
            if chunk < chunks - 1:
                descriptor_ref[band, 128 * chunk : 128 * chunk + 128] = total
            else:
                descriptor_ref[band, 128 * chunk : 128 * chunk + last] = total[:, 0:last]
        return carry

    lax.fori_loop(0, atoms // 8, describe, 0)

    store = pltpu.make_async_copy(descriptor_ref, descriptor_hbm, semaphores.at[2])
    store.start()
    for fetch in fetches:
        fetch.wait()
    shift = fitting_rows(descriptor_ref, weight_in_ref, weight_hidden_ref, weight_out_ref)
    kind = types_ref[...].astype(jnp.float32)
    charge = (1.0 - kind) * charges_ref[0] + kind * charges_ref[1] + natural_order(shift)
    charge_ref[...] = charge
    fields = jnp.concatenate(
        [
            cell_x_ref[...].astype(jnp.float32),
            (cell_y_ref[...] + base_ref[0]).astype(jnp.float32),
            cell_z_ref[...].astype(jnp.float32),
        ]
        + [fraction_ref[axis] for axis in range(3)]
        + [charge, jnp.zeros((1, atoms), jnp.float32)],
        axis=0,
    )
    for copy in range(copies_ref.shape[0]):
        copies_ref[copy] = fields
    store.wait()


def spot_table(embed, desc):
    column = np.arange(desc) // AXIS
    quarter = embed // 4
    place = 32 * (column // quarter) + column % quarter
    chunks = (desc + 127) // 128
    table = np.zeros((chunks * 128,), np.int32)
    table[:desc] = place
    padded = np.zeros(((chunks + 7) // 8 * 8, 128), np.int32)
    padded[:chunks] = table.reshape(chunks, 128)
    return padded


def networks(
    copies,
    ghosts,
    base,
    charge_base,
    own,
    lower,
    upper,
    neighbours,
    types,
    cells,
    fraction,
    embed,
    weight_in,
    weight_hidden,
    weight_out,
):
    atoms = types.shape[1]
    desc, width = weight_in.shape
    spots = jnp.asarray(spot_table(embed[2].shape[1], desc))
    anywhere = pl.BlockSpec(memory_space=pl.ANY)
    scalars = pl.BlockSpec(memory_space=pltpu.SMEM)
    blocks = (own, lower, upper, neighbours[0].T, types, *cells, fraction, *embed, spots)
    weight_out = weight_out.reshape(1, -1)
    results = [
        jax.ShapeDtypeStruct((atoms, desc), jnp.float32),
        jax.ShapeDtypeStruct((1, atoms), jnp.float32),
        jax.ShapeDtypeStruct((copies, 8, atoms), jnp.float32),
    ]
    return pl.pallas_call(
        functools.partial(network_kernel, ghosts),
        grid=(1,),
        out_shape=results,
        in_specs=[scalars, scalars]
        + whole_specs(*blocks)
        + [anywhere, anywhere]
        + whole_specs(weight_out),
        out_specs=[anywhere] + whole_specs(*results[1:]),
        scratch_shapes=[
            pltpu.VMEM((atoms, desc), jnp.float32),
            pltpu.VMEM((4, atoms // 2, 128), jnp.float32),
            pltpu.VMEM((atoms // 2, 128), jnp.float32),
            pltpu.VMEM((4, atoms, 128), jnp.float32),
            pltpu.VMEM((3, 128, 128), jnp.float32),
            pltpu.VMEM((width, desc), jnp.float32),
            pltpu.VMEM(weight_hidden.shape, jnp.float32),
            pltpu.SemaphoreType.DMA((3,)),
        ],
        compiler_params=pltpu.CompilerParams(vmem_limit_bytes=VMEM_BYTES),
        name="networks",
    )(base, charge_base, *blocks, weight_in.T, weight_hidden, weight_out)


def energy_kernel(descriptor_ref, weight_in_ref, weight_hidden_ref, weight_out_ref, energy_ref):
    energy_ref[...] = natural_order(
        fitting_rows(descriptor_ref, weight_in_ref, weight_hidden_ref, weight_out_ref)
    )


def energies(descriptor, weight_in, weight_hidden, weight_out):
    atoms, desc = descriptor.shape
    width = weight_in.shape[1]
    arrays = (descriptor, weight_in.T, weight_hidden, weight_out.reshape(1, -1))
    result = jax.ShapeDtypeStruct((1, atoms), jnp.float32)
    return pl.pallas_call(
        energy_kernel,
        grid=(1,),
        out_shape=result,
        in_specs=whole_specs(*arrays),
        out_specs=whole(result.shape),
        compiler_params=pltpu.CompilerParams(vmem_limit_bytes=VMEM_BYTES),
        cost_estimate=pl.CostEstimate(
            flops=6 * atoms * desc * width, bytes_accessed=4 * desc * width, transcendentals=0
        ),
        name="energies",
    )(*arrays)


def weight_rows(fraction):
    square = fraction * fraction
    cubed = square * fraction
    rest = 1.0 - fraction
    return [
        rest * rest * rest / 6.0,
        (3.0 * cubed - 6.0 * square + 4.0) / 6.0,
        (-3.0 * cubed + 3.0 * square + 3.0 * fraction + 1.0) / 6.0,
        cubed / 6.0,
    ]


def placed_weights(distance, weights):
    shape = distance.shape
    result = jnp.zeros(shape, jnp.float32)
    for step in range(4):
        result = jnp.where(
            distance == step, jnp.broadcast_to(weights[step], shape), result
        )
    return result


def third_factors(fields, waves_ref, cosine_ref):
    atoms = fields.shape[1]
    start = fields[2:3, :].astype(jnp.int32)
    along = weight_rows(fields[5:6, :])
    parts = waves_ref.shape[0]
    cosine = jnp.broadcast_to(cosine_ref[...], (parts, 128))
    wave = jnp.broadcast_to(waves_ref[:, 0:1], (parts, 128))
    shift = jnp.broadcast_to(waves_ref[:, 1:2], (parts, 128))
    pieces = []
    for chunk in range(atoms // 128):
        lanes = slice(128 * chunk, 128 * chunk + 128)
        total = jnp.zeros((parts, 128), jnp.float32)
        for step in range(4):
            place = jnp.broadcast_to(start[:, lanes] + step, (parts, 128))
            phase = (wave * place + shift) & (NG - 1)
            value = lane_pick(cosine, phase & 127)
            value = jnp.where(phase < 128, value, -value)
            total = total + value * jnp.broadcast_to(along[step][:, lanes], (parts, 128))
        pieces.append(total)
    return jnp.concatenate(pieces, axis=1)


def first_third(fields, waves_ref, cosine_ref, window, scale):
    atoms = fields.shape[1]
    third = third_factors(fields, waves_ref, cosine_ref)
    if scale is not None:
        third = third * scale
    rows = lax.broadcasted_iota(jnp.int32, (window, atoms), 0)
    first = placed_weights(
        rows - fields[0:1, :].astype(jnp.int32), weight_rows(fields[3:4, :])
    )
    return jnp.concatenate(
        [first * third[part : part + 1, :] for part in range(third.shape[0])], axis=0
    )


def second_factors(fields, base):
    rows = lax.broadcasted_iota(jnp.int32, (NG, fields.shape[1]), 0)
    start = fields[1:2, :].astype(jnp.int32) - base
    return placed_weights((rows - start) & (NG - 1), weight_rows(fields[4:5, :]))


def wave_of(index):
    return jnp.where(index <= NG // 2, index, index - NG // 2)


def damping(index):
    kappa = wave_of(index).astype(jnp.float32) * (2.0 * math.pi / NG)
    squared = kappa * kappa
    ends = (index == 0) | (index == NG // 2)
    return squared, jnp.exp(-0.5 * squared) * jnp.where(ends, 1.0 / NG, 2.0 / NG)


def transform(planes, kappa_ref, first_part, tables_ref, last_ref):
    count = len(planes)
    basis = (tables_ref[0], tables_ref[1])
    turned = (tables_ref[2], tables_ref[3])
    last = (last_ref[0], last_ref[1])
    square_x, damp_x = damping(lax.broadcasted_iota(jnp.int32, (NG, 1), 0))
    square_y, damp_y = damping(lax.broadcasted_iota(jnp.int32, (1, NG), 1))
    square_xy = square_x + square_y
    damp_xy = damp_x * damp_y
    columns = [slice(NG * part, NG * (part + 1)) for part in range(count)]
    first = triple(basis, split(jnp.concatenate(planes, axis=1)))
    first = jnp.concatenate([first[:, column] for column in columns], axis=0)
    both = triple(split(first), turned)
    scaled = []
    for part in range(count):
        squared = square_xy + kappa_ref[first_part + part, 0]
        root = jnp.where(squared == 0.0, 1.0, 0.0)
        green = (1.0 - root) * (damp_xy * kappa_ref[first_part + part, 1]) / (squared + root)
        scaled.append(both[columns[part]] * green)
    back = triple(turned, split(jnp.concatenate(scaled, axis=1)))
    back = jnp.concatenate([back[:, column] for column in columns], axis=0)
    return triple(split(back), last)


def send_blocks(full, block_x, block_y, put):
    low_lanes = lax.broadcasted_iota(jnp.int32, (NG, 128), 1) < block_y
    for pair in range(full.shape[0] // (2 * NG)):
        even = full[2 * NG * pair : 2 * NG * pair + NG, 0:128]
        odd = full[2 * NG * pair + NG : 2 * NG * (pair + 1), 0:128]
        blocks = [
            jnp.where(low_lanes, even, pltpu.roll(odd, block_y, 1)),
            jnp.where(low_lanes, pltpu.roll(even, block_y, 1), odd),
        ]
        for brick in range(NG // block_x):
            for side in range(2):
                for group in range(block_x // 8):
                    start = block_x * brick + 8 * group
                    put(pair, brick, side, group, blocks[side][start : start + 8])


def spread_kernel(
    block_x,
    block_y,
    window,
    kappa_ref,
    pair_ref,
    static_ref,
    waves_ref,
    cosine_ref,
    tables_hbm,
    last_hbm,
    sent_ref,
    full_ref,
    atoms_ref,
    later_hbm,
    grid_ref,
    tables_ref,
    last_ref,
    semaphores,
):
    slabs = NG // block_y
    bricks = NG // block_x
    parts = waves_ref.shape[0]
    block = static_ref.shape[2]
    count = full_ref.shape[0]
    step = pl.program_id(0)
    store = pltpu.make_async_copy(
        grid_ref.at[pl.ds(parts // 2, parts // 2), pl.ds(0, NG)], later_hbm, semaphores.at[2]
    )

    @pl.when(step == 0)
    def _():
        fetches = [
            pltpu.make_async_copy(tables_hbm, tables_ref, semaphores.at[0]),
            pltpu.make_async_copy(last_hbm.at[pair_ref[0]], last_ref, semaphores.at[1]),
        ]
        for fetch in fetches:
            fetch.start()
        for slab in range(slabs):
            lanes = slice(block * slab, block * (slab + 1))
            for brick in range(bricks):
                atoms_ref[brick, :, lanes] = static_ref[slab * bricks + brick]
        grid_ref[...] = jnp.zeros_like(grid_ref)
        for brick in range(bricks):
            fields = atoms_ref[brick]
            table = split(first_third(fields, waves_ref, cosine_ref, window, fields[6:7, :]))
            spread = triple(table, split(second_factors(fields, 0)), LANES)
            rows = slice(block_x * brick, block_x * brick + window)
            for part in range(parts):
                grid_ref[part, rows, :] += spread[part * window : part * window + window]
        extra = window - block_x
        for part in range(parts):
            grid_ref[part, 0:extra, :] += grid_ref[part, NG : NG + extra, :]
        store.start()
        for fetch in fetches:
            fetch.wait()

    planes = [grid_ref[count * step + part, 0:NG, :] for part in range(count)]
    full = transform(planes, kappa_ref, count * step, tables_ref, last_ref)
    for part in range(count):
        full_ref[part] = full[NG * part : NG * (part + 1)]

    def put(pair, brick, side, group, tile):
        sent_ref[2 * brick + side, group, pair] = tile

    send_blocks(full, block_x, block_y, put)

    @pl.when(step == pl.num_programs(0) - 1)
    def _():
        store.wait()


def spread_and_solve(
    block_x, block_y, window, kappa, pair, static, waves, cosine_row, tables, last
):
    devices, _, atoms = static.shape
    slabs = NG // block_y
    bricks = NG // block_x
    parts = waves.shape[0]
    pairs = parts // 4
    count = 4
    anywhere = pl.BlockSpec(memory_space=pl.ANY)
    scalars = pl.BlockSpec(memory_space=pltpu.SMEM)
    sent_block = (2 * bricks, block_x // 8, count // 2, 8, 128)
    return pl.pallas_call(
        functools.partial(spread_kernel, block_x, block_y, window),
        grid=(parts // 2 // count,),
        out_shape=[
            jax.ShapeDtypeStruct((2 * bricks, block_x // 8, pairs, 8, 128), jnp.float32),
            jax.ShapeDtypeStruct((parts // 2, NG, NG), jnp.float32),
            jax.ShapeDtypeStruct((bricks, 8, slabs * atoms), jnp.float32),
            jax.ShapeDtypeStruct((parts // 2, NG, NG), jnp.float32),
        ],
        in_specs=[scalars, scalars]
        + whole_specs(static, waves, cosine_row)
        + [anywhere, anywhere],
        out_specs=[
            pl.BlockSpec(sent_block, lambda step: (0, 0, step, 0, 0)),
            pl.BlockSpec((count, NG, NG), lambda step: (step, 0, 0)),
            whole((bricks, 8, slabs * atoms)),
            anywhere,
        ],
        scratch_shapes=[
            pltpu.VMEM((parts, NG + window - block_x, NG), jnp.float32),
            pltpu.VMEM(tables.shape, tables.dtype),
            pltpu.VMEM(last.shape[1:], last.dtype),
            pltpu.SemaphoreType.DMA((3,)),
        ],
        compiler_params=pltpu.CompilerParams(vmem_limit_bytes=VMEM_BYTES),
        name="spread_and_solve",
    )(kappa, pair, static, waves, cosine_row, tables, last)


def sample_kernel(
    block_x,
    block_y,
    window,
    kappa_ref,
    pair_ref,
    atoms_ref,
    waves_ref,
    cosine_ref,
    tables_hbm,
    last_hbm,
    later_hbm,
    early_hbm,
    sent_ref,
    later_ref,
    full_ref,
    tables_ref,
    last_ref,
    semaphores,
):
    bricks = atoms_ref.shape[0]
    parts = waves_ref.shape[0]
    half = parts // 2
    count = 4
    block = atoms_ref.shape[2] * block_y // NG
    fetches = [
        pltpu.make_async_copy(tables_hbm, tables_ref, semaphores.at[0]),
        pltpu.make_async_copy(last_hbm.at[pair_ref[0]], last_ref, semaphores.at[1]),
        pltpu.make_async_copy(later_hbm, later_ref, semaphores.at[2]),
        pltpu.make_async_copy(early_hbm, full_ref.at[pl.ds(0, half)], semaphores.at[3]),
    ]
    for fetch in fetches:
        fetch.start()
    for fetch in fetches[:3]:
        fetch.wait()
    pairs = half // 2
    for step in range(half // count):
        planes = [later_ref[count * step + part] for part in range(count)]
        full = transform(planes, kappa_ref, half + count * step, tables_ref, last_ref)
        for part in range(count):
            full_ref[half + count * step + part] = full[NG * part : NG * (part + 1)]

        def put(pair, brick, side, group, tile):
            sent_ref[2 * brick + side, pairs * group + count // 2 * step + pair] = tile

        send_blocks(full, block_x, block_y, put)
    fetches[3].wait()

    extra = sent_ref.shape[1] - 1
    base = 2 * block_y * pair_ref[0]
    lanes = pl.ds(pl.multiple_of(2 * block * pair_ref[0], 128), 2 * block)
    for brick in range(bricks):
        fields = atoms_ref[brick, :, lanes]
        weights = first_third(fields, waves_ref, cosine_ref, window, None)
        start = block_x * brick
        inside = min(window, NG - start)
        values = []
        for part in range(parts):
            values.append(full_ref[part, start : start + inside, :])
            if inside < window:
                values.append(full_ref[part, 0 : window - inside, :])
        values = split(jnp.concatenate(values, axis=0))
        along = triple(values, split(second_factors(fields, base)))
        sums = jnp.sum(along * weights, axis=0, keepdims=True)
        for side in range(2):
            row = sums[:, block * side : block * (side + 1)]
            sent_ref[2 * brick + side, extra] = jnp.zeros((8, 128), jnp.float32)
            sent_ref[2 * brick + side, extra, 0:1, :] = row[:, 0:128]
            sent_ref[2 * brick + side, extra, 1:2, 0 : block - 128] = row[:, 128:block]


def solve_and_sample(
    block_x, block_y, window, kappa, pair, atoms, waves, cosine_row, tables, last, later, early
):
    bricks = atoms.shape[0]
    parts = waves.shape[0]
    pairs = parts // 4
    anywhere = pl.BlockSpec(memory_space=pl.ANY)
    scalars = pl.BlockSpec(memory_space=pltpu.SMEM)
    result = jax.ShapeDtypeStruct((2 * bricks, block_x // 8 * pairs + 1, 8, 128), jnp.float32)
    return pl.pallas_call(
        functools.partial(sample_kernel, block_x, block_y, window),
        grid=(1,),
        out_shape=result,
        in_specs=[scalars, scalars] + whole_specs(atoms, waves, cosine_row) + [anywhere] * 4,
        out_specs=whole(result.shape),
        scratch_shapes=[
            pltpu.VMEM((parts // 2, NG, NG), jnp.float32),
            pltpu.VMEM((parts, NG, NG), jnp.float32),
            pltpu.VMEM(tables.shape, tables.dtype),
            pltpu.VMEM(last.shape[1:], last.dtype),
            pltpu.SemaphoreType.DMA((4,)),
        ],
        compiler_params=pltpu.CompilerParams(vmem_limit_bytes=VMEM_BYTES),
        cost_estimate=pl.CostEstimate(
            flops=24 * parts * NG * NG * NG, bytes_accessed=4 * early.size, transcendentals=0
        ),
        name="solve_and_sample",
    )(kappa, pair, atoms, waves, cosine_row, tables, last, later, early)


def finish_kernel(
    block_y, early_ref, later_ref, sums_ref, short_ref, charge_ref, table_ref, out_ref, energy_ref
):
    atoms = short_ref.shape[1]
    table = (table_ref[0], table_ref[1])
    lines = early_ref.shape[3]
    rows = early_ref.shape[0] * early_ref.shape[2]
    early = early_ref.reshape(rows, lines, 128)
    later = later_ref.reshape(rows, lines, 128)
    pieces = []
    for line in range(lines):
        turned = jnp.concatenate([early[:, line, :], later[:, line, :]], axis=0).T
        pieces.append(jnp.concatenate([turned[0:block_y], turned[block_y:]], axis=1))
    result = triple(split(jnp.concatenate(pieces, axis=0)), table)
    for line in range(lines):
        out_ref[line] = result[block_y * line : block_y * (line + 1)]

    @pl.when(pl.program_id(0) == 0)
    def _():
        total = jnp.sum(sums_ref[:, 0], axis=0)
        potential_at = jnp.concatenate([total[0:1, :], total[1:2, 0 : atoms - 128]], axis=1)
        energy_ref[...] = short_ref[...] + 0.5 * charge_ref[...] * potential_at


def finish(block_x, block_y, early, later, short, charge, table):
    bricks2, groups, pairs = early.shape[:3]
    atoms = short.shape[1]
    return pl.pallas_call(
        functools.partial(finish_kernel, block_y),
        grid=(groups,),
        out_shape=[
            jax.ShapeDtypeStruct((block_x, block_y, NG), jnp.float32),
            jax.ShapeDtypeStruct((1, atoms), jnp.float32),
        ],
        in_specs=[
            pl.BlockSpec((bricks2, 1, pairs, 8, 128), lambda index: (0, index, 0, 0, 0)),
            pl.BlockSpec((bricks2, pairs, 8, 128), lambda index: (0, index, 0, 0)),
            pl.BlockSpec((bricks2, 1, 8, 128), lambda index: (0, groups * pairs, 0, 0)),
            whole((1, atoms)),
            whole((1, atoms)),
            whole(table.shape),
        ],
        out_specs=[
            pl.BlockSpec((8, block_y, NG), lambda index: (index, 0, 0)),
            whole((1, atoms)),
        ],
        compiler_params=pltpu.CompilerParams(vmem_limit_bytes=32 * 2**20),
        name="finish",
    )(early, later, later, short, charge, table)


def two_parts(table):
    table = np.asarray(table, np.float32)
    high = table.astype(ml_dtypes.bfloat16)
    low = (table - high.astype(np.float32)).astype(ml_dtypes.bfloat16)
    return np.stack([high, low])


def real_basis():
    index = np.arange(NG)
    wave = np.where(index <= NG // 2, index, index - NG // 2)
    angle = (wave[:, None] * index[None, :] % NG) * (2.0 * math.pi / NG)
    return np.where((index <= NG // 2)[:, None], np.cos(angle), np.sin(angle))


def per_device(
    positions,
    types,
    neighbours,
    neighbour_count,
    send_index,
    cell_x,
    cell_y,
    cell_z,
    spline_fraction,
    embed_first,
    embed_second,
    embed_third,
    energy_in,
    energy_hidden,
    energy_out,
    wannier_in,
    wannier_hidden,
    wannier_out,
    charge_base,
):
    atoms = types.shape[1]
    ghosts = send_index.shape[1] // 2
    count_x = lax.axis_size("brick")
    count_y = lax.axis_size("slab")
    block_x = NG // count_x
    block_y = NG // count_y
    window = block_x + 8
    parts = NG // (2 * count_x)
    brick = lax.axis_index("brick")
    slab = lax.axis_index("slab")
    pair = (slab // 2).astype(jnp.int32).reshape(1)
    halves = [
        [b * count_y + 2 * p + side for b in range(count_x) for side in range(2)]
        for p in range(count_y // 2)
    ]

    def exchange(values, axes, groups=None):
        return lax.all_to_all(
            values, axes, split_axis=0, concat_axis=0, tiled=True, axis_index_groups=groups
        )

    own, outgoing = collect(positions, types, neighbour_count, send_index)
    up = [(i, (i + 1) % count_x) for i in range(count_x)]
    down = [((i + 1) % count_x, i) for i in range(count_x)]
    lower = lax.ppermute(outgoing, "brick", up)
    upper = lax.ppermute(outgoing, "brick", down)
    descriptor, charge, fields = networks(
        count_x * count_y,
        ghosts,
        (slab * block_y).astype(jnp.int32).reshape(1),
        charge_base,
        own,
        lower,
        upper,
        neighbours,
        types,
        (cell_x, cell_y, cell_z),
        spline_fraction,
        (embed_first, embed_second, embed_third),
        wannier_in,
        wannier_hidden,
        wannier_out,
    )
    every_field = exchange(fields, ("slab", "brick"))

    part = (2 * brick + slab % 2) * parts + jnp.arange(parts, dtype=jnp.int32)
    wave = wave_of(part)
    waves = jnp.stack([wave, jnp.where(part <= NG // 2, 0, 3 * NG // 4)], axis=1)
    kappa = wave.astype(jnp.float32) * (2.0 * math.pi / NG)
    squared = kappa * kappa
    ends = (part == 0) | (part == NG // 2)
    kappa = jnp.stack(
        [squared, jnp.exp(-0.5 * squared) * jnp.where(ends, 1.0 / NG, 2.0 / NG)], axis=1
    )
    basis = real_basis()
    tables = np.concatenate([two_parts(basis), two_parts(basis.T)])
    last = []
    for p in range(count_y // 2):
        points = (2 * block_y * p + np.arange(2 * block_y + 8)) % NG
        columns = np.zeros((NG, NG))
        columns[:, : points.size] = basis[:, points]
        last.append(two_parts(columns))
    cosine_row = np.cos(np.arange(128) * (2.0 * math.pi / NG)).astype(np.float32)[None]
    cosine_row = jnp.asarray(cosine_row)
    tables = jnp.asarray(tables)
    last = jnp.asarray(np.stack(last))
    early, full, every_atom, later = spread_and_solve(
        block_x, block_y, window, kappa, pair, every_field, waves, cosine_row, tables, last
    )

    def send(values):
        got = exchange(values.reshape(values.shape[0], -1, 128), ("brick", "slab"), halves)
        return got.reshape(values.shape)

    early = send(early)
    later = solve_and_sample(
        block_x,
        block_y,
        window,
        kappa,
        pair,
        every_atom,
        waves,
        cosine_row,
        tables,
        last,
        later,
        full,
    )
    later = send(later)
    energy_short = energies(descriptor, energy_in, energy_hidden, energy_out)
    source = np.arange(2 * count_x)[:, None] * parts
    pairs = 2 * np.arange(parts // 2)[None, :]
    order = np.concatenate(
        [(source + pairs[:, : parts // 4]).ravel(), (source + pairs[:, parts // 4 :]).ravel()]
    )
    order = np.concatenate([order, order + 1])
    potential, atom_energy = finish(
        block_x,
        block_y,
        early,
        later,
        energy_short,
        charge,
        jnp.asarray(two_parts(basis[order])),
    )
    return atom_energy, potential


def solution(mesh):
    placed = (
        P(None, "slab", "brick"),
        P("slab", "brick"),
        P("slab", "brick", None),
        P("slab", "brick"),
        P("slab", "brick"),
        P("slab", "brick"),
        P("slab", "brick"),
        P("slab", "brick"),
        P(None, "slab", "brick"),
    ) + (P(),) * 10
    bricks, slabs = mesh.shape["brick"], mesh.shape["slab"]
    fits = 2 * NG == 128 * slabs and NG % (16 * bricks) == 0
    return jax.shard_map(
        per_device if fits else per_device_general,
        mesh=mesh,
        in_specs=placed,
        out_specs=(P("slab", "brick"), P("brick", "slab", None)),
        check_vma=False,
    )
```

```python
import functools
import math

import jax
import jax.numpy as jnp
import ml_dtypes
import numpy as np
from jax import lax
from jax.experimental import pallas as pl
from jax.experimental.pallas import tpu as pltpu
from jax.sharding import PartitionSpec as P

NG = 256
AXIS = 16
VMEM_BYTES = 60 * 2**20


HIGH = lax.Precision.HIGHEST


def with_halo(cells, sides, width):
    for axis, dim in sides:
        count = lax.axis_size(axis)
        head = lax.slice_in_dim(cells, 0, width, axis=dim)
        tail = lax.slice_in_dim(cells, cells.shape[dim] - width, cells.shape[dim], axis=dim)
        cells = jnp.concatenate(
            [
                lax.ppermute(tail, axis, [(i, (i + 1) % count) for i in range(count)]),
                cells,
                lax.ppermute(head, axis, [((i + 1) % count, i) for i in range(count)]),
            ],
            axis=dim,
        )
    return cells


def spline_weights(fraction):
    cubed = fraction * fraction * fraction
    square = fraction * fraction
    return jnp.stack(
        [
            (1.0 - fraction) * (1.0 - fraction) * (1.0 - fraction) / 6.0,
            (3.0 * cubed - 6.0 * square + 4.0) / 6.0,
            (-3.0 * cubed + 3.0 * square + 3.0 * fraction + 1.0) / 6.0,
            cubed / 6.0,
        ]
    )


def fitting(descriptor, weight_in, weight_hidden, weight_out):
    hidden = jnp.tanh(jnp.dot(descriptor, weight_in, precision=HIGH))
    for depth_index in range(weight_hidden.shape[0]):
        hidden = jnp.tanh(jnp.dot(hidden, weight_hidden[depth_index], precision=HIGH)) + hidden
    return jnp.dot(hidden, weight_out, precision=HIGH)


def atom_terms(
    extended,
    neighbour_rows,
    neighbour_total,
    embed_first,
    embed_second,
    embed_third,
    energy_in,
    energy_hidden,
    energy_out,
    wannier_in,
    wannier_hidden,
    wannier_out,
):
    atom_count, slots = neighbour_rows.shape
    ghost_rows = (extended.shape[1] - atom_count) // 2
    block_size = 64
    blocks = atom_count // block_size
    present = (jnp.arange(slots, dtype=jnp.int32)[None, :] < neighbour_total[:, None]).astype(
        jnp.float32
    )
    centre_ids = (ghost_rows + jnp.arange(atom_count, dtype=jnp.int32)).reshape(blocks, block_size)
    second_weight = embed_second.T
    third_weight = embed_third.T

    def one_block(pieces):
        centre_rows, rows_block, present_block = pieces
        centre_block = extended[:3, centre_rows]
        gathered = extended[:, rows_block]
        offsets = gathered[:3] - centre_block[:, :, None]
        smooth = present_block / (1.0 + jnp.sum(offsets * offsets, axis=0))
        environment = jnp.stack(
            [smooth, smooth * offsets[0], smooth * offsets[1], smooth * offsets[2]], axis=0
        )
        kind = gathered[3][None]
        mixing = (1.0 - kind) * embed_first[0][:, None, None] + kind * embed_first[1][:, None, None]
        first = jnp.tanh(smooth[None] * mixing).reshape(embed_first.shape[1], block_size * slots)
        second = jnp.tanh(jnp.dot(second_weight, first, precision=HIGH)) + jnp.concatenate(
            [first, first], axis=0
        )
        third = jnp.tanh(jnp.dot(third_weight, second, precision=HIGH)) + jnp.concatenate(
            [second, second], axis=0
        )
        third_blocks = third.reshape(third.shape[0], block_size, slots)
        moments = jnp.einsum("kan,can->akc", third_blocks, environment, precision=HIGH) / slots
        descriptor = jnp.einsum("amc,akc->amk", moments, moments[:, :AXIS], precision=HIGH).reshape(
            block_size, -1
        )
        return (
            fitting(descriptor, energy_in, energy_hidden, energy_out),
            fitting(descriptor, wannier_in, wannier_hidden, wannier_out),
        )

    energy_short, charge_shift = lax.map(
        one_block,
        (
            centre_ids,
            neighbour_rows.reshape(blocks, block_size, slots),
            present.reshape(blocks, block_size, slots),
        ),
    )
    return (energy_short.reshape(atom_count), charge_shift.reshape(atom_count))


def green_table(first, second, third, size):

    def folded(index):
        return jnp.where(index < size // 2, index, index - size).astype(jnp.float32) * (
            2.0 * math.pi / size
        )

    kappa_x = folded(first)[:, None, None]
    kappa_y = folded(second)[None, :, None]
    kappa_z = folded(third)[None, None, :]
    squared = kappa_x * kappa_x + kappa_y * kappa_y + kappa_z * kappa_z
    root = (
        (first[:, None, None] == 0) & (second[None, :, None] == 0) & (third[None, None, :] == 0)
    ).astype(jnp.float32)
    return (1.0 - root) * jnp.exp(-0.5 * squared) / (squared + root)


def dft_tables(size):
    index = jnp.arange(size, dtype=jnp.int32)
    phase = (index[:, None] * index[None, :] % size).astype(jnp.float32) * (2.0 * math.pi / size)
    return (jnp.cos(phase), jnp.sin(phase))


def along(values, table, axis_index):
    result = jnp.tensordot(values, table, axes=([axis_index], [0]), precision=HIGH)
    return jnp.moveaxis(result, -1, axis_index)


def complex_transform(paired, axis_index, cosine, sine, inverse):
    real_part = paired[0]
    imag_part = paired[1]
    inner = axis_index - 1
    real_cos = along(real_part, cosine, inner)
    real_sin = along(real_part, sine, inner)
    imag_cos = along(imag_part, cosine, inner)
    imag_sin = along(imag_part, sine, inner)
    if inverse:
        return jnp.stack([real_cos - imag_sin, imag_cos + real_sin])
    return jnp.stack([real_cos + imag_sin, imag_cos - real_sin])


def fold_windows(values, axis_index, block, count):
    front = jnp.moveaxis(values, axis_index, 0)
    rest = front.shape[1:]
    windows = front.reshape((count, block + 3) + rest)
    main_part = windows[:, :block]
    carried = jnp.roll(windows[:, block:], 1, axis=0)
    main_part = main_part.at[:, :3].add(carried)
    return jnp.moveaxis(main_part.reshape((count * block,) + rest), 0, axis_index)


def make_windows(values, axis_index, block, count):
    front = jnp.moveaxis(values, axis_index, 0)
    rest = front.shape[1:]
    pieces = front.reshape((count, block) + rest)
    trailing = jnp.roll(pieces, -1, axis=0)[:, :3]
    windows = jnp.concatenate([pieces, trailing], axis=1)
    return jnp.moveaxis(windows.reshape((count * (block + 3),) + rest), 0, axis_index)


def spread_matrix(start, weights, width, wrap_size):
    offsets = jnp.arange(4, dtype=jnp.int32)[:, None, None]
    target = start[None, :, None] + offsets
    if wrap_size > 0:
        target = target % wrap_size
    hits = (target == jnp.arange(width, dtype=jnp.int32)[None, None, :]).astype(jnp.float32)
    return jnp.sum(weights[:, :, None] * hits, axis=0)


def per_device_general(
    positions,
    types,
    neighbours,
    neighbour_count,
    send_index,
    cell_x,
    cell_y,
    cell_z,
    spline_fraction,
    embed_first,
    embed_second,
    embed_third,
    energy_in,
    energy_hidden,
    energy_out,
    wannier_in,
    wannier_hidden,
    wannier_out,
    charge_base,
):
    atom_count = types.shape[1]
    ghost_rows = send_index.shape[1] // 2
    kind_float = types[0].astype(jnp.float32)
    own_atoms = jnp.concatenate([positions[:, 0], kind_float[None]], axis=0)
    outgoing = own_atoms[:, send_index[0]]
    padded_ghosts = with_halo(outgoing, (("brick", 1),), ghost_rows)
    extended = jnp.concatenate(
        [padded_ghosts[:, :ghost_rows], own_atoms, padded_ghosts[:, 3 * ghost_rows :]], axis=1
    )
    energy_short, charge_shift = atom_terms(
        extended,
        neighbours[0],
        neighbour_count[0],
        embed_first,
        embed_second,
        embed_third,
        energy_in,
        energy_hidden,
        energy_out,
        wannier_in,
        wannier_hidden,
        wannier_out,
    )
    charge = (1.0 - kind_float) * charge_base[0] + kind_float * charge_base[1] + charge_shift
    count_x = lax.axis_size("brick")
    count_y = lax.axis_size("slab")
    block_x = NG // count_x
    block_y = NG // count_y
    wide_x = block_x + 3
    wide_y = block_y + 3
    spread_x = spread_matrix(cell_x[0], spline_weights(spline_fraction[0, 0]), wide_x, 0)
    spread_y = spread_matrix(cell_y[0], spline_weights(spline_fraction[1, 0]), wide_y, 0)
    spread_z = spread_matrix(cell_z[0], spline_weights(spline_fraction[2, 0]), NG, NG)
    spread_xy = (spread_x[:, :, None] * spread_y[:, None, :]).reshape(atom_count, wide_x * wide_y)
    charge_grid = jnp.einsum(
        "ap,az->pz", spread_xy, charge[:, None] * spread_z, precision=HIGH
    ).reshape(wide_x, wide_y, NG)
    cosine, sine = dft_tables(NG)
    scale = 1.0 / (NG * NG * NG)
    full_index = jnp.arange(NG, dtype=jnp.int32)
    paired = jnp.stack([along(charge_grid, cosine, 2), -along(charge_grid, sine, 2)])
    moved = lax.all_to_all(paired, "slab", split_axis=3, concat_axis=2, tiled=True)
    moved = complex_transform(fold_windows(moved, 2, block_y, count_y), 2, cosine, sine, False)
    moved = lax.all_to_all(moved, "brick", split_axis=2, concat_axis=1, tiled=True)
    moved = complex_transform(fold_windows(moved, 1, block_x, count_x), 1, cosine, sine, False)
    part_y = NG // count_x
    part_z = NG // count_y
    index_y = lax.axis_index("brick") * part_y + jnp.arange(part_y, dtype=jnp.int32)
    index_z = lax.axis_index("slab") * part_z + jnp.arange(part_z, dtype=jnp.int32)
    moved = moved * (green_table(full_index, index_y, index_z, NG) * scale)[None]
    moved = make_windows(complex_transform(moved, 1, cosine, sine, True), 1, block_x, count_x)
    moved = lax.all_to_all(moved, "brick", split_axis=1, concat_axis=2, tiled=True)
    moved = make_windows(complex_transform(moved, 2, cosine, sine, True), 2, block_y, count_y)
    moved = lax.all_to_all(moved, "slab", split_axis=2, concat_axis=3, tiled=True)
    potential_wide = along(moved[0], cosine, 2) - along(moved[1], sine, 2)
    sampled = jnp.einsum(
        "ap,pz->az", spread_xy, potential_wide.reshape(wide_x * wide_y, NG), precision=HIGH
    )
    potential_at = jnp.sum(sampled * spread_z, axis=1)
    atom_energy = energy_short + 0.5 * charge * potential_at
    return (atom_energy[None, :], potential_wide[:block_x, :block_y])


def split(values):
    high = values.astype(jnp.bfloat16)
    low = (values - high.astype(jnp.float32)).astype(jnp.bfloat16)
    return high, low


def multiply(left, right, dims):
    return lax.dot_general(left, right, (dims, ((), ())), preferred_element_type=jnp.float32)


def triple(left, right, dims=((1,), (0,))):
    (left_axis,), (right_axis,) = dims
    if left[0].shape[left_axis] % 128 == 0:
        return multiply(
            jnp.concatenate([left[0], left[0], left[1]], axis=left_axis),
            jnp.concatenate([right[0], right[1], right[0]], axis=right_axis),
            dims,
        )
    return (
        multiply(left[0], right[0], dims)
        + multiply(left[0], right[1], dims)
        + multiply(left[1], right[0], dims)
    )


LANES = ((1,), (1,))


def lane_pick(table, index):
    return jnp.take_along_axis(table, index, axis=1, mode="promise_in_bounds")


def whole(shape):
    return pl.BlockSpec(tuple(shape), lambda step: (0,) * len(shape))


def whole_specs(*arrays):
    return [whole(array.shape) for array in arrays]


def collect_kernel(
    positions_ref, types_ref, count_ref, send_ref, own_ref, outgoing_ref
):
    atoms = types_ref.shape[1]
    own_ref[...] = jnp.zeros_like(own_ref)
    for axis in range(3):
        own_ref[axis : axis + 1, 0:atoms] = positions_ref[axis]
    own_ref[3:4, 0:atoms] = types_ref[...].astype(jnp.float32)
    own_ref[4:5, 0:atoms] = count_ref[...].astype(jnp.float32)
    own_ref[5:6, 0:atoms] = send_ref[...].astype(jnp.float32)
    for chunk in range(2):
        lanes = slice(128 * chunk, 128 * chunk + 128)
        wanted = jnp.broadcast_to(own_ref[5:6, lanes], (8, 128)).astype(jnp.int32)
        within = wanted & 127
        outgoing_ref[:, lanes] = jnp.where(
            wanted < 128,
            lane_pick(own_ref[:, 0:128], within),
            lane_pick(own_ref[:, 128:256], within),
        )


def collect(positions, types, counts, send_index):
    arrays = (positions, types, counts, send_index)
    result = jax.ShapeDtypeStruct((8, 256), jnp.float32)
    return pl.pallas_call(
        collect_kernel,
        grid=(1,),
        out_shape=[result, result],
        in_specs=whole_specs(*arrays),
        out_specs=whole_specs(result, result),
        compiler_params=pltpu.CompilerParams(vmem_limit_bytes=VMEM_BYTES),
        name="collect_atoms",
    )(*arrays)


def fitting_rows(descriptor_ref, weight_in_ref, weight_hidden_ref, weight_out_ref):
    depth = weight_in_ref.shape[1]
    first = depth // 256 * 256
    hidden = triple(
        split(descriptor_ref[:, 0:first]), split(weight_in_ref[:, 0:first]), LANES
    )
    if first < depth:
        hidden = hidden + triple(
            split(descriptor_ref[:, first:depth]), split(weight_in_ref[:, first:depth]), LANES
        )
    hidden = jnp.tanh(hidden)
    for layer in range(weight_hidden_ref.shape[0]):
        hidden = jnp.tanh(triple(split(hidden), split(weight_hidden_ref[layer]))) + hidden
    width = hidden.shape[1]
    out_weight = jnp.broadcast_to(weight_out_ref[...], (8, width))
    return triple(split(out_weight), split(hidden), LANES)


def natural_order(rows):
    atoms = rows.shape[1]
    padded = jnp.concatenate([rows, jnp.zeros((8, 256 - atoms), jnp.float32)], axis=1)
    pieces = []
    for chunk in range(2):
        atom = 128 * chunk + lax.broadcasted_iota(jnp.int32, (8, 128), 1)
        late = atom >= atoms // 2
        within = jnp.where(late, atom - atoms // 2, atom)
        place = 8 * (within >> 2) + (within & 3) + jnp.where(late, 4, 0)
        place = jnp.minimum(place, 255)
        pieces.append(
            jnp.where(
                place < 128,
                lane_pick(padded[:, 0:128], place & 127),
                lane_pick(padded[:, 128:256], place & 127),
            )
        )
    return jnp.concatenate(pieces, axis=1)[0:1, 0:atoms]


def network_kernel(
    ghosts,
    base_ref,
    charges_ref,
    own_ref,
    lower_ref,
    upper_ref,
    slots_ref,
    types_ref,
    cell_x_ref,
    cell_y_ref,
    cell_z_ref,
    fraction_ref,
    first_ref,
    second_ref,
    third_ref,
    spot_ref,
    weight_in_hbm,
    weight_hidden_hbm,
    weight_out_ref,
    descriptor_hbm,
    charge_ref,
    copies_ref,
    descriptor_ref,
    environment_ref,
    kind_ref,
    moments_ref,
    padded_ref,
    weight_in_ref,
    weight_hidden_ref,
    semaphores,
):
    fetches = [
        pltpu.make_async_copy(weight_in_hbm, weight_in_ref, semaphores.at[0]),
        pltpu.make_async_copy(weight_hidden_hbm, weight_hidden_ref, semaphores.at[1]),
    ]
    for fetch in fetches:
        fetch.start()
    slots, atoms = slots_ref.shape
    rows = atoms // 2
    lane = lax.broadcasted_iota(jnp.int32, (8, 128), 1)
    sub = lax.broadcasted_iota(jnp.int32, (8, 128), 0)

    width = first_ref.shape[1]
    padded_ref[...] = jnp.zeros_like(padded_ref)
    padded_ref[0, 0:2, 0:width] = first_ref[...]
    for column in range(2):
        padded_ref[1, 0:width, 32 * column : 32 * column + width] = second_ref[
            :, width * column : width * (column + 1)
        ]
    for row in range(2):
        for column in range(4):
            padded_ref[2, 32 * row : 32 * row + width, 32 * column : 32 * column + width] = (
                third_ref[
                    width * row : width * (row + 1), width * column : width * (column + 1)
                ]
            )
    first_table = padded_ref[0].T
    embed_zero = jnp.broadcast_to(first_table[0:32, 0:1], (32, 128))
    embed_one = jnp.broadcast_to(first_table[0:32, 1:2], (32, 128))
    second_high, second_low = split(padded_ref[1].T[0:64, 0:32])
    second_weight = jnp.concatenate([second_high, second_high, second_low], axis=1)
    third_high, third_low = split(padded_ref[2].T[:, 0:64])
    third_weight = jnp.concatenate([third_high, third_high, third_low], axis=1)

    def spread(ref, field, chunk):
        return jnp.broadcast_to(ref[field : field + 1, 128 * chunk : 128 * chunk + 128], (8, 128))

    own = [[spread(own_ref, field, chunk) for chunk in range(2)] for field in range(5)]
    lower = [[spread(lower_ref, field, chunk) for chunk in range(2)] for field in range(4)]
    upper = [spread(upper_ref, field, 0) for field in range(4)]

    def pick_two(tables, index):
        within = index & 127
        return jnp.where(index < 128, lane_pick(tables[0], within), lane_pick(tables[1], within))

    pairs = jnp.concatenate([slots_ref[:, 0:rows], slots_ref[:, rows:atoms]], axis=0).T
    for tile in range(rows // 8):
        band = slice(8 * tile, 8 * tile + 8)
        index = pairs[band, :]
        centre = 8 * tile + sub + jnp.where(lane < 64, 0, rows)
        from_own = jnp.clip(index - ghosts, 0, atoms - 1)
        from_lower = jnp.minimum(index + (atoms - ghosts), 255)
        from_upper = jnp.clip(index - (ghosts + atoms), 0, 127)

        def neighbour(field):
            below = pick_two(lower[field], from_lower)
            inside = pick_two(own[field], from_own)
            above = lane_pick(upper[field], from_upper)
            return jnp.where(
                index < ghosts, below, jnp.where(index < ghosts + atoms, inside, above)
            )

        offsets = [neighbour(field) - pick_two(own[field], centre) for field in range(3)]
        live = pick_two(own[4], centre)
        present = jnp.where((lane & 63).astype(jnp.float32) < live, 1.0, 0.0)
        smooth = present / (
            1.0 + (offsets[0] * offsets[0] + offsets[1] * offsets[1] + offsets[2] * offsets[2])
        )
        environment_ref[0, band, :] = smooth
        for field in range(3):
            environment_ref[1 + field, band, :] = smooth * offsets[field]
        kind_ref[band, :] = neighbour(3)

    group = 8

    def stacked(values):
        high, low = split(values)
        return jnp.concatenate([high, low, high], axis=0)

    def one_group(start):
        pieces = []
        for row in range(group):
            smooth = jnp.broadcast_to(environment_ref[0, pl.ds(start + row, 1), :], (32, 128))
            kind = jnp.broadcast_to(kind_ref[pl.ds(start + row, 1), :], (32, 128))
            pieces.append(
                jnp.tanh(smooth * ((1.0 - kind) * embed_zero + kind * embed_one))
            )
        first = jnp.concatenate(pieces, axis=1)
        second = jnp.tanh(multiply(second_weight, stacked(first), ((1,), (0,))))
        second = second + jnp.concatenate([first, first], axis=0)
        third = jnp.tanh(multiply(third_weight, stacked(second), ((1,), (0,))))
        third = third + jnp.concatenate([second, second], axis=0)
        third_pair = split(third)
        for half in range(group // 4):
            columns = slice(512 * half, 512 * half + 512)
            bands = []
            for part in range(4):
                bands.append(
                    jnp.concatenate(
                        [
                            jnp.where(
                                sub == row + jnp.where(lane < 64, 0, 4),
                                jnp.broadcast_to(
                                    environment_ref[part, pl.ds(start + 4 * half + row, 1), :],
                                    (8, 128),
                                ),
                                0.0,
                            )
                            for row in range(4)
                        ],
                        axis=1,
                    )
                )
            environment = split(jnp.concatenate(bands, axis=0))
            both = multiply(
                jnp.concatenate(environment, axis=0), third_pair[0][:, columns], LANES
            )
            sums = both[0:32] + both[32:64]
            sums = sums + multiply(environment[0], third_pair[1][:, columns], LANES)
            sums = sums * (1.0 / slots)
            for part in range(4):
                moments_ref[part, pl.ds(2 * start + 8 * half, 8), :] = sums[
                    8 * part : 8 * part + 8
                ]

    def body(step, carry):
        for part in range(unroll):
            one_group(pl.multiple_of(step * unroll * group + part * group, group))
        return carry

    unroll = 4 if rows % (4 * group) == 0 else 1
    lax.fori_loop(0, rows // (unroll * group), body, 0)

    chunks = (descriptor_ref.shape[1] + 127) // 128
    last = descriptor_ref.shape[1] - 128 * (chunks - 1)

    def describe_band(start):
        band = pl.ds(start, 8)
        moments = [moments_ref[part, band, :] for part in range(4)]
        axis_part = [lane_pick(moments[part], lane & 15) for part in range(4)]
        for chunk in range(chunks):
            spot = jnp.broadcast_to(spot_ref[chunk : chunk + 1, :], (8, 128))
            total = lane_pick(moments[0], spot) * axis_part[0]
            for part in range(1, 4):
                total = total + lane_pick(moments[part], spot) * axis_part[part]
            if chunk < chunks - 1:
                descriptor_ref[band, 128 * chunk : 128 * chunk + 128] = total
            else:
                descriptor_ref[band, 128 * chunk : 128 * chunk + last] = total[:, 0:last]

    bands = 4 if atoms % 32 == 0 else 1

    def describe(step, carry):
        for part in range(bands):
            describe_band(pl.multiple_of(step * 8 * bands + 8 * part, 8))
        return carry

    lax.fori_loop(0, atoms // (8 * bands), describe, 0)

    store = pltpu.make_async_copy(descriptor_ref, descriptor_hbm, semaphores.at[2])
    store.start()
    for fetch in fetches:
        fetch.wait()
    shift = fitting_rows(descriptor_ref, weight_in_ref, weight_hidden_ref, weight_out_ref)
    kind = types_ref[...].astype(jnp.float32)
    charge = (1.0 - kind) * charges_ref[0] + kind * charges_ref[1] + natural_order(shift)
    charge_ref[...] = charge
    fields = jnp.concatenate(
        [
            cell_x_ref[...].astype(jnp.float32),
            (cell_y_ref[...] + base_ref[0]).astype(jnp.float32),
            cell_z_ref[...].astype(jnp.float32),
        ]
        + [fraction_ref[axis] for axis in range(3)]
        + [charge, jnp.zeros((1, atoms), jnp.float32)],
        axis=0,
    )
    for copy in range(copies_ref.shape[0]):
        copies_ref[copy] = fields
    store.wait()


def spot_table(embed, desc):
    column = np.arange(desc) // AXIS
    quarter = embed // 4
    place = 32 * (column // quarter) + column % quarter
    chunks = (desc + 127) // 128
    table = np.zeros((chunks * 128,), np.int32)
    table[:desc] = place
    padded = np.zeros(((chunks + 7) // 8 * 8, 128), np.int32)
    padded[:chunks] = table.reshape(chunks, 128)
    return padded


def networks(
    copies,
    ghosts,
    base,
    charge_base,
    own,
    lower,
    upper,
    neighbours,
    types,
    cells,
    fraction,
    embed,
    weight_in,
    weight_hidden,
    weight_out,
):
    atoms = types.shape[1]
    desc, width = weight_in.shape
    spots = jnp.asarray(spot_table(embed[2].shape[1], desc))
    anywhere = pl.BlockSpec(memory_space=pl.ANY)
    scalars = pl.BlockSpec(memory_space=pltpu.SMEM)
    blocks = (own, lower, upper, neighbours[0].T, types, *cells, fraction, *embed, spots)
    weight_out = weight_out.reshape(1, -1)
    results = [
        jax.ShapeDtypeStruct((atoms, desc), jnp.float32),
        jax.ShapeDtypeStruct((1, atoms), jnp.float32),
        jax.ShapeDtypeStruct((copies, 8, atoms), jnp.float32),
    ]
    return pl.pallas_call(
        functools.partial(network_kernel, ghosts),
        grid=(1,),
        out_shape=results,
        in_specs=[scalars, scalars]
        + whole_specs(*blocks)
        + [anywhere, anywhere]
        + whole_specs(weight_out),
        out_specs=[anywhere] + whole_specs(*results[1:]),
        scratch_shapes=[
            pltpu.VMEM((atoms, desc), jnp.float32),
            pltpu.VMEM((4, atoms // 2, 128), jnp.float32),
            pltpu.VMEM((atoms // 2, 128), jnp.float32),
            pltpu.VMEM((4, atoms, 128), jnp.float32),
            pltpu.VMEM((3, 128, 128), jnp.float32),
            pltpu.VMEM((width, desc), jnp.float32),
            pltpu.VMEM(weight_hidden.shape, jnp.float32),
            pltpu.SemaphoreType.DMA((3,)),
        ],
        compiler_params=pltpu.CompilerParams(vmem_limit_bytes=VMEM_BYTES),
        name="networks",
    )(base, charge_base, *blocks, weight_in.T, weight_hidden, weight_out)


def energy_kernel(descriptor_ref, weight_in_ref, weight_hidden_ref, weight_out_ref, energy_ref):
    energy_ref[...] = natural_order(
        fitting_rows(descriptor_ref, weight_in_ref, weight_hidden_ref, weight_out_ref)
    )


def energies(descriptor, weight_in, weight_hidden, weight_out):
    atoms, desc = descriptor.shape
    width = weight_in.shape[1]
    arrays = (descriptor, weight_in.T, weight_hidden, weight_out.reshape(1, -1))
    result = jax.ShapeDtypeStruct((1, atoms), jnp.float32)
    return pl.pallas_call(
        energy_kernel,
        grid=(1,),
        out_shape=result,
        in_specs=whole_specs(*arrays),
        out_specs=whole(result.shape),
        compiler_params=pltpu.CompilerParams(vmem_limit_bytes=VMEM_BYTES),
        cost_estimate=pl.CostEstimate(
            flops=6 * atoms * desc * width, bytes_accessed=4 * desc * width, transcendentals=0
        ),
        name="energies",
    )(*arrays)


def weight_rows(fraction):
    square = fraction * fraction
    cubed = square * fraction
    rest = 1.0 - fraction
    return [
        rest * rest * rest / 6.0,
        (3.0 * cubed - 6.0 * square + 4.0) / 6.0,
        (-3.0 * cubed + 3.0 * square + 3.0 * fraction + 1.0) / 6.0,
        cubed / 6.0,
    ]


def placed_weights(distance, weights):
    shape = distance.shape
    result = jnp.zeros(shape, jnp.float32)
    for step in range(4):
        result = jnp.where(
            distance == step, jnp.broadcast_to(weights[step], shape), result
        )
    return result


def third_factors(fields, waves_ref, cosine_ref):
    atoms = fields.shape[1]
    start = fields[2:3, :].astype(jnp.int32)
    along = weight_rows(fields[5:6, :])
    parts = waves_ref.shape[0]
    cosine = jnp.broadcast_to(cosine_ref[...], (parts, 128))
    wave = jnp.broadcast_to(waves_ref[:, 0:1], (parts, 128))
    shift = jnp.broadcast_to(waves_ref[:, 1:2], (parts, 128))
    pieces = []
    for chunk in range(atoms // 128):
        lanes = slice(128 * chunk, 128 * chunk + 128)
        total = jnp.zeros((parts, 128), jnp.float32)
        for step in range(4):
            place = jnp.broadcast_to(start[:, lanes] + step, (parts, 128))
            phase = (wave * place + shift) & (NG - 1)
            value = lane_pick(cosine, phase & 127)
            value = jnp.where(phase < 128, value, -value)
            total = total + value * jnp.broadcast_to(along[step][:, lanes], (parts, 128))
        pieces.append(total)
    return jnp.concatenate(pieces, axis=1)


def first_third(fields, waves_ref, cosine_ref, window, scale):
    atoms = fields.shape[1]
    third = third_factors(fields, waves_ref, cosine_ref)
    if scale is not None:
        third = third * scale
    rows = lax.broadcasted_iota(jnp.int32, (window, atoms), 0)
    first = placed_weights(
        rows - fields[0:1, :].astype(jnp.int32), weight_rows(fields[3:4, :])
    )
    return jnp.concatenate(
        [first * third[part : part + 1, :] for part in range(third.shape[0])], axis=0
    )


def second_factors(fields, base, block_y, slabs, high_ref, low_ref):
    atoms = fields.shape[1]
    block = atoms // slabs
    reach = block_y + 16
    start = fields[1:2, :].astype(jnp.int32) - base
    weights = weight_rows(fields[4:5, :])
    for chunk in range(atoms // 128):
        lanes = slice(128 * chunk, 128 * (chunk + 1))
        first = 128 * chunk // block
        last = (128 * chunk + 127) // block
        top = first * block_y
        rows = (last - first) * block_y + reach
        pieces = [(top, min(rows, NG - top))]
        if top + rows > NG:
            pieces.append((0, top + rows - NG))
        for row, count in pieces:
            index = row + lax.broadcasted_iota(jnp.int32, (count, 128), 0)
            table = split(
                placed_weights(
                    (index - start[:, lanes]) & (NG - 1), [weight[:, lanes] for weight in weights]
                )
            )
            high_ref[row : row + count, lanes] = table[0]
            low_ref[row : row + count, lanes] = table[1]
    return high_ref[...], low_ref[...]


def wave_of(index):
    return jnp.where(index <= NG // 2, index, index - NG // 2)


def damping(index):
    kappa = wave_of(index).astype(jnp.float32) * (2.0 * math.pi / NG)
    squared = kappa * kappa
    ends = (index == 0) | (index == NG // 2)
    return squared, jnp.exp(-0.5 * squared) * jnp.where(ends, 1.0 / NG, 2.0 / NG)


def transform(planes, kappa_ref, first_part, tables_ref, last_ref):
    count = len(planes)
    basis = (tables_ref[0], tables_ref[1])
    turned = (tables_ref[2], tables_ref[3])
    last = (last_ref[0], last_ref[1])
    square_x, damp_x = damping(lax.broadcasted_iota(jnp.int32, (NG, 1), 0))
    square_y, damp_y = damping(lax.broadcasted_iota(jnp.int32, (1, NG), 1))
    square_xy = square_x + square_y
    damp_xy = damp_x * damp_y
    columns = [slice(NG * part, NG * (part + 1)) for part in range(count)]
    first = triple(basis, split(jnp.concatenate(planes, axis=1)))
    first = jnp.concatenate([first[:, column] for column in columns], axis=0)
    both = triple(split(first), turned)
    scaled = []
    for part in range(count):
        squared = square_xy + kappa_ref[first_part + part, 0]
        root = jnp.where(squared == 0.0, 1.0, 0.0)
        green = (1.0 - root) * (damp_xy * kappa_ref[first_part + part, 1]) / (squared + root)
        scaled.append(both[columns[part]] * green)
    back = triple(turned, split(jnp.concatenate(scaled, axis=1)))
    back = jnp.concatenate([back[:, column] for column in columns], axis=0)
    return triple(split(back), last)


def send_blocks(full, block_x, block_y, put):
    low_lanes = lax.broadcasted_iota(jnp.int32, (NG, 128), 1) < block_y
    for pair in range(full.shape[0] // (2 * NG)):
        even = full[2 * NG * pair : 2 * NG * pair + NG, 0:128]
        odd = full[2 * NG * pair + NG : 2 * NG * (pair + 1), 0:128]
        blocks = [
            jnp.where(low_lanes, even, pltpu.roll(odd, block_y, 1)),
            jnp.where(low_lanes, pltpu.roll(even, block_y, 1), odd),
        ]
        for brick in range(NG // block_x):
            for side in range(2):
                for group in range(block_x // 8):
                    start = block_x * brick + 8 * group
                    put(pair, brick, side, group, blocks[side][start : start + 8])


def spread_kernel(
    block_x,
    block_y,
    window,
    kappa_ref,
    pair_ref,
    static_ref,
    waves_ref,
    cosine_ref,
    tables_hbm,
    last_hbm,
    sent_ref,
    full_ref,
    atoms_ref,
    later_hbm,
    grid_ref,
    tables_ref,
    last_ref,
    semaphores,
    *second_refs,
):
    slabs = NG // block_y
    bricks = NG // block_x
    parts = waves_ref.shape[0]
    block = static_ref.shape[2]
    count = full_ref.shape[0]
    step = pl.program_id(0)
    later = later_hbm.shape[0]
    store = pltpu.make_async_copy(
        grid_ref.at[pl.ds(parts - later, later), pl.ds(0, NG)], later_hbm, semaphores.at[2]
    )

    @pl.when(step == 0)
    def _():
        fetches = [
            pltpu.make_async_copy(tables_hbm, tables_ref, semaphores.at[0]),
            pltpu.make_async_copy(last_hbm.at[pair_ref[0]], last_ref, semaphores.at[1]),
        ]
        for fetch in fetches:
            fetch.start()
        for slab in range(slabs):
            lanes = slice(block * slab, block * (slab + 1))
            for brick in range(bricks):
                atoms_ref[brick, :, lanes] = static_ref[slab * bricks + brick]
        grid_ref[...] = jnp.zeros_like(grid_ref)
        for ref in second_refs:
            ref[...] = jnp.zeros_like(ref)
        for brick in range(bricks):
            fields = atoms_ref[brick]
            table = split(first_third(fields, waves_ref, cosine_ref, window, fields[6:7, :]))
            second = second_factors(
                fields, 0, block_y, slabs, second_refs[2 * (brick % 2)], second_refs[2 * (brick % 2) + 1]
            )
            spread = triple(table, second, LANES)
            rows = slice(block_x * brick, block_x * brick + window)
            for part in range(parts):
                grid_ref[part, rows, :] += spread[part * window : part * window + window]
        extra = window - block_x
        for part in range(parts):
            grid_ref[part, 0:extra, :] += grid_ref[part, NG : NG + extra, :]
        store.start()
        for fetch in fetches:
            fetch.wait()

    planes = [grid_ref[count * step + part, 0:NG, :] for part in range(count)]
    full = transform(planes, kappa_ref, count * step, tables_ref, last_ref)
    for part in range(count):
        full_ref[part] = full[NG * part : NG * (part + 1)]

    def put(pair, brick, side, group, tile):
        sent_ref[2 * brick + side, group, pair] = tile

    send_blocks(full, block_x, block_y, put)

    @pl.when(step == pl.num_programs(0) - 1)
    def _():
        store.wait()


def early_pairs(parts):
    return (5 * parts + 8) // 16


def spread_and_solve(
    block_x, block_y, window, kappa, pair, static, waves, cosine_row, tables, last
):
    devices, _, atoms = static.shape
    slabs = NG // block_y
    bricks = NG // block_x
    parts = waves.shape[0]
    pairs = early_pairs(parts)
    count = 2
    anywhere = pl.BlockSpec(memory_space=pl.ANY)
    scalars = pl.BlockSpec(memory_space=pltpu.SMEM)
    sent_block = (2 * bricks, block_x // 8, count // 2, 8, 128)
    return pl.pallas_call(
        functools.partial(spread_kernel, block_x, block_y, window),
        grid=(2 * pairs // count,),
        out_shape=[
            jax.ShapeDtypeStruct((2 * bricks, block_x // 8, pairs, 8, 128), jnp.float32),
            jax.ShapeDtypeStruct((2 * pairs, NG, NG), jnp.float32),
            jax.ShapeDtypeStruct((bricks, 8, slabs * atoms), jnp.float32),
            jax.ShapeDtypeStruct((parts - 2 * pairs, NG, NG), jnp.float32),
        ],
        in_specs=[scalars, scalars]
        + whole_specs(static, waves, cosine_row)
        + [anywhere, anywhere],
        out_specs=[
            pl.BlockSpec(sent_block, lambda step: (0, 0, step, 0, 0)),
            pl.BlockSpec((count, NG, NG), lambda step: (step, 0, 0)),
            whole((bricks, 8, slabs * atoms)),
            anywhere,
        ],
        scratch_shapes=[
            pltpu.VMEM((parts, NG + window - block_x, NG), jnp.float32),
            pltpu.VMEM(tables.shape, tables.dtype),
            pltpu.VMEM(last.shape[1:], last.dtype),
            pltpu.SemaphoreType.DMA((3,)),
        ]
        + [pltpu.VMEM((NG, slabs * atoms), jnp.bfloat16)] * 4,
        compiler_params=pltpu.CompilerParams(vmem_limit_bytes=VMEM_BYTES),
        name="spread_and_solve",
    )(kappa, pair, static, waves, cosine_row, tables, last)


def sample_kernel(
    block_x,
    block_y,
    window,
    kappa_ref,
    pair_ref,
    atoms_ref,
    waves_ref,
    cosine_ref,
    tables_hbm,
    last_hbm,
    later_hbm,
    early_hbm,
    sent_ref,
    later_ref,
    full_ref,
    tables_ref,
    last_ref,
    semaphores,
    *second_refs,
):
    bricks = atoms_ref.shape[0]
    parts = waves_ref.shape[0]
    early = 2 * early_pairs(parts)
    block = atoms_ref.shape[2] * block_y // NG
    fetches = [
        pltpu.make_async_copy(tables_hbm, tables_ref, semaphores.at[0]),
        pltpu.make_async_copy(last_hbm.at[pair_ref[0]], last_ref, semaphores.at[1]),
        pltpu.make_async_copy(later_hbm, later_ref, semaphores.at[2]),
        pltpu.make_async_copy(early_hbm, full_ref.at[pl.ds(0, early)], semaphores.at[3]),
    ]
    for fetch in fetches:
        fetch.start()
    for fetch in fetches[:3]:
        fetch.wait()
    pairs = (parts - early) // 2
    planes = [later_ref[part] for part in range(parts - early)]
    full = transform(planes, kappa_ref, early, tables_ref, last_ref)
    for part in range(parts - early):
        full_ref[early + part] = full[NG * part : NG * (part + 1)]

    def put(pair, brick, side, group, tile):
        sent_ref[2 * brick + side, pairs * group + pair] = tile

    send_blocks(full, block_x, block_y, put)
    fetches[3].wait()

    for ref in second_refs:
        ref[...] = jnp.zeros_like(ref)
    extra = sent_ref.shape[1] - 1
    base = 2 * block_y * pair_ref[0]
    lanes = pl.ds(pl.multiple_of(2 * block * pair_ref[0], 128), 2 * block)
    for brick in range(bricks):
        fields = atoms_ref[brick, :, lanes]
        weights = first_third(fields, waves_ref, cosine_ref, window, None)
        start = block_x * brick
        inside = min(window, NG - start)
        values = []
        for part in range(parts):
            values.append(full_ref[part, start : start + inside, :])
            if inside < window:
                values.append(full_ref[part, 0 : window - inside, :])
        values = split(jnp.concatenate(values, axis=0))
        second = second_factors(
            fields, base, block_y, 2, second_refs[2 * (brick % 2)], second_refs[2 * (brick % 2) + 1]
        )
        along = triple(values, second)
        sums = jnp.sum(along * weights, axis=0, keepdims=True)
        for side in range(2):
            row = sums[:, block * side : block * (side + 1)]
            sent_ref[2 * brick + side, extra] = jnp.zeros((8, 128), jnp.float32)
            sent_ref[2 * brick + side, extra, 0:1, :] = row[:, 0:128]
            sent_ref[2 * brick + side, extra, 1:2, 0 : block - 128] = row[:, 128:block]


def solve_and_sample(
    block_x, block_y, window, kappa, pair, atoms, waves, cosine_row, tables, last, later, early
):
    bricks = atoms.shape[0]
    parts = waves.shape[0]
    pairs = parts // 2 - early_pairs(parts)
    anywhere = pl.BlockSpec(memory_space=pl.ANY)
    scalars = pl.BlockSpec(memory_space=pltpu.SMEM)
    result = jax.ShapeDtypeStruct((2 * bricks, block_x // 8 * pairs + 1, 8, 128), jnp.float32)
    return pl.pallas_call(
        functools.partial(sample_kernel, block_x, block_y, window),
        grid=(1,),
        out_shape=result,
        in_specs=[scalars, scalars] + whole_specs(atoms, waves, cosine_row) + [anywhere] * 4,
        out_specs=whole(result.shape),
        scratch_shapes=[
            pltpu.VMEM((2 * pairs, NG, NG), jnp.float32),
            pltpu.VMEM((parts, NG, NG), jnp.float32),
            pltpu.VMEM(tables.shape, tables.dtype),
            pltpu.VMEM(last.shape[1:], last.dtype),
            pltpu.SemaphoreType.DMA((4,)),
        ]
        + [pltpu.VMEM((NG, 2 * atoms.shape[2] * block_y // NG), jnp.bfloat16)] * 4,
        compiler_params=pltpu.CompilerParams(vmem_limit_bytes=VMEM_BYTES),
        cost_estimate=pl.CostEstimate(
            flops=24 * parts * NG * NG * NG, bytes_accessed=4 * early.size, transcendentals=0
        ),
        name="solve_and_sample",
    )(kappa, pair, atoms, waves, cosine_row, tables, last, later, early)


def finish_kernel(
    block_y, early_ref, later_ref, sums_ref, short_ref, charge_ref, table_ref, out_ref, energy_ref
):
    atoms = short_ref.shape[1]
    table = (table_ref[0], table_ref[1])
    lines = early_ref.shape[3]
    sources, _, pairs = early_ref.shape[:3]
    early = early_ref.reshape(sources * pairs, lines, 128)
    later = later_ref.reshape(sources * later_ref.shape[1], lines, 128)
    pieces = []
    for line in range(lines):
        turned = jnp.concatenate([early[:, line, :], later[:, line, :]], axis=0).T
        pieces.append(jnp.concatenate([turned[0:block_y], turned[block_y:]], axis=1))
    result = triple(split(jnp.concatenate(pieces, axis=0)), table)
    for line in range(lines):
        out_ref[line] = result[block_y * line : block_y * (line + 1)]

    @pl.when(pl.program_id(0) == 0)
    def _():
        total = jnp.sum(sums_ref[:, 0], axis=0)
        potential_at = jnp.concatenate([total[0:1, :], total[1:2, 0 : atoms - 128]], axis=1)
        energy_ref[...] = short_ref[...] + 0.5 * charge_ref[...] * potential_at


def finish(block_x, block_y, early, later, short, charge, table):
    bricks2, groups, pairs = early.shape[:3]
    rest = (later.shape[1] - 1) // groups
    atoms = short.shape[1]
    return pl.pallas_call(
        functools.partial(finish_kernel, block_y),
        grid=(groups,),
        out_shape=[
            jax.ShapeDtypeStruct((block_x, block_y, NG), jnp.float32),
            jax.ShapeDtypeStruct((1, atoms), jnp.float32),
        ],
        in_specs=[
            pl.BlockSpec((bricks2, 1, pairs, 8, 128), lambda index: (0, index, 0, 0, 0)),
            pl.BlockSpec((bricks2, rest, 8, 128), lambda index: (0, index, 0, 0)),
            pl.BlockSpec((bricks2, 1, 8, 128), lambda index: (0, groups * rest, 0, 0)),
            whole((1, atoms)),
            whole((1, atoms)),
            whole(table.shape),
        ],
        out_specs=[
            pl.BlockSpec((8, block_y, NG), lambda index: (index, 0, 0)),
            whole((1, atoms)),
        ],
        compiler_params=pltpu.CompilerParams(vmem_limit_bytes=32 * 2**20),
        name="finish",
    )(early, later, later, short, charge, table)


def two_parts(table):
    table = np.asarray(table, np.float32)
    high = table.astype(ml_dtypes.bfloat16)
    low = (table - high.astype(np.float32)).astype(ml_dtypes.bfloat16)
    return np.stack([high, low])


def real_basis():
    index = np.arange(NG)
    wave = np.where(index <= NG // 2, index, index - NG // 2)
    angle = (wave[:, None] * index[None, :] % NG) * (2.0 * math.pi / NG)
    return np.where((index <= NG // 2)[:, None], np.cos(angle), np.sin(angle))


def per_device(
    positions,
    types,
    neighbours,
    neighbour_count,
    send_index,
    cell_x,
    cell_y,
    cell_z,
    spline_fraction,
    embed_first,
    embed_second,
    embed_third,
    energy_in,
    energy_hidden,
    energy_out,
    wannier_in,
    wannier_hidden,
    wannier_out,
    charge_base,
):
    atoms = types.shape[1]
    ghosts = send_index.shape[1] // 2
    count_x = lax.axis_size("brick")
    count_y = lax.axis_size("slab")
    block_x = NG // count_x
    block_y = NG // count_y
    window = block_x + 8
    parts = NG // (2 * count_x)
    brick = lax.axis_index("brick")
    slab = lax.axis_index("slab")
    pair = (slab // 2).astype(jnp.int32).reshape(1)
    halves = [
        [b * count_y + 2 * p + side for b in range(count_x) for side in range(2)]
        for p in range(count_y // 2)
    ]

    def exchange(values, axes, groups=None):
        return lax.all_to_all(
            values, axes, split_axis=0, concat_axis=0, tiled=True, axis_index_groups=groups
        )

    own, outgoing = collect(positions, types, neighbour_count, send_index)
    up = [(i, (i + 1) % count_x) for i in range(count_x)]
    down = [((i + 1) % count_x, i) for i in range(count_x)]
    lower = lax.ppermute(outgoing, "brick", up)
    upper = lax.ppermute(outgoing, "brick", down)
    descriptor, charge, fields = networks(
        count_x * count_y,
        ghosts,
        (slab * block_y).astype(jnp.int32).reshape(1),
        charge_base,
        own,
        lower,
        upper,
        neighbours,
        types,
        (cell_x, cell_y, cell_z),
        spline_fraction,
        (embed_first, embed_second, embed_third),
        wannier_in,
        wannier_hidden,
        wannier_out,
    )
    every_field = exchange(fields, ("slab", "brick"))

    part = (2 * brick + slab % 2) * parts + jnp.arange(parts, dtype=jnp.int32)
    wave = wave_of(part)
    waves = jnp.stack([wave, jnp.where(part <= NG // 2, 0, 3 * NG // 4)], axis=1)
    kappa = wave.astype(jnp.float32) * (2.0 * math.pi / NG)
    squared = kappa * kappa
    ends = (part == 0) | (part == NG // 2)
    kappa = jnp.stack(
        [squared, jnp.exp(-0.5 * squared) * jnp.where(ends, 1.0 / NG, 2.0 / NG)], axis=1
    )
    basis = real_basis()
    tables = np.concatenate([two_parts(basis), two_parts(basis.T)])
    last = []
    for p in range(count_y // 2):
        points = (2 * block_y * p + np.arange(2 * block_y + 8)) % NG
        columns = np.zeros((NG, NG))
        columns[:, : points.size] = basis[:, points]
        last.append(two_parts(columns))
    cosine_row = np.cos(np.arange(128) * (2.0 * math.pi / NG)).astype(np.float32)[None]
    cosine_row = jnp.asarray(cosine_row)
    tables = jnp.asarray(tables)
    last = jnp.asarray(np.stack(last))
    early, full, every_atom, later = spread_and_solve(
        block_x, block_y, window, kappa, pair, every_field, waves, cosine_row, tables, last
    )

    def send(values):
        got = exchange(values.reshape(values.shape[0], -1, 128), ("brick", "slab"), halves)
        return got.reshape(values.shape)

    early = send(early)
    later = solve_and_sample(
        block_x,
        block_y,
        window,
        kappa,
        pair,
        every_atom,
        waves,
        cosine_row,
        tables,
        last,
        later,
        full,
    )
    later = send(later)
    energy_short = energies(descriptor, energy_in, energy_hidden, energy_out)
    source = np.arange(2 * count_x)[:, None] * parts
    pairs = 2 * np.arange(parts // 2)[None, :]
    order = np.concatenate(
        [
            (source + pairs[:, : early_pairs(parts)]).ravel(),
            (source + pairs[:, early_pairs(parts) :]).ravel(),
        ]
    )
    order = np.concatenate([order, order + 1])
    potential, atom_energy = finish(
        block_x,
        block_y,
        early,
        later,
        energy_short,
        charge,
        jnp.asarray(two_parts(basis[order])),
    )
    return atom_energy, potential


def solution(mesh):
    placed = (
        P(None, "slab", "brick"),
        P("slab", "brick"),
        P("slab", "brick", None),
        P("slab", "brick"),
        P("slab", "brick"),
        P("slab", "brick"),
        P("slab", "brick"),
        P("slab", "brick"),
        P(None, "slab", "brick"),
    ) + (P(),) * 10
    bricks, slabs = mesh.shape["brick"], mesh.shape["slab"]
    fits = 2 * NG == 128 * slabs and NG % (32 * bricks) == 0
    return jax.shard_map(
        per_device if fits else per_device_general,
        mesh=mesh,
        in_specs=placed,
        out_specs=(P("slab", "brick"), P("brick", "slab", None)),
        check_vma=False,
    )
```

```python
import functools
import math

import jax
import jax.numpy as jnp
import numpy as np
from jax import lax
from jax.experimental import pallas as pl
from jax.experimental.pallas import tpu as pltpu
from jax.sharding import PartitionSpec as P

NG = 256
AXIS = 16
VMEM_BYTES = 60 * 2**20


HIGH = lax.Precision.HIGHEST


def with_halo(cells, sides, width):
    for axis, dim in sides:
        count = lax.axis_size(axis)
        head = lax.slice_in_dim(cells, 0, width, axis=dim)
        tail = lax.slice_in_dim(cells, cells.shape[dim] - width, cells.shape[dim], axis=dim)
        cells = jnp.concatenate(
            [
                lax.ppermute(tail, axis, [(i, (i + 1) % count) for i in range(count)]),
                cells,
                lax.ppermute(head, axis, [((i + 1) % count, i) for i in range(count)]),
            ],
            axis=dim,
        )
    return cells


def spline_weights(fraction):
    cubed = fraction * fraction * fraction
    square = fraction * fraction
    return jnp.stack(
        [
            (1.0 - fraction) * (1.0 - fraction) * (1.0 - fraction) / 6.0,
            (3.0 * cubed - 6.0 * square + 4.0) / 6.0,
            (-3.0 * cubed + 3.0 * square + 3.0 * fraction + 1.0) / 6.0,
            cubed / 6.0,
        ]
    )


def fitting(descriptor, weight_in, weight_hidden, weight_out):
    hidden = jnp.tanh(jnp.dot(descriptor, weight_in, precision=HIGH))
    for depth_index in range(weight_hidden.shape[0]):
        hidden = jnp.tanh(jnp.dot(hidden, weight_hidden[depth_index], precision=HIGH)) + hidden
    return jnp.dot(hidden, weight_out, precision=HIGH)


def atom_terms(
    extended,
    neighbour_rows,
    neighbour_total,
    embed_first,
    embed_second,
    embed_third,
    energy_in,
    energy_hidden,
    energy_out,
    wannier_in,
    wannier_hidden,
    wannier_out,
):
    atom_count, slots = neighbour_rows.shape
    ghost_rows = (extended.shape[1] - atom_count) // 2
    block_size = 64
    blocks = atom_count // block_size
    present = (jnp.arange(slots, dtype=jnp.int32)[None, :] < neighbour_total[:, None]).astype(
        jnp.float32
    )
    centre_ids = (ghost_rows + jnp.arange(atom_count, dtype=jnp.int32)).reshape(blocks, block_size)
    second_weight = embed_second.T
    third_weight = embed_third.T

    def one_block(pieces):
        centre_rows, rows_block, present_block = pieces
        centre_block = extended[:3, centre_rows]
        gathered = extended[:, rows_block]
        offsets = gathered[:3] - centre_block[:, :, None]
        smooth = present_block / (1.0 + jnp.sum(offsets * offsets, axis=0))
        environment = jnp.stack(
            [smooth, smooth * offsets[0], smooth * offsets[1], smooth * offsets[2]], axis=0
        )
        kind = gathered[3][None]
        mixing = (1.0 - kind) * embed_first[0][:, None, None] + kind * embed_first[1][:, None, None]
        first = jnp.tanh(smooth[None] * mixing).reshape(embed_first.shape[1], block_size * slots)
        second = jnp.tanh(jnp.dot(second_weight, first, precision=HIGH)) + jnp.concatenate(
            [first, first], axis=0
        )
        third = jnp.tanh(jnp.dot(third_weight, second, precision=HIGH)) + jnp.concatenate(
            [second, second], axis=0
        )
        third_blocks = third.reshape(third.shape[0], block_size, slots)
        moments = jnp.einsum("kan,can->akc", third_blocks, environment, precision=HIGH) / slots
        descriptor = jnp.einsum("amc,akc->amk", moments, moments[:, :AXIS], precision=HIGH).reshape(
            block_size, -1
        )
        return (
            fitting(descriptor, energy_in, energy_hidden, energy_out),
            fitting(descriptor, wannier_in, wannier_hidden, wannier_out),
        )

    energy_short, charge_shift = lax.map(
        one_block,
        (
            centre_ids,
            neighbour_rows.reshape(blocks, block_size, slots),
            present.reshape(blocks, block_size, slots),
        ),
    )
    return (energy_short.reshape(atom_count), charge_shift.reshape(atom_count))


def green_table(first, second, third, size):

    def folded(index):
        return jnp.where(index < size // 2, index, index - size).astype(jnp.float32) * (
            2.0 * math.pi / size
        )

    kappa_x = folded(first)[:, None, None]
    kappa_y = folded(second)[None, :, None]
    kappa_z = folded(third)[None, None, :]
    squared = kappa_x * kappa_x + kappa_y * kappa_y + kappa_z * kappa_z
    root = (
        (first[:, None, None] == 0) & (second[None, :, None] == 0) & (third[None, None, :] == 0)
    ).astype(jnp.float32)
    return (1.0 - root) * jnp.exp(-0.5 * squared) / (squared + root)


def dft_tables(size):
    index = jnp.arange(size, dtype=jnp.int32)
    phase = (index[:, None] * index[None, :] % size).astype(jnp.float32) * (2.0 * math.pi / size)
    return (jnp.cos(phase), jnp.sin(phase))


def along(values, table, axis_index):
    result = jnp.tensordot(values, table, axes=([axis_index], [0]), precision=HIGH)
    return jnp.moveaxis(result, -1, axis_index)


def complex_transform(paired, axis_index, cosine, sine, inverse):
    real_part = paired[0]
    imag_part = paired[1]
    inner = axis_index - 1
    real_cos = along(real_part, cosine, inner)
    real_sin = along(real_part, sine, inner)
    imag_cos = along(imag_part, cosine, inner)
    imag_sin = along(imag_part, sine, inner)
    if inverse:
        return jnp.stack([real_cos - imag_sin, imag_cos + real_sin])
    return jnp.stack([real_cos + imag_sin, imag_cos - real_sin])


def fold_windows(values, axis_index, block, count):
    front = jnp.moveaxis(values, axis_index, 0)
    rest = front.shape[1:]
    windows = front.reshape((count, block + 3) + rest)
    main_part = windows[:, :block]
    carried = jnp.roll(windows[:, block:], 1, axis=0)
    main_part = main_part.at[:, :3].add(carried)
    return jnp.moveaxis(main_part.reshape((count * block,) + rest), 0, axis_index)


def make_windows(values, axis_index, block, count):
    front = jnp.moveaxis(values, axis_index, 0)
    rest = front.shape[1:]
    pieces = front.reshape((count, block) + rest)
    trailing = jnp.roll(pieces, -1, axis=0)[:, :3]
    windows = jnp.concatenate([pieces, trailing], axis=1)
    return jnp.moveaxis(windows.reshape((count * (block + 3),) + rest), 0, axis_index)


def spread_matrix(start, weights, width, wrap_size):
    offsets = jnp.arange(4, dtype=jnp.int32)[:, None, None]
    target = start[None, :, None] + offsets
    if wrap_size > 0:
        target = target % wrap_size
    hits = (target == jnp.arange(width, dtype=jnp.int32)[None, None, :]).astype(jnp.float32)
    return jnp.sum(weights[:, :, None] * hits, axis=0)


def per_device_general(
    positions,
    types,
    neighbours,
    neighbour_count,
    send_index,
    cell_x,
    cell_y,
    cell_z,
    spline_fraction,
    embed_first,
    embed_second,
    embed_third,
    energy_in,
    energy_hidden,
    energy_out,
    wannier_in,
    wannier_hidden,
    wannier_out,
    charge_base,
):
    atom_count = types.shape[1]
    ghost_rows = send_index.shape[1] // 2
    kind_float = types[0].astype(jnp.float32)
    own_atoms = jnp.concatenate([positions[:, 0], kind_float[None]], axis=0)
    outgoing = own_atoms[:, send_index[0]]
    padded_ghosts = with_halo(outgoing, (("brick", 1),), ghost_rows)
    extended = jnp.concatenate(
        [padded_ghosts[:, :ghost_rows], own_atoms, padded_ghosts[:, 3 * ghost_rows :]], axis=1
    )
    energy_short, charge_shift = atom_terms(
        extended,
        neighbours[0],
        neighbour_count[0],
        embed_first,
        embed_second,
        embed_third,
        energy_in,
        energy_hidden,
        energy_out,
        wannier_in,
        wannier_hidden,
        wannier_out,
    )
    charge = (1.0 - kind_float) * charge_base[0] + kind_float * charge_base[1] + charge_shift
    count_x = lax.axis_size("brick")
    count_y = lax.axis_size("slab")
    block_x = NG // count_x
    block_y = NG // count_y
    wide_x = block_x + 3
    wide_y = block_y + 3
    spread_x = spread_matrix(cell_x[0], spline_weights(spline_fraction[0, 0]), wide_x, 0)
    spread_y = spread_matrix(cell_y[0], spline_weights(spline_fraction[1, 0]), wide_y, 0)
    spread_z = spread_matrix(cell_z[0], spline_weights(spline_fraction[2, 0]), NG, NG)
    spread_xy = (spread_x[:, :, None] * spread_y[:, None, :]).reshape(atom_count, wide_x * wide_y)
    charge_grid = jnp.einsum(
        "ap,az->pz", spread_xy, charge[:, None] * spread_z, precision=HIGH
    ).reshape(wide_x, wide_y, NG)
    cosine, sine = dft_tables(NG)
    scale = 1.0 / (NG * NG * NG)
    full_index = jnp.arange(NG, dtype=jnp.int32)
    paired = jnp.stack([along(charge_grid, cosine, 2), -along(charge_grid, sine, 2)])
    moved = lax.all_to_all(paired, "slab", split_axis=3, concat_axis=2, tiled=True)
    moved = complex_transform(fold_windows(moved, 2, block_y, count_y), 2, cosine, sine, False)
    moved = lax.all_to_all(moved, "brick", split_axis=2, concat_axis=1, tiled=True)
    moved = complex_transform(fold_windows(moved, 1, block_x, count_x), 1, cosine, sine, False)
    part_y = NG // count_x
    part_z = NG // count_y
    index_y = lax.axis_index("brick") * part_y + jnp.arange(part_y, dtype=jnp.int32)
    index_z = lax.axis_index("slab") * part_z + jnp.arange(part_z, dtype=jnp.int32)
    moved = moved * (green_table(full_index, index_y, index_z, NG) * scale)[None]
    moved = make_windows(complex_transform(moved, 1, cosine, sine, True), 1, block_x, count_x)
    moved = lax.all_to_all(moved, "brick", split_axis=1, concat_axis=2, tiled=True)
    moved = make_windows(complex_transform(moved, 2, cosine, sine, True), 2, block_y, count_y)
    moved = lax.all_to_all(moved, "slab", split_axis=2, concat_axis=3, tiled=True)
    potential_wide = along(moved[0], cosine, 2) - along(moved[1], sine, 2)
    sampled = jnp.einsum(
        "ap,pz->az", spread_xy, potential_wide.reshape(wide_x * wide_y, NG), precision=HIGH
    )
    potential_at = jnp.sum(sampled * spread_z, axis=1)
    atom_energy = energy_short + 0.5 * charge * potential_at
    return (atom_energy[None, :], potential_wide[:block_x, :block_y])


def split(values):
    high = values.astype(jnp.bfloat16)
    low = (values - high.astype(jnp.float32)).astype(jnp.bfloat16)
    return high, low


def multiply(left, right, dims):
    return lax.dot_general(left, right, (dims, ((), ())), preferred_element_type=jnp.float32)


def triple(left, right, dims=((1,), (0,))):
    (left_axis,), (right_axis,) = dims
    if left[0].shape[left_axis] % 128 == 0:
        return multiply(
            jnp.concatenate([left[0], left[0], left[1]], axis=left_axis),
            jnp.concatenate([right[0], right[1], right[0]], axis=right_axis),
            dims,
        )
    return (
        multiply(left[0], right[0], dims)
        + multiply(left[0], right[1], dims)
        + multiply(left[1], right[0], dims)
    )


LANES = ((1,), (1,))


def product(left, right, dims=((1,), (0,))):
    return lax.dot_general(
        left,
        right,
        (dims, ((), ())),
        precision=lax.Precision.HIGH,
        preferred_element_type=jnp.float32,
    )


def lane_pick(table, index):
    return jnp.take_along_axis(table, index, axis=1, mode="promise_in_bounds")


def whole(shape):
    return pl.BlockSpec(tuple(shape), lambda step: (0,) * len(shape))


def whole_specs(*arrays):
    return [whole(array.shape) for array in arrays]


def collect_kernel(
    positions_ref, types_ref, count_ref, send_ref, own_ref, outgoing_ref
):
    atoms = types_ref.shape[1]
    own_ref[...] = jnp.zeros_like(own_ref)
    for axis in range(3):
        own_ref[axis : axis + 1, 0:atoms] = positions_ref[axis]
    own_ref[3:4, 0:atoms] = types_ref[...].astype(jnp.float32)
    own_ref[4:5, 0:atoms] = count_ref[...].astype(jnp.float32)
    own_ref[5:6, 0:atoms] = send_ref[...].astype(jnp.float32)
    for chunk in range(2):
        lanes = slice(128 * chunk, 128 * chunk + 128)
        wanted = jnp.broadcast_to(own_ref[5:6, lanes], (8, 128)).astype(jnp.int32)
        within = wanted & 127
        outgoing_ref[:, lanes] = jnp.where(
            wanted < 128,
            lane_pick(own_ref[:, 0:128], within),
            lane_pick(own_ref[:, 128:256], within),
        )


def collect(positions, types, counts, send_index):
    arrays = (positions, types, counts, send_index)
    result = jax.ShapeDtypeStruct((8, 256), jnp.float32)
    return pl.pallas_call(
        collect_kernel,
        grid=(1,),
        out_shape=[result, result],
        in_specs=whole_specs(*arrays),
        out_specs=whole_specs(result, result),
        compiler_params=pltpu.CompilerParams(vmem_limit_bytes=VMEM_BYTES),
        name="collect_atoms",
    )(*arrays)


def fitting_rows(descriptor_ref, weight_in_ref, weight_hidden_ref, weight_out_ref):
    hidden = jnp.tanh(product(descriptor_ref[...], weight_in_ref[...], LANES))
    for layer in range(weight_hidden_ref.shape[0]):
        hidden = jnp.tanh(product(hidden, weight_hidden_ref[layer])) + hidden
    width = hidden.shape[1]
    return product(jnp.broadcast_to(weight_out_ref[...], (8, width)), hidden, LANES)


def natural_order(rows):
    atoms = rows.shape[1]
    padded = jnp.concatenate([rows, jnp.zeros((8, 256 - atoms), jnp.float32)], axis=1)
    pieces = []
    for chunk in range(2):
        atom = 128 * chunk + lax.broadcasted_iota(jnp.int32, (8, 128), 1)
        late = atom >= atoms // 2
        within = jnp.where(late, atom - atoms // 2, atom)
        place = 8 * (within >> 2) + (within & 3) + jnp.where(late, 4, 0)
        place = jnp.minimum(place, 255)
        pieces.append(
            jnp.where(
                place < 128,
                lane_pick(padded[:, 0:128], place & 127),
                lane_pick(padded[:, 128:256], place & 127),
            )
        )
    return jnp.concatenate(pieces, axis=1)[0:1, 0:atoms]


def network_kernel(
    ghosts,
    base_ref,
    charges_ref,
    own_ref,
    lower_ref,
    upper_ref,
    slots_ref,
    types_ref,
    cell_x_ref,
    cell_y_ref,
    cell_z_ref,
    fraction_ref,
    first_ref,
    second_ref,
    third_ref,
    spot_ref,
    weight_in_hbm,
    weight_hidden_hbm,
    weight_out_ref,
    descriptor_hbm,
    charge_ref,
    copies_ref,
    descriptor_ref,
    environment_ref,
    kind_ref,
    moments_ref,
    padded_ref,
    weight_in_ref,
    weight_hidden_ref,
    semaphores,
):
    fetches = [
        pltpu.make_async_copy(weight_in_hbm, weight_in_ref, semaphores.at[0]),
        pltpu.make_async_copy(weight_hidden_hbm, weight_hidden_ref, semaphores.at[1]),
    ]
    for fetch in fetches:
        fetch.start()
    slots, atoms = slots_ref.shape
    rows = atoms // 2
    lane = lax.broadcasted_iota(jnp.int32, (8, 128), 1)
    sub = lax.broadcasted_iota(jnp.int32, (8, 128), 0)

    width = first_ref.shape[1]
    padded_ref[...] = jnp.zeros_like(padded_ref)
    padded_ref[0, 0:2, 0:width] = first_ref[...]
    for column in range(2):
        padded_ref[1, 0:width, 32 * column : 32 * column + width] = second_ref[
            :, width * column : width * (column + 1)
        ]
    for row in range(2):
        for column in range(4):
            padded_ref[2, 32 * row : 32 * row + width, 32 * column : 32 * column + width] = (
                third_ref[
                    width * row : width * (row + 1), width * column : width * (column + 1)
                ]
            )
    first_table = padded_ref[0].T
    embed_zero = jnp.broadcast_to(first_table[0:32, 0:1], (32, 128))
    embed_one = jnp.broadcast_to(first_table[0:32, 1:2], (32, 128))
    second_high, second_low = split(padded_ref[1].T[0:64, 0:32])
    second_weight = jnp.concatenate([second_high, second_high, second_low], axis=1)
    third_high, third_low = split(padded_ref[2].T[:, 0:64])
    third_weight = jnp.concatenate([third_high, third_high, third_low], axis=1)

    def spread(ref, field, chunk):
        return jnp.broadcast_to(ref[field : field + 1, 128 * chunk : 128 * chunk + 128], (8, 128))

    own = [[spread(own_ref, field, chunk) for chunk in range(2)] for field in range(5)]
    lower = [[spread(lower_ref, field, chunk) for chunk in range(2)] for field in range(4)]
    upper = [spread(upper_ref, field, 0) for field in range(4)]

    def pick_two(tables, index):
        within = index & 127
        return jnp.where(index < 128, lane_pick(tables[0], within), lane_pick(tables[1], within))

    pairs = jnp.concatenate([slots_ref[:, 0:rows], slots_ref[:, rows:atoms]], axis=0).T
    for tile in range(rows // 8):
        band = slice(8 * tile, 8 * tile + 8)
        index = pairs[band, :]
        centre = 8 * tile + sub + jnp.where(lane < 64, 0, rows)
        from_own = jnp.clip(index - ghosts, 0, atoms - 1)
        from_lower = jnp.minimum(index + (atoms - ghosts), 255)
        from_upper = jnp.clip(index - (ghosts + atoms), 0, 127)

        def neighbour(field):
            below = pick_two(lower[field], from_lower)
            inside = pick_two(own[field], from_own)
            above = lane_pick(upper[field], from_upper)
            return jnp.where(
                index < ghosts, below, jnp.where(index < ghosts + atoms, inside, above)
            )

        offsets = [neighbour(field) - pick_two(own[field], centre) for field in range(3)]
        live = pick_two(own[4], centre)
        present = jnp.where((lane & 63).astype(jnp.float32) < live, 1.0, 0.0)
        smooth = present / (
            1.0 + (offsets[0] * offsets[0] + offsets[1] * offsets[1] + offsets[2] * offsets[2])
        )
        environment_ref[0, band, :] = smooth
        for field in range(3):
            environment_ref[1 + field, band, :] = smooth * offsets[field]
        kind_ref[band, :] = neighbour(3)

    group = 8

    def stacked(values):
        high, low = split(values)
        return jnp.concatenate([high, low, high], axis=0)

    def one_group(start):
        pieces = []
        for row in range(group):
            smooth = jnp.broadcast_to(environment_ref[0, pl.ds(start + row, 1), :], (32, 128))
            kind = jnp.broadcast_to(kind_ref[pl.ds(start + row, 1), :], (32, 128))
            pieces.append(
                jnp.tanh(smooth * ((1.0 - kind) * embed_zero + kind * embed_one))
            )
        first = jnp.concatenate(pieces, axis=1)
        second = jnp.tanh(multiply(second_weight, stacked(first), ((1,), (0,))))
        second = second + jnp.concatenate([first, first], axis=0)
        third = jnp.tanh(multiply(third_weight, stacked(second), ((1,), (0,))))
        third = third + jnp.concatenate([second, second], axis=0)
        third_pair = split(third)
        for half in range(group // 4):
            columns = slice(512 * half, 512 * half + 512)
            bands = []
            for part in range(4):
                bands.append(
                    jnp.concatenate(
                        [
                            jnp.where(
                                sub == row + jnp.where(lane < 64, 0, 4),
                                jnp.broadcast_to(
                                    environment_ref[part, pl.ds(start + 4 * half + row, 1), :],
                                    (8, 128),
                                ),
                                0.0,
                            )
                            for row in range(4)
                        ],
                        axis=1,
                    )
                )
            environment = split(jnp.concatenate(bands, axis=0))
            both = multiply(
                jnp.concatenate(environment, axis=0), third_pair[0][:, columns], LANES
            )
            sums = both[0:32] + both[32:64]
            sums = sums + multiply(environment[0], third_pair[1][:, columns], LANES)
            sums = sums * (1.0 / slots)
            for part in range(4):
                moments_ref[part, pl.ds(2 * start + 8 * half, 8), :] = sums[
                    8 * part : 8 * part + 8
                ]

    def body(step, carry):
        for part in range(unroll):
            one_group(pl.multiple_of(step * unroll * group + part * group, group))
        return carry

    unroll = 4 if rows % (4 * group) == 0 else 1
    lax.fori_loop(0, rows // (unroll * group), body, 0)

    chunks = (descriptor_ref.shape[1] + 127) // 128
    last = descriptor_ref.shape[1] - 128 * (chunks - 1)

    def describe_band(start):
        band = pl.ds(start, 8)
        moments = [moments_ref[part, band, :] for part in range(4)]
        axis_part = [lane_pick(moments[part], lane & 15) for part in range(4)]
        for chunk in range(chunks):
            spot = jnp.broadcast_to(spot_ref[chunk : chunk + 1, :], (8, 128))
            total = lane_pick(moments[0], spot) * axis_part[0]
            for part in range(1, 4):
                total = total + lane_pick(moments[part], spot) * axis_part[part]
            if chunk < chunks - 1:
                descriptor_ref[band, 128 * chunk : 128 * chunk + 128] = total
            else:
                descriptor_ref[band, 128 * chunk : 128 * chunk + last] = total[:, 0:last]

    bands = 4 if atoms % 32 == 0 else 1

    def describe(step, carry):
        for part in range(bands):
            describe_band(pl.multiple_of(step * 8 * bands + 8 * part, 8))
        return carry

    lax.fori_loop(0, atoms // (8 * bands), describe, 0)

    store = pltpu.make_async_copy(descriptor_ref, descriptor_hbm, semaphores.at[2])
    store.start()
    for fetch in fetches:
        fetch.wait()
    shift = fitting_rows(descriptor_ref, weight_in_ref, weight_hidden_ref, weight_out_ref)
    kind = types_ref[...].astype(jnp.float32)
    charge = (1.0 - kind) * charges_ref[0] + kind * charges_ref[1] + natural_order(shift)
    charge_ref[...] = charge
    fields = jnp.concatenate(
        [
            cell_x_ref[...].astype(jnp.float32),
            (cell_y_ref[...] + base_ref[0]).astype(jnp.float32),
            cell_z_ref[...].astype(jnp.float32),
        ]
        + [fraction_ref[axis] for axis in range(3)]
        + [charge, jnp.zeros((1, atoms), jnp.float32)],
        axis=0,
    )
    for copy in range(copies_ref.shape[0]):
        copies_ref[copy] = fields
    store.wait()


def spot_table(embed, desc):
    column = np.arange(desc) // AXIS
    quarter = embed // 4
    place = 32 * (column // quarter) + column % quarter
    chunks = (desc + 127) // 128
    table = np.zeros((chunks * 128,), np.int32)
    table[:desc] = place
    padded = np.zeros(((chunks + 7) // 8 * 8, 128), np.int32)
    padded[:chunks] = table.reshape(chunks, 128)
    return padded


def networks(
    copies,
    ghosts,
    base,
    charge_base,
    own,
    lower,
    upper,
    neighbours,
    types,
    cells,
    fraction,
    embed,
    weight_in,
    weight_hidden,
    weight_out,
):
    atoms = types.shape[1]
    desc, width = weight_in.shape
    spots = jnp.asarray(spot_table(embed[2].shape[1], desc))
    anywhere = pl.BlockSpec(memory_space=pl.ANY)
    scalars = pl.BlockSpec(memory_space=pltpu.SMEM)
    blocks = (own, lower, upper, neighbours[0].T, types, *cells, fraction, *embed, spots)
    weight_out = weight_out.reshape(1, -1)
    results = [
        jax.ShapeDtypeStruct((atoms, desc), jnp.float32),
        jax.ShapeDtypeStruct((1, atoms), jnp.float32),
        jax.ShapeDtypeStruct((copies, 8, atoms), jnp.float32),
    ]
    return pl.pallas_call(
        functools.partial(network_kernel, ghosts),
        grid=(1,),
        out_shape=results,
        in_specs=[scalars, scalars]
        + whole_specs(*blocks)
        + [anywhere, anywhere]
        + whole_specs(weight_out),
        out_specs=[anywhere] + whole_specs(*results[1:]),
        scratch_shapes=[
            pltpu.VMEM((atoms, desc), jnp.float32),
            pltpu.VMEM((4, atoms // 2, 128), jnp.float32),
            pltpu.VMEM((atoms // 2, 128), jnp.float32),
            pltpu.VMEM((4, atoms, 128), jnp.float32),
            pltpu.VMEM((3, 128, 128), jnp.float32),
            pltpu.VMEM((width, desc), jnp.float32),
            pltpu.VMEM(weight_hidden.shape, jnp.float32),
            pltpu.SemaphoreType.DMA((3,)),
        ],
        compiler_params=pltpu.CompilerParams(vmem_limit_bytes=VMEM_BYTES),
        name="networks",
    )(base, charge_base, *blocks, weight_in.T, weight_hidden, weight_out)


def energy_kernel(descriptor_ref, weight_in_ref, weight_hidden_ref, weight_out_ref, energy_ref):
    energy_ref[...] = natural_order(
        fitting_rows(descriptor_ref, weight_in_ref, weight_hidden_ref, weight_out_ref)
    )


def energies(descriptor, weight_in, weight_hidden, weight_out):
    atoms, desc = descriptor.shape
    width = weight_in.shape[1]
    arrays = (descriptor, weight_in.T, weight_hidden, weight_out.reshape(1, -1))
    result = jax.ShapeDtypeStruct((1, atoms), jnp.float32)
    return pl.pallas_call(
        energy_kernel,
        grid=(1,),
        out_shape=result,
        in_specs=whole_specs(*arrays),
        out_specs=whole(result.shape),
        compiler_params=pltpu.CompilerParams(vmem_limit_bytes=VMEM_BYTES),
        cost_estimate=pl.CostEstimate(
            flops=6 * atoms * desc * width, bytes_accessed=4 * desc * width, transcendentals=0
        ),
        name="energies",
    )(*arrays)


def weight_rows(fraction):
    square = fraction * fraction
    cubed = square * fraction
    rest = 1.0 - fraction
    return [
        rest * rest * rest / 6.0,
        (3.0 * cubed - 6.0 * square + 4.0) / 6.0,
        (-3.0 * cubed + 3.0 * square + 3.0 * fraction + 1.0) / 6.0,
        cubed / 6.0,
    ]


def placed_weights(distance, weights):
    shape = distance.shape
    result = jnp.zeros(shape, jnp.float32)
    for step in range(4):
        result = jnp.where(
            distance == step, jnp.broadcast_to(weights[step], shape), result
        )
    return result


def third_factors(fields, waves_ref, cosine_ref):
    atoms = fields.shape[1]
    start = fields[2:3, :].astype(jnp.int32)
    along = weight_rows(fields[5:6, :])
    parts = waves_ref.shape[0]
    cosine = jnp.broadcast_to(cosine_ref[...], (parts, 128))
    wave = jnp.broadcast_to(waves_ref[:, 0:1], (parts, 128))
    shift = jnp.broadcast_to(waves_ref[:, 1:2], (parts, 128))
    pieces = []
    for chunk in range(atoms // 128):
        lanes = slice(128 * chunk, 128 * chunk + 128)
        total = jnp.zeros((parts, 128), jnp.float32)
        for step in range(4):
            place = jnp.broadcast_to(start[:, lanes] + step, (parts, 128))
            phase = (wave * place + shift) & (NG - 1)
            value = lane_pick(cosine, phase & 127)
            value = jnp.where(phase < 128, value, -value)
            total = total + value * jnp.broadcast_to(along[step][:, lanes], (parts, 128))
        pieces.append(total)
    return jnp.concatenate(pieces, axis=1)


def first_third(fields, waves_ref, cosine_ref, window, scale):
    atoms = fields.shape[1]
    third = third_factors(fields, waves_ref, cosine_ref)
    if scale is not None:
        third = third * scale
    rows = lax.broadcasted_iota(jnp.int32, (window, atoms), 0)
    first = placed_weights(
        rows - fields[0:1, :].astype(jnp.int32), weight_rows(fields[3:4, :])
    )
    return jnp.concatenate(
        [first * third[part : part + 1, :] for part in range(third.shape[0])], axis=0
    )


def first_third_split(fields, waves_ref, cosine_ref, window, scale, high_ref, low_ref):
    atoms = fields.shape[1]
    third = third_factors(fields, waves_ref, cosine_ref) * scale
    rows = lax.broadcasted_iota(jnp.int32, (window, atoms), 0)
    first = placed_weights(
        rows - fields[0:1, :].astype(jnp.int32), weight_rows(fields[3:4, :])
    )
    for chunk in range(atoms // 128):
        lanes = slice(128 * chunk, 128 * (chunk + 1))
        for part in range(0, third.shape[0], 2):
            high, low = split(
                jnp.concatenate(
                    [first[:, lanes] * third[part + side : part + side + 1, lanes] for side in range(2)],
                    axis=0,
                )
            )
            place = slice(part * window, (part + 2) * window)
            high_ref[place, lanes] = high
            low_ref[place, lanes] = low
    return high_ref[...], low_ref[...]


def second_factors(fields, base, block_y, slabs, high_ref, low_ref):
    atoms = fields.shape[1]
    block = atoms // slabs
    reach = block_y + 16
    start = fields[1:2, :].astype(jnp.int32) - base
    weights = weight_rows(fields[4:5, :])
    for chunk in range(atoms // 128):
        lanes = slice(128 * chunk, 128 * (chunk + 1))
        first = 128 * chunk // block
        last = (128 * chunk + 127) // block
        top = first * block_y
        rows = (last - first) * block_y + reach
        pieces = [(top, min(rows, NG - top))]
        if top + rows > NG:
            pieces.append((0, top + rows - NG))
        for row, count in pieces:
            index = row + lax.broadcasted_iota(jnp.int32, (count, 128), 0)
            table = split(
                placed_weights(
                    (index - start[:, lanes]) & (NG - 1), [weight[:, lanes] for weight in weights]
                )
            )
            high_ref[row : row + count, lanes] = table[0]
            low_ref[row : row + count, lanes] = table[1]
    return high_ref[...], low_ref[...]


def wave_of(index):
    return jnp.where(index <= NG // 2, index, index - NG // 2)


def damping(index):
    kappa = wave_of(index).astype(jnp.float32) * (2.0 * math.pi / NG)
    squared = kappa * kappa
    ends = (index == 0) | (index == NG // 2)
    return squared, jnp.exp(-0.5 * squared) * jnp.where(ends, 1.0 / NG, 2.0 / NG)


def transform(planes, kappa_ref, first_part, tables_ref, last_ref):
    count = len(planes)
    basis = tables_ref[0]
    turned = tables_ref[1]
    square_x, damp_x = damping(lax.broadcasted_iota(jnp.int32, (NG, 1), 0))
    square_y, damp_y = damping(lax.broadcasted_iota(jnp.int32, (1, NG), 1))
    square_xy = square_x + square_y
    damp_xy = damp_x * damp_y
    columns = [slice(NG * part, NG * (part + 1)) for part in range(count)]
    first = product(basis, jnp.concatenate(planes, axis=1))
    first = jnp.concatenate([first[:, column] for column in columns], axis=0)
    both = product(first, turned)
    scaled = []
    for part in range(count):
        squared = square_xy + kappa_ref[first_part + part, 0]
        root = jnp.where(squared == 0.0, 1.0, 0.0)
        green = (1.0 - root) * (damp_xy * kappa_ref[first_part + part, 1]) / (squared + root)
        scaled.append(both[columns[part]] * green)
    back = product(turned, jnp.concatenate(scaled, axis=1))
    back = jnp.concatenate([back[:, column] for column in columns], axis=0)
    return product(back, last_ref[...])


def send_blocks(full, block_x, block_y, put):
    low_lanes = lax.broadcasted_iota(jnp.int32, (NG, 128), 1) < block_y
    for pair in range(full.shape[0] // (2 * NG)):
        even = full[2 * NG * pair : 2 * NG * pair + NG, 0:128]
        odd = full[2 * NG * pair + NG : 2 * NG * (pair + 1), 0:128]
        blocks = [
            jnp.where(low_lanes, even, pltpu.roll(odd, block_y, 1)),
            jnp.where(low_lanes, pltpu.roll(even, block_y, 1), odd),
        ]
        for brick in range(NG // block_x):
            for side in range(2):
                for group in range(block_x // 8):
                    start = block_x * brick + 8 * group
                    put(pair, brick, side, group, blocks[side][start : start + 8])


def spread_kernel(
    block_x,
    block_y,
    window,
    kappa_ref,
    pair_ref,
    static_ref,
    waves_ref,
    cosine_ref,
    tables_hbm,
    last_hbm,
    sent_ref,
    full_ref,
    atoms_ref,
    later_hbm,
    grid_ref,
    tables_ref,
    last_ref,
    semaphores,
    *pair_refs,
):
    slabs = NG // block_y
    second_refs, first_refs = pair_refs[:4], pair_refs[4:]
    bricks = NG // block_x
    parts = waves_ref.shape[0]
    block = static_ref.shape[2]
    count = full_ref.shape[0]
    step = pl.program_id(0)
    later = later_hbm.shape[0]
    store = pltpu.make_async_copy(
        grid_ref.at[pl.ds(parts - later, later), pl.ds(0, NG)], later_hbm, semaphores.at[2]
    )

    @pl.when(step == 0)
    def _():
        fetches = [
            pltpu.make_async_copy(tables_hbm, tables_ref, semaphores.at[0]),
            pltpu.make_async_copy(last_hbm.at[pair_ref[0]], last_ref, semaphores.at[1]),
        ]
        for fetch in fetches:
            fetch.start()
        for slab in range(slabs):
            lanes = slice(block * slab, block * (slab + 1))
            for brick in range(bricks):
                atoms_ref[brick, :, lanes] = static_ref[slab * bricks + brick]
        grid_ref[...] = jnp.zeros_like(grid_ref)
        for ref in second_refs:
            ref[...] = jnp.zeros_like(ref)
        for brick in range(bricks):
            fields = atoms_ref[brick]
            table = first_third_split(
                fields,
                waves_ref,
                cosine_ref,
                window,
                fields[6:7, :],
                first_refs[2 * (brick % 2)],
                first_refs[2 * (brick % 2) + 1],
            )
            second = second_factors(
                fields, 0, block_y, slabs, second_refs[2 * (brick % 2)], second_refs[2 * (brick % 2) + 1]
            )
            spread = triple(table, second, LANES)
            rows = slice(block_x * brick, block_x * brick + window)
            for part in range(parts):
                grid_ref[part, rows, :] += spread[part * window : part * window + window]
        extra = window - block_x
        for part in range(parts):
            grid_ref[part, 0:extra, :] += grid_ref[part, NG : NG + extra, :]
        store.start()
        for fetch in fetches:
            fetch.wait()

    planes = [grid_ref[count * step + part, 0:NG, :] for part in range(count)]
    full = transform(planes, kappa_ref, count * step, tables_ref, last_ref)
    for part in range(count):
        full_ref[part] = full[NG * part : NG * (part + 1)]

    def put(pair, brick, side, group, tile):
        sent_ref[2 * brick + side, group, pair] = tile

    send_blocks(full, block_x, block_y, put)

    @pl.when(step == pl.num_programs(0) - 1)
    def _():
        store.wait()


def early_pairs(parts):
    return parts // 4


def spread_and_solve(
    block_x, block_y, window, kappa, pair, static, waves, cosine_row, tables, last
):
    devices, _, atoms = static.shape
    slabs = NG // block_y
    bricks = NG // block_x
    parts = waves.shape[0]
    pairs = early_pairs(parts)
    count = 4
    anywhere = pl.BlockSpec(memory_space=pl.ANY)
    scalars = pl.BlockSpec(memory_space=pltpu.SMEM)
    sent_block = (2 * bricks, block_x // 8, count // 2, 8, 128)
    return pl.pallas_call(
        functools.partial(spread_kernel, block_x, block_y, window),
        grid=(2 * pairs // count,),
        out_shape=[
            jax.ShapeDtypeStruct((2 * bricks, block_x // 8, pairs, 8, 128), jnp.float32),
            jax.ShapeDtypeStruct((2 * pairs, NG, NG), jnp.float32),
            jax.ShapeDtypeStruct((bricks, 8, slabs * atoms), jnp.float32),
            jax.ShapeDtypeStruct((parts - 2 * pairs, NG, NG), jnp.float32),
        ],
        in_specs=[scalars, scalars]
        + whole_specs(static, waves, cosine_row)
        + [anywhere, anywhere],
        out_specs=[
            pl.BlockSpec(sent_block, lambda step: (0, 0, step, 0, 0)),
            pl.BlockSpec((count, NG, NG), lambda step: (step, 0, 0)),
            whole((bricks, 8, slabs * atoms)),
            anywhere,
        ],
        scratch_shapes=[
            pltpu.VMEM((parts, NG + window - block_x, NG), jnp.float32),
            pltpu.VMEM(tables.shape, tables.dtype),
            pltpu.VMEM(last.shape[1:], last.dtype),
            pltpu.SemaphoreType.DMA((3,)),
        ]
        + [pltpu.VMEM((NG, slabs * atoms), jnp.bfloat16)] * 4
        + [pltpu.VMEM((parts * window, slabs * atoms), jnp.bfloat16)] * 4,
        compiler_params=pltpu.CompilerParams(vmem_limit_bytes=VMEM_BYTES),
        name="spread_and_solve",
    )(kappa, pair, static, waves, cosine_row, tables, last)


def sample_kernel(
    block_x,
    block_y,
    window,
    kappa_ref,
    pair_ref,
    atoms_ref,
    waves_ref,
    cosine_ref,
    tables_hbm,
    last_hbm,
    later_hbm,
    early_hbm,
    sent_ref,
    later_ref,
    full_ref,
    tables_ref,
    last_ref,
    semaphores,
    *second_refs,
):
    bricks = atoms_ref.shape[0]
    parts = waves_ref.shape[0]
    early = 2 * early_pairs(parts)
    block = atoms_ref.shape[2] * block_y // NG
    fetches = [
        pltpu.make_async_copy(tables_hbm, tables_ref, semaphores.at[0]),
        pltpu.make_async_copy(last_hbm.at[pair_ref[0]], last_ref, semaphores.at[1]),
        pltpu.make_async_copy(later_hbm, later_ref, semaphores.at[2]),
        pltpu.make_async_copy(early_hbm, full_ref.at[pl.ds(0, early)], semaphores.at[3]),
    ]
    for fetch in fetches:
        fetch.start()
    for fetch in fetches[:3]:
        fetch.wait()
    pairs = (parts - early) // 2
    planes = [later_ref[part] for part in range(parts - early)]
    full = transform(planes, kappa_ref, early, tables_ref, last_ref)
    for part in range(parts - early):
        full_ref[early + part] = full[NG * part : NG * (part + 1)]

    def put(pair, brick, side, group, tile):
        sent_ref[2 * brick + side, pairs * group + pair] = tile

    send_blocks(full, block_x, block_y, put)
    fetches[3].wait()

    for ref in second_refs:
        ref[...] = jnp.zeros_like(ref)
    extra = sent_ref.shape[1] - 1
    base = 2 * block_y * pair_ref[0]
    lanes = pl.ds(pl.multiple_of(2 * block * pair_ref[0], 128), 2 * block)
    for brick in range(bricks):
        fields = atoms_ref[brick, :, lanes]
        weights = first_third(fields, waves_ref, cosine_ref, window, None)
        start = block_x * brick
        inside = min(window, NG - start)
        values = []
        for part in range(parts):
            values.append(full_ref[part, start : start + inside, :])
            if inside < window:
                values.append(full_ref[part, 0 : window - inside, :])
        values = split(jnp.concatenate(values, axis=0))
        second = second_factors(
            fields, base, block_y, 2, second_refs[2 * (brick % 2)], second_refs[2 * (brick % 2) + 1]
        )
        along = triple(values, second)
        sums = jnp.sum(along * weights, axis=0, keepdims=True)
        for side in range(2):
            row = sums[:, block * side : block * (side + 1)]
            sent_ref[2 * brick + side, extra] = jnp.zeros((8, 128), jnp.float32)
            sent_ref[2 * brick + side, extra, 0:1, :] = row[:, 0:128]
            sent_ref[2 * brick + side, extra, 1:2, 0 : block - 128] = row[:, 128:block]


def solve_and_sample(
    block_x, block_y, window, kappa, pair, atoms, waves, cosine_row, tables, last, later, early
):
    bricks = atoms.shape[0]
    parts = waves.shape[0]
    pairs = parts // 2 - early_pairs(parts)
    anywhere = pl.BlockSpec(memory_space=pl.ANY)
    scalars = pl.BlockSpec(memory_space=pltpu.SMEM)
    result = jax.ShapeDtypeStruct((2 * bricks, block_x // 8 * pairs + 1, 8, 128), jnp.float32)
    return pl.pallas_call(
        functools.partial(sample_kernel, block_x, block_y, window),
        grid=(1,),
        out_shape=result,
        in_specs=[scalars, scalars] + whole_specs(atoms, waves, cosine_row) + [anywhere] * 4,
        out_specs=whole(result.shape),
        scratch_shapes=[
            pltpu.VMEM((2 * pairs, NG, NG), jnp.float32),
            pltpu.VMEM((parts, NG, NG), jnp.float32),
            pltpu.VMEM(tables.shape, tables.dtype),
            pltpu.VMEM(last.shape[1:], last.dtype),
            pltpu.SemaphoreType.DMA((4,)),
        ]
        + [pltpu.VMEM((NG, 2 * atoms.shape[2] * block_y // NG), jnp.bfloat16)] * 4,
        compiler_params=pltpu.CompilerParams(vmem_limit_bytes=VMEM_BYTES),
        cost_estimate=pl.CostEstimate(
            flops=24 * parts * NG * NG * NG, bytes_accessed=4 * early.size, transcendentals=0
        ),
        name="solve_and_sample",
    )(kappa, pair, atoms, waves, cosine_row, tables, last, later, early)


def finish_kernel(
    block_y, early_ref, later_ref, sums_ref, short_ref, charge_ref, table_ref, out_ref, energy_ref
):
    atoms = short_ref.shape[1]
    lines = early_ref.shape[3]
    sources, _, pairs = early_ref.shape[:3]
    early = early_ref.reshape(sources * pairs, lines, 128)
    later = later_ref.reshape(sources * later_ref.shape[1], lines, 128)
    pieces = []
    for line in range(lines):
        turned = jnp.concatenate([early[:, line, :], later[:, line, :]], axis=0).T
        pieces.append(jnp.concatenate([turned[0:block_y], turned[block_y:]], axis=1))
    result = product(jnp.concatenate(pieces, axis=0), table_ref[...])
    for line in range(lines):
        out_ref[line] = result[block_y * line : block_y * (line + 1)]

    @pl.when(pl.program_id(0) == 0)
    def _():
        total = jnp.sum(sums_ref[:, 0], axis=0)
        potential_at = jnp.concatenate([total[0:1, :], total[1:2, 0 : atoms - 128]], axis=1)
        energy_ref[...] = short_ref[...] + 0.5 * charge_ref[...] * potential_at


def finish(block_x, block_y, early, later, short, charge, table):
    bricks2, groups, pairs = early.shape[:3]
    rest = (later.shape[1] - 1) // groups
    atoms = short.shape[1]
    return pl.pallas_call(
        functools.partial(finish_kernel, block_y),
        grid=(groups,),
        out_shape=[
            jax.ShapeDtypeStruct((block_x, block_y, NG), jnp.float32),
            jax.ShapeDtypeStruct((1, atoms), jnp.float32),
        ],
        in_specs=[
            pl.BlockSpec((bricks2, 1, pairs, 8, 128), lambda index: (0, index, 0, 0, 0)),
            pl.BlockSpec((bricks2, rest, 8, 128), lambda index: (0, index, 0, 0)),
            pl.BlockSpec((bricks2, 1, 8, 128), lambda index: (0, groups * rest, 0, 0)),
            whole((1, atoms)),
            whole((1, atoms)),
            whole(table.shape),
        ],
        out_specs=[
            pl.BlockSpec((8, block_y, NG), lambda index: (index, 0, 0)),
            whole((1, atoms)),
        ],
        compiler_params=pltpu.CompilerParams(vmem_limit_bytes=32 * 2**20),
        name="finish",
    )(early, later, later, short, charge, table)


def real_basis():
    index = np.arange(NG)
    wave = np.where(index <= NG // 2, index, index - NG // 2)
    angle = (wave[:, None] * index[None, :] % NG) * (2.0 * math.pi / NG)
    return np.where((index <= NG // 2)[:, None], np.cos(angle), np.sin(angle))


def per_device(
    positions,
    types,
    neighbours,
    neighbour_count,
    send_index,
    cell_x,
    cell_y,
    cell_z,
    spline_fraction,
    embed_first,
    embed_second,
    embed_third,
    energy_in,
    energy_hidden,
    energy_out,
    wannier_in,
    wannier_hidden,
    wannier_out,
    charge_base,
):
    atoms = types.shape[1]
    ghosts = send_index.shape[1] // 2
    count_x = lax.axis_size("brick")
    count_y = lax.axis_size("slab")
    block_x = NG // count_x
    block_y = NG // count_y
    window = block_x + 8
    parts = NG // (2 * count_x)
    brick = lax.axis_index("brick")
    slab = lax.axis_index("slab")
    pair = (slab // 2).astype(jnp.int32).reshape(1)
    halves = [
        [b * count_y + 2 * p + side for b in range(count_x) for side in range(2)]
        for p in range(count_y // 2)
    ]

    def exchange(values, axes, groups=None):
        return lax.all_to_all(
            values, axes, split_axis=0, concat_axis=0, tiled=True, axis_index_groups=groups
        )

    own, outgoing = collect(positions, types, neighbour_count, send_index)
    up = [(i, (i + 1) % count_x) for i in range(count_x)]
    down = [((i + 1) % count_x, i) for i in range(count_x)]
    lower = lax.ppermute(outgoing, "brick", up)
    upper = lax.ppermute(outgoing, "brick", down)
    descriptor, charge, fields = networks(
        count_x * count_y,
        ghosts,
        (slab * block_y).astype(jnp.int32).reshape(1),
        charge_base,
        own,
        lower,
        upper,
        neighbours,
        types,
        (cell_x, cell_y, cell_z),
        spline_fraction,
        (embed_first, embed_second, embed_third),
        wannier_in,
        wannier_hidden,
        wannier_out,
    )
    every_field = exchange(fields, ("slab", "brick"))

    part = (2 * brick + slab % 2) * parts + jnp.arange(parts, dtype=jnp.int32)
    wave = wave_of(part)
    waves = jnp.stack([wave, jnp.where(part <= NG // 2, 0, 3 * NG // 4)], axis=1)
    kappa = wave.astype(jnp.float32) * (2.0 * math.pi / NG)
    squared = kappa * kappa
    ends = (part == 0) | (part == NG // 2)
    kappa = jnp.stack(
        [squared, jnp.exp(-0.5 * squared) * jnp.where(ends, 1.0 / NG, 2.0 / NG)], axis=1
    )
    basis = real_basis()
    tables = np.stack([basis, basis.T]).astype(np.float32)
    last = []
    for p in range(count_y // 2):
        points = (2 * block_y * p + np.arange(2 * block_y + 8)) % NG
        columns = np.zeros((NG, NG))
        columns[:, : points.size] = basis[:, points]
        last.append(columns.astype(np.float32))
    cosine_row = np.cos(np.arange(128) * (2.0 * math.pi / NG)).astype(np.float32)[None]
    cosine_row = jnp.asarray(cosine_row)
    tables = jnp.asarray(tables)
    last = jnp.asarray(np.stack(last))
    early, full, every_atom, later = spread_and_solve(
        block_x, block_y, window, kappa, pair, every_field, waves, cosine_row, tables, last
    )

    def send(values):
        got = exchange(values.reshape(values.shape[0], -1, 128), ("brick", "slab"), halves)
        return got.reshape(values.shape)

    early = send(early)
    later = solve_and_sample(
        block_x,
        block_y,
        window,
        kappa,
        pair,
        every_atom,
        waves,
        cosine_row,
        tables,
        last,
        later,
        full,
    )
    later = send(later)
    energy_short = energies(descriptor, energy_in, energy_hidden, energy_out)
    source = np.arange(2 * count_x)[:, None] * parts
    pairs = 2 * np.arange(parts // 2)[None, :]
    order = np.concatenate(
        [
            (source + pairs[:, : early_pairs(parts)]).ravel(),
            (source + pairs[:, early_pairs(parts) :]).ravel(),
        ]
    )
    order = np.concatenate([order, order + 1])
    potential, atom_energy = finish(
        block_x,
        block_y,
        early,
        later,
        energy_short,
        charge,
        jnp.asarray(basis[order].astype(np.float32)),
    )
    return atom_energy, potential


def solution(mesh):
    placed = (
        P(None, "slab", "brick"),
        P("slab", "brick"),
        P("slab", "brick", None),
        P("slab", "brick"),
        P("slab", "brick"),
        P("slab", "brick"),
        P("slab", "brick"),
        P("slab", "brick"),
        P(None, "slab", "brick"),
    ) + (P(),) * 10
    bricks, slabs = mesh.shape["brick"], mesh.shape["slab"]
    fits = 2 * NG == 128 * slabs and NG % (32 * bricks) == 0
    return jax.shard_map(
        per_device if fits else per_device_general,
        mesh=mesh,
        in_specs=placed,
        out_specs=(P("slab", "brick"), P("brick", "slab", None)),
        check_vma=False,
    )
```

```python
import functools
import math

import jax
import jax.numpy as jnp
import numpy as np
from jax import lax
from jax.experimental import pallas as pl
from jax.experimental.pallas import tpu as pltpu
from jax.sharding import PartitionSpec as P

NG = 256
AXIS = 16
VMEM_BYTES = 60 * 2**20
REACH = 16


HIGH = lax.Precision.HIGHEST


def with_halo(cells, sides, width):
    for axis, dim in sides:
        count = lax.axis_size(axis)
        head = lax.slice_in_dim(cells, 0, width, axis=dim)
        tail = lax.slice_in_dim(cells, cells.shape[dim] - width, cells.shape[dim], axis=dim)
        cells = jnp.concatenate(
            [
                lax.ppermute(tail, axis, [(i, (i + 1) % count) for i in range(count)]),
                cells,
                lax.ppermute(head, axis, [((i + 1) % count, i) for i in range(count)]),
            ],
            axis=dim,
        )
    return cells


def spline_weights(fraction):
    cubed = fraction * fraction * fraction
    square = fraction * fraction
    return jnp.stack(
        [
            (1.0 - fraction) * (1.0 - fraction) * (1.0 - fraction) / 6.0,
            (3.0 * cubed - 6.0 * square + 4.0) / 6.0,
            (-3.0 * cubed + 3.0 * square + 3.0 * fraction + 1.0) / 6.0,
            cubed / 6.0,
        ]
    )


def fitting(descriptor, weight_in, weight_hidden, weight_out):
    hidden = jnp.tanh(jnp.dot(descriptor, weight_in, precision=HIGH))
    for depth_index in range(weight_hidden.shape[0]):
        hidden = jnp.tanh(jnp.dot(hidden, weight_hidden[depth_index], precision=HIGH)) + hidden
    return jnp.dot(hidden, weight_out, precision=HIGH)


def atom_terms(
    extended,
    neighbour_rows,
    neighbour_total,
    embed_first,
    embed_second,
    embed_third,
    energy_in,
    energy_hidden,
    energy_out,
    wannier_in,
    wannier_hidden,
    wannier_out,
):
    atom_count, slots = neighbour_rows.shape
    ghost_rows = (extended.shape[1] - atom_count) // 2
    block_size = 64
    blocks = atom_count // block_size
    present = (jnp.arange(slots, dtype=jnp.int32)[None, :] < neighbour_total[:, None]).astype(
        jnp.float32
    )
    centre_ids = (ghost_rows + jnp.arange(atom_count, dtype=jnp.int32)).reshape(blocks, block_size)
    second_weight = embed_second.T
    third_weight = embed_third.T

    def one_block(pieces):
        centre_rows, rows_block, present_block = pieces
        centre_block = extended[:3, centre_rows]
        gathered = extended[:, rows_block]
        offsets = gathered[:3] - centre_block[:, :, None]
        smooth = present_block / (1.0 + jnp.sum(offsets * offsets, axis=0))
        environment = jnp.stack(
            [smooth, smooth * offsets[0], smooth * offsets[1], smooth * offsets[2]], axis=0
        )
        kind = gathered[3][None]
        mixing = (1.0 - kind) * embed_first[0][:, None, None] + kind * embed_first[1][:, None, None]
        first = jnp.tanh(smooth[None] * mixing).reshape(embed_first.shape[1], block_size * slots)
        second = jnp.tanh(jnp.dot(second_weight, first, precision=HIGH)) + jnp.concatenate(
            [first, first], axis=0
        )
        third = jnp.tanh(jnp.dot(third_weight, second, precision=HIGH)) + jnp.concatenate(
            [second, second], axis=0
        )
        third_blocks = third.reshape(third.shape[0], block_size, slots)
        moments = jnp.einsum("kan,can->akc", third_blocks, environment, precision=HIGH) / slots
        descriptor = jnp.einsum("amc,akc->amk", moments, moments[:, :AXIS], precision=HIGH).reshape(
            block_size, -1
        )
        return (
            fitting(descriptor, energy_in, energy_hidden, energy_out),
            fitting(descriptor, wannier_in, wannier_hidden, wannier_out),
        )

    energy_short, charge_shift = lax.map(
        one_block,
        (
            centre_ids,
            neighbour_rows.reshape(blocks, block_size, slots),
            present.reshape(blocks, block_size, slots),
        ),
    )
    return (energy_short.reshape(atom_count), charge_shift.reshape(atom_count))


def green_table(first, second, third, size):

    def folded(index):
        return jnp.where(index < size // 2, index, index - size).astype(jnp.float32) * (
            2.0 * math.pi / size
        )

    kappa_x = folded(first)[:, None, None]
    kappa_y = folded(second)[None, :, None]
    kappa_z = folded(third)[None, None, :]
    squared = kappa_x * kappa_x + kappa_y * kappa_y + kappa_z * kappa_z
    root = (
        (first[:, None, None] == 0) & (second[None, :, None] == 0) & (third[None, None, :] == 0)
    ).astype(jnp.float32)
    return (1.0 - root) * jnp.exp(-0.5 * squared) / (squared + root)


def dft_tables(size):
    index = jnp.arange(size, dtype=jnp.int32)
    phase = (index[:, None] * index[None, :] % size).astype(jnp.float32) * (2.0 * math.pi / size)
    return (jnp.cos(phase), jnp.sin(phase))


def along(values, table, axis_index):
    result = jnp.tensordot(values, table, axes=([axis_index], [0]), precision=HIGH)
    return jnp.moveaxis(result, -1, axis_index)


def complex_transform(paired, axis_index, cosine, sine, inverse):
    real_part = paired[0]
    imag_part = paired[1]
    inner = axis_index - 1
    real_cos = along(real_part, cosine, inner)
    real_sin = along(real_part, sine, inner)
    imag_cos = along(imag_part, cosine, inner)
    imag_sin = along(imag_part, sine, inner)
    if inverse:
        return jnp.stack([real_cos - imag_sin, imag_cos + real_sin])
    return jnp.stack([real_cos + imag_sin, imag_cos - real_sin])


def fold_windows(values, axis_index, block, count):
    front = jnp.moveaxis(values, axis_index, 0)
    rest = front.shape[1:]
    windows = front.reshape((count, block + 3) + rest)
    main_part = windows[:, :block]
    carried = jnp.roll(windows[:, block:], 1, axis=0)
    main_part = main_part.at[:, :3].add(carried)
    return jnp.moveaxis(main_part.reshape((count * block,) + rest), 0, axis_index)


def make_windows(values, axis_index, block, count):
    front = jnp.moveaxis(values, axis_index, 0)
    rest = front.shape[1:]
    pieces = front.reshape((count, block) + rest)
    trailing = jnp.roll(pieces, -1, axis=0)[:, :3]
    windows = jnp.concatenate([pieces, trailing], axis=1)
    return jnp.moveaxis(windows.reshape((count * (block + 3),) + rest), 0, axis_index)


def spread_matrix(start, weights, width, wrap_size):
    offsets = jnp.arange(4, dtype=jnp.int32)[:, None, None]
    target = start[None, :, None] + offsets
    if wrap_size > 0:
        target = target % wrap_size
    hits = (target == jnp.arange(width, dtype=jnp.int32)[None, None, :]).astype(jnp.float32)
    return jnp.sum(weights[:, :, None] * hits, axis=0)


def per_device_general(
    positions,
    types,
    neighbours,
    neighbour_count,
    send_index,
    cell_x,
    cell_y,
    cell_z,
    spline_fraction,
    embed_first,
    embed_second,
    embed_third,
    energy_in,
    energy_hidden,
    energy_out,
    wannier_in,
    wannier_hidden,
    wannier_out,
    charge_base,
):
    atom_count = types.shape[1]
    ghost_rows = send_index.shape[1] // 2
    kind_float = types[0].astype(jnp.float32)
    own_atoms = jnp.concatenate([positions[:, 0], kind_float[None]], axis=0)
    outgoing = own_atoms[:, send_index[0]]
    padded_ghosts = with_halo(outgoing, (("brick", 1),), ghost_rows)
    extended = jnp.concatenate(
        [padded_ghosts[:, :ghost_rows], own_atoms, padded_ghosts[:, 3 * ghost_rows :]], axis=1
    )
    energy_short, charge_shift = atom_terms(
        extended,
        neighbours[0],
        neighbour_count[0],
        embed_first,
        embed_second,
        embed_third,
        energy_in,
        energy_hidden,
        energy_out,
        wannier_in,
        wannier_hidden,
        wannier_out,
    )
    charge = (1.0 - kind_float) * charge_base[0] + kind_float * charge_base[1] + charge_shift
    count_x = lax.axis_size("brick")
    count_y = lax.axis_size("slab")
    block_x = NG // count_x
    block_y = NG // count_y
    wide_x = block_x + 3
    wide_y = block_y + 3
    spread_x = spread_matrix(cell_x[0], spline_weights(spline_fraction[0, 0]), wide_x, 0)
    spread_y = spread_matrix(cell_y[0], spline_weights(spline_fraction[1, 0]), wide_y, 0)
    spread_z = spread_matrix(cell_z[0], spline_weights(spline_fraction[2, 0]), NG, NG)
    spread_xy = (spread_x[:, :, None] * spread_y[:, None, :]).reshape(atom_count, wide_x * wide_y)
    charge_grid = jnp.einsum(
        "ap,az->pz", spread_xy, charge[:, None] * spread_z, precision=HIGH
    ).reshape(wide_x, wide_y, NG)
    cosine, sine = dft_tables(NG)
    scale = 1.0 / (NG * NG * NG)
    full_index = jnp.arange(NG, dtype=jnp.int32)
    paired = jnp.stack([along(charge_grid, cosine, 2), -along(charge_grid, sine, 2)])
    moved = lax.all_to_all(paired, "slab", split_axis=3, concat_axis=2, tiled=True)
    moved = complex_transform(fold_windows(moved, 2, block_y, count_y), 2, cosine, sine, False)
    moved = lax.all_to_all(moved, "brick", split_axis=2, concat_axis=1, tiled=True)
    moved = complex_transform(fold_windows(moved, 1, block_x, count_x), 1, cosine, sine, False)
    part_y = NG // count_x
    part_z = NG // count_y
    index_y = lax.axis_index("brick") * part_y + jnp.arange(part_y, dtype=jnp.int32)
    index_z = lax.axis_index("slab") * part_z + jnp.arange(part_z, dtype=jnp.int32)
    moved = moved * (green_table(full_index, index_y, index_z, NG) * scale)[None]
    moved = make_windows(complex_transform(moved, 1, cosine, sine, True), 1, block_x, count_x)
    moved = lax.all_to_all(moved, "brick", split_axis=1, concat_axis=2, tiled=True)
    moved = make_windows(complex_transform(moved, 2, cosine, sine, True), 2, block_y, count_y)
    moved = lax.all_to_all(moved, "slab", split_axis=2, concat_axis=3, tiled=True)
    potential_wide = along(moved[0], cosine, 2) - along(moved[1], sine, 2)
    sampled = jnp.einsum(
        "ap,pz->az", spread_xy, potential_wide.reshape(wide_x * wide_y, NG), precision=HIGH
    )
    potential_at = jnp.sum(sampled * spread_z, axis=1)
    atom_energy = energy_short + 0.5 * charge * potential_at
    return (atom_energy[None, :], potential_wide[:block_x, :block_y])


def split(values):
    high = values.astype(jnp.bfloat16)
    low = (values - high.astype(jnp.float32)).astype(jnp.bfloat16)
    return high, low


def multiply(left, right, dims):
    return lax.dot_general(left, right, (dims, ((), ())), preferred_element_type=jnp.float32)


def triple(left, right, dims=((1,), (0,))):
    (left_axis,), (right_axis,) = dims
    if left[0].shape[left_axis] % 128 == 0:
        return multiply(
            jnp.concatenate([left[0], left[0], left[1]], axis=left_axis),
            jnp.concatenate([right[0], right[1], right[0]], axis=right_axis),
            dims,
        )
    return (
        multiply(left[0], right[0], dims)
        + multiply(left[0], right[1], dims)
        + multiply(left[1], right[0], dims)
    )


LANES = ((1,), (1,))


def product(left, right, dims=((1,), (0,))):
    return lax.dot_general(
        left,
        right,
        (dims, ((), ())),
        precision=lax.Precision.HIGH,
        preferred_element_type=jnp.float32,
    )


def lane_pick(table, index):
    return jnp.take_along_axis(table, index, axis=1, mode="promise_in_bounds")


def whole(shape):
    return pl.BlockSpec(tuple(shape), lambda step: (0,) * len(shape))


def whole_specs(*arrays):
    return [whole(array.shape) for array in arrays]


def collect_kernel(
    positions_ref, types_ref, count_ref, send_ref, own_ref, outgoing_ref
):
    atoms = types_ref.shape[1]
    own_ref[...] = jnp.zeros_like(own_ref)
    for axis in range(3):
        own_ref[axis : axis + 1, 0:atoms] = positions_ref[axis]
    own_ref[3:4, 0:atoms] = types_ref[...].astype(jnp.float32)
    own_ref[4:5, 0:atoms] = count_ref[...].astype(jnp.float32)
    own_ref[5:6, 0:atoms] = send_ref[...].astype(jnp.float32)
    for chunk in range(2):
        lanes = slice(128 * chunk, 128 * chunk + 128)
        wanted = jnp.broadcast_to(own_ref[5:6, lanes], (8, 128)).astype(jnp.int32)
        within = wanted & 127
        outgoing_ref[:, lanes] = jnp.where(
            wanted < 128,
            lane_pick(own_ref[:, 0:128], within),
            lane_pick(own_ref[:, 128:256], within),
        )


def collect(positions, types, counts, send_index):
    arrays = (positions, types, counts, send_index)
    result = jax.ShapeDtypeStruct((8, 256), jnp.float32)
    return pl.pallas_call(
        collect_kernel,
        grid=(1,),
        out_shape=[result, result],
        in_specs=whole_specs(*arrays),
        out_specs=whole_specs(result, result),
        compiler_params=pltpu.CompilerParams(vmem_limit_bytes=VMEM_BYTES),
        name="collect_atoms",
    )(*arrays)


def fitting_rows(descriptor_ref, weight_in_ref, weight_hidden_ref, weight_out_ref):
    hidden = jnp.tanh(product(descriptor_ref[...], weight_in_ref[...], LANES))
    for layer in range(weight_hidden_ref.shape[0]):
        hidden = jnp.tanh(product(hidden, weight_hidden_ref[layer])) + hidden
    width = hidden.shape[1]
    return product(jnp.broadcast_to(weight_out_ref[...], (8, width)), hidden, LANES)


def natural_order(rows):
    atoms = rows.shape[1]
    padded = jnp.concatenate([rows, jnp.zeros((8, 256 - atoms), jnp.float32)], axis=1)
    pieces = []
    for chunk in range(2):
        atom = 128 * chunk + lax.broadcasted_iota(jnp.int32, (8, 128), 1)
        late = atom >= atoms // 2
        within = jnp.where(late, atom - atoms // 2, atom)
        place = 8 * (within >> 2) + (within & 3) + jnp.where(late, 4, 0)
        place = jnp.minimum(place, 255)
        pieces.append(
            jnp.where(
                place < 128,
                lane_pick(padded[:, 0:128], place & 127),
                lane_pick(padded[:, 128:256], place & 127),
            )
        )
    return jnp.concatenate(pieces, axis=1)[0:1, 0:atoms]


def network_kernel(
    ghosts,
    base_ref,
    charges_ref,
    own_ref,
    lower_ref,
    upper_ref,
    slots_ref,
    types_ref,
    cell_x_ref,
    cell_y_ref,
    cell_z_ref,
    fraction_ref,
    first_ref,
    second_ref,
    third_ref,
    spot_ref,
    weight_in_hbm,
    weight_hidden_hbm,
    weight_out_ref,
    descriptor_hbm,
    charge_ref,
    copies_ref,
    descriptor_ref,
    environment_ref,
    kind_ref,
    moments_ref,
    padded_ref,
    weight_in_ref,
    weight_hidden_ref,
    semaphores,
):
    fetches = [
        pltpu.make_async_copy(weight_in_hbm, weight_in_ref, semaphores.at[0]),
        pltpu.make_async_copy(weight_hidden_hbm, weight_hidden_ref, semaphores.at[1]),
    ]
    for fetch in fetches:
        fetch.start()
    slots, atoms = slots_ref.shape
    rows = atoms // 2
    lane = lax.broadcasted_iota(jnp.int32, (8, 128), 1)
    sub = lax.broadcasted_iota(jnp.int32, (8, 128), 0)

    width = first_ref.shape[1]
    padded_ref[...] = jnp.zeros_like(padded_ref)
    padded_ref[0, 0:2, 0:width] = first_ref[...]
    for column in range(2):
        padded_ref[1, 0:width, 32 * column : 32 * column + width] = second_ref[
            :, width * column : width * (column + 1)
        ]
    for row in range(2):
        for column in range(4):
            padded_ref[2, 32 * row : 32 * row + width, 32 * column : 32 * column + width] = (
                third_ref[
                    width * row : width * (row + 1), width * column : width * (column + 1)
                ]
            )
    first_table = padded_ref[0].T
    embed_zero = jnp.broadcast_to(first_table[0:32, 0:1], (32, 128))
    embed_one = jnp.broadcast_to(first_table[0:32, 1:2], (32, 128))
    second_high, second_low = split(padded_ref[1].T[0:64, 0:32])
    second_weight = jnp.concatenate([second_high, second_high, second_low], axis=1)
    third_high, third_low = split(padded_ref[2].T[:, 0:64])
    third_weight = jnp.concatenate([third_high, third_high, third_low], axis=1)

    def spread(ref, field, chunk):
        return jnp.broadcast_to(ref[field : field + 1, 128 * chunk : 128 * chunk + 128], (8, 128))

    own = [[spread(own_ref, field, chunk) for chunk in range(2)] for field in range(5)]
    lower = [[spread(lower_ref, field, chunk) for chunk in range(2)] for field in range(4)]
    upper = [spread(upper_ref, field, 0) for field in range(4)]

    def pick_two(tables, index):
        within = index & 127
        return jnp.where(index < 128, lane_pick(tables[0], within), lane_pick(tables[1], within))

    pairs = jnp.concatenate([slots_ref[:, 0:rows], slots_ref[:, rows:atoms]], axis=0).T
    for tile in range(rows // 8):
        band = slice(8 * tile, 8 * tile + 8)
        index = pairs[band, :]
        centre = 8 * tile + sub + jnp.where(lane < 64, 0, rows)
        from_own = jnp.clip(index - ghosts, 0, atoms - 1)
        from_lower = jnp.minimum(index + (atoms - ghosts), 255)
        from_upper = jnp.clip(index - (ghosts + atoms), 0, 127)

        def neighbour(field):
            below = pick_two(lower[field], from_lower)
            inside = pick_two(own[field], from_own)
            above = lane_pick(upper[field], from_upper)
            return jnp.where(
                index < ghosts, below, jnp.where(index < ghosts + atoms, inside, above)
            )

        offsets = [neighbour(field) - pick_two(own[field], centre) for field in range(3)]
        live = pick_two(own[4], centre)
        present = jnp.where((lane & 63).astype(jnp.float32) < live, 1.0, 0.0)
        smooth = present / (
            1.0 + (offsets[0] * offsets[0] + offsets[1] * offsets[1] + offsets[2] * offsets[2])
        )
        environment_ref[0, band, :] = smooth
        for field in range(3):
            environment_ref[1 + field, band, :] = smooth * offsets[field]
        kind_ref[band, :] = neighbour(3)

    group = 8

    def stacked(values):
        high, low = split(values)
        return jnp.concatenate([high, low, high], axis=0)

    def one_group(start):
        pieces = []
        for row in range(group):
            smooth = jnp.broadcast_to(environment_ref[0, pl.ds(start + row, 1), :], (32, 128))
            kind = jnp.broadcast_to(kind_ref[pl.ds(start + row, 1), :], (32, 128))
            pieces.append(
                jnp.tanh(smooth * ((1.0 - kind) * embed_zero + kind * embed_one))
            )
        first = jnp.concatenate(pieces, axis=1)
        second = jnp.tanh(multiply(second_weight, stacked(first), ((1,), (0,))))
        second = second + jnp.concatenate([first, first], axis=0)
        third = jnp.tanh(multiply(third_weight, stacked(second), ((1,), (0,))))
        third = third + jnp.concatenate([second, second], axis=0)
        third_pair = split(third)
        for half in range(group // 4):
            columns = slice(512 * half, 512 * half + 512)
            bands = []
            for part in range(4):
                bands.append(
                    jnp.concatenate(
                        [
                            jnp.where(
                                sub == row + jnp.where(lane < 64, 0, 4),
                                jnp.broadcast_to(
                                    environment_ref[part, pl.ds(start + 4 * half + row, 1), :],
                                    (8, 128),
                                ),
                                0.0,
                            )
                            for row in range(4)
                        ],
                        axis=1,
                    )
                )
            environment = split(jnp.concatenate(bands, axis=0))
            both = multiply(
                jnp.concatenate(environment, axis=0), third_pair[0][:, columns], LANES
            )
            sums = both[0:32] + both[32:64]
            sums = sums + multiply(environment[0], third_pair[1][:, columns], LANES)
            sums = sums * (1.0 / slots)
            for part in range(4):
                moments_ref[part, pl.ds(2 * start + 8 * half, 8), :] = sums[
                    8 * part : 8 * part + 8
                ]

    def body(step, carry):
        for part in range(unroll):
            one_group(pl.multiple_of(step * unroll * group + part * group, group))
        return carry

    unroll = 4 if rows % (4 * group) == 0 else 1
    lax.fori_loop(0, rows // (unroll * group), body, 0)

    chunks = (descriptor_ref.shape[1] + 127) // 128
    last = descriptor_ref.shape[1] - 128 * (chunks - 1)

    def describe_band(start):
        band = pl.ds(start, 8)
        moments = [moments_ref[part, band, :] for part in range(4)]
        axis_part = [lane_pick(moments[part], lane & 15) for part in range(4)]
        for chunk in range(chunks):
            spot = jnp.broadcast_to(spot_ref[chunk : chunk + 1, :], (8, 128))
            total = lane_pick(moments[0], spot) * axis_part[0]
            for part in range(1, 4):
                total = total + lane_pick(moments[part], spot) * axis_part[part]
            if chunk < chunks - 1:
                descriptor_ref[band, 128 * chunk : 128 * chunk + 128] = total
            else:
                descriptor_ref[band, 128 * chunk : 128 * chunk + last] = total[:, 0:last]

    bands = 4 if atoms % 32 == 0 else 1

    def describe(step, carry):
        for part in range(bands):
            describe_band(pl.multiple_of(step * 8 * bands + 8 * part, 8))
        return carry

    lax.fori_loop(0, atoms // (8 * bands), describe, 0)

    store = pltpu.make_async_copy(descriptor_ref, descriptor_hbm, semaphores.at[2])
    store.start()
    for fetch in fetches:
        fetch.wait()
    shift = fitting_rows(descriptor_ref, weight_in_ref, weight_hidden_ref, weight_out_ref)
    kind = types_ref[...].astype(jnp.float32)
    charge = (1.0 - kind) * charges_ref[0] + kind * charges_ref[1] + natural_order(shift)
    charge_ref[...] = charge
    fields = jnp.concatenate(
        [
            cell_x_ref[...].astype(jnp.float32),
            (cell_y_ref[...] + base_ref[0]).astype(jnp.float32),
            cell_z_ref[...].astype(jnp.float32),
        ]
        + [fraction_ref[axis] for axis in range(3)]
        + [charge, jnp.zeros((1, atoms), jnp.float32)],
        axis=0,
    )
    for copy in range(copies_ref.shape[0]):
        copies_ref[copy] = fields
    store.wait()


def spot_table(embed, desc):
    column = np.arange(desc) // AXIS
    quarter = embed // 4
    place = 32 * (column // quarter) + column % quarter
    chunks = (desc + 127) // 128
    table = np.zeros((chunks * 128,), np.int32)
    table[:desc] = place
    padded = np.zeros(((chunks + 7) // 8 * 8, 128), np.int32)
    padded[:chunks] = table.reshape(chunks, 128)
    return padded


def networks(
    copies,
    ghosts,
    base,
    charge_base,
    own,
    lower,
    upper,
    neighbours,
    types,
    cells,
    fraction,
    embed,
    weight_in,
    weight_hidden,
    weight_out,
):
    atoms = types.shape[1]
    desc, width = weight_in.shape
    spots = jnp.asarray(spot_table(embed[2].shape[1], desc))
    anywhere = pl.BlockSpec(memory_space=pl.ANY)
    scalars = pl.BlockSpec(memory_space=pltpu.SMEM)
    blocks = (own, lower, upper, neighbours[0].T, types, *cells, fraction, *embed, spots)
    weight_out = weight_out.reshape(1, -1)
    results = [
        jax.ShapeDtypeStruct((atoms, desc), jnp.float32),
        jax.ShapeDtypeStruct((1, atoms), jnp.float32),
        jax.ShapeDtypeStruct((copies, 8, atoms), jnp.float32),
    ]
    return pl.pallas_call(
        functools.partial(network_kernel, ghosts),
        grid=(1,),
        out_shape=results,
        in_specs=[scalars, scalars]
        + whole_specs(*blocks)
        + [anywhere, anywhere]
        + whole_specs(weight_out),
        out_specs=[anywhere] + whole_specs(*results[1:]),
        scratch_shapes=[
            pltpu.VMEM((atoms, desc), jnp.float32),
            pltpu.VMEM((4, atoms // 2, 128), jnp.float32),
            pltpu.VMEM((atoms // 2, 128), jnp.float32),
            pltpu.VMEM((4, atoms, 128), jnp.float32),
            pltpu.VMEM((3, 128, 128), jnp.float32),
            pltpu.VMEM((width, desc), jnp.float32),
            pltpu.VMEM(weight_hidden.shape, jnp.float32),
            pltpu.SemaphoreType.DMA((3,)),
        ],
        compiler_params=pltpu.CompilerParams(vmem_limit_bytes=VMEM_BYTES),
        name="networks",
    )(base, charge_base, *blocks, weight_in.T, weight_hidden, weight_out)


def energy_kernel(descriptor_ref, weight_in_ref, weight_hidden_ref, weight_out_ref, energy_ref):
    energy_ref[...] = natural_order(
        fitting_rows(descriptor_ref, weight_in_ref, weight_hidden_ref, weight_out_ref)
    )


def energies(descriptor, weight_in, weight_hidden, weight_out):
    atoms, desc = descriptor.shape
    width = weight_in.shape[1]
    arrays = (descriptor, weight_in.T, weight_hidden, weight_out.reshape(1, -1))
    result = jax.ShapeDtypeStruct((1, atoms), jnp.float32)
    return pl.pallas_call(
        energy_kernel,
        grid=(1,),
        out_shape=result,
        in_specs=whole_specs(*arrays),
        out_specs=whole(result.shape),
        compiler_params=pltpu.CompilerParams(vmem_limit_bytes=VMEM_BYTES),
        cost_estimate=pl.CostEstimate(
            flops=6 * atoms * desc * width, bytes_accessed=4 * desc * width, transcendentals=0
        ),
        name="energies",
    )(*arrays)


def weight_rows(fraction):
    square = fraction * fraction
    cubed = square * fraction
    rest = 1.0 - fraction
    return [
        rest * rest * rest / 6.0,
        (3.0 * cubed - 6.0 * square + 4.0) / 6.0,
        (-3.0 * cubed + 3.0 * square + 3.0 * fraction + 1.0) / 6.0,
        cubed / 6.0,
    ]


def placed_weights(distance, weights):
    shape = distance.shape
    result = jnp.zeros(shape, jnp.float32)
    for step in range(4):
        result = jnp.where(
            distance == step, jnp.broadcast_to(weights[step], shape), result
        )
    return result


def third_factors(fields, waves_ref, cosine_ref):
    atoms = fields.shape[1]
    start = fields[2:3, :].astype(jnp.int32)
    along = weight_rows(fields[5:6, :])
    parts = waves_ref.shape[0]
    cosine = jnp.broadcast_to(cosine_ref[...], (parts, 128))
    wave = jnp.broadcast_to(waves_ref[:, 0:1], (parts, 128))
    shift = jnp.broadcast_to(waves_ref[:, 1:2], (parts, 128))
    pieces = []
    for chunk in range(atoms // 128):
        lanes = slice(128 * chunk, 128 * chunk + 128)
        total = jnp.zeros((parts, 128), jnp.float32)
        for step in range(4):
            place = jnp.broadcast_to(start[:, lanes] + step, (parts, 128))
            phase = (wave * place + shift) & (NG - 1)
            value = lane_pick(cosine, phase & 127)
            value = jnp.where(phase < 128, value, -value)
            total = total + value * jnp.broadcast_to(along[step][:, lanes], (parts, 128))
        pieces.append(total)
    return jnp.concatenate(pieces, axis=1)


def first_third_split(fields, waves_ref, cosine_ref, window, scale, high_ref, low_ref):
    atoms = fields.shape[1]
    third = third_factors(fields, waves_ref, cosine_ref) * scale
    rows = lax.broadcasted_iota(jnp.int32, (window, atoms), 0)
    first = placed_weights(
        rows - fields[0:1, :].astype(jnp.int32), weight_rows(fields[3:4, :])
    )
    for chunk in range(atoms // 128):
        lanes = slice(128 * chunk, 128 * (chunk + 1))
        for part in range(0, third.shape[0], 2):
            high, low = split(
                jnp.concatenate(
                    [first[:, lanes] * third[part + side : part + side + 1, lanes] for side in range(2)],
                    axis=0,
                )
            )
            place = slice(part * window, (part + 2) * window)
            high_ref[place, lanes] = high
            low_ref[place, lanes] = low
    return high_ref[...], low_ref[...]


def second_factors(fields, base, block_y, slabs, high_ref, low_ref):
    atoms = fields.shape[1]
    block = atoms // slabs
    reach = block_y + REACH
    start = fields[1:2, :].astype(jnp.int32) - base
    weights = weight_rows(fields[4:5, :])
    for chunk in range(atoms // 128):
        lanes = slice(128 * chunk, 128 * (chunk + 1))
        first = 128 * chunk // block
        last = (128 * chunk + 127) // block
        top = first * block_y
        rows = (last - first) * block_y + reach
        pieces = [(top, min(rows, NG - top))]
        if top + rows > NG:
            pieces.append((0, top + rows - NG))
        for row, count in pieces:
            index = row + lax.broadcasted_iota(jnp.int32, (count, 128), 0)
            table = split(
                placed_weights(
                    (index - start[:, lanes]) & (NG - 1), [weight[:, lanes] for weight in weights]
                )
            )
            high_ref[row : row + count, lanes] = table[0]
            low_ref[row : row + count, lanes] = table[1]
    return high_ref[...], low_ref[...]


def wave_of(index):
    return jnp.where(index <= NG // 2, index, index - NG // 2)


def damping(index):
    kappa = wave_of(index).astype(jnp.float32) * (2.0 * math.pi / NG)
    squared = kappa * kappa
    ends = (index == 0) | (index == NG // 2)
    return squared, jnp.exp(-0.5 * squared) * jnp.where(ends, 1.0 / NG, 2.0 / NG)


def transform(planes, kappa_ref, first_part, tables_ref, last_ref):
    count = len(planes)
    basis = tables_ref[0]
    turned = tables_ref[1]
    square_x, damp_x = damping(lax.broadcasted_iota(jnp.int32, (NG, 1), 0))
    square_y, damp_y = damping(lax.broadcasted_iota(jnp.int32, (1, NG), 1))
    square_xy = square_x + square_y
    damp_xy = damp_x * damp_y
    bands = [slice(NG * part, NG * (part + 1)) for part in range(count)]

    def flip(values):
        return jnp.concatenate([values[band].T for band in bands], axis=0)

    both = product(flip(product(jnp.concatenate(planes, axis=0), turned)), turned)
    scaled = []
    for part in range(count):
        squared = square_xy + kappa_ref[first_part + part, 0]
        root = jnp.where(squared == 0.0, 1.0, 0.0)
        green = (1.0 - root) * (damp_xy * kappa_ref[first_part + part, 1]) / (squared + root)
        scaled.append(both[bands[part]] * green)
    return product(flip(product(jnp.concatenate(scaled, axis=0), basis)), last_ref[...])


def send_blocks(full, block_x, block_y, put):
    low_lanes = lax.broadcasted_iota(jnp.int32, (NG, 128), 1) < block_y
    for pair in range(full.shape[0] // (2 * NG)):
        even = full[2 * NG * pair : 2 * NG * pair + NG, 0:128]
        odd = full[2 * NG * pair + NG : 2 * NG * (pair + 1), 0:128]
        blocks = [
            jnp.where(low_lanes, even, pltpu.roll(odd, block_y, 1)),
            jnp.where(low_lanes, pltpu.roll(even, block_y, 1), odd),
        ]
        for brick in range(NG // block_x):
            for side in range(2):
                for group in range(block_x // 8):
                    start = block_x * brick + 8 * group
                    put(pair, brick, side, group, blocks[side][start : start + 8])


def spread_kernel(
    block_x,
    block_y,
    window,
    kappa_ref,
    pair_ref,
    static_ref,
    waves_ref,
    cosine_ref,
    tables_hbm,
    last_hbm,
    sent_ref,
    full_ref,
    atoms_ref,
    later_hbm,
    grid_ref,
    tables_ref,
    last_ref,
    semaphores,
    *pair_refs,
):
    slabs = NG // block_y
    second_refs, first_refs = pair_refs[:4], pair_refs[4:]
    bricks = NG // block_x
    parts = waves_ref.shape[0]
    block = static_ref.shape[2]
    count = full_ref.shape[0]
    step = pl.program_id(0)
    later = later_hbm.shape[0]
    store = pltpu.make_async_copy(
        grid_ref.at[pl.ds(parts - later, later), pl.ds(0, NG)], later_hbm, semaphores.at[2]
    )

    @pl.when(step == 0)
    def _():
        fetches = [
            pltpu.make_async_copy(tables_hbm, tables_ref, semaphores.at[0]),
            pltpu.make_async_copy(last_hbm.at[pair_ref[0]], last_ref, semaphores.at[1]),
        ]
        for fetch in fetches:
            fetch.start()
        for slab in range(slabs):
            lanes = slice(block * slab, block * (slab + 1))
            for brick in range(bricks):
                atoms_ref[brick, :, lanes] = static_ref[slab * bricks + brick]
        grid_ref[...] = jnp.zeros_like(grid_ref)
        for ref in second_refs:
            ref[...] = jnp.zeros_like(ref)
        for brick in range(bricks):
            fields = atoms_ref[brick]
            table = first_third_split(
                fields,
                waves_ref,
                cosine_ref,
                window,
                fields[6:7, :],
                first_refs[2 * (brick % 2)],
                first_refs[2 * (brick % 2) + 1],
            )
            second = second_factors(
                fields, 0, block_y, slabs, second_refs[2 * (brick % 2)], second_refs[2 * (brick % 2) + 1]
            )
            spread = triple(table, second, LANES)
            rows = slice(block_x * brick, block_x * brick + window)
            for part in range(parts):
                grid_ref[part, rows, :] += spread[part * window : part * window + window]
        extra = window - block_x
        for part in range(parts):
            grid_ref[part, 0:extra, :] += grid_ref[part, NG : NG + extra, :]
        store.start()
        for fetch in fetches:
            fetch.wait()

    planes = [grid_ref[count * step + part, 0:NG, :] for part in range(count)]
    full = transform(planes, kappa_ref, count * step, tables_ref, last_ref)
    for part in range(count):
        full_ref[part] = full[NG * part : NG * (part + 1)]

    def put(pair, brick, side, group, tile):
        sent_ref[2 * brick + side, group, pair] = tile

    send_blocks(full, block_x, block_y, put)

    @pl.when(step == pl.num_programs(0) - 1)
    def _():
        store.wait()


def early_pairs(parts):
    return parts // 4


def spread_and_solve(
    block_x, block_y, window, kappa, pair, static, waves, cosine_row, tables, last
):
    devices, _, atoms = static.shape
    slabs = NG // block_y
    bricks = NG // block_x
    parts = waves.shape[0]
    pairs = early_pairs(parts)
    count = 4
    anywhere = pl.BlockSpec(memory_space=pl.ANY)
    scalars = pl.BlockSpec(memory_space=pltpu.SMEM)
    sent_block = (2 * bricks, block_x // 8, count // 2, 8, 128)
    return pl.pallas_call(
        functools.partial(spread_kernel, block_x, block_y, window),
        grid=(2 * pairs // count,),
        out_shape=[
            jax.ShapeDtypeStruct((2 * bricks, block_x // 8, pairs, 8, 128), jnp.float32),
            jax.ShapeDtypeStruct((2 * pairs, NG, NG), jnp.float32),
            jax.ShapeDtypeStruct((bricks, 8, slabs * atoms), jnp.float32),
            jax.ShapeDtypeStruct((parts - 2 * pairs, NG, NG), jnp.float32),
        ],
        in_specs=[scalars, scalars]
        + whole_specs(static, waves, cosine_row)
        + [anywhere, anywhere],
        out_specs=[
            pl.BlockSpec(sent_block, lambda step: (0, 0, step, 0, 0)),
            pl.BlockSpec((count, NG, NG), lambda step: (step, 0, 0)),
            whole((bricks, 8, slabs * atoms)),
            anywhere,
        ],
        scratch_shapes=[
            pltpu.VMEM((parts, NG + window - block_x, NG), jnp.float32),
            pltpu.VMEM(tables.shape, tables.dtype),
            pltpu.VMEM(last.shape[1:], last.dtype),
            pltpu.SemaphoreType.DMA((3,)),
        ]
        + [pltpu.VMEM((NG, slabs * atoms), jnp.bfloat16)] * 4
        + [pltpu.VMEM((parts * window, slabs * atoms), jnp.bfloat16)] * 4,
        compiler_params=pltpu.CompilerParams(vmem_limit_bytes=VMEM_BYTES),
        name="spread_and_solve",
    )(kappa, pair, static, waves, cosine_row, tables, last)


def sample_kernel(
    block_x,
    block_y,
    window,
    kappa_ref,
    pair_ref,
    atoms_ref,
    waves_ref,
    cosine_ref,
    tables_hbm,
    last_hbm,
    later_hbm,
    early_hbm,
    sent_ref,
    later_ref,
    full_ref,
    tables_ref,
    last_ref,
    semaphores,
    packed_ref,
):
    bricks = atoms_ref.shape[0]
    parts = waves_ref.shape[0]
    early = 2 * early_pairs(parts)
    block = atoms_ref.shape[2] * block_y // NG
    fetches = [
        pltpu.make_async_copy(tables_hbm, tables_ref, semaphores.at[0]),
        pltpu.make_async_copy(last_hbm.at[pair_ref[0]], last_ref, semaphores.at[1]),
        pltpu.make_async_copy(later_hbm, later_ref, semaphores.at[2]),
        pltpu.make_async_copy(early_hbm, full_ref.at[pl.ds(0, early)], semaphores.at[3]),
    ]
    for fetch in fetches:
        fetch.start()
    for fetch in fetches[:3]:
        fetch.wait()
    pairs = (parts - early) // 2
    planes = [later_ref[part] for part in range(parts - early)]
    full = transform(planes, kappa_ref, early, tables_ref, last_ref)
    for part in range(parts - early):
        full_ref[early + part] = full[NG * part : NG * (part + 1)]

    def put(pair, brick, side, group, tile):
        sent_ref[2 * brick + side, pairs * group + pair] = tile

    send_blocks(full, block_x, block_y, put)
    fetches[3].wait()

    reach = block_y + REACH
    lane = lax.broadcasted_iota(jnp.int32, (NG, 128), 1)
    for part in range(parts):
        for side in range(2):
            values = full_ref[part, :, 128 * side : 128 * (side + 1)]
            high = values.astype(jnp.bfloat16).astype(jnp.float32)
            again = pltpu.roll(high, reach, 1)
            low = pltpu.roll(values - high, 2 * reach - 128, 1)
            packed_ref[side, part, 0:NG, 0:128] = jnp.where(lane < reach, high, again)
            packed_ref[side, part, 0:NG, 128:NG] = jnp.where(
                lane < 2 * reach - 128, again, jnp.where(lane < 3 * reach - 128, low, 0.0)
            )
            packed_ref[side, part, NG : NG + window - block_x, :] = packed_ref[
                side, part, 0 : window - block_x, :
            ]
    extra = sent_ref.shape[1] - 1
    base = 2 * block_y * pair_ref[0]
    lanes = pl.ds(pl.multiple_of(2 * block * pair_ref[0], 128), 2 * block)
    for brick in range(bricks):
        fields = atoms_ref[brick, :, lanes]
        thirds = third_factors(fields, waves_ref, cosine_ref)
        rows = slice(block_x * brick, block_x * brick + window)
        for side in range(2):
            here = slice(block * side, block * (side + 1))
            third = thirds[:, here]
            ours = fields[:, here]
            index = lax.broadcasted_iota(jnp.int32, (window, block), 0)
            first = placed_weights(
                index - ours[0:1, :].astype(jnp.int32), weight_rows(ours[3:4, :])
            )
            index = lax.broadcasted_iota(jnp.int32, (reach, block), 0)
            start = ours[1:2, :].astype(jnp.int32) - (base + block_y * side)
            high, low = split(placed_weights(index - start, weight_rows(ours[4:5, :])))
            rest = jnp.zeros((NG - 3 * reach, block), jnp.bfloat16)
            second = jnp.concatenate([high, low, high, rest], axis=0)
            values = jnp.concatenate(
                [packed_ref[side, part, rows, :] for part in range(parts)], axis=0
            )
            along = multiply(values.astype(jnp.bfloat16), second, ((1,), (0,)))
            total = jnp.zeros((window, block), jnp.float32)
            for part in range(parts):
                total = total + along[window * part : window * (part + 1)] * third[part : part + 1]
            row = jnp.sum(total * first, axis=0, keepdims=True)
            sent_ref[2 * brick + side, extra] = jnp.zeros((8, 128), jnp.float32)
            sent_ref[2 * brick + side, extra, 0:1, :] = row[:, 0:128]
            sent_ref[2 * brick + side, extra, 1:2, 0 : block - 128] = row[:, 128:block]


def solve_and_sample(
    block_x, block_y, window, kappa, pair, atoms, waves, cosine_row, tables, last, later, early
):
    bricks = atoms.shape[0]
    parts = waves.shape[0]
    pairs = parts // 2 - early_pairs(parts)
    anywhere = pl.BlockSpec(memory_space=pl.ANY)
    scalars = pl.BlockSpec(memory_space=pltpu.SMEM)
    result = jax.ShapeDtypeStruct((2 * bricks, block_x // 8 * pairs + 1, 8, 128), jnp.float32)
    return pl.pallas_call(
        functools.partial(sample_kernel, block_x, block_y, window),
        grid=(1,),
        out_shape=result,
        in_specs=[scalars, scalars] + whole_specs(atoms, waves, cosine_row) + [anywhere] * 4,
        out_specs=whole(result.shape),
        scratch_shapes=[
            pltpu.VMEM((2 * pairs, NG, NG), jnp.float32),
            pltpu.VMEM((parts, NG, NG), jnp.float32),
            pltpu.VMEM(tables.shape, tables.dtype),
            pltpu.VMEM(last.shape[1:], last.dtype),
            pltpu.SemaphoreType.DMA((4,)),
        ]
        + [pltpu.VMEM((2, parts, NG + window - block_x, NG), jnp.float32)],
        compiler_params=pltpu.CompilerParams(vmem_limit_bytes=VMEM_BYTES),
        cost_estimate=pl.CostEstimate(
            flops=24 * parts * NG * NG * NG, bytes_accessed=4 * early.size, transcendentals=0
        ),
        name="solve_and_sample",
    )(kappa, pair, atoms, waves, cosine_row, tables, last, later, early)


def finish_kernel(
    block_y, early_ref, later_ref, sums_ref, short_ref, charge_ref, table_ref, out_ref, energy_ref
):
    atoms = short_ref.shape[1]
    lines = early_ref.shape[3]
    sources, _, pairs = early_ref.shape[:3]
    early = early_ref.reshape(sources * pairs, lines, 128)
    later = later_ref.reshape(sources * later_ref.shape[1], lines, 128)
    pieces = []
    for line in range(lines):
        turned = jnp.concatenate([early[:, line, :], later[:, line, :]], axis=0).T
        pieces.append(jnp.concatenate([turned[0:block_y], turned[block_y:]], axis=1))
    result = product(jnp.concatenate(pieces, axis=0), table_ref[...])
    for line in range(lines):
        out_ref[line] = result[block_y * line : block_y * (line + 1)]

    @pl.when(pl.program_id(0) == 0)
    def _():
        total = jnp.sum(sums_ref[:, 0], axis=0)
        potential_at = jnp.concatenate([total[0:1, :], total[1:2, 0 : atoms - 128]], axis=1)
        energy_ref[...] = short_ref[...] + 0.5 * charge_ref[...] * potential_at


def finish(block_x, block_y, early, later, short, charge, table):
    bricks2, groups, pairs = early.shape[:3]
    rest = (later.shape[1] - 1) // groups
    atoms = short.shape[1]
    return pl.pallas_call(
        functools.partial(finish_kernel, block_y),
        grid=(groups,),
        out_shape=[
            jax.ShapeDtypeStruct((block_x, block_y, NG), jnp.float32),
            jax.ShapeDtypeStruct((1, atoms), jnp.float32),
        ],
        in_specs=[
            pl.BlockSpec((bricks2, 1, pairs, 8, 128), lambda index: (0, index, 0, 0, 0)),
            pl.BlockSpec((bricks2, rest, 8, 128), lambda index: (0, index, 0, 0)),
            pl.BlockSpec((bricks2, 1, 8, 128), lambda index: (0, groups * rest, 0, 0)),
            whole((1, atoms)),
            whole((1, atoms)),
            whole(table.shape),
        ],
        out_specs=[
            pl.BlockSpec((8, block_y, NG), lambda index: (index, 0, 0)),
            whole((1, atoms)),
        ],
        compiler_params=pltpu.CompilerParams(vmem_limit_bytes=32 * 2**20),
        name="finish",
    )(early, later, later, short, charge, table)


def real_basis():
    index = np.arange(NG)
    wave = np.where(index <= NG // 2, index, index - NG // 2)
    angle = (wave[:, None] * index[None, :] % NG) * (2.0 * math.pi / NG)
    return np.where((index <= NG // 2)[:, None], np.cos(angle), np.sin(angle))


def per_device(
    positions,
    types,
    neighbours,
    neighbour_count,
    send_index,
    cell_x,
    cell_y,
    cell_z,
    spline_fraction,
    embed_first,
    embed_second,
    embed_third,
    energy_in,
    energy_hidden,
    energy_out,
    wannier_in,
    wannier_hidden,
    wannier_out,
    charge_base,
):
    atoms = types.shape[1]
    ghosts = send_index.shape[1] // 2
    count_x = lax.axis_size("brick")
    count_y = lax.axis_size("slab")
    block_x = NG // count_x
    block_y = NG // count_y
    window = block_x + 8
    parts = NG // (2 * count_x)
    brick = lax.axis_index("brick")
    slab = lax.axis_index("slab")
    pair = (slab // 2).astype(jnp.int32).reshape(1)
    halves = [
        [b * count_y + 2 * p + side for b in range(count_x) for side in range(2)]
        for p in range(count_y // 2)
    ]

    def exchange(values, axes, groups=None):
        return lax.all_to_all(
            values, axes, split_axis=0, concat_axis=0, tiled=True, axis_index_groups=groups
        )

    own, outgoing = collect(positions, types, neighbour_count, send_index)
    up = [(i, (i + 1) % count_x) for i in range(count_x)]
    down = [((i + 1) % count_x, i) for i in range(count_x)]
    lower = lax.ppermute(outgoing, "brick", up)
    upper = lax.ppermute(outgoing, "brick", down)
    descriptor, charge, fields = networks(
        count_x * count_y,
        ghosts,
        (slab * block_y).astype(jnp.int32).reshape(1),
        charge_base,
        own,
        lower,
        upper,
        neighbours,
        types,
        (cell_x, cell_y, cell_z),
        spline_fraction,
        (embed_first, embed_second, embed_third),
        wannier_in,
        wannier_hidden,
        wannier_out,
    )
    every_field = exchange(fields, ("slab", "brick"))

    part = (2 * brick + slab % 2) * parts + jnp.arange(parts, dtype=jnp.int32)
    wave = wave_of(part)
    waves = jnp.stack([wave, jnp.where(part <= NG // 2, 0, 3 * NG // 4)], axis=1)
    kappa = wave.astype(jnp.float32) * (2.0 * math.pi / NG)
    squared = kappa * kappa
    ends = (part == 0) | (part == NG // 2)
    kappa = jnp.stack(
        [squared, jnp.exp(-0.5 * squared) * jnp.where(ends, 1.0 / NG, 2.0 / NG)], axis=1
    )
    basis = real_basis()
    tables = np.stack([basis, basis.T]).astype(np.float32)
    last = []
    for p in range(count_y // 2):
        points = np.concatenate(
            [np.arange(2 * block_y), block_y + np.arange(block_y + REACH)]
        )
        points = (2 * block_y * p + points) % NG
        columns = np.zeros((NG, NG))
        columns[:, : points.size] = basis[:, points]
        last.append(columns.astype(np.float32))
    cosine_row = np.cos(np.arange(128) * (2.0 * math.pi / NG)).astype(np.float32)[None]
    cosine_row = jnp.asarray(cosine_row)
    tables = jnp.asarray(tables)
    last = jnp.asarray(np.stack(last))
    early, full, every_atom, later = spread_and_solve(
        block_x, block_y, window, kappa, pair, every_field, waves, cosine_row, tables, last
    )

    def send(values):
        got = exchange(values.reshape(values.shape[0], -1, 128), ("brick", "slab"), halves)
        return got.reshape(values.shape)

    early = send(early)
    later = solve_and_sample(
        block_x,
        block_y,
        window,
        kappa,
        pair,
        every_atom,
        waves,
        cosine_row,
        tables,
        last,
        later,
        full,
    )
    later = send(later)
    energy_short = energies(descriptor, energy_in, energy_hidden, energy_out)
    source = np.arange(2 * count_x)[:, None] * parts
    pairs = 2 * np.arange(parts // 2)[None, :]
    order = np.concatenate(
        [
            (source + pairs[:, : early_pairs(parts)]).ravel(),
            (source + pairs[:, early_pairs(parts) :]).ravel(),
        ]
    )
    order = np.concatenate([order, order + 1])
    potential, atom_energy = finish(
        block_x,
        block_y,
        early,
        later,
        energy_short,
        charge,
        jnp.asarray(basis[order].astype(np.float32)),
    )
    return atom_energy, potential


def solution(mesh):
    placed = (
        P(None, "slab", "brick"),
        P("slab", "brick"),
        P("slab", "brick", None),
        P("slab", "brick"),
        P("slab", "brick"),
        P("slab", "brick"),
        P("slab", "brick"),
        P("slab", "brick"),
        P(None, "slab", "brick"),
    ) + (P(),) * 10
    bricks, slabs = mesh.shape["brick"], mesh.shape["slab"]
    fits = 2 * NG == 128 * slabs and NG % (32 * bricks) == 0
    return jax.shard_map(
        per_device if fits else per_device_general,
        mesh=mesh,
        in_specs=placed,
        out_specs=(P("slab", "brick"), P("brick", "slab", None)),
        check_vma=False,
    )
```

```python
import functools
import math

import jax
import jax.numpy as jnp
import numpy as np
from jax import lax
from jax.experimental import pallas as pl
from jax.experimental.pallas import tpu as pltpu
from jax.sharding import PartitionSpec as P

NG = 256
AXIS = 16
VMEM_BYTES = 60 * 2**20
REACH = 16


HIGH = lax.Precision.HIGHEST


def with_halo(cells, sides, width):
    for axis, dim in sides:
        count = lax.axis_size(axis)
        head = lax.slice_in_dim(cells, 0, width, axis=dim)
        tail = lax.slice_in_dim(cells, cells.shape[dim] - width, cells.shape[dim], axis=dim)
        cells = jnp.concatenate(
            [
                lax.ppermute(tail, axis, [(i, (i + 1) % count) for i in range(count)]),
                cells,
                lax.ppermute(head, axis, [((i + 1) % count, i) for i in range(count)]),
            ],
            axis=dim,
        )
    return cells


def spline_weights(fraction):
    cubed = fraction * fraction * fraction
    square = fraction * fraction
    return jnp.stack(
        [
            (1.0 - fraction) * (1.0 - fraction) * (1.0 - fraction) / 6.0,
            (3.0 * cubed - 6.0 * square + 4.0) / 6.0,
            (-3.0 * cubed + 3.0 * square + 3.0 * fraction + 1.0) / 6.0,
            cubed / 6.0,
        ]
    )


def fitting(descriptor, weight_in, weight_hidden, weight_out):
    hidden = jnp.tanh(jnp.dot(descriptor, weight_in, precision=HIGH))
    for depth_index in range(weight_hidden.shape[0]):
        hidden = jnp.tanh(jnp.dot(hidden, weight_hidden[depth_index], precision=HIGH)) + hidden
    return jnp.dot(hidden, weight_out, precision=HIGH)


def atom_terms(
    extended,
    neighbour_rows,
    neighbour_total,
    embed_first,
    embed_second,
    embed_third,
    energy_in,
    energy_hidden,
    energy_out,
    wannier_in,
    wannier_hidden,
    wannier_out,
):
    atom_count, slots = neighbour_rows.shape
    ghost_rows = (extended.shape[1] - atom_count) // 2
    block_size = 64
    blocks = atom_count // block_size
    present = (jnp.arange(slots, dtype=jnp.int32)[None, :] < neighbour_total[:, None]).astype(
        jnp.float32
    )
    centre_ids = (ghost_rows + jnp.arange(atom_count, dtype=jnp.int32)).reshape(blocks, block_size)
    second_weight = embed_second.T
    third_weight = embed_third.T

    def one_block(pieces):
        centre_rows, rows_block, present_block = pieces
        centre_block = extended[:3, centre_rows]
        gathered = extended[:, rows_block]
        offsets = gathered[:3] - centre_block[:, :, None]
        smooth = present_block / (1.0 + jnp.sum(offsets * offsets, axis=0))
        environment = jnp.stack(
            [smooth, smooth * offsets[0], smooth * offsets[1], smooth * offsets[2]], axis=0
        )
        kind = gathered[3][None]
        mixing = (1.0 - kind) * embed_first[0][:, None, None] + kind * embed_first[1][:, None, None]
        first = jnp.tanh(smooth[None] * mixing).reshape(embed_first.shape[1], block_size * slots)
        second = jnp.tanh(jnp.dot(second_weight, first, precision=HIGH)) + jnp.concatenate(
            [first, first], axis=0
        )
        third = jnp.tanh(jnp.dot(third_weight, second, precision=HIGH)) + jnp.concatenate(
            [second, second], axis=0
        )
        third_blocks = third.reshape(third.shape[0], block_size, slots)
        moments = jnp.einsum("kan,can->akc", third_blocks, environment, precision=HIGH) / slots
        descriptor = jnp.einsum("amc,akc->amk", moments, moments[:, :AXIS], precision=HIGH).reshape(
            block_size, -1
        )
        return (
            fitting(descriptor, energy_in, energy_hidden, energy_out),
            fitting(descriptor, wannier_in, wannier_hidden, wannier_out),
        )

    energy_short, charge_shift = lax.map(
        one_block,
        (
            centre_ids,
            neighbour_rows.reshape(blocks, block_size, slots),
            present.reshape(blocks, block_size, slots),
        ),
    )
    return (energy_short.reshape(atom_count), charge_shift.reshape(atom_count))


def green_table(first, second, third, size):

    def folded(index):
        return jnp.where(index < size // 2, index, index - size).astype(jnp.float32) * (
            2.0 * math.pi / size
        )

    kappa_x = folded(first)[:, None, None]
    kappa_y = folded(second)[None, :, None]
    kappa_z = folded(third)[None, None, :]
    squared = kappa_x * kappa_x + kappa_y * kappa_y + kappa_z * kappa_z
    root = (
        (first[:, None, None] == 0) & (second[None, :, None] == 0) & (third[None, None, :] == 0)
    ).astype(jnp.float32)
    return (1.0 - root) * jnp.exp(-0.5 * squared) / (squared + root)


def dft_tables(size):
    index = jnp.arange(size, dtype=jnp.int32)
    phase = (index[:, None] * index[None, :] % size).astype(jnp.float32) * (2.0 * math.pi / size)
    return (jnp.cos(phase), jnp.sin(phase))


def along(values, table, axis_index):
    result = jnp.tensordot(values, table, axes=([axis_index], [0]), precision=HIGH)
    return jnp.moveaxis(result, -1, axis_index)


def complex_transform(paired, axis_index, cosine, sine, inverse):
    real_part = paired[0]
    imag_part = paired[1]
    inner = axis_index - 1
    real_cos = along(real_part, cosine, inner)
    real_sin = along(real_part, sine, inner)
    imag_cos = along(imag_part, cosine, inner)
    imag_sin = along(imag_part, sine, inner)
    if inverse:
        return jnp.stack([real_cos - imag_sin, imag_cos + real_sin])
    return jnp.stack([real_cos + imag_sin, imag_cos - real_sin])


def fold_windows(values, axis_index, block, count):
    front = jnp.moveaxis(values, axis_index, 0)
    rest = front.shape[1:]
    windows = front.reshape((count, block + 3) + rest)
    main_part = windows[:, :block]
    carried = jnp.roll(windows[:, block:], 1, axis=0)
    main_part = main_part.at[:, :3].add(carried)
    return jnp.moveaxis(main_part.reshape((count * block,) + rest), 0, axis_index)


def make_windows(values, axis_index, block, count):
    front = jnp.moveaxis(values, axis_index, 0)
    rest = front.shape[1:]
    pieces = front.reshape((count, block) + rest)
    trailing = jnp.roll(pieces, -1, axis=0)[:, :3]
    windows = jnp.concatenate([pieces, trailing], axis=1)
    return jnp.moveaxis(windows.reshape((count * (block + 3),) + rest), 0, axis_index)


def spread_matrix(start, weights, width, wrap_size):
    offsets = jnp.arange(4, dtype=jnp.int32)[:, None, None]
    target = start[None, :, None] + offsets
    if wrap_size > 0:
        target = target % wrap_size
    hits = (target == jnp.arange(width, dtype=jnp.int32)[None, None, :]).astype(jnp.float32)
    return jnp.sum(weights[:, :, None] * hits, axis=0)


def per_device_general(
    positions,
    types,
    neighbours,
    neighbour_count,
    send_index,
    cell_x,
    cell_y,
    cell_z,
    spline_fraction,
    embed_first,
    embed_second,
    embed_third,
    energy_in,
    energy_hidden,
    energy_out,
    wannier_in,
    wannier_hidden,
    wannier_out,
    charge_base,
):
    atom_count = types.shape[1]
    ghost_rows = send_index.shape[1] // 2
    kind_float = types[0].astype(jnp.float32)
    own_atoms = jnp.concatenate([positions[:, 0], kind_float[None]], axis=0)
    outgoing = own_atoms[:, send_index[0]]
    padded_ghosts = with_halo(outgoing, (("brick", 1),), ghost_rows)
    extended = jnp.concatenate(
        [padded_ghosts[:, :ghost_rows], own_atoms, padded_ghosts[:, 3 * ghost_rows :]], axis=1
    )
    energy_short, charge_shift = atom_terms(
        extended,
        neighbours[0],
        neighbour_count[0],
        embed_first,
        embed_second,
        embed_third,
        energy_in,
        energy_hidden,
        energy_out,
        wannier_in,
        wannier_hidden,
        wannier_out,
    )
    charge = (1.0 - kind_float) * charge_base[0] + kind_float * charge_base[1] + charge_shift
    count_x = lax.axis_size("brick")
    count_y = lax.axis_size("slab")
    block_x = NG // count_x
    block_y = NG // count_y
    wide_x = block_x + 3
    wide_y = block_y + 3
    spread_x = spread_matrix(cell_x[0], spline_weights(spline_fraction[0, 0]), wide_x, 0)
    spread_y = spread_matrix(cell_y[0], spline_weights(spline_fraction[1, 0]), wide_y, 0)
    spread_z = spread_matrix(cell_z[0], spline_weights(spline_fraction[2, 0]), NG, NG)
    spread_xy = (spread_x[:, :, None] * spread_y[:, None, :]).reshape(atom_count, wide_x * wide_y)
    charge_grid = jnp.einsum(
        "ap,az->pz", spread_xy, charge[:, None] * spread_z, precision=HIGH
    ).reshape(wide_x, wide_y, NG)
    cosine, sine = dft_tables(NG)
    scale = 1.0 / (NG * NG * NG)
    full_index = jnp.arange(NG, dtype=jnp.int32)
    paired = jnp.stack([along(charge_grid, cosine, 2), -along(charge_grid, sine, 2)])
    moved = lax.all_to_all(paired, "slab", split_axis=3, concat_axis=2, tiled=True)
    moved = complex_transform(fold_windows(moved, 2, block_y, count_y), 2, cosine, sine, False)
    moved = lax.all_to_all(moved, "brick", split_axis=2, concat_axis=1, tiled=True)
    moved = complex_transform(fold_windows(moved, 1, block_x, count_x), 1, cosine, sine, False)
    part_y = NG // count_x
    part_z = NG // count_y
    index_y = lax.axis_index("brick") * part_y + jnp.arange(part_y, dtype=jnp.int32)
    index_z = lax.axis_index("slab") * part_z + jnp.arange(part_z, dtype=jnp.int32)
    moved = moved * (green_table(full_index, index_y, index_z, NG) * scale)[None]
    moved = make_windows(complex_transform(moved, 1, cosine, sine, True), 1, block_x, count_x)
    moved = lax.all_to_all(moved, "brick", split_axis=1, concat_axis=2, tiled=True)
    moved = make_windows(complex_transform(moved, 2, cosine, sine, True), 2, block_y, count_y)
    moved = lax.all_to_all(moved, "slab", split_axis=2, concat_axis=3, tiled=True)
    potential_wide = along(moved[0], cosine, 2) - along(moved[1], sine, 2)
    sampled = jnp.einsum(
        "ap,pz->az", spread_xy, potential_wide.reshape(wide_x * wide_y, NG), precision=HIGH
    )
    potential_at = jnp.sum(sampled * spread_z, axis=1)
    atom_energy = energy_short + 0.5 * charge * potential_at
    return (atom_energy[None, :], potential_wide[:block_x, :block_y])


def split(values):
    high = values.astype(jnp.bfloat16)
    low = (values - high.astype(jnp.float32)).astype(jnp.bfloat16)
    return high, low


def multiply(left, right, dims):
    return lax.dot_general(left, right, (dims, ((), ())), preferred_element_type=jnp.float32)


def triple(left, right, dims=((1,), (0,))):
    (left_axis,), (right_axis,) = dims
    if left[0].shape[left_axis] % 128 == 0:
        return multiply(
            jnp.concatenate([left[0], left[0], left[1]], axis=left_axis),
            jnp.concatenate([right[0], right[1], right[0]], axis=right_axis),
            dims,
        )
    return (
        multiply(left[0], right[0], dims)
        + multiply(left[0], right[1], dims)
        + multiply(left[1], right[0], dims)
    )


LANES = ((1,), (1,))


def product(left, right, dims=((1,), (0,))):
    return lax.dot_general(
        left,
        right,
        (dims, ((), ())),
        precision=lax.Precision.HIGH,
        preferred_element_type=jnp.float32,
    )


def lane_pick(table, index):
    return jnp.take_along_axis(table, index, axis=1, mode="promise_in_bounds")


def whole(shape):
    return pl.BlockSpec(tuple(shape), lambda step: (0,) * len(shape))


def whole_specs(*arrays):
    return [whole(array.shape) for array in arrays]


def collect_kernel(
    positions_ref, types_ref, count_ref, send_ref, own_ref, outgoing_ref
):
    atoms = types_ref.shape[1]
    own_ref[...] = jnp.zeros_like(own_ref)
    for axis in range(3):
        own_ref[axis : axis + 1, 0:atoms] = positions_ref[axis]
    own_ref[3:4, 0:atoms] = types_ref[...].astype(jnp.float32)
    own_ref[4:5, 0:atoms] = count_ref[...].astype(jnp.float32)
    own_ref[5:6, 0:atoms] = send_ref[...].astype(jnp.float32)
    for chunk in range(2):
        lanes = slice(128 * chunk, 128 * chunk + 128)
        wanted = jnp.broadcast_to(own_ref[5:6, lanes], (8, 128)).astype(jnp.int32)
        within = wanted & 127
        outgoing_ref[:, lanes] = jnp.where(
            wanted < 128,
            lane_pick(own_ref[:, 0:128], within),
            lane_pick(own_ref[:, 128:256], within),
        )


def collect(positions, types, counts, send_index):
    arrays = (positions, types, counts, send_index)
    result = jax.ShapeDtypeStruct((8, 256), jnp.float32)
    return pl.pallas_call(
        collect_kernel,
        grid=(1,),
        out_shape=[result, result],
        in_specs=whole_specs(*arrays),
        out_specs=whole_specs(result, result),
        compiler_params=pltpu.CompilerParams(vmem_limit_bytes=VMEM_BYTES),
        name="collect_atoms",
    )(*arrays)


def fitting_rows(descriptor_ref, weight_in_ref, weight_hidden_ref, weight_out_ref):
    hidden = jnp.tanh(product(descriptor_ref[...], weight_in_ref[...], LANES))
    for layer in range(weight_hidden_ref.shape[0]):
        hidden = jnp.tanh(product(hidden, weight_hidden_ref[layer])) + hidden
    width = hidden.shape[1]
    return product(jnp.broadcast_to(weight_out_ref[...], (8, width)), hidden, LANES)


def natural_order(rows):
    atoms = rows.shape[1]
    padded = jnp.concatenate([rows, jnp.zeros((8, 256 - atoms), jnp.float32)], axis=1)
    pieces = []
    for chunk in range(2):
        atom = 128 * chunk + lax.broadcasted_iota(jnp.int32, (8, 128), 1)
        late = atom >= atoms // 2
        within = jnp.where(late, atom - atoms // 2, atom)
        place = 8 * (within >> 2) + (within & 3) + jnp.where(late, 4, 0)
        place = jnp.minimum(place, 255)
        pieces.append(
            jnp.where(
                place < 128,
                lane_pick(padded[:, 0:128], place & 127),
                lane_pick(padded[:, 128:256], place & 127),
            )
        )
    return jnp.concatenate(pieces, axis=1)[0:1, 0:atoms]


def network_kernel(
    ghosts,
    base_ref,
    charges_ref,
    own_ref,
    lower_ref,
    upper_ref,
    slots_ref,
    types_ref,
    cell_x_ref,
    cell_y_ref,
    cell_z_ref,
    fraction_ref,
    first_ref,
    second_ref,
    third_ref,
    spot_ref,
    weight_in_hbm,
    weight_hidden_hbm,
    weight_out_ref,
    descriptor_hbm,
    charge_ref,
    copies_ref,
    descriptor_ref,
    environment_ref,
    kind_ref,
    moments_ref,
    padded_ref,
    weight_in_ref,
    weight_hidden_ref,
    semaphores,
):
    fetches = [
        pltpu.make_async_copy(weight_in_hbm, weight_in_ref, semaphores.at[0]),
        pltpu.make_async_copy(weight_hidden_hbm, weight_hidden_ref, semaphores.at[1]),
    ]
    for fetch in fetches:
        fetch.start()
    slots, atoms = slots_ref.shape
    rows = atoms // 2
    lane = lax.broadcasted_iota(jnp.int32, (8, 128), 1)
    sub = lax.broadcasted_iota(jnp.int32, (8, 128), 0)

    width = first_ref.shape[1]
    padded_ref[...] = jnp.zeros_like(padded_ref)
    padded_ref[0, 0:2, 0:width] = first_ref[...]
    for column in range(2):
        padded_ref[1, 0:width, 32 * column : 32 * column + width] = second_ref[
            :, width * column : width * (column + 1)
        ]
    for row in range(2):
        for column in range(4):
            padded_ref[2, 32 * row : 32 * row + width, 32 * column : 32 * column + width] = (
                third_ref[
                    width * row : width * (row + 1), width * column : width * (column + 1)
                ]
            )
    first_table = padded_ref[0].T
    embed_zero = jnp.broadcast_to(first_table[0:32, 0:1], (32, 128))
    embed_one = jnp.broadcast_to(first_table[0:32, 1:2], (32, 128))
    second_high, second_low = split(padded_ref[1].T[0:64, 0:32])
    second_weight = jnp.concatenate([second_high, second_high, second_low], axis=1)
    third_high, third_low = split(padded_ref[2].T[:, 0:64])
    third_weight = jnp.concatenate([third_high, third_high, third_low], axis=1)

    def spread(ref, field, chunk):
        return jnp.broadcast_to(ref[field : field + 1, 128 * chunk : 128 * chunk + 128], (8, 128))

    own = [[spread(own_ref, field, chunk) for chunk in range(2)] for field in range(5)]
    lower = [[spread(lower_ref, field, chunk) for chunk in range(2)] for field in range(4)]
    upper = [spread(upper_ref, field, 0) for field in range(4)]

    def pick_two(tables, index):
        within = index & 127
        return jnp.where(index < 128, lane_pick(tables[0], within), lane_pick(tables[1], within))

    pairs = jnp.concatenate([slots_ref[:, 0:rows], slots_ref[:, rows:atoms]], axis=0).T
    for tile in range(rows // 8):
        band = slice(8 * tile, 8 * tile + 8)
        index = pairs[band, :]
        centre = 8 * tile + sub + jnp.where(lane < 64, 0, rows)
        from_own = jnp.clip(index - ghosts, 0, atoms - 1)
        from_lower = jnp.minimum(index + (atoms - ghosts), 255)
        from_upper = jnp.clip(index - (ghosts + atoms), 0, 127)

        def neighbour(field):
            below = pick_two(lower[field], from_lower)
            inside = pick_two(own[field], from_own)
            above = lane_pick(upper[field], from_upper)
            return jnp.where(
                index < ghosts, below, jnp.where(index < ghosts + atoms, inside, above)
            )

        offsets = [neighbour(field) - pick_two(own[field], centre) for field in range(3)]
        live = pick_two(own[4], centre)
        present = jnp.where((lane & 63).astype(jnp.float32) < live, 1.0, 0.0)
        smooth = present / (
            1.0 + (offsets[0] * offsets[0] + offsets[1] * offsets[1] + offsets[2] * offsets[2])
        )
        environment_ref[0, band, :] = smooth
        for field in range(3):
            environment_ref[1 + field, band, :] = smooth * offsets[field]
        kind_ref[band, :] = neighbour(3)

    group = 8

    def stacked(values):
        high, low = split(values)
        return jnp.concatenate([high, low, high], axis=0)

    def one_group(start):
        pieces = []
        for row in range(group):
            smooth = jnp.broadcast_to(environment_ref[0, pl.ds(start + row, 1), :], (32, 128))
            kind = jnp.broadcast_to(kind_ref[pl.ds(start + row, 1), :], (32, 128))
            pieces.append(
                jnp.tanh(smooth * ((1.0 - kind) * embed_zero + kind * embed_one))
            )
        first = jnp.concatenate(pieces, axis=1)
        second = jnp.tanh(multiply(second_weight, stacked(first), ((1,), (0,))))
        second = second + jnp.concatenate([first, first], axis=0)
        third = jnp.tanh(multiply(third_weight, stacked(second), ((1,), (0,))))
        third = third + jnp.concatenate([second, second], axis=0)
        third_pair = split(third)
        for half in range(group // 4):
            columns = slice(512 * half, 512 * half + 512)
            bands = []
            for part in range(4):
                bands.append(
                    jnp.concatenate(
                        [
                            jnp.where(
                                sub == row + jnp.where(lane < 64, 0, 4),
                                jnp.broadcast_to(
                                    environment_ref[part, pl.ds(start + 4 * half + row, 1), :],
                                    (8, 128),
                                ),
                                0.0,
                            )
                            for row in range(4)
                        ],
                        axis=1,
                    )
                )
            environment = split(jnp.concatenate(bands, axis=0))
            both = multiply(
                jnp.concatenate(environment, axis=0), third_pair[0][:, columns], LANES
            )
            sums = both[0:32] + both[32:64]
            sums = sums + multiply(environment[0], third_pair[1][:, columns], LANES)
            sums = sums * (1.0 / slots)
            for part in range(4):
                moments_ref[part, pl.ds(2 * start + 8 * half, 8), :] = sums[
                    8 * part : 8 * part + 8
                ]

    def body(step, carry):
        for part in range(unroll):
            one_group(pl.multiple_of(step * unroll * group + part * group, group))
        return carry

    unroll = 4 if rows % (4 * group) == 0 else 1
    lax.fori_loop(0, rows // (unroll * group), body, 0)

    chunks = (descriptor_ref.shape[1] + 127) // 128
    last = descriptor_ref.shape[1] - 128 * (chunks - 1)

    def describe_band(start):
        band = pl.ds(start, 8)
        moments = [moments_ref[part, band, :] for part in range(4)]
        axis_part = [lane_pick(moments[part], lane & 15) for part in range(4)]
        for chunk in range(chunks):
            spot = jnp.broadcast_to(spot_ref[chunk : chunk + 1, :], (8, 128))
            total = lane_pick(moments[0], spot) * axis_part[0]
            for part in range(1, 4):
                total = total + lane_pick(moments[part], spot) * axis_part[part]
            if chunk < chunks - 1:
                descriptor_ref[band, 128 * chunk : 128 * chunk + 128] = total
            else:
                descriptor_ref[band, 128 * chunk : 128 * chunk + last] = total[:, 0:last]

    bands = 4 if atoms % 32 == 0 else 1

    def describe(step, carry):
        for part in range(bands):
            describe_band(pl.multiple_of(step * 8 * bands + 8 * part, 8))
        return carry

    lax.fori_loop(0, atoms // (8 * bands), describe, 0)

    store = pltpu.make_async_copy(descriptor_ref, descriptor_hbm, semaphores.at[2])
    store.start()
    for fetch in fetches:
        fetch.wait()
    shift = fitting_rows(descriptor_ref, weight_in_ref, weight_hidden_ref, weight_out_ref)
    kind = types_ref[...].astype(jnp.float32)
    charge = (1.0 - kind) * charges_ref[0] + kind * charges_ref[1] + natural_order(shift)
    charge_ref[...] = charge
    fields = jnp.concatenate(
        [
            cell_x_ref[...].astype(jnp.float32),
            (cell_y_ref[...] + base_ref[0]).astype(jnp.float32),
            cell_z_ref[...].astype(jnp.float32),
        ]
        + [fraction_ref[axis] for axis in range(3)]
        + [charge, jnp.zeros((1, atoms), jnp.float32)],
        axis=0,
    )
    for copy in range(copies_ref.shape[0]):
        copies_ref[copy] = fields
    store.wait()


def spot_table(embed, desc):
    column = np.arange(desc) // AXIS
    quarter = embed // 4
    place = 32 * (column // quarter) + column % quarter
    chunks = (desc + 127) // 128
    table = np.zeros((chunks * 128,), np.int32)
    table[:desc] = place
    padded = np.zeros(((chunks + 7) // 8 * 8, 128), np.int32)
    padded[:chunks] = table.reshape(chunks, 128)
    return padded


def networks(
    copies,
    ghosts,
    base,
    charge_base,
    own,
    lower,
    upper,
    neighbours,
    types,
    cells,
    fraction,
    embed,
    weight_in,
    weight_hidden,
    weight_out,
):
    atoms = types.shape[1]
    desc, width = weight_in.shape
    spots = jnp.asarray(spot_table(embed[2].shape[1], desc))
    anywhere = pl.BlockSpec(memory_space=pl.ANY)
    scalars = pl.BlockSpec(memory_space=pltpu.SMEM)
    blocks = (own, lower, upper, neighbours[0].T, types, *cells, fraction, *embed, spots)
    weight_out = weight_out.reshape(1, -1)
    results = [
        jax.ShapeDtypeStruct((atoms, desc), jnp.float32),
        jax.ShapeDtypeStruct((1, atoms), jnp.float32),
        jax.ShapeDtypeStruct((copies, 8, atoms), jnp.float32),
    ]
    return pl.pallas_call(
        functools.partial(network_kernel, ghosts),
        grid=(1,),
        out_shape=results,
        in_specs=[scalars, scalars]
        + whole_specs(*blocks)
        + [anywhere, anywhere]
        + whole_specs(weight_out),
        out_specs=[anywhere] + whole_specs(*results[1:]),
        scratch_shapes=[
            pltpu.VMEM((atoms, desc), jnp.float32),
            pltpu.VMEM((4, atoms // 2, 128), jnp.float32),
            pltpu.VMEM((atoms // 2, 128), jnp.float32),
            pltpu.VMEM((4, atoms, 128), jnp.float32),
            pltpu.VMEM((3, 128, 128), jnp.float32),
            pltpu.VMEM((width, desc), jnp.float32),
            pltpu.VMEM(weight_hidden.shape, jnp.float32),
            pltpu.SemaphoreType.DMA((3,)),
        ],
        compiler_params=pltpu.CompilerParams(vmem_limit_bytes=VMEM_BYTES),
        name="networks",
    )(base, charge_base, *blocks, weight_in.T, weight_hidden, weight_out)


def energy_kernel(descriptor_ref, weight_in_ref, weight_hidden_ref, weight_out_ref, energy_ref):
    energy_ref[...] = natural_order(
        fitting_rows(descriptor_ref, weight_in_ref, weight_hidden_ref, weight_out_ref)
    )


def energies(descriptor, weight_in, weight_hidden, weight_out):
    atoms, desc = descriptor.shape
    width = weight_in.shape[1]
    arrays = (descriptor, weight_in.T, weight_hidden, weight_out.reshape(1, -1))
    result = jax.ShapeDtypeStruct((1, atoms), jnp.float32)
    return pl.pallas_call(
        energy_kernel,
        grid=(1,),
        out_shape=result,
        in_specs=whole_specs(*arrays),
        out_specs=whole(result.shape),
        compiler_params=pltpu.CompilerParams(vmem_limit_bytes=VMEM_BYTES),
        cost_estimate=pl.CostEstimate(
            flops=6 * atoms * desc * width, bytes_accessed=4 * desc * width, transcendentals=0
        ),
        name="energies",
    )(*arrays)


def weight_rows(fraction):
    square = fraction * fraction
    cubed = square * fraction
    rest = 1.0 - fraction
    return [
        rest * rest * rest / 6.0,
        (3.0 * cubed - 6.0 * square + 4.0) / 6.0,
        (-3.0 * cubed + 3.0 * square + 3.0 * fraction + 1.0) / 6.0,
        cubed / 6.0,
    ]


def placed_weights(distance, weights):
    shape = distance.shape
    result = jnp.zeros(shape, jnp.float32)
    for step in range(4):
        result = jnp.where(
            distance == step, jnp.broadcast_to(weights[step], shape), result
        )
    return result


def third_factors(fields, waves_ref, cosine_ref):
    atoms = fields.shape[1]
    start = fields[2:3, :].astype(jnp.int32)
    along = weight_rows(fields[5:6, :])
    parts = waves_ref.shape[0]
    cosine = jnp.broadcast_to(cosine_ref[...], (parts, 128))
    wave = jnp.broadcast_to(waves_ref[:, 0:1], (parts, 128))
    shift = jnp.broadcast_to(waves_ref[:, 1:2], (parts, 128))
    pieces = []
    for chunk in range(atoms // 128):
        lanes = slice(128 * chunk, 128 * chunk + 128)
        total = jnp.zeros((parts, 128), jnp.float32)
        for step in range(4):
            place = jnp.broadcast_to(start[:, lanes] + step, (parts, 128))
            phase = (wave * place + shift) & (NG - 1)
            value = lane_pick(cosine, phase & 127)
            value = jnp.where(phase < 128, value, -value)
            total = total + value * jnp.broadcast_to(along[step][:, lanes], (parts, 128))
        pieces.append(total)
    return jnp.concatenate(pieces, axis=1)


def first_third_split(fields, waves_ref, cosine_ref, window, scale, high_ref, low_ref):
    atoms = fields.shape[1]
    third = third_factors(fields, waves_ref, cosine_ref) * scale
    rows = lax.broadcasted_iota(jnp.int32, (window, atoms), 0)
    first = placed_weights(
        rows - fields[0:1, :].astype(jnp.int32), weight_rows(fields[3:4, :])
    )
    for chunk in range(atoms // 128):
        lanes = slice(128 * chunk, 128 * (chunk + 1))
        for part in range(0, third.shape[0], 2):
            high, low = split(
                jnp.concatenate(
                    [first[:, lanes] * third[part + side : part + side + 1, lanes] for side in range(2)],
                    axis=0,
                )
            )
            place = slice(part * window, (part + 2) * window)
            high_ref[place, lanes] = high
            low_ref[place, lanes] = low
    return high_ref[...], low_ref[...]


def second_factors(fields, base, block_y, slabs, high_ref, low_ref):
    atoms = fields.shape[1]
    block = atoms // slabs
    reach = block_y + REACH
    start = fields[1:2, :].astype(jnp.int32) - base
    weights = weight_rows(fields[4:5, :])
    for chunk in range(atoms // 128):
        lanes = slice(128 * chunk, 128 * (chunk + 1))
        first = 128 * chunk // block
        last = (128 * chunk + 127) // block
        top = first * block_y
        rows = (last - first) * block_y + reach
        pieces = [(top, min(rows, NG - top))]
        if top + rows > NG:
            pieces.append((0, top + rows - NG))
        for row, count in pieces:
            index = row + lax.broadcasted_iota(jnp.int32, (count, 128), 0)
            table = split(
                placed_weights(
                    (index - start[:, lanes]) & (NG - 1), [weight[:, lanes] for weight in weights]
                )
            )
            high_ref[row : row + count, lanes] = table[0]
            low_ref[row : row + count, lanes] = table[1]
    return high_ref[...], low_ref[...]


def wave_of(index):
    return jnp.where(index <= NG // 2, index, index - NG // 2)


def damping(index):
    kappa = wave_of(index).astype(jnp.float32) * (2.0 * math.pi / NG)
    squared = kappa * kappa
    ends = (index == 0) | (index == NG // 2)
    return squared, jnp.exp(-0.5 * squared) * jnp.where(ends, 1.0 / NG, 2.0 / NG)


def transform(planes, kappa_ref, first_part, tables_ref, last_ref):
    count = len(planes)
    basis = tables_ref[0]
    turned = tables_ref[1]
    square_x, damp_x = damping(lax.broadcasted_iota(jnp.int32, (NG, 1), 0))
    square_y, damp_y = damping(lax.broadcasted_iota(jnp.int32, (1, NG), 1))
    square_xy = square_x + square_y
    damp_xy = damp_x * damp_y
    columns = [slice(NG * part, NG * (part + 1)) for part in range(count)]
    first = product(basis, jnp.concatenate(planes, axis=1))
    first = jnp.concatenate([first[:, column] for column in columns], axis=0)
    both = product(first, turned)
    scaled = []
    for part in range(count):
        squared = square_xy + kappa_ref[first_part + part, 0]
        root = jnp.where(squared == 0.0, 1.0, 0.0)
        green = (1.0 - root) * (damp_xy * kappa_ref[first_part + part, 1]) / (squared + root)
        scaled.append(both[columns[part]] * green)
    back = product(turned, jnp.concatenate(scaled, axis=1))
    back = jnp.concatenate([back[:, column] for column in columns], axis=0)
    return product(back, last_ref[...])


def send_blocks(full, block_x, block_y, put):
    low_lanes = lax.broadcasted_iota(jnp.int32, (NG, 128), 1) < block_y
    for pair in range(full.shape[0] // (2 * NG)):
        even = full[2 * NG * pair : 2 * NG * pair + NG, 0:128]
        odd = full[2 * NG * pair + NG : 2 * NG * (pair + 1), 0:128]
        blocks = [
            jnp.where(low_lanes, even, pltpu.roll(odd, block_y, 1)),
            jnp.where(low_lanes, pltpu.roll(even, block_y, 1), odd),
        ]
        for brick in range(NG // block_x):
            for side in range(2):
                for group in range(block_x // 8):
                    start = block_x * brick + 8 * group
                    put(pair, brick, side, group, blocks[side][start : start + 8])


def spread_kernel(
    block_x,
    block_y,
    window,
    kappa_ref,
    pair_ref,
    static_ref,
    waves_ref,
    cosine_ref,
    tables_hbm,
    last_hbm,
    short_hbm,
    sent_ref,
    full_ref,
    atoms_ref,
    later_hbm,
    grid_ref,
    tables_ref,
    last_ref,
    semaphores,
    *pair_refs,
):
    slabs = NG // block_y
    second_refs, first_refs = pair_refs[:4], pair_refs[4:]
    bricks = NG // block_x
    parts = waves_ref.shape[0]
    block = static_ref.shape[2]
    count = full_ref.shape[0]
    step = pl.program_id(0)
    later = later_hbm.shape[0]
    store = pltpu.make_async_copy(
        grid_ref.at[pl.ds(parts - later, later), pl.ds(0, NG)], later_hbm, semaphores.at[2]
    )

    @pl.when(step == 0)
    def _():
        fetches = [
            pltpu.make_async_copy(tables_hbm, tables_ref, semaphores.at[0]),
            pltpu.make_async_copy(last_hbm.at[pair_ref[0]], last_ref, semaphores.at[1]),
        ]
        for fetch in fetches:
            fetch.start()
        for slab in range(slabs):
            lanes = slice(block * slab, block * (slab + 1))
            for brick in range(bricks):
                atoms_ref[brick, :, lanes] = static_ref[slab * bricks + brick]
        grid_ref[...] = jnp.zeros_like(grid_ref)
        for ref in second_refs:
            ref[...] = jnp.zeros_like(ref)
        for brick in range(bricks):
            fields = atoms_ref[brick]
            table = first_third_split(
                fields,
                waves_ref,
                cosine_ref,
                window,
                fields[6:7, :],
                first_refs[2 * (brick % 2)],
                first_refs[2 * (brick % 2) + 1],
            )
            second = second_factors(
                fields, 0, block_y, slabs, second_refs[2 * (brick % 2)], second_refs[2 * (brick % 2) + 1]
            )
            spread = triple(table, second, LANES)
            rows = slice(block_x * brick, block_x * brick + window)
            for part in range(parts):
                grid_ref[part, rows, :] += spread[part * window : part * window + window]
        extra = window - block_x
        for part in range(parts):
            grid_ref[part, 0:extra, :] += grid_ref[part, NG : NG + extra, :]
        store.start()
        for fetch in fetches:
            fetch.wait()

    planes = [grid_ref[count * step + part, 0:NG, :] for part in range(count)]
    full = transform(planes, kappa_ref, count * step, tables_ref, last_ref)
    for part in range(count):
        full_ref[part] = full[NG * part : NG * (part + 1)]

    def put(pair, brick, side, group, tile):
        sent_ref[2 * brick + side, group, pair] = tile

    send_blocks(full, block_x, block_y, put)

    @pl.when(step == pl.num_programs(0) - 1)
    def _():
        store.wait()


def early_pairs(parts):
    return parts // 4


def spread_and_solve(
    block_x, block_y, window, kappa, pair, static, waves, cosine_row, tables, last, short
):
    devices, _, atoms = static.shape
    slabs = NG // block_y
    bricks = NG // block_x
    parts = waves.shape[0]
    pairs = early_pairs(parts)
    count = 4
    anywhere = pl.BlockSpec(memory_space=pl.ANY)
    scalars = pl.BlockSpec(memory_space=pltpu.SMEM)
    sent_block = (2 * bricks, block_x // 8, count // 2, 8, 128)
    return pl.pallas_call(
        functools.partial(spread_kernel, block_x, block_y, window),
        grid=(2 * pairs // count,),
        out_shape=[
            jax.ShapeDtypeStruct((2 * bricks, block_x // 8, pairs, 8, 128), jnp.float32),
            jax.ShapeDtypeStruct((2 * pairs, NG, NG), jnp.float32),
            jax.ShapeDtypeStruct((bricks, 8, slabs * atoms), jnp.float32),
            jax.ShapeDtypeStruct((parts - 2 * pairs, NG, NG), jnp.float32),
        ],
        in_specs=[scalars, scalars]
        + whole_specs(static, waves, cosine_row)
        + [anywhere, anywhere, anywhere],
        out_specs=[
            pl.BlockSpec(sent_block, lambda step: (0, 0, step, 0, 0)),
            pl.BlockSpec((count, NG, NG), lambda step: (step, 0, 0)),
            whole((bricks, 8, slabs * atoms)),
            anywhere,
        ],
        scratch_shapes=[
            pltpu.VMEM((parts, NG + window - block_x, NG), jnp.float32),
            pltpu.VMEM(tables.shape, tables.dtype),
            pltpu.VMEM(last.shape[1:], last.dtype),
            pltpu.SemaphoreType.DMA((3,)),
        ]
        + [pltpu.VMEM((NG, slabs * atoms), jnp.bfloat16)] * 4
        + [pltpu.VMEM((parts * window, slabs * atoms), jnp.bfloat16)] * 4,
        compiler_params=pltpu.CompilerParams(vmem_limit_bytes=VMEM_BYTES),
        name="spread_and_solve",
    )(kappa, pair, static, waves, cosine_row, tables, last, short)


def sample_kernel(
    block_x,
    block_y,
    window,
    kappa_ref,
    pair_ref,
    atoms_ref,
    waves_ref,
    cosine_ref,
    tables_hbm,
    last_hbm,
    later_hbm,
    early_hbm,
    sent_ref,
    later_ref,
    full_ref,
    tables_ref,
    last_ref,
    semaphores,
    packed_ref,
):
    bricks = atoms_ref.shape[0]
    parts = waves_ref.shape[0]
    early = 2 * early_pairs(parts)
    block = atoms_ref.shape[2] * block_y // NG
    fetches = [
        pltpu.make_async_copy(tables_hbm, tables_ref, semaphores.at[0]),
        pltpu.make_async_copy(last_hbm.at[pair_ref[0]], last_ref, semaphores.at[1]),
        pltpu.make_async_copy(later_hbm, later_ref, semaphores.at[2]),
        pltpu.make_async_copy(early_hbm, full_ref.at[pl.ds(0, early)], semaphores.at[3]),
    ]
    for fetch in fetches:
        fetch.start()
    for fetch in fetches[:3]:
        fetch.wait()
    pairs = (parts - early) // 2
    planes = [later_ref[part] for part in range(parts - early)]
    full = transform(planes, kappa_ref, early, tables_ref, last_ref)
    for part in range(parts - early):
        full_ref[early + part] = full[NG * part : NG * (part + 1)]

    def put(pair, brick, side, group, tile):
        sent_ref[2 * brick + side, pairs * group + pair] = tile

    send_blocks(full, block_x, block_y, put)
    fetches[3].wait()

    reach = block_y + REACH
    lane = lax.broadcasted_iota(jnp.int32, (NG, 128), 1)
    for part in range(parts):
        for side in range(2):
            values = full_ref[part, :, 128 * side : 128 * (side + 1)]
            high = values.astype(jnp.bfloat16).astype(jnp.float32)
            again = pltpu.roll(high, reach, 1)
            low = pltpu.roll(values - high, 2 * reach - 128, 1)
            packed_ref[side, part, 0:NG, 0:128] = jnp.where(lane < reach, high, again)
            packed_ref[side, part, 0:NG, 128:NG] = jnp.where(
                lane < 2 * reach - 128, again, jnp.where(lane < 3 * reach - 128, low, 0.0)
            )
            packed_ref[side, part, NG : NG + window - block_x, :] = packed_ref[
                side, part, 0 : window - block_x, :
            ]
    extra = sent_ref.shape[1] - 1
    base = 2 * block_y * pair_ref[0]
    lanes = pl.ds(pl.multiple_of(2 * block * pair_ref[0], 128), 2 * block)
    for brick in range(bricks):
        fields = atoms_ref[brick, :, lanes]
        thirds = third_factors(fields, waves_ref, cosine_ref)
        rows = slice(block_x * brick, block_x * brick + window)
        for side in range(2):
            here = slice(block * side, block * (side + 1))
            third = thirds[:, here]
            ours = fields[:, here]
            index = lax.broadcasted_iota(jnp.int32, (window, block), 0)
            first = placed_weights(
                index - ours[0:1, :].astype(jnp.int32), weight_rows(ours[3:4, :])
            )
            index = lax.broadcasted_iota(jnp.int32, (reach, block), 0)
            start = ours[1:2, :].astype(jnp.int32) - (base + block_y * side)
            high, low = split(placed_weights(index - start, weight_rows(ours[4:5, :])))
            rest = jnp.zeros((NG - 3 * reach, block), jnp.bfloat16)
            second = jnp.concatenate([high, low, high, rest], axis=0)
            values = jnp.concatenate(
                [packed_ref[side, part, rows, :] for part in range(parts)], axis=0
            )
            along = multiply(values.astype(jnp.bfloat16), second, ((1,), (0,)))
            total = jnp.zeros((window, block), jnp.float32)
            for part in range(parts):
                total = total + along[window * part : window * (part + 1)] * third[part : part + 1]
            row = jnp.sum(total * first, axis=0, keepdims=True)
            sent_ref[2 * brick + side, extra] = jnp.zeros((8, 128), jnp.float32)
            sent_ref[2 * brick + side, extra, 0:1, :] = row[:, 0:128]
            sent_ref[2 * brick + side, extra, 1:2, 0 : block - 128] = row[:, 128:block]


def solve_and_sample(
    block_x, block_y, window, kappa, pair, atoms, waves, cosine_row, tables, last, later, early
):
    bricks = atoms.shape[0]
    parts = waves.shape[0]
    pairs = parts // 2 - early_pairs(parts)
    anywhere = pl.BlockSpec(memory_space=pl.ANY)
    scalars = pl.BlockSpec(memory_space=pltpu.SMEM)
    result = jax.ShapeDtypeStruct((2 * bricks, block_x // 8 * pairs + 1, 8, 128), jnp.float32)
    return pl.pallas_call(
        functools.partial(sample_kernel, block_x, block_y, window),
        grid=(1,),
        out_shape=result,
        in_specs=[scalars, scalars] + whole_specs(atoms, waves, cosine_row) + [anywhere] * 4,
        out_specs=whole(result.shape),
        scratch_shapes=[
            pltpu.VMEM((2 * pairs, NG, NG), jnp.float32),
            pltpu.VMEM((parts, NG, NG), jnp.float32),
            pltpu.VMEM(tables.shape, tables.dtype),
            pltpu.VMEM(last.shape[1:], last.dtype),
            pltpu.SemaphoreType.DMA((4,)),
        ]
        + [pltpu.VMEM((2, parts, NG + window - block_x, NG), jnp.float32)],
        compiler_params=pltpu.CompilerParams(vmem_limit_bytes=VMEM_BYTES),
        cost_estimate=pl.CostEstimate(
            flops=24 * parts * NG * NG * NG, bytes_accessed=4 * early.size, transcendentals=0
        ),
        name="solve_and_sample",
    )(kappa, pair, atoms, waves, cosine_row, tables, last, later, early)


def finish_kernel(
    block_y,
    early_ref,
    later_ref,
    sums_ref,
    short_hbm,
    charge_hbm,
    table_ref,
    out_ref,
    energy_ref,
    short_ref,
    charge_ref,
    semaphores,
):
    atoms = short_ref.shape[1]
    fetches = [
        pltpu.make_async_copy(short_hbm, short_ref, semaphores.at[0]),
        pltpu.make_async_copy(charge_hbm, charge_ref, semaphores.at[1]),
    ]

    @pl.when(pl.program_id(0) == 0)
    def _():
        for fetch in fetches:
            fetch.start()

    lines = early_ref.shape[3]
    sources, _, pairs = early_ref.shape[:3]
    early = early_ref.reshape(sources * pairs, lines, 128)
    later = later_ref.reshape(sources * later_ref.shape[1], lines, 128)
    pieces = []
    for line in range(lines):
        turned = jnp.concatenate([early[:, line, :], later[:, line, :]], axis=0).T
        pieces.append(jnp.concatenate([turned[0:block_y], turned[block_y:]], axis=1))
    result = product(jnp.concatenate(pieces, axis=0), table_ref[...])
    for line in range(lines):
        out_ref[line] = result[block_y * line : block_y * (line + 1)]

    @pl.when(pl.program_id(0) == 0)
    def _():
        for fetch in fetches:
            fetch.wait()
        total = jnp.sum(sums_ref[:, 0], axis=0)
        potential_at = jnp.concatenate([total[0:1, :], total[1:2, 0 : atoms - 128]], axis=1)
        energy_ref[...] = short_ref[...] + 0.5 * charge_ref[...] * potential_at


def finish(block_x, block_y, early, later, short, charge, table):
    bricks2, groups, pairs = early.shape[:3]
    rest = (later.shape[1] - 1) // groups
    atoms = short.shape[1]
    return pl.pallas_call(
        functools.partial(finish_kernel, block_y),
        grid=(groups,),
        out_shape=[
            jax.ShapeDtypeStruct((block_x, block_y, NG), jnp.float32),
            jax.ShapeDtypeStruct((1, atoms), jnp.float32),
        ],
        in_specs=[
            pl.BlockSpec((bricks2, 1, pairs, 8, 128), lambda index: (0, index, 0, 0, 0)),
            pl.BlockSpec((bricks2, rest, 8, 128), lambda index: (0, index, 0, 0)),
            pl.BlockSpec((bricks2, 1, 8, 128), lambda index: (0, groups * rest, 0, 0)),
            pl.BlockSpec(memory_space=pltpu.HBM),
            pl.BlockSpec(memory_space=pltpu.HBM),
            whole(table.shape),
        ],
        out_specs=[
            pl.BlockSpec((8, block_y, NG), lambda index: (index, 0, 0)),
            whole((1, atoms)),
        ],
        scratch_shapes=[
            pltpu.VMEM((1, atoms), jnp.float32),
            pltpu.VMEM((1, atoms), jnp.float32),
            pltpu.SemaphoreType.DMA((2,)),
        ],
        compiler_params=pltpu.CompilerParams(vmem_limit_bytes=32 * 2**20),
        name="finish",
    )(early, later, later, short, charge, table)


def real_basis():
    index = np.arange(NG)
    wave = np.where(index <= NG // 2, index, index - NG // 2)
    angle = (wave[:, None] * index[None, :] % NG) * (2.0 * math.pi / NG)
    return np.where((index <= NG // 2)[:, None], np.cos(angle), np.sin(angle))


def per_device(
    positions,
    types,
    neighbours,
    neighbour_count,
    send_index,
    cell_x,
    cell_y,
    cell_z,
    spline_fraction,
    embed_first,
    embed_second,
    embed_third,
    energy_in,
    energy_hidden,
    energy_out,
    wannier_in,
    wannier_hidden,
    wannier_out,
    charge_base,
):
    atoms = types.shape[1]
    ghosts = send_index.shape[1] // 2
    count_x = lax.axis_size("brick")
    count_y = lax.axis_size("slab")
    block_x = NG // count_x
    block_y = NG // count_y
    window = block_x + 8
    parts = NG // (2 * count_x)
    brick = lax.axis_index("brick")
    slab = lax.axis_index("slab")
    pair = (slab // 2).astype(jnp.int32).reshape(1)
    halves = [
        [b * count_y + 2 * p + side for b in range(count_x) for side in range(2)]
        for p in range(count_y // 2)
    ]

    def exchange(values, axes, groups=None):
        return lax.all_to_all(
            values, axes, split_axis=0, concat_axis=0, tiled=True, axis_index_groups=groups
        )

    own, outgoing = collect(positions, types, neighbour_count, send_index)
    up = [(i, (i + 1) % count_x) for i in range(count_x)]
    down = [((i + 1) % count_x, i) for i in range(count_x)]
    lower = lax.ppermute(outgoing, "brick", up)
    upper = lax.ppermute(outgoing, "brick", down)
    descriptor, charge, fields = networks(
        count_x * count_y,
        ghosts,
        (slab * block_y).astype(jnp.int32).reshape(1),
        charge_base,
        own,
        lower,
        upper,
        neighbours,
        types,
        (cell_x, cell_y, cell_z),
        spline_fraction,
        (embed_first, embed_second, embed_third),
        wannier_in,
        wannier_hidden,
        wannier_out,
    )
    every_field = exchange(fields, ("slab", "brick"))

    part = (2 * brick + slab % 2) * parts + jnp.arange(parts, dtype=jnp.int32)
    wave = wave_of(part)
    waves = jnp.stack([wave, jnp.where(part <= NG // 2, 0, 3 * NG // 4)], axis=1)
    kappa = wave.astype(jnp.float32) * (2.0 * math.pi / NG)
    squared = kappa * kappa
    ends = (part == 0) | (part == NG // 2)
    kappa = jnp.stack(
        [squared, jnp.exp(-0.5 * squared) * jnp.where(ends, 1.0 / NG, 2.0 / NG)], axis=1
    )
    basis = real_basis()
    tables = np.stack([basis, basis.T]).astype(np.float32)
    last = []
    for p in range(count_y // 2):
        points = np.concatenate(
            [np.arange(2 * block_y), block_y + np.arange(block_y + REACH)]
        )
        points = (2 * block_y * p + points) % NG
        columns = np.zeros((NG, NG))
        columns[:, : points.size] = basis[:, points]
        last.append(columns.astype(np.float32))
    cosine_row = np.cos(np.arange(128) * (2.0 * math.pi / NG)).astype(np.float32)[None]
    cosine_row = jnp.asarray(cosine_row)
    tables = jnp.asarray(tables)
    last = jnp.asarray(np.stack(last))
    energy_short = energies(descriptor, energy_in, energy_hidden, energy_out)
    early, full, every_atom, later = spread_and_solve(
        block_x,
        block_y,
        window,
        kappa,
        pair,
        every_field,
        waves,
        cosine_row,
        tables,
        last,
        energy_short,
    )

    def send(values):
        got = exchange(values.reshape(values.shape[0], -1, 128), ("brick", "slab"), halves)
        return got.reshape(values.shape)

    early = send(early)
    later = solve_and_sample(
        block_x,
        block_y,
        window,
        kappa,
        pair,
        every_atom,
        waves,
        cosine_row,
        tables,
        last,
        later,
        full,
    )
    later = send(later)
    source = np.arange(2 * count_x)[:, None] * parts
    pairs = 2 * np.arange(parts // 2)[None, :]
    order = np.concatenate(
        [
            (source + pairs[:, : early_pairs(parts)]).ravel(),
            (source + pairs[:, early_pairs(parts) :]).ravel(),
        ]
    )
    order = np.concatenate([order, order + 1])
    potential, atom_energy = finish(
        block_x,
        block_y,
        early,
        later,
        energy_short,
        charge,
        jnp.asarray(basis[order].astype(np.float32)),
    )
    return atom_energy, potential


def solution(mesh):
    placed = (
        P(None, "slab", "brick"),
        P("slab", "brick"),
        P("slab", "brick", None),
        P("slab", "brick"),
        P("slab", "brick"),
        P("slab", "brick"),
        P("slab", "brick"),
        P("slab", "brick"),
        P(None, "slab", "brick"),
    ) + (P(),) * 10
    bricks, slabs = mesh.shape["brick"], mesh.shape["slab"]
    fits = 2 * NG == 128 * slabs and NG % (32 * bricks) == 0
    return jax.shard_map(
        per_device if fits else per_device_general,
        mesh=mesh,
        in_specs=placed,
        out_specs=(P("slab", "brick"), P("brick", "slab", None)),
        check_vma=False,
    )
```

```python
import functools
import math

import jax
import jax.numpy as jnp
import numpy as np
from jax import lax
from jax.experimental import pallas as pl
from jax.experimental.pallas import tpu as pltpu
from jax.sharding import PartitionSpec as P

NG = 256
AXIS = 16
VMEM_BYTES = 60 * 2**20
REACH = 16


HIGH = lax.Precision.HIGHEST


def with_halo(cells, sides, width):
    for axis, dim in sides:
        count = lax.axis_size(axis)
        head = lax.slice_in_dim(cells, 0, width, axis=dim)
        tail = lax.slice_in_dim(cells, cells.shape[dim] - width, cells.shape[dim], axis=dim)
        cells = jnp.concatenate(
            [
                lax.ppermute(tail, axis, [(i, (i + 1) % count) for i in range(count)]),
                cells,
                lax.ppermute(head, axis, [((i + 1) % count, i) for i in range(count)]),
            ],
            axis=dim,
        )
    return cells


def spline_weights(fraction):
    cubed = fraction * fraction * fraction
    square = fraction * fraction
    return jnp.stack(
        [
            (1.0 - fraction) * (1.0 - fraction) * (1.0 - fraction) / 6.0,
            (3.0 * cubed - 6.0 * square + 4.0) / 6.0,
            (-3.0 * cubed + 3.0 * square + 3.0 * fraction + 1.0) / 6.0,
            cubed / 6.0,
        ]
    )


def fitting(descriptor, weight_in, weight_hidden, weight_out):
    hidden = jnp.tanh(jnp.dot(descriptor, weight_in, precision=HIGH))
    for depth_index in range(weight_hidden.shape[0]):
        hidden = jnp.tanh(jnp.dot(hidden, weight_hidden[depth_index], precision=HIGH)) + hidden
    return jnp.dot(hidden, weight_out, precision=HIGH)


def atom_terms(
    extended,
    neighbour_rows,
    neighbour_total,
    embed_first,
    embed_second,
    embed_third,
    energy_in,
    energy_hidden,
    energy_out,
    wannier_in,
    wannier_hidden,
    wannier_out,
):
    atom_count, slots = neighbour_rows.shape
    ghost_rows = (extended.shape[1] - atom_count) // 2
    block_size = 64
    blocks = atom_count // block_size
    present = (jnp.arange(slots, dtype=jnp.int32)[None, :] < neighbour_total[:, None]).astype(
        jnp.float32
    )
    centre_ids = (ghost_rows + jnp.arange(atom_count, dtype=jnp.int32)).reshape(blocks, block_size)
    second_weight = embed_second.T
    third_weight = embed_third.T

    def one_block(pieces):
        centre_rows, rows_block, present_block = pieces
        centre_block = extended[:3, centre_rows]
        gathered = extended[:, rows_block]
        offsets = gathered[:3] - centre_block[:, :, None]
        smooth = present_block / (1.0 + jnp.sum(offsets * offsets, axis=0))
        environment = jnp.stack(
            [smooth, smooth * offsets[0], smooth * offsets[1], smooth * offsets[2]], axis=0
        )
        kind = gathered[3][None]
        mixing = (1.0 - kind) * embed_first[0][:, None, None] + kind * embed_first[1][:, None, None]
        first = jnp.tanh(smooth[None] * mixing).reshape(embed_first.shape[1], block_size * slots)
        second = jnp.tanh(jnp.dot(second_weight, first, precision=HIGH)) + jnp.concatenate(
            [first, first], axis=0
        )
        third = jnp.tanh(jnp.dot(third_weight, second, precision=HIGH)) + jnp.concatenate(
            [second, second], axis=0
        )
        third_blocks = third.reshape(third.shape[0], block_size, slots)
        moments = jnp.einsum("kan,can->akc", third_blocks, environment, precision=HIGH) / slots
        descriptor = jnp.einsum("amc,akc->amk", moments, moments[:, :AXIS], precision=HIGH).reshape(
            block_size, -1
        )
        return (
            fitting(descriptor, energy_in, energy_hidden, energy_out),
            fitting(descriptor, wannier_in, wannier_hidden, wannier_out),
        )

    energy_short, charge_shift = lax.map(
        one_block,
        (
            centre_ids,
            neighbour_rows.reshape(blocks, block_size, slots),
            present.reshape(blocks, block_size, slots),
        ),
    )
    return (energy_short.reshape(atom_count), charge_shift.reshape(atom_count))


def green_table(first, second, third, size):

    def folded(index):
        return jnp.where(index < size // 2, index, index - size).astype(jnp.float32) * (
            2.0 * math.pi / size
        )

    kappa_x = folded(first)[:, None, None]
    kappa_y = folded(second)[None, :, None]
    kappa_z = folded(third)[None, None, :]
    squared = kappa_x * kappa_x + kappa_y * kappa_y + kappa_z * kappa_z
    root = (
        (first[:, None, None] == 0) & (second[None, :, None] == 0) & (third[None, None, :] == 0)
    ).astype(jnp.float32)
    return (1.0 - root) * jnp.exp(-0.5 * squared) / (squared + root)


def dft_tables(size):
    index = jnp.arange(size, dtype=jnp.int32)
    phase = (index[:, None] * index[None, :] % size).astype(jnp.float32) * (2.0 * math.pi / size)
    return (jnp.cos(phase), jnp.sin(phase))


def along(values, table, axis_index):
    result = jnp.tensordot(values, table, axes=([axis_index], [0]), precision=HIGH)
    return jnp.moveaxis(result, -1, axis_index)


def complex_transform(paired, axis_index, cosine, sine, inverse):
    real_part = paired[0]
    imag_part = paired[1]
    inner = axis_index - 1
    real_cos = along(real_part, cosine, inner)
    real_sin = along(real_part, sine, inner)
    imag_cos = along(imag_part, cosine, inner)
    imag_sin = along(imag_part, sine, inner)
    if inverse:
        return jnp.stack([real_cos - imag_sin, imag_cos + real_sin])
    return jnp.stack([real_cos + imag_sin, imag_cos - real_sin])


def fold_windows(values, axis_index, block, count):
    front = jnp.moveaxis(values, axis_index, 0)
    rest = front.shape[1:]
    windows = front.reshape((count, block + 3) + rest)
    main_part = windows[:, :block]
    carried = jnp.roll(windows[:, block:], 1, axis=0)
    main_part = main_part.at[:, :3].add(carried)
    return jnp.moveaxis(main_part.reshape((count * block,) + rest), 0, axis_index)


def make_windows(values, axis_index, block, count):
    front = jnp.moveaxis(values, axis_index, 0)
    rest = front.shape[1:]
    pieces = front.reshape((count, block) + rest)
    trailing = jnp.roll(pieces, -1, axis=0)[:, :3]
    windows = jnp.concatenate([pieces, trailing], axis=1)
    return jnp.moveaxis(windows.reshape((count * (block + 3),) + rest), 0, axis_index)


def spread_matrix(start, weights, width, wrap_size):
    offsets = jnp.arange(4, dtype=jnp.int32)[:, None, None]
    target = start[None, :, None] + offsets
    if wrap_size > 0:
        target = target % wrap_size
    hits = (target == jnp.arange(width, dtype=jnp.int32)[None, None, :]).astype(jnp.float32)
    return jnp.sum(weights[:, :, None] * hits, axis=0)


def per_device_general(
    positions,
    types,
    neighbours,
    neighbour_count,
    send_index,
    cell_x,
    cell_y,
    cell_z,
    spline_fraction,
    embed_first,
    embed_second,
    embed_third,
    energy_in,
    energy_hidden,
    energy_out,
    wannier_in,
    wannier_hidden,
    wannier_out,
    charge_base,
):
    atom_count = types.shape[1]
    ghost_rows = send_index.shape[1] // 2
    kind_float = types[0].astype(jnp.float32)
    own_atoms = jnp.concatenate([positions[:, 0], kind_float[None]], axis=0)
    outgoing = own_atoms[:, send_index[0]]
    padded_ghosts = with_halo(outgoing, (("brick", 1),), ghost_rows)
    extended = jnp.concatenate(
        [padded_ghosts[:, :ghost_rows], own_atoms, padded_ghosts[:, 3 * ghost_rows :]], axis=1
    )
    energy_short, charge_shift = atom_terms(
        extended,
        neighbours[0],
        neighbour_count[0],
        embed_first,
        embed_second,
        embed_third,
        energy_in,
        energy_hidden,
        energy_out,
        wannier_in,
        wannier_hidden,
        wannier_out,
    )
    charge = (1.0 - kind_float) * charge_base[0] + kind_float * charge_base[1] + charge_shift
    count_x = lax.axis_size("brick")
    count_y = lax.axis_size("slab")
    block_x = NG // count_x
    block_y = NG // count_y
    wide_x = block_x + 3
    wide_y = block_y + 3
    spread_x = spread_matrix(cell_x[0], spline_weights(spline_fraction[0, 0]), wide_x, 0)
    spread_y = spread_matrix(cell_y[0], spline_weights(spline_fraction[1, 0]), wide_y, 0)
    spread_z = spread_matrix(cell_z[0], spline_weights(spline_fraction[2, 0]), NG, NG)
    spread_xy = (spread_x[:, :, None] * spread_y[:, None, :]).reshape(atom_count, wide_x * wide_y)
    charge_grid = jnp.einsum(
        "ap,az->pz", spread_xy, charge[:, None] * spread_z, precision=HIGH
    ).reshape(wide_x, wide_y, NG)
    cosine, sine = dft_tables(NG)
    scale = 1.0 / (NG * NG * NG)
    full_index = jnp.arange(NG, dtype=jnp.int32)
    paired = jnp.stack([along(charge_grid, cosine, 2), -along(charge_grid, sine, 2)])
    moved = lax.all_to_all(paired, "slab", split_axis=3, concat_axis=2, tiled=True)
    moved = complex_transform(fold_windows(moved, 2, block_y, count_y), 2, cosine, sine, False)
    moved = lax.all_to_all(moved, "brick", split_axis=2, concat_axis=1, tiled=True)
    moved = complex_transform(fold_windows(moved, 1, block_x, count_x), 1, cosine, sine, False)
    part_y = NG // count_x
    part_z = NG // count_y
    index_y = lax.axis_index("brick") * part_y + jnp.arange(part_y, dtype=jnp.int32)
    index_z = lax.axis_index("slab") * part_z + jnp.arange(part_z, dtype=jnp.int32)
    moved = moved * (green_table(full_index, index_y, index_z, NG) * scale)[None]
    moved = make_windows(complex_transform(moved, 1, cosine, sine, True), 1, block_x, count_x)
    moved = lax.all_to_all(moved, "brick", split_axis=1, concat_axis=2, tiled=True)
    moved = make_windows(complex_transform(moved, 2, cosine, sine, True), 2, block_y, count_y)
    moved = lax.all_to_all(moved, "slab", split_axis=2, concat_axis=3, tiled=True)
    potential_wide = along(moved[0], cosine, 2) - along(moved[1], sine, 2)
    sampled = jnp.einsum(
        "ap,pz->az", spread_xy, potential_wide.reshape(wide_x * wide_y, NG), precision=HIGH
    )
    potential_at = jnp.sum(sampled * spread_z, axis=1)
    atom_energy = energy_short + 0.5 * charge * potential_at
    return (atom_energy[None, :], potential_wide[:block_x, :block_y])


def split(values):
    high = values.astype(jnp.bfloat16)
    low = (values - high.astype(jnp.float32)).astype(jnp.bfloat16)
    return high, low


def multiply(left, right, dims):
    return lax.dot_general(left, right, (dims, ((), ())), preferred_element_type=jnp.float32)


def triple(left, right, dims=((1,), (0,))):
    (left_axis,), (right_axis,) = dims
    if left[0].shape[left_axis] % 128 == 0:
        return multiply(
            jnp.concatenate([left[0], left[0], left[1]], axis=left_axis),
            jnp.concatenate([right[0], right[1], right[0]], axis=right_axis),
            dims,
        )
    return (
        multiply(left[0], right[0], dims)
        + multiply(left[0], right[1], dims)
        + multiply(left[1], right[0], dims)
    )


LANES = ((1,), (1,))


def product(left, right, dims=((1,), (0,))):
    return lax.dot_general(
        left,
        right,
        (dims, ((), ())),
        precision=lax.Precision.HIGH,
        preferred_element_type=jnp.float32,
    )


def lane_pick(table, index):
    return jnp.take_along_axis(table, index, axis=1, mode="promise_in_bounds")


def whole(shape):
    return pl.BlockSpec(tuple(shape), lambda step: (0,) * len(shape))


def whole_specs(*arrays):
    return [whole(array.shape) for array in arrays]


def collect_kernel(
    positions_ref, types_ref, count_ref, send_ref, own_ref, outgoing_ref
):
    atoms = types_ref.shape[1]
    own_ref[...] = jnp.zeros_like(own_ref)
    for axis in range(3):
        own_ref[axis : axis + 1, 0:atoms] = positions_ref[axis]
    own_ref[3:4, 0:atoms] = types_ref[...].astype(jnp.float32)
    own_ref[4:5, 0:atoms] = count_ref[...].astype(jnp.float32)
    own_ref[5:6, 0:atoms] = send_ref[...].astype(jnp.float32)
    for chunk in range(2):
        lanes = slice(128 * chunk, 128 * chunk + 128)
        wanted = jnp.broadcast_to(own_ref[5:6, lanes], (8, 128)).astype(jnp.int32)
        within = wanted & 127
        outgoing_ref[:, lanes] = jnp.where(
            wanted < 128,
            lane_pick(own_ref[:, 0:128], within),
            lane_pick(own_ref[:, 128:256], within),
        )


def collect(positions, types, counts, send_index):
    arrays = (positions, types, counts, send_index)
    result = jax.ShapeDtypeStruct((8, 256), jnp.float32)
    return pl.pallas_call(
        collect_kernel,
        grid=(1,),
        out_shape=[result, result],
        in_specs=whole_specs(*arrays),
        out_specs=whole_specs(result, result),
        compiler_params=pltpu.CompilerParams(vmem_limit_bytes=VMEM_BYTES),
        name="collect_atoms",
    )(*arrays)


def place_kernel(base_ref, cell_x_ref, cell_y_ref, cell_z_ref, fraction_ref, copies_ref):
    atoms = cell_x_ref.shape[1]
    fields = jnp.concatenate(
        [
            cell_x_ref[...].astype(jnp.float32),
            (cell_y_ref[...] + base_ref[0]).astype(jnp.float32),
            cell_z_ref[...].astype(jnp.float32),
        ]
        + [fraction_ref[axis] for axis in range(3)]
        + [jnp.zeros((2, atoms), jnp.float32)],
        axis=0,
    )
    for copy in range(copies_ref.shape[0]):
        copies_ref[copy] = fields


def place_rows(copies, base, cells, fraction):
    arrays = (*cells, fraction)
    result = jax.ShapeDtypeStruct((copies, 8, cells[0].shape[1]), jnp.float32)
    return pl.pallas_call(
        place_kernel,
        grid=(1,),
        out_shape=result,
        in_specs=[pl.BlockSpec(memory_space=pltpu.SMEM)] + whole_specs(*arrays),
        out_specs=whole(result.shape),
        compiler_params=pltpu.CompilerParams(vmem_limit_bytes=VMEM_BYTES),
        name="place_rows",
    )(base, *arrays)


def fitting_rows(descriptor_ref, weight_in_ref, weight_hidden_ref, weight_out_ref):
    hidden = jnp.tanh(product(descriptor_ref[...], weight_in_ref[...], LANES))
    for layer in range(weight_hidden_ref.shape[0]):
        hidden = jnp.tanh(product(hidden, weight_hidden_ref[layer])) + hidden
    width = hidden.shape[1]
    return product(jnp.broadcast_to(weight_out_ref[...], (8, width)), hidden, LANES)


def natural_order(rows):
    atoms = rows.shape[1]
    padded = jnp.concatenate([rows, jnp.zeros((8, 256 - atoms), jnp.float32)], axis=1)
    pieces = []
    for chunk in range(2):
        atom = 128 * chunk + lax.broadcasted_iota(jnp.int32, (8, 128), 1)
        late = atom >= atoms // 2
        within = jnp.where(late, atom - atoms // 2, atom)
        place = 8 * (within >> 2) + (within & 3) + jnp.where(late, 4, 0)
        place = jnp.minimum(place, 255)
        pieces.append(
            jnp.where(
                place < 128,
                lane_pick(padded[:, 0:128], place & 127),
                lane_pick(padded[:, 128:256], place & 127),
            )
        )
    return jnp.concatenate(pieces, axis=1)[0:1, 0:atoms]


def network_kernel(
    ghosts,
    charges_ref,
    own_ref,
    lower_ref,
    upper_ref,
    slots_ref,
    types_ref,
    first_ref,
    second_ref,
    third_ref,
    spot_ref,
    weight_in_hbm,
    weight_hidden_hbm,
    weight_out_ref,
    descriptor_hbm,
    charge_ref,
    copies_ref,
    descriptor_ref,
    environment_ref,
    kind_ref,
    moments_ref,
    padded_ref,
    weight_in_ref,
    weight_hidden_ref,
    semaphores,
):
    fetches = [
        pltpu.make_async_copy(weight_in_hbm, weight_in_ref, semaphores.at[0]),
        pltpu.make_async_copy(weight_hidden_hbm, weight_hidden_ref, semaphores.at[1]),
    ]
    for fetch in fetches:
        fetch.start()
    slots, atoms = slots_ref.shape
    rows = atoms // 2
    lane = lax.broadcasted_iota(jnp.int32, (8, 128), 1)
    sub = lax.broadcasted_iota(jnp.int32, (8, 128), 0)

    width = first_ref.shape[1]
    padded_ref[...] = jnp.zeros_like(padded_ref)
    padded_ref[0, 0:2, 0:width] = first_ref[...]
    for column in range(2):
        padded_ref[1, 0:width, 32 * column : 32 * column + width] = second_ref[
            :, width * column : width * (column + 1)
        ]
    for row in range(2):
        for column in range(4):
            padded_ref[2, 32 * row : 32 * row + width, 32 * column : 32 * column + width] = (
                third_ref[
                    width * row : width * (row + 1), width * column : width * (column + 1)
                ]
            )
    first_table = padded_ref[0].T
    embed_zero = jnp.broadcast_to(first_table[0:32, 0:1], (32, 128))
    embed_one = jnp.broadcast_to(first_table[0:32, 1:2], (32, 128))
    second_high, second_low = split(padded_ref[1].T[0:64, 0:32])
    second_weight = jnp.concatenate([second_high, second_high, second_low], axis=1)
    third_high, third_low = split(padded_ref[2].T[:, 0:64])
    third_weight = jnp.concatenate([third_high, third_high, third_low], axis=1)

    def spread(ref, field, chunk):
        return jnp.broadcast_to(ref[field : field + 1, 128 * chunk : 128 * chunk + 128], (8, 128))

    own = [[spread(own_ref, field, chunk) for chunk in range(2)] for field in range(5)]
    lower = [[spread(lower_ref, field, chunk) for chunk in range(2)] for field in range(4)]
    upper = [spread(upper_ref, field, 0) for field in range(4)]

    def pick_two(tables, index):
        within = index & 127
        return jnp.where(index < 128, lane_pick(tables[0], within), lane_pick(tables[1], within))

    pairs = jnp.concatenate([slots_ref[:, 0:rows], slots_ref[:, rows:atoms]], axis=0).T
    for tile in range(rows // 8):
        band = slice(8 * tile, 8 * tile + 8)
        index = pairs[band, :]
        centre = 8 * tile + sub + jnp.where(lane < 64, 0, rows)
        from_own = jnp.clip(index - ghosts, 0, atoms - 1)
        from_lower = jnp.minimum(index + (atoms - ghosts), 255)
        from_upper = jnp.clip(index - (ghosts + atoms), 0, 127)

        def neighbour(field):
            below = pick_two(lower[field], from_lower)
            inside = pick_two(own[field], from_own)
            above = lane_pick(upper[field], from_upper)
            return jnp.where(
                index < ghosts, below, jnp.where(index < ghosts + atoms, inside, above)
            )

        offsets = [neighbour(field) - pick_two(own[field], centre) for field in range(3)]
        live = pick_two(own[4], centre)
        present = jnp.where((lane & 63).astype(jnp.float32) < live, 1.0, 0.0)
        smooth = present / (
            1.0 + (offsets[0] * offsets[0] + offsets[1] * offsets[1] + offsets[2] * offsets[2])
        )
        environment_ref[0, band, :] = smooth
        for field in range(3):
            environment_ref[1 + field, band, :] = smooth * offsets[field]
        kind_ref[band, :] = neighbour(3)

    group = 8

    def stacked(values):
        high, low = split(values)
        return jnp.concatenate([high, low, high], axis=0)

    def one_group(start):
        pieces = []
        for row in range(group):
            smooth = jnp.broadcast_to(environment_ref[0, pl.ds(start + row, 1), :], (32, 128))
            kind = jnp.broadcast_to(kind_ref[pl.ds(start + row, 1), :], (32, 128))
            pieces.append(
                jnp.tanh(smooth * ((1.0 - kind) * embed_zero + kind * embed_one))
            )
        first = jnp.concatenate(pieces, axis=1)
        second = jnp.tanh(multiply(second_weight, stacked(first), ((1,), (0,))))
        second = second + jnp.concatenate([first, first], axis=0)
        third = jnp.tanh(multiply(third_weight, stacked(second), ((1,), (0,))))
        third = third + jnp.concatenate([second, second], axis=0)
        third_pair = split(third)
        for half in range(group // 4):
            columns = slice(512 * half, 512 * half + 512)
            bands = []
            for part in range(4):
                bands.append(
                    jnp.concatenate(
                        [
                            jnp.where(
                                sub == row + jnp.where(lane < 64, 0, 4),
                                jnp.broadcast_to(
                                    environment_ref[part, pl.ds(start + 4 * half + row, 1), :],
                                    (8, 128),
                                ),
                                0.0,
                            )
                            for row in range(4)
                        ],
                        axis=1,
                    )
                )
            environment = split(jnp.concatenate(bands, axis=0))
            both = multiply(
                jnp.concatenate(environment, axis=0), third_pair[0][:, columns], LANES
            )
            sums = both[0:32] + both[32:64]
            sums = sums + multiply(environment[0], third_pair[1][:, columns], LANES)
            sums = sums * (1.0 / slots)
            for part in range(4):
                moments_ref[part, pl.ds(2 * start + 8 * half, 8), :] = sums[
                    8 * part : 8 * part + 8
                ]

    def body(step, carry):
        for part in range(unroll):
            one_group(pl.multiple_of(step * unroll * group + part * group, group))
        return carry

    unroll = rows // group
    lax.fori_loop(0, rows // (unroll * group), body, 0)

    chunks = (descriptor_ref.shape[1] + 127) // 128
    last = descriptor_ref.shape[1] - 128 * (chunks - 1)

    def describe_band(start):
        band = pl.ds(start, 8)
        moments = [moments_ref[part, band, :] for part in range(4)]
        axis_part = [lane_pick(moments[part], lane & 15) for part in range(4)]
        for chunk in range(chunks):
            spot = jnp.broadcast_to(spot_ref[chunk : chunk + 1, :], (8, 128))
            total = lane_pick(moments[0], spot) * axis_part[0]
            for part in range(1, 4):
                total = total + lane_pick(moments[part], spot) * axis_part[part]
            if chunk < chunks - 1:
                descriptor_ref[band, 128 * chunk : 128 * chunk + 128] = total
            else:
                descriptor_ref[band, 128 * chunk : 128 * chunk + last] = total[:, 0:last]

    bands = 8 if atoms % 64 == 0 else 1

    def describe(step, carry):
        for part in range(bands):
            describe_band(pl.multiple_of(step * 8 * bands + 8 * part, 8))
        return carry

    lax.fori_loop(0, atoms // (8 * bands), describe, 0)

    store = pltpu.make_async_copy(descriptor_ref, descriptor_hbm, semaphores.at[2])
    store.start()
    for fetch in fetches:
        fetch.wait()
    shift = fitting_rows(descriptor_ref, weight_in_ref, weight_hidden_ref, weight_out_ref)
    kind = types_ref[...].astype(jnp.float32)
    charge = (1.0 - kind) * charges_ref[0] + kind * charges_ref[1] + natural_order(shift)
    charge_ref[...] = charge
    for copy in range(copies_ref.shape[0]):
        copies_ref[copy] = charge
    store.wait()


def spot_table(embed, desc):
    column = np.arange(desc) // AXIS
    quarter = embed // 4
    place = 32 * (column // quarter) + column % quarter
    chunks = (desc + 127) // 128
    table = np.zeros((chunks * 128,), np.int32)
    table[:desc] = place
    padded = np.zeros(((chunks + 7) // 8 * 8, 128), np.int32)
    padded[:chunks] = table.reshape(chunks, 128)
    return padded


def networks(
    copies,
    ghosts,
    charge_base,
    own,
    lower,
    upper,
    neighbours,
    types,
    embed,
    weight_in,
    weight_hidden,
    weight_out,
):
    atoms = types.shape[1]
    desc, width = weight_in.shape
    spots = jnp.asarray(spot_table(embed[2].shape[1], desc))
    anywhere = pl.BlockSpec(memory_space=pl.ANY)
    scalars = pl.BlockSpec(memory_space=pltpu.SMEM)
    blocks = (own, lower, upper, neighbours[0].T, types, *embed, spots)
    weight_out = weight_out.reshape(1, -1)
    results = [
        jax.ShapeDtypeStruct((atoms, desc), jnp.float32),
        jax.ShapeDtypeStruct((1, atoms), jnp.float32),
        jax.ShapeDtypeStruct((copies, 1, atoms), jnp.float32),
    ]
    return pl.pallas_call(
        functools.partial(network_kernel, ghosts),
        grid=(1,),
        out_shape=results,
        in_specs=[scalars]
        + whole_specs(*blocks)
        + [anywhere, anywhere]
        + whole_specs(weight_out),
        out_specs=[anywhere] + whole_specs(*results[1:]),
        scratch_shapes=[
            pltpu.VMEM((atoms, desc), jnp.float32),
            pltpu.VMEM((4, atoms // 2, 128), jnp.float32),
            pltpu.VMEM((atoms // 2, 128), jnp.float32),
            pltpu.VMEM((4, atoms, 128), jnp.float32),
            pltpu.VMEM((3, 128, 128), jnp.float32),
            pltpu.VMEM((width, desc), jnp.float32),
            pltpu.VMEM(weight_hidden.shape, jnp.float32),
            pltpu.SemaphoreType.DMA((3,)),
        ],
        compiler_params=pltpu.CompilerParams(vmem_limit_bytes=VMEM_BYTES),
        name="networks",
    )(charge_base, *blocks, weight_in.T, weight_hidden, weight_out)


def energy_kernel(descriptor_ref, weight_in_ref, weight_hidden_ref, weight_out_ref, energy_ref):
    energy_ref[...] = natural_order(
        fitting_rows(descriptor_ref, weight_in_ref, weight_hidden_ref, weight_out_ref)
    )


def energies(descriptor, weight_in, weight_hidden, weight_out):
    atoms, desc = descriptor.shape
    width = weight_in.shape[1]
    arrays = (descriptor, weight_in.T, weight_hidden, weight_out.reshape(1, -1))
    result = jax.ShapeDtypeStruct((1, atoms), jnp.float32)
    return pl.pallas_call(
        energy_kernel,
        grid=(1,),
        out_shape=result,
        in_specs=whole_specs(*arrays),
        out_specs=whole(result.shape),
        compiler_params=pltpu.CompilerParams(vmem_limit_bytes=VMEM_BYTES),
        cost_estimate=pl.CostEstimate(
            flops=6 * atoms * desc * width, bytes_accessed=4 * desc * width, transcendentals=0
        ),
        name="energies",
    )(*arrays)


def weight_rows(fraction):
    square = fraction * fraction
    cubed = square * fraction
    rest = 1.0 - fraction
    return [
        rest * rest * rest / 6.0,
        (3.0 * cubed - 6.0 * square + 4.0) / 6.0,
        (-3.0 * cubed + 3.0 * square + 3.0 * fraction + 1.0) / 6.0,
        cubed / 6.0,
    ]


def placed_weights(distance, weights):
    shape = distance.shape
    result = jnp.zeros(shape, jnp.float32)
    for step in range(4):
        result = jnp.where(
            distance == step, jnp.broadcast_to(weights[step], shape), result
        )
    return result


def third_factors(fields, waves_ref, cosine_ref):
    atoms = fields.shape[1]
    start = fields[2:3, :].astype(jnp.int32)
    along = weight_rows(fields[5:6, :])
    parts = waves_ref.shape[0]
    cosine = jnp.broadcast_to(cosine_ref[...], (parts, 128))
    wave = jnp.broadcast_to(waves_ref[:, 0:1], (parts, 128))
    shift = jnp.broadcast_to(waves_ref[:, 1:2], (parts, 128))
    pieces = []
    for chunk in range(atoms // 128):
        lanes = slice(128 * chunk, 128 * chunk + 128)
        total = jnp.zeros((parts, 128), jnp.float32)
        for step in range(4):
            place = jnp.broadcast_to(start[:, lanes] + step, (parts, 128))
            phase = (wave * place + shift) & (NG - 1)
            value = lane_pick(cosine, phase & 127)
            value = jnp.where(phase < 128, value, -value)
            total = total + value * jnp.broadcast_to(along[step][:, lanes], (parts, 128))
        pieces.append(total)
    return jnp.concatenate(pieces, axis=1)


def first_third_split(fields, waves_ref, cosine_ref, window, scale, high_ref, low_ref):
    atoms = fields.shape[1]
    third = third_factors(fields, waves_ref, cosine_ref) * scale
    rows = lax.broadcasted_iota(jnp.int32, (window, atoms), 0)
    first = placed_weights(
        rows - fields[0:1, :].astype(jnp.int32), weight_rows(fields[3:4, :])
    )
    for chunk in range(atoms // 128):
        lanes = slice(128 * chunk, 128 * (chunk + 1))
        for part in range(0, third.shape[0], 2):
            high, low = split(
                jnp.concatenate(
                    [first[:, lanes] * third[part + side : part + side + 1, lanes] for side in range(2)],
                    axis=0,
                )
            )
            place = slice(part * window, (part + 2) * window)
            high_ref[place, lanes] = high
            low_ref[place, lanes] = low
    return high_ref[...], low_ref[...]


def second_factors(fields, base, block_y, slabs, high_ref, low_ref):
    atoms = fields.shape[1]
    block = atoms // slabs
    reach = block_y + REACH
    start = fields[1:2, :].astype(jnp.int32) - base
    weights = weight_rows(fields[4:5, :])
    for chunk in range(atoms // 128):
        lanes = slice(128 * chunk, 128 * (chunk + 1))
        first = 128 * chunk // block
        last = (128 * chunk + 127) // block
        top = first * block_y
        rows = (last - first) * block_y + reach
        pieces = [(top, min(rows, NG - top))]
        if top + rows > NG:
            pieces.append((0, top + rows - NG))
        for row, count in pieces:
            index = row + lax.broadcasted_iota(jnp.int32, (count, 128), 0)
            table = split(
                placed_weights(
                    (index - start[:, lanes]) & (NG - 1), [weight[:, lanes] for weight in weights]
                )
            )
            high_ref[row : row + count, lanes] = table[0]
            low_ref[row : row + count, lanes] = table[1]
    return high_ref[...], low_ref[...]


def wave_of(index):
    return jnp.where(index <= NG // 2, index, index - NG // 2)


def damping(index):
    kappa = wave_of(index).astype(jnp.float32) * (2.0 * math.pi / NG)
    squared = kappa * kappa
    ends = (index == 0) | (index == NG // 2)
    return squared, jnp.exp(-0.5 * squared) * jnp.where(ends, 1.0 / NG, 2.0 / NG)


def transform(planes, kappa_ref, first_part, tables_ref, last_ref):
    count = len(planes)
    basis = tables_ref[0]
    turned = tables_ref[1]
    square_x, damp_x = damping(lax.broadcasted_iota(jnp.int32, (NG, 1), 0))
    square_y, damp_y = damping(lax.broadcasted_iota(jnp.int32, (1, NG), 1))
    square_xy = square_x + square_y
    damp_xy = damp_x * damp_y
    columns = [slice(NG * part, NG * (part + 1)) for part in range(count)]
    first = product(basis, jnp.concatenate(planes, axis=1))
    first = jnp.concatenate([first[:, column] for column in columns], axis=0)
    both = product(first, turned)
    scaled = []
    for part in range(count):
        squared = square_xy + kappa_ref[first_part + part, 0]
        root = jnp.where(squared == 0.0, 1.0, 0.0)
        green = (1.0 - root) * (damp_xy * kappa_ref[first_part + part, 1]) / (squared + root)
        scaled.append(both[columns[part]] * green)
    back = product(turned, jnp.concatenate(scaled, axis=1))
    back = jnp.concatenate([back[:, column] for column in columns], axis=0)
    return product(back, last_ref[...])


def send_blocks(full, block_x, block_y, put):
    low_lanes = lax.broadcasted_iota(jnp.int32, (NG, 128), 1) < block_y
    for pair in range(full.shape[0] // (2 * NG)):
        even = full[2 * NG * pair : 2 * NG * pair + NG, 0:128]
        odd = full[2 * NG * pair + NG : 2 * NG * (pair + 1), 0:128]
        blocks = [
            jnp.where(low_lanes, even, pltpu.roll(odd, block_y, 1)),
            jnp.where(low_lanes, pltpu.roll(even, block_y, 1), odd),
        ]
        for brick in range(NG // block_x):
            for side in range(2):
                for group in range(block_x // 8):
                    start = block_x * brick + 8 * group
                    put(pair, brick, side, group, blocks[side][start : start + 8])


def spread_kernel(
    block_x,
    block_y,
    window,
    kappa_ref,
    pair_ref,
    static_ref,
    charge_ref,
    waves_ref,
    cosine_ref,
    tables_hbm,
    last_hbm,
    short_hbm,
    sent_ref,
    full_ref,
    atoms_ref,
    later_hbm,
    grid_ref,
    tables_ref,
    last_ref,
    semaphores,
    *pair_refs,
):
    slabs = NG // block_y
    second_refs, first_refs = pair_refs[:4], pair_refs[4:]
    bricks = NG // block_x
    parts = waves_ref.shape[0]
    block = static_ref.shape[2]
    count = full_ref.shape[0]
    step = pl.program_id(0)
    later = later_hbm.shape[0]
    store = pltpu.make_async_copy(
        grid_ref.at[pl.ds(parts - later, later), pl.ds(0, NG)], later_hbm, semaphores.at[2]
    )

    @pl.when(step == 0)
    def _():
        fetches = [
            pltpu.make_async_copy(tables_hbm, tables_ref, semaphores.at[0]),
            pltpu.make_async_copy(last_hbm.at[pair_ref[0]], last_ref, semaphores.at[1]),
        ]
        for fetch in fetches:
            fetch.start()
        for slab in range(slabs):
            lanes = slice(block * slab, block * (slab + 1))
            for brick in range(bricks):
                atoms_ref[brick, :, lanes] = static_ref[slab * bricks + brick]
                atoms_ref[brick, 6:7, lanes] = charge_ref[slab * bricks + brick]
        grid_ref[...] = jnp.zeros_like(grid_ref)
        for ref in second_refs:
            ref[...] = jnp.zeros_like(ref)
        for brick in range(bricks):
            fields = atoms_ref[brick]
            table = first_third_split(
                fields,
                waves_ref,
                cosine_ref,
                window,
                fields[6:7, :],
                first_refs[2 * (brick % 2)],
                first_refs[2 * (brick % 2) + 1],
            )
            second = second_factors(
                fields, 0, block_y, slabs, second_refs[2 * (brick % 2)], second_refs[2 * (brick % 2) + 1]
            )
            spread = triple(table, second, LANES)
            rows = slice(block_x * brick, block_x * brick + window)
            for part in range(parts):
                grid_ref[part, rows, :] += spread[part * window : part * window + window]
        extra = window - block_x
        for part in range(parts):
            grid_ref[part, 0:extra, :] += grid_ref[part, NG : NG + extra, :]
        store.start()
        for fetch in fetches:
            fetch.wait()

    planes = [grid_ref[count * step + part, 0:NG, :] for part in range(count)]
    full = transform(planes, kappa_ref, count * step, tables_ref, last_ref)
    for part in range(count):
        full_ref[part] = full[NG * part : NG * (part + 1)]

    def put(pair, brick, side, group, tile):
        sent_ref[2 * brick + side, group, pair] = tile

    send_blocks(full, block_x, block_y, put)

    @pl.when(step == pl.num_programs(0) - 1)
    def _():
        store.wait()


def early_pairs(parts):
    return parts // 4


def spread_and_solve(
    block_x, block_y, window, kappa, pair, static, charge, waves, cosine_row, tables, last, short
):
    devices, _, atoms = static.shape
    slabs = NG // block_y
    bricks = NG // block_x
    parts = waves.shape[0]
    pairs = early_pairs(parts)
    count = 4
    anywhere = pl.BlockSpec(memory_space=pl.ANY)
    scalars = pl.BlockSpec(memory_space=pltpu.SMEM)
    sent_block = (2 * bricks, block_x // 8, count // 2, 8, 128)
    return pl.pallas_call(
        functools.partial(spread_kernel, block_x, block_y, window),
        grid=(2 * pairs // count,),
        out_shape=[
            jax.ShapeDtypeStruct((2 * bricks, block_x // 8, pairs, 8, 128), jnp.float32),
            jax.ShapeDtypeStruct((2 * pairs, NG, NG), jnp.float32),
            jax.ShapeDtypeStruct((bricks, 8, slabs * atoms), jnp.float32),
            jax.ShapeDtypeStruct((parts - 2 * pairs, NG, NG), jnp.float32),
        ],
        in_specs=[scalars, scalars]
        + whole_specs(static, charge, waves, cosine_row)
        + [anywhere, anywhere, anywhere],
        out_specs=[
            pl.BlockSpec(sent_block, lambda step: (0, 0, step, 0, 0)),
            pl.BlockSpec((count, NG, NG), lambda step: (step, 0, 0)),
            whole((bricks, 8, slabs * atoms)),
            anywhere,
        ],
        scratch_shapes=[
            pltpu.VMEM((parts, NG + window - block_x, NG), jnp.float32),
            pltpu.VMEM(tables.shape, tables.dtype),
            pltpu.VMEM(last.shape[1:], last.dtype),
            pltpu.SemaphoreType.DMA((3,)),
        ]
        + [pltpu.VMEM((NG, slabs * atoms), jnp.bfloat16)] * 4
        + [pltpu.VMEM((parts * window, slabs * atoms), jnp.bfloat16)] * 4,
        compiler_params=pltpu.CompilerParams(vmem_limit_bytes=VMEM_BYTES),
        name="spread_and_solve",
    )(kappa, pair, static, charge, waves, cosine_row, tables, last, short)


def sample_kernel(
    block_x,
    block_y,
    window,
    kappa_ref,
    pair_ref,
    atoms_ref,
    waves_ref,
    cosine_ref,
    tables_hbm,
    last_hbm,
    later_hbm,
    early_hbm,
    sent_ref,
    later_ref,
    full_ref,
    tables_ref,
    last_ref,
    semaphores,
    packed_ref,
):
    bricks = atoms_ref.shape[0]
    parts = waves_ref.shape[0]
    early = 2 * early_pairs(parts)
    block = atoms_ref.shape[2] * block_y // NG
    fetches = [
        pltpu.make_async_copy(tables_hbm, tables_ref, semaphores.at[0]),
        pltpu.make_async_copy(last_hbm.at[pair_ref[0]], last_ref, semaphores.at[1]),
        pltpu.make_async_copy(later_hbm, later_ref, semaphores.at[2]),
        pltpu.make_async_copy(early_hbm, full_ref.at[pl.ds(0, early)], semaphores.at[3]),
    ]
    for fetch in fetches:
        fetch.start()
    for fetch in fetches[:3]:
        fetch.wait()
    pairs = (parts - early) // 2
    planes = [later_ref[part] for part in range(parts - early)]
    full = transform(planes, kappa_ref, early, tables_ref, last_ref)
    for part in range(parts - early):
        full_ref[early + part] = full[NG * part : NG * (part + 1)]

    def put(pair, brick, side, group, tile):
        sent_ref[2 * brick + side, pairs * group + pair] = tile

    send_blocks(full, block_x, block_y, put)
    fetches[3].wait()

    reach = block_y + REACH
    lane = lax.broadcasted_iota(jnp.int32, (NG, 128), 1)
    for part in range(parts):
        for side in range(2):
            values = full_ref[part, :, 128 * side : 128 * (side + 1)]
            high = values.astype(jnp.bfloat16).astype(jnp.float32)
            again = pltpu.roll(high, reach, 1)
            low = pltpu.roll(values - high, 2 * reach - 128, 1)
            packed_ref[side, part, 0:NG, 0:128] = jnp.where(lane < reach, high, again)
            packed_ref[side, part, 0:NG, 128:NG] = jnp.where(
                lane < 2 * reach - 128, again, jnp.where(lane < 3 * reach - 128, low, 0.0)
            )
            packed_ref[side, part, NG : NG + window - block_x, :] = packed_ref[
                side, part, 0 : window - block_x, :
            ]
    extra = sent_ref.shape[1] - 1
    base = 2 * block_y * pair_ref[0]
    lanes = pl.ds(pl.multiple_of(2 * block * pair_ref[0], 128), 2 * block)
    for brick in range(bricks):
        fields = atoms_ref[brick, :, lanes]
        thirds = third_factors(fields, waves_ref, cosine_ref)
        rows = slice(block_x * brick, block_x * brick + window)
        for side in range(2):
            here = slice(block * side, block * (side + 1))
            third = thirds[:, here]
            ours = fields[:, here]
            index = lax.broadcasted_iota(jnp.int32, (window, block), 0)
            first = placed_weights(
                index - ours[0:1, :].astype(jnp.int32), weight_rows(ours[3:4, :])
            )
            index = lax.broadcasted_iota(jnp.int32, (reach, block), 0)
            start = ours[1:2, :].astype(jnp.int32) - (base + block_y * side)
            high, low = split(placed_weights(index - start, weight_rows(ours[4:5, :])))
            rest = jnp.zeros((NG - 3 * reach, block), jnp.bfloat16)
            second = jnp.concatenate([high, low, high, rest], axis=0)
            values = jnp.concatenate(
                [packed_ref[side, part, rows, :] for part in range(parts)], axis=0
            )
            along = multiply(values.astype(jnp.bfloat16), second, ((1,), (0,)))
            total = jnp.zeros((window, block), jnp.float32)
            for part in range(parts):
                total = total + along[window * part : window * (part + 1)] * third[part : part + 1]
            row = jnp.sum(total * first, axis=0, keepdims=True)
            sent_ref[2 * brick + side, extra] = jnp.zeros((8, 128), jnp.float32)
            sent_ref[2 * brick + side, extra, 0:1, :] = row[:, 0:128]
            sent_ref[2 * brick + side, extra, 1:2, 0 : block - 128] = row[:, 128:block]


def solve_and_sample(
    block_x, block_y, window, kappa, pair, atoms, waves, cosine_row, tables, last, later, early
):
    bricks = atoms.shape[0]
    parts = waves.shape[0]
    pairs = parts // 2 - early_pairs(parts)
    anywhere = pl.BlockSpec(memory_space=pl.ANY)
    scalars = pl.BlockSpec(memory_space=pltpu.SMEM)
    result = jax.ShapeDtypeStruct((2 * bricks, block_x // 8 * pairs + 1, 8, 128), jnp.float32)
    return pl.pallas_call(
        functools.partial(sample_kernel, block_x, block_y, window),
        grid=(1,),
        out_shape=result,
        in_specs=[scalars, scalars] + whole_specs(atoms, waves, cosine_row) + [anywhere] * 4,
        out_specs=whole(result.shape),
        scratch_shapes=[
            pltpu.VMEM((2 * pairs, NG, NG), jnp.float32),
            pltpu.VMEM((parts, NG, NG), jnp.float32),
            pltpu.VMEM(tables.shape, tables.dtype),
            pltpu.VMEM(last.shape[1:], last.dtype),
            pltpu.SemaphoreType.DMA((4,)),
        ]
        + [pltpu.VMEM((2, parts, NG + window - block_x, NG), jnp.float32)],
        compiler_params=pltpu.CompilerParams(vmem_limit_bytes=VMEM_BYTES),
        cost_estimate=pl.CostEstimate(
            flops=24 * parts * NG * NG * NG, bytes_accessed=4 * early.size, transcendentals=0
        ),
        name="solve_and_sample",
    )(kappa, pair, atoms, waves, cosine_row, tables, last, later, early)


def finish_kernel(
    block_y,
    early_ref,
    later_ref,
    sums_ref,
    short_hbm,
    charge_hbm,
    table_ref,
    out_ref,
    energy_ref,
    short_ref,
    charge_ref,
    semaphores,
):
    atoms = short_ref.shape[1]
    fetches = [
        pltpu.make_async_copy(short_hbm, short_ref, semaphores.at[0]),
        pltpu.make_async_copy(charge_hbm, charge_ref, semaphores.at[1]),
    ]

    @pl.when(pl.program_id(0) == 0)
    def _():
        for fetch in fetches:
            fetch.start()

    lines = early_ref.shape[3]
    sources, _, pairs = early_ref.shape[:3]
    early = early_ref.reshape(sources * pairs, lines, 128)
    later = later_ref.reshape(sources * later_ref.shape[1], lines, 128)
    pieces = []
    for line in range(lines):
        turned = jnp.concatenate([early[:, line, :], later[:, line, :]], axis=0).T
        pieces.append(jnp.concatenate([turned[0:block_y], turned[block_y:]], axis=1))
    result = product(jnp.concatenate(pieces, axis=0), table_ref[...])
    for line in range(lines):
        out_ref[line] = result[block_y * line : block_y * (line + 1)]

    @pl.when(pl.program_id(0) == 0)
    def _():
        for fetch in fetches:
            fetch.wait()
        total = jnp.sum(sums_ref[:, 0], axis=0)
        potential_at = jnp.concatenate([total[0:1, :], total[1:2, 0 : atoms - 128]], axis=1)
        energy_ref[...] = short_ref[...] + 0.5 * charge_ref[...] * potential_at


def finish(block_x, block_y, early, later, short, charge, table):
    bricks2, groups, pairs = early.shape[:3]
    rest = (later.shape[1] - 1) // groups
    atoms = short.shape[1]
    return pl.pallas_call(
        functools.partial(finish_kernel, block_y),
        grid=(groups,),
        out_shape=[
            jax.ShapeDtypeStruct((block_x, block_y, NG), jnp.float32),
            jax.ShapeDtypeStruct((1, atoms), jnp.float32),
        ],
        in_specs=[
            pl.BlockSpec((bricks2, 1, pairs, 8, 128), lambda index: (0, index, 0, 0, 0)),
            pl.BlockSpec((bricks2, rest, 8, 128), lambda index: (0, index, 0, 0)),
            pl.BlockSpec((bricks2, 1, 8, 128), lambda index: (0, groups * rest, 0, 0)),
            pl.BlockSpec(memory_space=pltpu.HBM),
            pl.BlockSpec(memory_space=pltpu.HBM),
            whole(table.shape),
        ],
        out_specs=[
            pl.BlockSpec((8, block_y, NG), lambda index: (index, 0, 0)),
            whole((1, atoms)),
        ],
        scratch_shapes=[
            pltpu.VMEM((1, atoms), jnp.float32),
            pltpu.VMEM((1, atoms), jnp.float32),
            pltpu.SemaphoreType.DMA((2,)),
        ],
        compiler_params=pltpu.CompilerParams(vmem_limit_bytes=32 * 2**20),
        name="finish",
    )(early, later, later, short, charge, table)


def real_basis():
    index = np.arange(NG)
    wave = np.where(index <= NG // 2, index, index - NG // 2)
    angle = (wave[:, None] * index[None, :] % NG) * (2.0 * math.pi / NG)
    return np.where((index <= NG // 2)[:, None], np.cos(angle), np.sin(angle))


def per_device(
    positions,
    types,
    neighbours,
    neighbour_count,
    send_index,
    cell_x,
    cell_y,
    cell_z,
    spline_fraction,
    embed_first,
    embed_second,
    embed_third,
    energy_in,
    energy_hidden,
    energy_out,
    wannier_in,
    wannier_hidden,
    wannier_out,
    charge_base,
):
    atoms = types.shape[1]
    ghosts = send_index.shape[1] // 2
    count_x = lax.axis_size("brick")
    count_y = lax.axis_size("slab")
    block_x = NG // count_x
    block_y = NG // count_y
    window = block_x + 8
    parts = NG // (2 * count_x)
    brick = lax.axis_index("brick")
    slab = lax.axis_index("slab")
    pair = (slab // 2).astype(jnp.int32).reshape(1)
    halves = [
        [b * count_y + 2 * p + side for b in range(count_x) for side in range(2)]
        for p in range(count_y // 2)
    ]

    def exchange(values, axes, groups=None):
        return lax.all_to_all(
            values, axes, split_axis=0, concat_axis=0, tiled=True, axis_index_groups=groups
        )

    own, outgoing = collect(positions, types, neighbour_count, send_index)
    up = [(i, (i + 1) % count_x) for i in range(count_x)]
    down = [((i + 1) % count_x, i) for i in range(count_x)]
    lower = lax.ppermute(outgoing, "brick", up)
    upper = lax.ppermute(outgoing, "brick", down)
    places = place_rows(
        count_x * count_y,
        (slab * block_y).astype(jnp.int32).reshape(1),
        (cell_x, cell_y, cell_z),
        spline_fraction,
    )
    every_place = exchange(places, ("slab", "brick"))
    descriptor, charge, charge_copies = networks(
        count_x * count_y,
        ghosts,
        charge_base,
        own,
        lower,
        upper,
        neighbours,
        types,
        (embed_first, embed_second, embed_third),
        wannier_in,
        wannier_hidden,
        wannier_out,
    )
    charge_copies, every_place = lax.optimization_barrier((charge_copies, every_place))
    every_charge = exchange(charge_copies, ("slab", "brick"))

    part = (2 * brick + slab % 2) * parts + jnp.arange(parts, dtype=jnp.int32)
    wave = wave_of(part)
    waves = jnp.stack([wave, jnp.where(part <= NG // 2, 0, 3 * NG // 4)], axis=1)
    kappa = wave.astype(jnp.float32) * (2.0 * math.pi / NG)
    squared = kappa * kappa
    ends = (part == 0) | (part == NG // 2)
    kappa = jnp.stack(
        [squared, jnp.exp(-0.5 * squared) * jnp.where(ends, 1.0 / NG, 2.0 / NG)], axis=1
    )
    basis = real_basis()
    tables = np.stack([basis, basis.T]).astype(np.float32)
    last = []
    for p in range(count_y // 2):
        points = np.concatenate(
            [np.arange(2 * block_y), block_y + np.arange(block_y + REACH)]
        )
        points = (2 * block_y * p + points) % NG
        columns = np.zeros((NG, NG))
        columns[:, : points.size] = basis[:, points]
        last.append(columns.astype(np.float32))
    cosine_row = np.cos(np.arange(128) * (2.0 * math.pi / NG)).astype(np.float32)[None]
    cosine_row = jnp.asarray(cosine_row)
    tables = jnp.asarray(tables)
    last = jnp.asarray(np.stack(last))
    energy_short = energies(descriptor, energy_in, energy_hidden, energy_out)
    early, full, every_atom, later = spread_and_solve(
        block_x,
        block_y,
        window,
        kappa,
        pair,
        every_place,
        every_charge,
        waves,
        cosine_row,
        tables,
        last,
        energy_short,
    )

    def send(values):
        got = exchange(values.reshape(values.shape[0], -1, 128), ("brick", "slab"), halves)
        return got.reshape(values.shape)

    early = send(early)
    later = solve_and_sample(
        block_x,
        block_y,
        window,
        kappa,
        pair,
        every_atom,
        waves,
        cosine_row,
        tables,
        last,
        later,
        full,
    )
    later = send(later)
    source = np.arange(2 * count_x)[:, None] * parts
    pairs = 2 * np.arange(parts // 2)[None, :]
    order = np.concatenate(
        [
            (source + pairs[:, : early_pairs(parts)]).ravel(),
            (source + pairs[:, early_pairs(parts) :]).ravel(),
        ]
    )
    order = np.concatenate([order, order + 1])
    potential, atom_energy = finish(
        block_x,
        block_y,
        early,
        later,
        energy_short,
        charge,
        jnp.asarray(basis[order].astype(np.float32)),
    )
    return atom_energy, potential


def solution(mesh):
    placed = (
        P(None, "slab", "brick"),
        P("slab", "brick"),
        P("slab", "brick", None),
        P("slab", "brick"),
        P("slab", "brick"),
        P("slab", "brick"),
        P("slab", "brick"),
        P("slab", "brick"),
        P(None, "slab", "brick"),
    ) + (P(),) * 10
    bricks, slabs = mesh.shape["brick"], mesh.shape["slab"]
    fits = 2 * NG == 128 * slabs and NG % (32 * bricks) == 0
    return jax.shard_map(
        per_device if fits else per_device_general,
        mesh=mesh,
        in_specs=placed,
        out_specs=(P("slab", "brick"), P("brick", "slab", None)),
        check_vma=False,
    )
```

```python
import functools
import math

import jax
import jax.numpy as jnp
import numpy as np
from jax import lax
from jax.experimental import pallas as pl
from jax.experimental.pallas import tpu as pltpu
from jax.sharding import PartitionSpec as P

NG = 256
AXIS = 16
VMEM_BYTES = 60 * 2**20
REACH = 16


HIGH = lax.Precision.HIGHEST


def with_halo(cells, sides, width):
    for axis, dim in sides:
        count = lax.axis_size(axis)
        head = lax.slice_in_dim(cells, 0, width, axis=dim)
        tail = lax.slice_in_dim(cells, cells.shape[dim] - width, cells.shape[dim], axis=dim)
        cells = jnp.concatenate(
            [
                lax.ppermute(tail, axis, [(i, (i + 1) % count) for i in range(count)]),
                cells,
                lax.ppermute(head, axis, [((i + 1) % count, i) for i in range(count)]),
            ],
            axis=dim,
        )
    return cells


def spline_weights(fraction):
    cubed = fraction * fraction * fraction
    square = fraction * fraction
    return jnp.stack(
        [
            (1.0 - fraction) * (1.0 - fraction) * (1.0 - fraction) / 6.0,
            (3.0 * cubed - 6.0 * square + 4.0) / 6.0,
            (-3.0 * cubed + 3.0 * square + 3.0 * fraction + 1.0) / 6.0,
            cubed / 6.0,
        ]
    )


def fitting(descriptor, weight_in, weight_hidden, weight_out):
    hidden = jnp.tanh(jnp.dot(descriptor, weight_in, precision=HIGH))
    for depth_index in range(weight_hidden.shape[0]):
        hidden = jnp.tanh(jnp.dot(hidden, weight_hidden[depth_index], precision=HIGH)) + hidden
    return jnp.dot(hidden, weight_out, precision=HIGH)


def atom_terms(
    extended,
    neighbour_rows,
    neighbour_total,
    embed_first,
    embed_second,
    embed_third,
    energy_in,
    energy_hidden,
    energy_out,
    wannier_in,
    wannier_hidden,
    wannier_out,
):
    atom_count, slots = neighbour_rows.shape
    ghost_rows = (extended.shape[1] - atom_count) // 2
    block_size = 64
    blocks = atom_count // block_size
    present = (jnp.arange(slots, dtype=jnp.int32)[None, :] < neighbour_total[:, None]).astype(
        jnp.float32
    )
    centre_ids = (ghost_rows + jnp.arange(atom_count, dtype=jnp.int32)).reshape(blocks, block_size)
    second_weight = embed_second.T
    third_weight = embed_third.T

    def one_block(pieces):
        centre_rows, rows_block, present_block = pieces
        centre_block = extended[:3, centre_rows]
        gathered = extended[:, rows_block]
        offsets = gathered[:3] - centre_block[:, :, None]
        smooth = present_block / (1.0 + jnp.sum(offsets * offsets, axis=0))
        environment = jnp.stack(
            [smooth, smooth * offsets[0], smooth * offsets[1], smooth * offsets[2]], axis=0
        )
        kind = gathered[3][None]
        mixing = (1.0 - kind) * embed_first[0][:, None, None] + kind * embed_first[1][:, None, None]
        first = jnp.tanh(smooth[None] * mixing).reshape(embed_first.shape[1], block_size * slots)
        second = jnp.tanh(jnp.dot(second_weight, first, precision=HIGH)) + jnp.concatenate(
            [first, first], axis=0
        )
        third = jnp.tanh(jnp.dot(third_weight, second, precision=HIGH)) + jnp.concatenate(
            [second, second], axis=0
        )
        third_blocks = third.reshape(third.shape[0], block_size, slots)
        moments = jnp.einsum("kan,can->akc", third_blocks, environment, precision=HIGH) / slots
        descriptor = jnp.einsum("amc,akc->amk", moments, moments[:, :AXIS], precision=HIGH).reshape(
            block_size, -1
        )
        return (
            fitting(descriptor, energy_in, energy_hidden, energy_out),
            fitting(descriptor, wannier_in, wannier_hidden, wannier_out),
        )

    energy_short, charge_shift = lax.map(
        one_block,
        (
            centre_ids,
            neighbour_rows.reshape(blocks, block_size, slots),
            present.reshape(blocks, block_size, slots),
        ),
    )
    return (energy_short.reshape(atom_count), charge_shift.reshape(atom_count))


def green_table(first, second, third, size):

    def folded(index):
        return jnp.where(index < size // 2, index, index - size).astype(jnp.float32) * (
            2.0 * math.pi / size
        )

    kappa_x = folded(first)[:, None, None]
    kappa_y = folded(second)[None, :, None]
    kappa_z = folded(third)[None, None, :]
    squared = kappa_x * kappa_x + kappa_y * kappa_y + kappa_z * kappa_z
    root = (
        (first[:, None, None] == 0) & (second[None, :, None] == 0) & (third[None, None, :] == 0)
    ).astype(jnp.float32)
    return (1.0 - root) * jnp.exp(-0.5 * squared) / (squared + root)


def dft_tables(size):
    index = jnp.arange(size, dtype=jnp.int32)
    phase = (index[:, None] * index[None, :] % size).astype(jnp.float32) * (2.0 * math.pi / size)
    return (jnp.cos(phase), jnp.sin(phase))


def along(values, table, axis_index):
    result = jnp.tensordot(values, table, axes=([axis_index], [0]), precision=HIGH)
    return jnp.moveaxis(result, -1, axis_index)


def complex_transform(paired, axis_index, cosine, sine, inverse):
    real_part = paired[0]
    imag_part = paired[1]
    inner = axis_index - 1
    real_cos = along(real_part, cosine, inner)
    real_sin = along(real_part, sine, inner)
    imag_cos = along(imag_part, cosine, inner)
    imag_sin = along(imag_part, sine, inner)
    if inverse:
        return jnp.stack([real_cos - imag_sin, imag_cos + real_sin])
    return jnp.stack([real_cos + imag_sin, imag_cos - real_sin])


def fold_windows(values, axis_index, block, count):
    front = jnp.moveaxis(values, axis_index, 0)
    rest = front.shape[1:]
    windows = front.reshape((count, block + 3) + rest)
    main_part = windows[:, :block]
    carried = jnp.roll(windows[:, block:], 1, axis=0)
    main_part = main_part.at[:, :3].add(carried)
    return jnp.moveaxis(main_part.reshape((count * block,) + rest), 0, axis_index)


def make_windows(values, axis_index, block, count):
    front = jnp.moveaxis(values, axis_index, 0)
    rest = front.shape[1:]
    pieces = front.reshape((count, block) + rest)
    trailing = jnp.roll(pieces, -1, axis=0)[:, :3]
    windows = jnp.concatenate([pieces, trailing], axis=1)
    return jnp.moveaxis(windows.reshape((count * (block + 3),) + rest), 0, axis_index)


def spread_matrix(start, weights, width, wrap_size):
    offsets = jnp.arange(4, dtype=jnp.int32)[:, None, None]
    target = start[None, :, None] + offsets
    if wrap_size > 0:
        target = target % wrap_size
    hits = (target == jnp.arange(width, dtype=jnp.int32)[None, None, :]).astype(jnp.float32)
    return jnp.sum(weights[:, :, None] * hits, axis=0)


def per_device_general(
    positions,
    types,
    neighbours,
    neighbour_count,
    send_index,
    cell_x,
    cell_y,
    cell_z,
    spline_fraction,
    embed_first,
    embed_second,
    embed_third,
    energy_in,
    energy_hidden,
    energy_out,
    wannier_in,
    wannier_hidden,
    wannier_out,
    charge_base,
):
    atom_count = types.shape[1]
    ghost_rows = send_index.shape[1] // 2
    kind_float = types[0].astype(jnp.float32)
    own_atoms = jnp.concatenate([positions[:, 0], kind_float[None]], axis=0)
    outgoing = own_atoms[:, send_index[0]]
    padded_ghosts = with_halo(outgoing, (("brick", 1),), ghost_rows)
    extended = jnp.concatenate(
        [padded_ghosts[:, :ghost_rows], own_atoms, padded_ghosts[:, 3 * ghost_rows :]], axis=1
    )
    energy_short, charge_shift = atom_terms(
        extended,
        neighbours[0],
        neighbour_count[0],
        embed_first,
        embed_second,
        embed_third,
        energy_in,
        energy_hidden,
        energy_out,
        wannier_in,
        wannier_hidden,
        wannier_out,
    )
    charge = (1.0 - kind_float) * charge_base[0] + kind_float * charge_base[1] + charge_shift
    count_x = lax.axis_size("brick")
    count_y = lax.axis_size("slab")
    block_x = NG // count_x
    block_y = NG // count_y
    wide_x = block_x + 3
    wide_y = block_y + 3
    spread_x = spread_matrix(cell_x[0], spline_weights(spline_fraction[0, 0]), wide_x, 0)
    spread_y = spread_matrix(cell_y[0], spline_weights(spline_fraction[1, 0]), wide_y, 0)
    spread_z = spread_matrix(cell_z[0], spline_weights(spline_fraction[2, 0]), NG, NG)
    spread_xy = (spread_x[:, :, None] * spread_y[:, None, :]).reshape(atom_count, wide_x * wide_y)
    charge_grid = jnp.einsum(
        "ap,az->pz", spread_xy, charge[:, None] * spread_z, precision=HIGH
    ).reshape(wide_x, wide_y, NG)
    cosine, sine = dft_tables(NG)
    scale = 1.0 / (NG * NG * NG)
    full_index = jnp.arange(NG, dtype=jnp.int32)
    paired = jnp.stack([along(charge_grid, cosine, 2), -along(charge_grid, sine, 2)])
    moved = lax.all_to_all(paired, "slab", split_axis=3, concat_axis=2, tiled=True)
    moved = complex_transform(fold_windows(moved, 2, block_y, count_y), 2, cosine, sine, False)
    moved = lax.all_to_all(moved, "brick", split_axis=2, concat_axis=1, tiled=True)
    moved = complex_transform(fold_windows(moved, 1, block_x, count_x), 1, cosine, sine, False)
    part_y = NG // count_x
    part_z = NG // count_y
    index_y = lax.axis_index("brick") * part_y + jnp.arange(part_y, dtype=jnp.int32)
    index_z = lax.axis_index("slab") * part_z + jnp.arange(part_z, dtype=jnp.int32)
    moved = moved * (green_table(full_index, index_y, index_z, NG) * scale)[None]
    moved = make_windows(complex_transform(moved, 1, cosine, sine, True), 1, block_x, count_x)
    moved = lax.all_to_all(moved, "brick", split_axis=1, concat_axis=2, tiled=True)
    moved = make_windows(complex_transform(moved, 2, cosine, sine, True), 2, block_y, count_y)
    moved = lax.all_to_all(moved, "slab", split_axis=2, concat_axis=3, tiled=True)
    potential_wide = along(moved[0], cosine, 2) - along(moved[1], sine, 2)
    sampled = jnp.einsum(
        "ap,pz->az", spread_xy, potential_wide.reshape(wide_x * wide_y, NG), precision=HIGH
    )
    potential_at = jnp.sum(sampled * spread_z, axis=1)
    atom_energy = energy_short + 0.5 * charge * potential_at
    return (atom_energy[None, :], potential_wide[:block_x, :block_y])


def split(values):
    high = values.astype(jnp.bfloat16)
    low = (values - high.astype(jnp.float32)).astype(jnp.bfloat16)
    return high, low


def multiply(left, right, dims):
    return lax.dot_general(left, right, (dims, ((), ())), preferred_element_type=jnp.float32)


def triple(left, right, dims=((1,), (0,))):
    (left_axis,), (right_axis,) = dims
    if left[0].shape[left_axis] % 128 == 0:
        return multiply(
            jnp.concatenate([left[0], left[0], left[1]], axis=left_axis),
            jnp.concatenate([right[0], right[1], right[0]], axis=right_axis),
            dims,
        )
    return (
        multiply(left[0], right[0], dims)
        + multiply(left[0], right[1], dims)
        + multiply(left[1], right[0], dims)
    )


LANES = ((1,), (1,))


def product(left, right, dims=((1,), (0,))):
    return lax.dot_general(
        left,
        right,
        (dims, ((), ())),
        precision=lax.Precision.HIGH,
        preferred_element_type=jnp.float32,
    )


def lane_pick(table, index):
    return jnp.take_along_axis(table, index, axis=1, mode="promise_in_bounds")


def whole(shape):
    return pl.BlockSpec(tuple(shape), lambda step: (0,) * len(shape))


def whole_specs(*arrays):
    return [whole(array.shape) for array in arrays]


def collect_kernel(
    positions_ref, types_ref, count_ref, send_ref, own_ref, outgoing_ref
):
    atoms = types_ref.shape[1]
    own_ref[...] = jnp.zeros_like(own_ref)
    for axis in range(3):
        own_ref[axis : axis + 1, 0:atoms] = positions_ref[axis]
    own_ref[3:4, 0:atoms] = types_ref[...].astype(jnp.float32)
    own_ref[4:5, 0:atoms] = count_ref[...].astype(jnp.float32)
    own_ref[5:6, 0:atoms] = send_ref[...].astype(jnp.float32)
    for chunk in range(2):
        lanes = slice(128 * chunk, 128 * chunk + 128)
        wanted = jnp.broadcast_to(own_ref[5:6, lanes], (8, 128)).astype(jnp.int32)
        within = wanted & 127
        outgoing_ref[:, lanes] = jnp.where(
            wanted < 128,
            lane_pick(own_ref[:, 0:128], within),
            lane_pick(own_ref[:, 128:256], within),
        )


def collect(positions, types, counts, send_index):
    arrays = (positions, types, counts, send_index)
    result = jax.ShapeDtypeStruct((8, 256), jnp.float32)
    return pl.pallas_call(
        collect_kernel,
        grid=(1,),
        out_shape=[result, result],
        in_specs=whole_specs(*arrays),
        out_specs=whole_specs(result, result),
        compiler_params=pltpu.CompilerParams(vmem_limit_bytes=VMEM_BYTES),
        name="collect_atoms",
    )(*arrays)


def place_kernel(base_ref, cell_x_ref, cell_y_ref, cell_z_ref, fraction_ref, copies_ref):
    atoms = cell_x_ref.shape[1]
    fields = jnp.concatenate(
        [
            cell_x_ref[...].astype(jnp.float32),
            (cell_y_ref[...] + base_ref[0]).astype(jnp.float32),
            cell_z_ref[...].astype(jnp.float32),
        ]
        + [fraction_ref[axis] for axis in range(3)]
        + [jnp.zeros((2, atoms), jnp.float32)],
        axis=0,
    )
    for copy in range(copies_ref.shape[0]):
        copies_ref[copy] = fields


def place_rows(copies, base, cells, fraction):
    arrays = (*cells, fraction)
    result = jax.ShapeDtypeStruct((copies, 8, cells[0].shape[1]), jnp.float32)
    return pl.pallas_call(
        place_kernel,
        grid=(1,),
        out_shape=result,
        in_specs=[pl.BlockSpec(memory_space=pltpu.SMEM)] + whole_specs(*arrays),
        out_specs=whole(result.shape),
        compiler_params=pltpu.CompilerParams(vmem_limit_bytes=VMEM_BYTES),
        name="place_rows",
    )(base, *arrays)


def fitting_rows(descriptor_ref, weight_in_ref, weight_hidden_ref, weight_out_ref):
    hidden = jnp.tanh(product(descriptor_ref[...], weight_in_ref[...], LANES))
    for layer in range(weight_hidden_ref.shape[0]):
        hidden = jnp.tanh(product(hidden, weight_hidden_ref[layer])) + hidden
    width = hidden.shape[1]
    return product(jnp.broadcast_to(weight_out_ref[...], (8, width)), hidden, LANES)


def natural_order(rows):
    atoms = rows.shape[1]
    padded = jnp.concatenate([rows, jnp.zeros((8, 256 - atoms), jnp.float32)], axis=1)
    pieces = []
    for chunk in range(2):
        atom = 128 * chunk + lax.broadcasted_iota(jnp.int32, (8, 128), 1)
        late = atom >= atoms // 2
        within = jnp.where(late, atom - atoms // 2, atom)
        place = 8 * (within >> 2) + (within & 3) + jnp.where(late, 4, 0)
        place = jnp.minimum(place, 255)
        pieces.append(
            jnp.where(
                place < 128,
                lane_pick(padded[:, 0:128], place & 127),
                lane_pick(padded[:, 128:256], place & 127),
            )
        )
    return jnp.concatenate(pieces, axis=1)[0:1, 0:atoms]


def network_kernel(
    ghosts,
    charges_ref,
    own_ref,
    lower_ref,
    upper_ref,
    slots_ref,
    types_ref,
    first_ref,
    second_ref,
    third_ref,
    spot_ref,
    weight_in_hbm,
    weight_hidden_hbm,
    weight_out_ref,
    descriptor_hbm,
    charge_ref,
    copies_ref,
    descriptor_ref,
    environment_ref,
    kind_ref,
    moments_ref,
    padded_ref,
    weight_in_ref,
    weight_hidden_ref,
    semaphores,
):
    fetches = [
        pltpu.make_async_copy(weight_in_hbm, weight_in_ref, semaphores.at[0]),
        pltpu.make_async_copy(weight_hidden_hbm, weight_hidden_ref, semaphores.at[1]),
    ]
    for fetch in fetches:
        fetch.start()
    slots, atoms = slots_ref.shape
    rows = atoms // 2
    lane = lax.broadcasted_iota(jnp.int32, (8, 128), 1)
    sub = lax.broadcasted_iota(jnp.int32, (8, 128), 0)

    width = first_ref.shape[1]
    padded_ref[...] = jnp.zeros_like(padded_ref)
    padded_ref[0, 0:2, 0:width] = first_ref[...]
    for column in range(2):
        padded_ref[1, 0:width, 32 * column : 32 * column + width] = second_ref[
            :, width * column : width * (column + 1)
        ]
    for row in range(2):
        for column in range(4):
            padded_ref[2, 32 * row : 32 * row + width, 32 * column : 32 * column + width] = (
                third_ref[
                    width * row : width * (row + 1), width * column : width * (column + 1)
                ]
            )
    first_table = padded_ref[0].T
    embed_zero = jnp.broadcast_to(first_table[0:32, 0:1], (32, 128))
    embed_one = jnp.broadcast_to(first_table[0:32, 1:2], (32, 128))
    second_high, second_low = split(padded_ref[1].T[0:64, 0:32])
    second_weight = jnp.concatenate([second_high, second_high, second_low], axis=1)
    third_high, third_low = split(padded_ref[2].T[:, 0:64])
    third_weight = jnp.concatenate([third_high, third_high, third_low], axis=1)

    def spread(ref, field, chunk):
        return jnp.broadcast_to(ref[field : field + 1, 128 * chunk : 128 * chunk + 128], (8, 128))

    own = [[spread(own_ref, field, chunk) for chunk in range(2)] for field in range(5)]
    lower = [[spread(lower_ref, field, chunk) for chunk in range(2)] for field in range(4)]
    upper = [spread(upper_ref, field, 0) for field in range(4)]

    def pick_two(tables, index):
        within = index & 127
        return jnp.where(index < 128, lane_pick(tables[0], within), lane_pick(tables[1], within))

    pairs = jnp.concatenate([slots_ref[:, 0:rows], slots_ref[:, rows:atoms]], axis=0).T
    for tile in range(rows // 8):
        band = slice(8 * tile, 8 * tile + 8)
        index = pairs[band, :]
        centre = 8 * tile + sub + jnp.where(lane < 64, 0, rows)
        from_own = jnp.clip(index - ghosts, 0, atoms - 1)
        from_lower = jnp.minimum(index + (atoms - ghosts), 255)
        from_upper = jnp.clip(index - (ghosts + atoms), 0, 127)

        def neighbour(field):
            below = pick_two(lower[field], from_lower)
            inside = pick_two(own[field], from_own)
            above = lane_pick(upper[field], from_upper)
            return jnp.where(
                index < ghosts, below, jnp.where(index < ghosts + atoms, inside, above)
            )

        offsets = [neighbour(field) - pick_two(own[field], centre) for field in range(3)]
        live = pick_two(own[4], centre)
        present = jnp.where((lane & 63).astype(jnp.float32) < live, 1.0, 0.0)
        smooth = present / (
            1.0 + (offsets[0] * offsets[0] + offsets[1] * offsets[1] + offsets[2] * offsets[2])
        )
        environment_ref[0, band, :] = smooth
        for field in range(3):
            environment_ref[1 + field, band, :] = smooth * offsets[field]
        kind_ref[band, :] = neighbour(3)

    group = 8

    def stacked(values):
        high, low = split(values)
        return jnp.concatenate([high, low, high], axis=0)

    def one_group(start):
        pieces = []
        for row in range(group):
            smooth = jnp.broadcast_to(environment_ref[0, pl.ds(start + row, 1), :], (32, 128))
            kind = jnp.broadcast_to(kind_ref[pl.ds(start + row, 1), :], (32, 128))
            pieces.append(
                jnp.tanh(smooth * ((1.0 - kind) * embed_zero + kind * embed_one))
            )
        first = jnp.concatenate(pieces, axis=1)
        second = jnp.tanh(multiply(second_weight, stacked(first), ((1,), (0,))))
        second = second + jnp.concatenate([first, first], axis=0)
        third = jnp.tanh(multiply(third_weight, stacked(second), ((1,), (0,))))
        third = third + jnp.concatenate([second, second], axis=0)
        third_pair = split(third)
        for half in range(group // 4):
            columns = slice(512 * half, 512 * half + 512)
            bands = []
            for part in range(4):
                bands.append(
                    jnp.concatenate(
                        [
                            jnp.where(
                                sub == row + jnp.where(lane < 64, 0, 4),
                                jnp.broadcast_to(
                                    environment_ref[part, pl.ds(start + 4 * half + row, 1), :],
                                    (8, 128),
                                ),
                                0.0,
                            )
                            for row in range(4)
                        ],
                        axis=1,
                    )
                )
            environment = split(jnp.concatenate(bands, axis=0))
            both = multiply(
                jnp.concatenate(environment, axis=0), third_pair[0][:, columns], LANES
            )
            sums = both[0:32] + both[32:64]
            sums = sums + multiply(environment[0], third_pair[1][:, columns], LANES)
            sums = sums * (1.0 / slots)
            for part in range(4):
                moments_ref[part, pl.ds(2 * start + 8 * half, 8), :] = sums[
                    8 * part : 8 * part + 8
                ]

    def body(step, carry):
        for part in range(unroll):
            one_group(pl.multiple_of(step * unroll * group + part * group, group))
        return carry

    unroll = rows // group
    lax.fori_loop(0, rows // (unroll * group), body, 0)

    chunks = (descriptor_ref.shape[1] + 127) // 128
    last = descriptor_ref.shape[1] - 128 * (chunks - 1)

    def describe_band(start):
        band = pl.ds(start, 8)
        moments = [moments_ref[part, band, :] for part in range(4)]
        axis_part = [lane_pick(moments[part], lane & 15) for part in range(4)]
        for chunk in range(chunks):
            spot = jnp.broadcast_to(spot_ref[chunk : chunk + 1, :], (8, 128))
            total = lane_pick(moments[0], spot) * axis_part[0]
            for part in range(1, 4):
                total = total + lane_pick(moments[part], spot) * axis_part[part]
            if chunk < chunks - 1:
                descriptor_ref[band, 128 * chunk : 128 * chunk + 128] = total
            else:
                descriptor_ref[band, 128 * chunk : 128 * chunk + last] = total[:, 0:last]

    bands = 8 if atoms % 64 == 0 else 1

    def describe(step, carry):
        for part in range(bands):
            describe_band(pl.multiple_of(step * 8 * bands + 8 * part, 8))
        return carry

    lax.fori_loop(0, atoms // (8 * bands), describe, 0)

    store = pltpu.make_async_copy(descriptor_ref, descriptor_hbm, semaphores.at[2])
    store.start()
    for fetch in fetches:
        fetch.wait()
    shift = fitting_rows(descriptor_ref, weight_in_ref, weight_hidden_ref, weight_out_ref)
    kind = types_ref[...].astype(jnp.float32)
    charge = (1.0 - kind) * charges_ref[0] + kind * charges_ref[1] + natural_order(shift)
    charge_ref[...] = charge
    for copy in range(copies_ref.shape[0]):
        copies_ref[copy] = charge
    store.wait()


def spot_table(embed, desc):
    column = np.arange(desc) // AXIS
    quarter = embed // 4
    place = 32 * (column // quarter) + column % quarter
    chunks = (desc + 127) // 128
    table = np.zeros((chunks * 128,), np.int32)
    table[:desc] = place
    padded = np.zeros(((chunks + 7) // 8 * 8, 128), np.int32)
    padded[:chunks] = table.reshape(chunks, 128)
    return padded


def networks(
    copies,
    ghosts,
    charge_base,
    own,
    lower,
    upper,
    neighbours,
    types,
    embed,
    weight_in,
    weight_hidden,
    weight_out,
):
    atoms = types.shape[1]
    desc, width = weight_in.shape
    spots = jnp.asarray(spot_table(embed[2].shape[1], desc))
    anywhere = pl.BlockSpec(memory_space=pl.ANY)
    scalars = pl.BlockSpec(memory_space=pltpu.SMEM)
    blocks = (own, lower, upper, neighbours[0].T, types, *embed, spots)
    weight_out = weight_out.reshape(1, -1)
    results = [
        jax.ShapeDtypeStruct((atoms, desc), jnp.float32),
        jax.ShapeDtypeStruct((1, atoms), jnp.float32),
        jax.ShapeDtypeStruct((copies, 1, atoms), jnp.float32),
    ]
    return pl.pallas_call(
        functools.partial(network_kernel, ghosts),
        grid=(1,),
        out_shape=results,
        in_specs=[scalars]
        + whole_specs(*blocks)
        + [anywhere, anywhere]
        + whole_specs(weight_out),
        out_specs=[anywhere] + whole_specs(*results[1:]),
        scratch_shapes=[
            pltpu.VMEM((atoms, desc), jnp.float32),
            pltpu.VMEM((4, atoms // 2, 128), jnp.float32),
            pltpu.VMEM((atoms // 2, 128), jnp.float32),
            pltpu.VMEM((4, atoms, 128), jnp.float32),
            pltpu.VMEM((3, 128, 128), jnp.float32),
            pltpu.VMEM((width, desc), jnp.float32),
            pltpu.VMEM(weight_hidden.shape, jnp.float32),
            pltpu.SemaphoreType.DMA((3,)),
        ],
        compiler_params=pltpu.CompilerParams(vmem_limit_bytes=VMEM_BYTES),
        name="networks",
    )(charge_base, *blocks, weight_in.T, weight_hidden, weight_out)


def energy_kernel(descriptor_ref, weight_in_ref, weight_hidden_ref, weight_out_ref, energy_ref):
    energy_ref[...] = natural_order(
        fitting_rows(descriptor_ref, weight_in_ref, weight_hidden_ref, weight_out_ref)
    )


def energies(descriptor, weight_in, weight_hidden, weight_out):
    atoms, desc = descriptor.shape
    width = weight_in.shape[1]
    arrays = (descriptor, weight_in.T, weight_hidden, weight_out.reshape(1, -1))
    result = jax.ShapeDtypeStruct((1, atoms), jnp.float32)
    return pl.pallas_call(
        energy_kernel,
        grid=(1,),
        out_shape=result,
        in_specs=whole_specs(*arrays),
        out_specs=whole(result.shape),
        compiler_params=pltpu.CompilerParams(vmem_limit_bytes=VMEM_BYTES),
        cost_estimate=pl.CostEstimate(
            flops=6 * atoms * desc * width, bytes_accessed=4 * desc * width, transcendentals=0
        ),
        name="energies",
    )(*arrays)


def weight_rows(fraction):
    square = fraction * fraction
    cubed = square * fraction
    rest = 1.0 - fraction
    return [
        rest * rest * rest / 6.0,
        (3.0 * cubed - 6.0 * square + 4.0) / 6.0,
        (-3.0 * cubed + 3.0 * square + 3.0 * fraction + 1.0) / 6.0,
        cubed / 6.0,
    ]


def placed_weights(distance, weights):
    shape = distance.shape
    result = jnp.zeros(shape, jnp.float32)
    for step in range(4):
        result = jnp.where(
            distance == step, jnp.broadcast_to(weights[step], shape), result
        )
    return result


def third_factors(fields, waves_ref, cosine_ref):
    atoms = fields.shape[1]
    start = fields[2:3, :].astype(jnp.int32)
    along = weight_rows(fields[5:6, :])
    parts = waves_ref.shape[0]
    cosine = jnp.broadcast_to(cosine_ref[...], (parts, 128))
    wave = jnp.broadcast_to(waves_ref[:, 0:1], (parts, 128))
    shift = jnp.broadcast_to(waves_ref[:, 1:2], (parts, 128))
    pieces = []
    for chunk in range(atoms // 128):
        lanes = slice(128 * chunk, 128 * chunk + 128)
        total = jnp.zeros((parts, 128), jnp.float32)
        for step in range(4):
            place = jnp.broadcast_to(start[:, lanes] + step, (parts, 128))
            phase = (wave * place + shift) & (NG - 1)
            value = lane_pick(cosine, phase & 127)
            value = jnp.where(phase < 128, value, -value)
            total = total + value * jnp.broadcast_to(along[step][:, lanes], (parts, 128))
        pieces.append(total)
    return jnp.concatenate(pieces, axis=1)


def first_third_split(fields, waves_ref, cosine_ref, window, scale, high_ref, low_ref):
    atoms = fields.shape[1]
    third = third_factors(fields, waves_ref, cosine_ref) * scale
    rows = lax.broadcasted_iota(jnp.int32, (window, atoms), 0)
    first = placed_weights(
        rows - fields[0:1, :].astype(jnp.int32), weight_rows(fields[3:4, :])
    )
    for chunk in range(atoms // 128):
        lanes = slice(128 * chunk, 128 * (chunk + 1))
        for part in range(0, third.shape[0], 2):
            high, low = split(
                jnp.concatenate(
                    [first[:, lanes] * third[part + side : part + side + 1, lanes] for side in range(2)],
                    axis=0,
                )
            )
            place = slice(part * window, (part + 2) * window)
            high_ref[place, lanes] = high
            low_ref[place, lanes] = low
    return high_ref[...], low_ref[...]


def second_factors(fields, base, block_y, slabs, high_ref, low_ref):
    atoms = fields.shape[1]
    block = atoms // slabs
    reach = block_y + REACH
    start = fields[1:2, :].astype(jnp.int32) - base
    weights = weight_rows(fields[4:5, :])
    for chunk in range(atoms // 128):
        lanes = slice(128 * chunk, 128 * (chunk + 1))
        first = 128 * chunk // block
        last = (128 * chunk + 127) // block
        top = first * block_y
        rows = (last - first) * block_y + reach
        pieces = [(top, min(rows, NG - top))]
        if top + rows > NG:
            pieces.append((0, top + rows - NG))
        for row, count in pieces:
            index = row + lax.broadcasted_iota(jnp.int32, (count, 128), 0)
            table = split(
                placed_weights(
                    (index - start[:, lanes]) & (NG - 1), [weight[:, lanes] for weight in weights]
                )
            )
            high_ref[row : row + count, lanes] = table[0]
            low_ref[row : row + count, lanes] = table[1]
    return high_ref[...], low_ref[...]


def wave_of(index):
    return jnp.where(index <= NG // 2, index, index - NG // 2)


def damping(index):
    kappa = wave_of(index).astype(jnp.float32) * (2.0 * math.pi / NG)
    squared = kappa * kappa
    ends = (index == 0) | (index == NG // 2)
    return squared, jnp.exp(-0.5 * squared) * jnp.where(ends, 1.0 / NG, 2.0 / NG)


def transform(planes, kappa_ref, first_part, tables_ref, last_ref):
    count = len(planes)
    basis = tables_ref[0]
    turned = tables_ref[1]
    square_x, damp_x = damping(lax.broadcasted_iota(jnp.int32, (NG, 1), 0))
    square_y, damp_y = damping(lax.broadcasted_iota(jnp.int32, (1, NG), 1))
    square_xy = square_x + square_y
    damp_xy = damp_x * damp_y
    columns = [slice(NG * part, NG * (part + 1)) for part in range(count)]
    first = product(basis, jnp.concatenate(planes, axis=1))
    first = jnp.concatenate([first[:, column] for column in columns], axis=0)
    both = product(first, turned)
    scaled = []
    for part in range(count):
        squared = square_xy + kappa_ref[first_part + part, 0]
        root = jnp.where(squared == 0.0, 1.0, 0.0)
        green = (1.0 - root) * (damp_xy * kappa_ref[first_part + part, 1]) / (squared + root)
        scaled.append(both[columns[part]] * green)
    back = product(turned, jnp.concatenate(scaled, axis=1))
    back = jnp.concatenate([back[:, column] for column in columns], axis=0)
    return product(back, last_ref[...])


def send_blocks(full, block_x, block_y, put):
    low_lanes = lax.broadcasted_iota(jnp.int32, (NG, 128), 1) < block_y
    for pair in range(full.shape[0] // (2 * NG)):
        even = full[2 * NG * pair : 2 * NG * pair + NG, 0:128]
        odd = full[2 * NG * pair + NG : 2 * NG * (pair + 1), 0:128]
        blocks = [
            jnp.where(low_lanes, even, pltpu.roll(odd, block_y, 1)),
            jnp.where(low_lanes, pltpu.roll(even, block_y, 1), odd),
        ]
        for brick in range(NG // block_x):
            for side in range(2):
                for group in range(block_x // 8):
                    start = block_x * brick + 8 * group
                    put(pair, brick, side, group, blocks[side][start : start + 8])


def spread_kernel(
    block_x,
    block_y,
    window,
    kappa_ref,
    pair_ref,
    static_ref,
    charge_ref,
    waves_ref,
    cosine_ref,
    tables_hbm,
    last_hbm,
    short_hbm,
    sent_ref,
    full_ref,
    atoms_ref,
    later_hbm,
    grid_ref,
    tables_ref,
    last_ref,
    semaphores,
    *pair_refs,
):
    slabs = NG // block_y
    second_refs, first_refs = pair_refs[:4], pair_refs[4:]
    bricks = NG // block_x
    parts = waves_ref.shape[0]
    block = static_ref.shape[2]
    count = full_ref.shape[0]
    step = pl.program_id(0)
    later = later_hbm.shape[0]
    store = pltpu.make_async_copy(
        grid_ref.at[pl.ds(parts - later, later), pl.ds(0, NG)], later_hbm, semaphores.at[2]
    )

    @pl.when(step == 0)
    def _():
        fetches = [
            pltpu.make_async_copy(tables_hbm, tables_ref, semaphores.at[0]),
            pltpu.make_async_copy(last_hbm.at[pair_ref[0]], last_ref, semaphores.at[1]),
        ]
        for fetch in fetches:
            fetch.start()
        for slab in range(slabs):
            lanes = slice(block * slab, block * (slab + 1))
            for brick in range(bricks):
                atoms_ref[brick, :, lanes] = static_ref[slab * bricks + brick]
                atoms_ref[brick, 6:7, lanes] = charge_ref[slab * bricks + brick]
        grid_ref[...] = jnp.zeros_like(grid_ref)
        for ref in second_refs:
            ref[...] = jnp.zeros_like(ref)
        for brick in range(bricks):
            fields = atoms_ref[brick]
            table = first_third_split(
                fields,
                waves_ref,
                cosine_ref,
                window,
                fields[6:7, :],
                first_refs[2 * (brick % 2)],
                first_refs[2 * (brick % 2) + 1],
            )
            second = second_factors(
                fields, 0, block_y, slabs, second_refs[2 * (brick % 2)], second_refs[2 * (brick % 2) + 1]
            )
            spread = triple(table, second, LANES)
            rows = slice(block_x * brick, block_x * brick + window)
            for part in range(parts):
                grid_ref[part, rows, :] += spread[part * window : part * window + window]
        extra = window - block_x
        for part in range(parts):
            grid_ref[part, 0:extra, :] += grid_ref[part, NG : NG + extra, :]
        store.start()
        for fetch in fetches:
            fetch.wait()

    planes = [grid_ref[count * step + part, 0:NG, :] for part in range(count)]
    full = transform(planes, kappa_ref, count * step, tables_ref, last_ref)
    for part in range(count):
        full_ref[part] = full[NG * part : NG * (part + 1)]

    def put(pair, brick, side, group, tile):
        sent_ref[2 * brick + side, group, pair] = tile

    send_blocks(full, block_x, block_y, put)

    @pl.when(step == pl.num_programs(0) - 1)
    def _():
        store.wait()


def early_pairs(parts):
    return parts // 4


def spread_and_solve(
    block_x, block_y, window, kappa, pair, static, charge, waves, cosine_row, tables, last, short
):
    devices, _, atoms = static.shape
    slabs = NG // block_y
    bricks = NG // block_x
    parts = waves.shape[0]
    pairs = early_pairs(parts)
    count = 4
    anywhere = pl.BlockSpec(memory_space=pl.ANY)
    scalars = pl.BlockSpec(memory_space=pltpu.SMEM)
    sent_block = (2 * bricks, block_x // 8, count // 2, 8, 128)
    return pl.pallas_call(
        functools.partial(spread_kernel, block_x, block_y, window),
        grid=(2 * pairs // count,),
        out_shape=[
            jax.ShapeDtypeStruct((2 * bricks, block_x // 8, pairs, 8, 128), jnp.float32),
            jax.ShapeDtypeStruct((2 * pairs, NG, NG), jnp.float32),
            jax.ShapeDtypeStruct((bricks, 8, slabs * atoms), jnp.float32),
            jax.ShapeDtypeStruct((parts - 2 * pairs, NG, NG), jnp.float32),
        ],
        in_specs=[scalars, scalars]
        + whole_specs(static, charge, waves, cosine_row)
        + [anywhere, anywhere, anywhere],
        out_specs=[
            pl.BlockSpec(sent_block, lambda step: (0, 0, step, 0, 0)),
            pl.BlockSpec((count, NG, NG), lambda step: (step, 0, 0)),
            whole((bricks, 8, slabs * atoms)),
            anywhere,
        ],
        scratch_shapes=[
            pltpu.VMEM((parts, NG + window - block_x, NG), jnp.float32),
            pltpu.VMEM(tables.shape, tables.dtype),
            pltpu.VMEM(last.shape[1:], last.dtype),
            pltpu.SemaphoreType.DMA((3,)),
        ]
        + [pltpu.VMEM((NG, slabs * atoms), jnp.bfloat16)] * 4
        + [pltpu.VMEM((parts * window, slabs * atoms), jnp.bfloat16)] * 4,
        compiler_params=pltpu.CompilerParams(vmem_limit_bytes=VMEM_BYTES),
        name="spread_and_solve",
    )(kappa, pair, static, charge, waves, cosine_row, tables, last, short)


def sample_kernel(
    block_x,
    block_y,
    window,
    kappa_ref,
    pair_ref,
    atoms_ref,
    waves_ref,
    cosine_ref,
    tables_hbm,
    last_hbm,
    later_hbm,
    early_hbm,
    sent_ref,
    later_ref,
    full_ref,
    tables_ref,
    last_ref,
    semaphores,
    packed_ref,
):
    bricks = atoms_ref.shape[0]
    parts = waves_ref.shape[0]
    early = 2 * early_pairs(parts)
    block = atoms_ref.shape[2] * block_y // NG
    fetches = [
        pltpu.make_async_copy(tables_hbm, tables_ref, semaphores.at[0]),
        pltpu.make_async_copy(last_hbm.at[pair_ref[0]], last_ref, semaphores.at[1]),
        pltpu.make_async_copy(later_hbm, later_ref, semaphores.at[2]),
        pltpu.make_async_copy(early_hbm, full_ref.at[pl.ds(0, early)], semaphores.at[3]),
    ]
    for fetch in fetches:
        fetch.start()
    for fetch in fetches[:3]:
        fetch.wait()
    pairs = (parts - early) // 2
    planes = [later_ref[part] for part in range(parts - early)]
    full = transform(planes, kappa_ref, early, tables_ref, last_ref)
    for part in range(parts - early):
        full_ref[early + part] = full[NG * part : NG * (part + 1)]

    def put(pair, brick, side, group, tile):
        sent_ref[2 * brick + side, pairs * group + pair] = tile

    send_blocks(full, block_x, block_y, put)
    fetches[3].wait()

    reach = block_y + REACH
    lane = lax.broadcasted_iota(jnp.int32, (NG, 128), 1)
    for part in range(parts):
        for side in range(2):
            values = full_ref[part, :, 128 * side : 128 * (side + 1)]
            high = values.astype(jnp.bfloat16).astype(jnp.float32)
            again = pltpu.roll(high, reach, 1)
            low = pltpu.roll(values - high, 2 * reach - 128, 1)
            packed_ref[side, part, 0:NG, 0:128] = jnp.where(lane < reach, high, again)
            packed_ref[side, part, 0:NG, 128:NG] = jnp.where(
                lane < 2 * reach - 128, again, jnp.where(lane < 3 * reach - 128, low, 0.0)
            )
            packed_ref[side, part, NG : NG + window - block_x, :] = packed_ref[
                side, part, 0 : window - block_x, :
            ]
    extra = sent_ref.shape[1] - 1
    base = 2 * block_y * pair_ref[0]
    lanes = pl.ds(pl.multiple_of(2 * block * pair_ref[0], 128), 2 * block)
    for brick in range(bricks):
        fields = atoms_ref[brick, :, lanes]
        thirds = third_factors(fields, waves_ref, cosine_ref)
        rows = slice(block_x * brick, block_x * brick + window)
        for side in range(2):
            here = slice(block * side, block * (side + 1))
            third = thirds[:, here]
            ours = fields[:, here]
            index = lax.broadcasted_iota(jnp.int32, (window, block), 0)
            first = placed_weights(
                index - ours[0:1, :].astype(jnp.int32), weight_rows(ours[3:4, :])
            )
            index = lax.broadcasted_iota(jnp.int32, (reach, block), 0)
            start = ours[1:2, :].astype(jnp.int32) - (base + block_y * side)
            high, low = split(placed_weights(index - start, weight_rows(ours[4:5, :])))
            rest = jnp.zeros((NG - 3 * reach, block), jnp.bfloat16)
            second = jnp.concatenate([high, low, high, rest], axis=0)
            values = jnp.concatenate(
                [packed_ref[side, part, rows, :] for part in range(parts)], axis=0
            )
            along = multiply(values.astype(jnp.bfloat16), second, ((1,), (0,)))
            total = jnp.zeros((window, block), jnp.float32)
            for part in range(parts):
                total = total + along[window * part : window * (part + 1)] * third[part : part + 1]
            row = jnp.sum(total * first, axis=0, keepdims=True)
            sent_ref[2 * brick + side, extra] = jnp.zeros((8, 128), jnp.float32)
            sent_ref[2 * brick + side, extra, 0:1, :] = row[:, 0:128]
            sent_ref[2 * brick + side, extra, 1:2, 0 : block - 128] = row[:, 128:block]


def solve_and_sample(
    block_x, block_y, window, kappa, pair, atoms, waves, cosine_row, tables, last, later, early
):
    bricks = atoms.shape[0]
    parts = waves.shape[0]
    pairs = parts // 2 - early_pairs(parts)
    anywhere = pl.BlockSpec(memory_space=pl.ANY)
    scalars = pl.BlockSpec(memory_space=pltpu.SMEM)
    result = jax.ShapeDtypeStruct((2 * bricks, block_x // 8 * pairs + 1, 8, 128), jnp.float32)
    return pl.pallas_call(
        functools.partial(sample_kernel, block_x, block_y, window),
        grid=(1,),
        out_shape=result,
        in_specs=[scalars, scalars] + whole_specs(atoms, waves, cosine_row) + [anywhere] * 4,
        out_specs=whole(result.shape),
        scratch_shapes=[
            pltpu.VMEM((2 * pairs, NG, NG), jnp.float32),
            pltpu.VMEM((parts, NG, NG), jnp.float32),
            pltpu.VMEM(tables.shape, tables.dtype),
            pltpu.VMEM(last.shape[1:], last.dtype),
            pltpu.SemaphoreType.DMA((4,)),
        ]
        + [pltpu.VMEM((2, parts, NG + window - block_x, NG), jnp.float32)],
        compiler_params=pltpu.CompilerParams(vmem_limit_bytes=VMEM_BYTES),
        cost_estimate=pl.CostEstimate(
            flops=24 * parts * NG * NG * NG, bytes_accessed=4 * early.size, transcendentals=0
        ),
        name="solve_and_sample",
    )(kappa, pair, atoms, waves, cosine_row, tables, last, later, early)


def finish_kernel(
    block_y,
    early_ref,
    later_ref,
    sums_ref,
    short_hbm,
    charge_hbm,
    table_ref,
    out_ref,
    energy_ref,
    short_ref,
    charge_ref,
    semaphores,
):
    atoms = short_ref.shape[1]
    fetches = [
        pltpu.make_async_copy(short_hbm, short_ref, semaphores.at[0]),
        pltpu.make_async_copy(charge_hbm, charge_ref, semaphores.at[1]),
    ]

    @pl.when(pl.program_id(0) == 0)
    def _():
        for fetch in fetches:
            fetch.start()

    lines = early_ref.shape[3]
    sources, _, pairs = early_ref.shape[:3]
    early = early_ref.reshape(sources * pairs, lines, 128)
    later = later_ref.reshape(sources * later_ref.shape[1], lines, 128)
    pieces = []
    for line in range(lines):
        turned = jnp.concatenate([early[:, line, :], later[:, line, :]], axis=0).T
        pieces.append(jnp.concatenate([turned[0:block_y], turned[block_y:]], axis=1))
    result = product(jnp.concatenate(pieces, axis=0), table_ref[...])
    for line in range(lines):
        out_ref[line] = result[block_y * line : block_y * (line + 1)]

    @pl.when(pl.program_id(0) == 0)
    def _():
        for fetch in fetches:
            fetch.wait()
        total = jnp.sum(sums_ref[:, 0], axis=0)
        potential_at = jnp.concatenate([total[0:1, :], total[1:2, 0 : atoms - 128]], axis=1)
        energy_ref[...] = short_ref[...] + 0.5 * charge_ref[...] * potential_at


def finish(block_x, block_y, early, later, short, charge, table):
    bricks2, groups, pairs = early.shape[:3]
    rest = (later.shape[1] - 1) // groups
    atoms = short.shape[1]
    return pl.pallas_call(
        functools.partial(finish_kernel, block_y),
        grid=(groups,),
        out_shape=[
            jax.ShapeDtypeStruct((block_x, block_y, NG), jnp.float32),
            jax.ShapeDtypeStruct((1, atoms), jnp.float32),
        ],
        in_specs=[
            pl.BlockSpec((bricks2, 1, pairs, 8, 128), lambda index: (0, index, 0, 0, 0)),
            pl.BlockSpec((bricks2, rest, 8, 128), lambda index: (0, index, 0, 0)),
            pl.BlockSpec((bricks2, 1, 8, 128), lambda index: (0, groups * rest, 0, 0)),
            pl.BlockSpec(memory_space=pltpu.HBM),
            pl.BlockSpec(memory_space=pltpu.HBM),
            whole(table.shape),
        ],
        out_specs=[
            pl.BlockSpec((8, block_y, NG), lambda index: (index, 0, 0)),
            whole((1, atoms)),
        ],
        scratch_shapes=[
            pltpu.VMEM((1, atoms), jnp.float32),
            pltpu.VMEM((1, atoms), jnp.float32),
            pltpu.SemaphoreType.DMA((2,)),
        ],
        compiler_params=pltpu.CompilerParams(vmem_limit_bytes=32 * 2**20),
        name="finish",
    )(early, later, later, short, charge, table)


def real_basis():
    index = np.arange(NG)
    wave = np.where(index <= NG // 2, index, index - NG // 2)
    angle = (wave[:, None] * index[None, :] % NG) * (2.0 * math.pi / NG)
    return np.where((index <= NG // 2)[:, None], np.cos(angle), np.sin(angle))


def per_device(
    positions,
    types,
    neighbours,
    neighbour_count,
    send_index,
    cell_x,
    cell_y,
    cell_z,
    spline_fraction,
    embed_first,
    embed_second,
    embed_third,
    energy_in,
    energy_hidden,
    energy_out,
    wannier_in,
    wannier_hidden,
    wannier_out,
    charge_base,
):
    atoms = types.shape[1]
    ghosts = send_index.shape[1] // 2
    count_x = lax.axis_size("brick")
    count_y = lax.axis_size("slab")
    block_x = NG // count_x
    block_y = NG // count_y
    window = block_x + 8
    parts = NG // (2 * count_x)
    brick = lax.axis_index("brick")
    slab = lax.axis_index("slab")
    pair = (slab // 2).astype(jnp.int32).reshape(1)
    halves = [
        [b * count_y + 2 * p + side for b in range(count_x) for side in range(2)]
        for p in range(count_y // 2)
    ]

    def exchange(values, axes, groups=None):
        return lax.all_to_all(
            values, axes, split_axis=0, concat_axis=0, tiled=True, axis_index_groups=groups
        )

    own, outgoing = collect(positions, types, neighbour_count, send_index)
    up = [(i, (i + 1) % count_x) for i in range(count_x)]
    down = [((i + 1) % count_x, i) for i in range(count_x)]
    lower = lax.ppermute(outgoing, "brick", up)
    upper = lax.ppermute(outgoing, "brick", down)
    places = place_rows(
        count_x * count_y,
        (slab * block_y).astype(jnp.int32).reshape(1),
        (cell_x, cell_y, cell_z),
        spline_fraction,
    )
    places, upper = lax.optimization_barrier((places, upper))
    every_place = exchange(places, ("slab", "brick"))
    descriptor, charge, charge_copies = networks(
        count_x * count_y,
        ghosts,
        charge_base,
        own,
        lower,
        upper,
        neighbours,
        types,
        (embed_first, embed_second, embed_third),
        wannier_in,
        wannier_hidden,
        wannier_out,
    )
    charge_copies, every_place = lax.optimization_barrier((charge_copies, every_place))
    every_charge = exchange(charge_copies, ("slab", "brick"))

    part = (2 * brick + slab % 2) * parts + jnp.arange(parts, dtype=jnp.int32)
    wave = wave_of(part)
    waves = jnp.stack([wave, jnp.where(part <= NG // 2, 0, 3 * NG // 4)], axis=1)
    kappa = wave.astype(jnp.float32) * (2.0 * math.pi / NG)
    squared = kappa * kappa
    ends = (part == 0) | (part == NG // 2)
    kappa = jnp.stack(
        [squared, jnp.exp(-0.5 * squared) * jnp.where(ends, 1.0 / NG, 2.0 / NG)], axis=1
    )
    basis = real_basis()
    tables = np.stack([basis, basis.T]).astype(np.float32)
    last = []
    for p in range(count_y // 2):
        points = np.concatenate(
            [np.arange(2 * block_y), block_y + np.arange(block_y + REACH)]
        )
        points = (2 * block_y * p + points) % NG
        columns = np.zeros((NG, NG))
        columns[:, : points.size] = basis[:, points]
        last.append(columns.astype(np.float32))
    cosine_row = np.cos(np.arange(128) * (2.0 * math.pi / NG)).astype(np.float32)[None]
    cosine_row = jnp.asarray(cosine_row)
    tables = jnp.asarray(tables)
    last = jnp.asarray(np.stack(last))
    energy_short = energies(descriptor, energy_in, energy_hidden, energy_out)
    early, full, every_atom, later = spread_and_solve(
        block_x,
        block_y,
        window,
        kappa,
        pair,
        every_place,
        every_charge,
        waves,
        cosine_row,
        tables,
        last,
        energy_short,
    )

    def send(values):
        got = exchange(values.reshape(values.shape[0], -1, 128), ("brick", "slab"), halves)
        return got.reshape(values.shape)

    early = send(early)
    later = solve_and_sample(
        block_x,
        block_y,
        window,
        kappa,
        pair,
        every_atom,
        waves,
        cosine_row,
        tables,
        last,
        later,
        full,
    )
    later = send(later)
    source = np.arange(2 * count_x)[:, None] * parts
    pairs = 2 * np.arange(parts // 2)[None, :]
    order = np.concatenate(
        [
            (source + pairs[:, : early_pairs(parts)]).ravel(),
            (source + pairs[:, early_pairs(parts) :]).ravel(),
        ]
    )
    order = np.concatenate([order, order + 1])
    potential, atom_energy = finish(
        block_x,
        block_y,
        early,
        later,
        energy_short,
        charge,
        jnp.asarray(basis[order].astype(np.float32)),
    )
    return atom_energy, potential


def solution(mesh):
    placed = (
        P(None, "slab", "brick"),
        P("slab", "brick"),
        P("slab", "brick", None),
        P("slab", "brick"),
        P("slab", "brick"),
        P("slab", "brick"),
        P("slab", "brick"),
        P("slab", "brick"),
        P(None, "slab", "brick"),
    ) + (P(),) * 10
    bricks, slabs = mesh.shape["brick"], mesh.shape["slab"]
    fits = 2 * NG == 128 * slabs and NG % (32 * bricks) == 0
    return jax.shard_map(
        per_device if fits else per_device_general,
        mesh=mesh,
        in_specs=placed,
        out_specs=(P("slab", "brick"), P("brick", "slab", None)),
        check_vma=False,
    )
```

```python
import functools
import math

import jax
import jax.numpy as jnp
import numpy as np
from jax import lax
from jax.experimental import pallas as pl
from jax.experimental.pallas import tpu as pltpu
from jax.sharding import PartitionSpec as P

NG = 256
AXIS = 16
VMEM_BYTES = 60 * 2**20
REACH = 16
FIELDS = 7


HIGH = lax.Precision.HIGHEST


def with_halo(cells, sides, width):
    for axis, dim in sides:
        count = lax.axis_size(axis)
        head = lax.slice_in_dim(cells, 0, width, axis=dim)
        tail = lax.slice_in_dim(cells, cells.shape[dim] - width, cells.shape[dim], axis=dim)
        cells = jnp.concatenate(
            [
                lax.ppermute(tail, axis, [(i, (i + 1) % count) for i in range(count)]),
                cells,
                lax.ppermute(head, axis, [((i + 1) % count, i) for i in range(count)]),
            ],
            axis=dim,
        )
    return cells


def spline_weights(fraction):
    cubed = fraction * fraction * fraction
    square = fraction * fraction
    return jnp.stack(
        [
            (1.0 - fraction) * (1.0 - fraction) * (1.0 - fraction) / 6.0,
            (3.0 * cubed - 6.0 * square + 4.0) / 6.0,
            (-3.0 * cubed + 3.0 * square + 3.0 * fraction + 1.0) / 6.0,
            cubed / 6.0,
        ]
    )


def fitting(descriptor, weight_in, weight_hidden, weight_out):
    hidden = jnp.tanh(jnp.dot(descriptor, weight_in, precision=HIGH))
    for depth_index in range(weight_hidden.shape[0]):
        hidden = jnp.tanh(jnp.dot(hidden, weight_hidden[depth_index], precision=HIGH)) + hidden
    return jnp.dot(hidden, weight_out, precision=HIGH)


def atom_terms(
    extended,
    neighbour_rows,
    neighbour_total,
    embed_first,
    embed_second,
    embed_third,
    energy_in,
    energy_hidden,
    energy_out,
    wannier_in,
    wannier_hidden,
    wannier_out,
):
    atom_count, slots = neighbour_rows.shape
    ghost_rows = (extended.shape[1] - atom_count) // 2
    block_size = 64
    blocks = atom_count // block_size
    present = (jnp.arange(slots, dtype=jnp.int32)[None, :] < neighbour_total[:, None]).astype(
        jnp.float32
    )
    centre_ids = (ghost_rows + jnp.arange(atom_count, dtype=jnp.int32)).reshape(blocks, block_size)
    second_weight = embed_second.T
    third_weight = embed_third.T

    def one_block(pieces):
        centre_rows, rows_block, present_block = pieces
        centre_block = extended[:3, centre_rows]
        gathered = extended[:, rows_block]
        offsets = gathered[:3] - centre_block[:, :, None]
        smooth = present_block / (1.0 + jnp.sum(offsets * offsets, axis=0))
        environment = jnp.stack(
            [smooth, smooth * offsets[0], smooth * offsets[1], smooth * offsets[2]], axis=0
        )
        kind = gathered[3][None]
        mixing = (1.0 - kind) * embed_first[0][:, None, None] + kind * embed_first[1][:, None, None]
        first = jnp.tanh(smooth[None] * mixing).reshape(embed_first.shape[1], block_size * slots)
        second = jnp.tanh(jnp.dot(second_weight, first, precision=HIGH)) + jnp.concatenate(
            [first, first], axis=0
        )
        third = jnp.tanh(jnp.dot(third_weight, second, precision=HIGH)) + jnp.concatenate(
            [second, second], axis=0
        )
        third_blocks = third.reshape(third.shape[0], block_size, slots)
        moments = jnp.einsum("kan,can->akc", third_blocks, environment, precision=HIGH) / slots
        descriptor = jnp.einsum("amc,akc->amk", moments, moments[:, :AXIS], precision=HIGH).reshape(
            block_size, -1
        )
        return (
            fitting(descriptor, energy_in, energy_hidden, energy_out),
            fitting(descriptor, wannier_in, wannier_hidden, wannier_out),
        )

    energy_short, charge_shift = lax.map(
        one_block,
        (
            centre_ids,
            neighbour_rows.reshape(blocks, block_size, slots),
            present.reshape(blocks, block_size, slots),
        ),
    )
    return (energy_short.reshape(atom_count), charge_shift.reshape(atom_count))


def green_table(first, second, third, size):

    def folded(index):
        return jnp.where(index < size // 2, index, index - size).astype(jnp.float32) * (
            2.0 * math.pi / size
        )

    kappa_x = folded(first)[:, None, None]
    kappa_y = folded(second)[None, :, None]
    kappa_z = folded(third)[None, None, :]
    squared = kappa_x * kappa_x + kappa_y * kappa_y + kappa_z * kappa_z
    root = (
        (first[:, None, None] == 0) & (second[None, :, None] == 0) & (third[None, None, :] == 0)
    ).astype(jnp.float32)
    return (1.0 - root) * jnp.exp(-0.5 * squared) / (squared + root)


def dft_tables(size):
    index = jnp.arange(size, dtype=jnp.int32)
    phase = (index[:, None] * index[None, :] % size).astype(jnp.float32) * (2.0 * math.pi / size)
    return (jnp.cos(phase), jnp.sin(phase))


def along(values, table, axis_index):
    result = jnp.tensordot(values, table, axes=([axis_index], [0]), precision=HIGH)
    return jnp.moveaxis(result, -1, axis_index)


def complex_transform(paired, axis_index, cosine, sine, inverse):
    real_part = paired[0]
    imag_part = paired[1]
    inner = axis_index - 1
    real_cos = along(real_part, cosine, inner)
    real_sin = along(real_part, sine, inner)
    imag_cos = along(imag_part, cosine, inner)
    imag_sin = along(imag_part, sine, inner)
    if inverse:
        return jnp.stack([real_cos - imag_sin, imag_cos + real_sin])
    return jnp.stack([real_cos + imag_sin, imag_cos - real_sin])


def fold_windows(values, axis_index, block, count):
    front = jnp.moveaxis(values, axis_index, 0)
    rest = front.shape[1:]
    windows = front.reshape((count, block + 3) + rest)
    main_part = windows[:, :block]
    carried = jnp.roll(windows[:, block:], 1, axis=0)
    main_part = main_part.at[:, :3].add(carried)
    return jnp.moveaxis(main_part.reshape((count * block,) + rest), 0, axis_index)


def make_windows(values, axis_index, block, count):
    front = jnp.moveaxis(values, axis_index, 0)
    rest = front.shape[1:]
    pieces = front.reshape((count, block) + rest)
    trailing = jnp.roll(pieces, -1, axis=0)[:, :3]
    windows = jnp.concatenate([pieces, trailing], axis=1)
    return jnp.moveaxis(windows.reshape((count * (block + 3),) + rest), 0, axis_index)


def spread_matrix(start, weights, width, wrap_size):
    offsets = jnp.arange(4, dtype=jnp.int32)[:, None, None]
    target = start[None, :, None] + offsets
    if wrap_size > 0:
        target = target % wrap_size
    hits = (target == jnp.arange(width, dtype=jnp.int32)[None, None, :]).astype(jnp.float32)
    return jnp.sum(weights[:, :, None] * hits, axis=0)


def per_device_general(
    positions,
    types,
    neighbours,
    neighbour_count,
    send_index,
    cell_x,
    cell_y,
    cell_z,
    spline_fraction,
    embed_first,
    embed_second,
    embed_third,
    energy_in,
    energy_hidden,
    energy_out,
    wannier_in,
    wannier_hidden,
    wannier_out,
    charge_base,
):
    atom_count = types.shape[1]
    ghost_rows = send_index.shape[1] // 2
    kind_float = types[0].astype(jnp.float32)
    own_atoms = jnp.concatenate([positions[:, 0], kind_float[None]], axis=0)
    outgoing = own_atoms[:, send_index[0]]
    padded_ghosts = with_halo(outgoing, (("brick", 1),), ghost_rows)
    extended = jnp.concatenate(
        [padded_ghosts[:, :ghost_rows], own_atoms, padded_ghosts[:, 3 * ghost_rows :]], axis=1
    )
    energy_short, charge_shift = atom_terms(
        extended,
        neighbours[0],
        neighbour_count[0],
        embed_first,
        embed_second,
        embed_third,
        energy_in,
        energy_hidden,
        energy_out,
        wannier_in,
        wannier_hidden,
        wannier_out,
    )
    charge = (1.0 - kind_float) * charge_base[0] + kind_float * charge_base[1] + charge_shift
    count_x = lax.axis_size("brick")
    count_y = lax.axis_size("slab")
    block_x = NG // count_x
    block_y = NG // count_y
    wide_x = block_x + 3
    wide_y = block_y + 3
    spread_x = spread_matrix(cell_x[0], spline_weights(spline_fraction[0, 0]), wide_x, 0)
    spread_y = spread_matrix(cell_y[0], spline_weights(spline_fraction[1, 0]), wide_y, 0)
    spread_z = spread_matrix(cell_z[0], spline_weights(spline_fraction[2, 0]), NG, NG)
    spread_xy = (spread_x[:, :, None] * spread_y[:, None, :]).reshape(atom_count, wide_x * wide_y)
    charge_grid = jnp.einsum(
        "ap,az->pz", spread_xy, charge[:, None] * spread_z, precision=HIGH
    ).reshape(wide_x, wide_y, NG)
    cosine, sine = dft_tables(NG)
    scale = 1.0 / (NG * NG * NG)
    full_index = jnp.arange(NG, dtype=jnp.int32)
    paired = jnp.stack([along(charge_grid, cosine, 2), -along(charge_grid, sine, 2)])
    moved = lax.all_to_all(paired, "slab", split_axis=3, concat_axis=2, tiled=True)
    moved = complex_transform(fold_windows(moved, 2, block_y, count_y), 2, cosine, sine, False)
    moved = lax.all_to_all(moved, "brick", split_axis=2, concat_axis=1, tiled=True)
    moved = complex_transform(fold_windows(moved, 1, block_x, count_x), 1, cosine, sine, False)
    part_y = NG // count_x
    part_z = NG // count_y
    index_y = lax.axis_index("brick") * part_y + jnp.arange(part_y, dtype=jnp.int32)
    index_z = lax.axis_index("slab") * part_z + jnp.arange(part_z, dtype=jnp.int32)
    moved = moved * (green_table(full_index, index_y, index_z, NG) * scale)[None]
    moved = make_windows(complex_transform(moved, 1, cosine, sine, True), 1, block_x, count_x)
    moved = lax.all_to_all(moved, "brick", split_axis=1, concat_axis=2, tiled=True)
    moved = make_windows(complex_transform(moved, 2, cosine, sine, True), 2, block_y, count_y)
    moved = lax.all_to_all(moved, "slab", split_axis=2, concat_axis=3, tiled=True)
    potential_wide = along(moved[0], cosine, 2) - along(moved[1], sine, 2)
    sampled = jnp.einsum(
        "ap,pz->az", spread_xy, potential_wide.reshape(wide_x * wide_y, NG), precision=HIGH
    )
    potential_at = jnp.sum(sampled * spread_z, axis=1)
    atom_energy = energy_short + 0.5 * charge * potential_at
    return (atom_energy[None, :], potential_wide[:block_x, :block_y])


def split(values):
    high = values.astype(jnp.bfloat16)
    low = (values - high.astype(jnp.float32)).astype(jnp.bfloat16)
    return high, low


def multiply(left, right, dims):
    return lax.dot_general(left, right, (dims, ((), ())), preferred_element_type=jnp.float32)


def triple(left, right, dims=((1,), (0,))):
    (left_axis,), (right_axis,) = dims
    if left[0].shape[left_axis] % 128 == 0:
        return multiply(
            jnp.concatenate([left[0], left[0], left[1]], axis=left_axis),
            jnp.concatenate([right[0], right[1], right[0]], axis=right_axis),
            dims,
        )
    return (
        multiply(left[0], right[0], dims)
        + multiply(left[0], right[1], dims)
        + multiply(left[1], right[0], dims)
    )


LANES = ((1,), (1,))


def product(left, right, dims=((1,), (0,))):
    return lax.dot_general(
        left,
        right,
        (dims, ((), ())),
        precision=lax.Precision.HIGH,
        preferred_element_type=jnp.float32,
    )


def lane_pick(table, index):
    return jnp.take_along_axis(table, index, axis=1, mode="promise_in_bounds")


def whole(shape):
    return pl.BlockSpec(tuple(shape), lambda step: (0,) * len(shape))


def whole_specs(*arrays):
    return [whole(array.shape) for array in arrays]


def collect_kernel(
    positions_ref, types_ref, count_ref, send_ref, own_ref, outgoing_ref
):
    atoms = types_ref.shape[1]
    own_ref[...] = jnp.zeros_like(own_ref)
    for axis in range(3):
        own_ref[axis : axis + 1, 0:atoms] = positions_ref[axis]
    own_ref[3:4, 0:atoms] = types_ref[...].astype(jnp.float32)
    own_ref[4:5, 0:atoms] = count_ref[...].astype(jnp.float32)
    own_ref[5:6, 0:atoms] = send_ref[...].astype(jnp.float32)
    for chunk in range(2):
        lanes = slice(128 * chunk, 128 * chunk + 128)
        wanted = jnp.broadcast_to(own_ref[5:6, lanes], (8, 128)).astype(jnp.int32)
        within = wanted & 127
        outgoing_ref[:, lanes] = jnp.where(
            wanted < 128,
            lane_pick(own_ref[:, 0:128], within),
            lane_pick(own_ref[:, 128:256], within),
        )


def collect(positions, types, counts, send_index):
    arrays = (positions, types, counts, send_index)
    result = jax.ShapeDtypeStruct((8, 256), jnp.float32)
    return pl.pallas_call(
        collect_kernel,
        grid=(1,),
        out_shape=[result, result],
        in_specs=whole_specs(*arrays),
        out_specs=whole_specs(result, result),
        compiler_params=pltpu.CompilerParams(vmem_limit_bytes=VMEM_BYTES),
        name="collect_atoms",
    )(*arrays)


def fitting_rows(descriptor_ref, weight_in_ref, weight_hidden_ref, weight_out_ref):
    hidden = jnp.tanh(product(descriptor_ref[...], weight_in_ref[...], LANES))
    for layer in range(weight_hidden_ref.shape[0]):
        hidden = jnp.tanh(product(hidden, weight_hidden_ref[layer])) + hidden
    width = hidden.shape[1]
    return product(jnp.broadcast_to(weight_out_ref[...], (8, width)), hidden, LANES)


def natural_order(rows):
    atoms = rows.shape[1]
    padded = jnp.concatenate([rows, jnp.zeros((8, 256 - atoms), jnp.float32)], axis=1)
    pieces = []
    for chunk in range(2):
        atom = 128 * chunk + lax.broadcasted_iota(jnp.int32, (8, 128), 1)
        late = atom >= atoms // 2
        within = jnp.where(late, atom - atoms // 2, atom)
        place = 8 * (within >> 2) + (within & 3) + jnp.where(late, 4, 0)
        place = jnp.minimum(place, 255)
        pieces.append(
            jnp.where(
                place < 128,
                lane_pick(padded[:, 0:128], place & 127),
                lane_pick(padded[:, 128:256], place & 127),
            )
        )
    return jnp.concatenate(pieces, axis=1)[0:1, 0:atoms]


def network_kernel(
    ghosts,
    base_ref,
    charges_ref,
    own_ref,
    lower_ref,
    upper_ref,
    slots_ref,
    types_ref,
    cell_x_ref,
    cell_y_ref,
    cell_z_ref,
    fraction_ref,
    first_ref,
    second_ref,
    third_ref,
    spot_ref,
    weight_in_hbm,
    weight_hidden_hbm,
    weight_out_ref,
    descriptor_hbm,
    charge_ref,
    copies_ref,
    descriptor_ref,
    environment_ref,
    kind_ref,
    moments_ref,
    padded_ref,
    weight_in_ref,
    weight_hidden_ref,
    row_ref,
    semaphores,
):
    fetches = [
        pltpu.make_async_copy(weight_in_hbm, weight_in_ref, semaphores.at[0]),
        pltpu.make_async_copy(weight_hidden_hbm, weight_hidden_ref, semaphores.at[1]),
    ]
    for fetch in fetches:
        fetch.start()
    slots, atoms = slots_ref.shape
    rows = atoms // 2
    lane = lax.broadcasted_iota(jnp.int32, (8, 128), 1)
    sub = lax.broadcasted_iota(jnp.int32, (8, 128), 0)

    width = first_ref.shape[1]
    padded_ref[...] = jnp.zeros_like(padded_ref)
    padded_ref[0, 0:2, 0:width] = first_ref[...]
    for column in range(2):
        padded_ref[1, 0:width, 32 * column : 32 * column + width] = second_ref[
            :, width * column : width * (column + 1)
        ]
    for row in range(2):
        for column in range(4):
            padded_ref[2, 32 * row : 32 * row + width, 32 * column : 32 * column + width] = (
                third_ref[
                    width * row : width * (row + 1), width * column : width * (column + 1)
                ]
            )
    first_table = padded_ref[0].T
    embed_zero = jnp.broadcast_to(first_table[0:32, 0:1], (32, 128))
    embed_one = jnp.broadcast_to(first_table[0:32, 1:2], (32, 128))
    second_high, second_low = split(padded_ref[1].T[0:64, 0:32])
    second_weight = jnp.concatenate([second_high, second_high, second_low], axis=1)
    third_high, third_low = split(padded_ref[2].T[:, 0:64])
    third_weight = jnp.concatenate([third_high, third_high, third_low], axis=1)

    def spread(ref, field, chunk):
        return jnp.broadcast_to(ref[field : field + 1, 128 * chunk : 128 * chunk + 128], (8, 128))

    own = [[spread(own_ref, field, chunk) for chunk in range(2)] for field in range(5)]
    lower = [[spread(lower_ref, field, chunk) for chunk in range(2)] for field in range(4)]
    upper = [spread(upper_ref, field, 0) for field in range(4)]

    def pick_two(tables, index):
        within = index & 127
        return jnp.where(index < 128, lane_pick(tables[0], within), lane_pick(tables[1], within))

    pairs = jnp.concatenate([slots_ref[:, 0:rows], slots_ref[:, rows:atoms]], axis=0).T
    for tile in range(rows // 8):
        band = slice(8 * tile, 8 * tile + 8)
        index = pairs[band, :]
        centre = 8 * tile + sub + jnp.where(lane < 64, 0, rows)
        from_own = jnp.clip(index - ghosts, 0, atoms - 1)
        from_lower = jnp.minimum(index + (atoms - ghosts), 255)
        from_upper = jnp.clip(index - (ghosts + atoms), 0, 127)

        def neighbour(field):
            below = pick_two(lower[field], from_lower)
            inside = pick_two(own[field], from_own)
            above = lane_pick(upper[field], from_upper)
            return jnp.where(
                index < ghosts, below, jnp.where(index < ghosts + atoms, inside, above)
            )

        offsets = [neighbour(field) - pick_two(own[field], centre) for field in range(3)]
        live = pick_two(own[4], centre)
        present = jnp.where((lane & 63).astype(jnp.float32) < live, 1.0, 0.0)
        smooth = present / (
            1.0 + (offsets[0] * offsets[0] + offsets[1] * offsets[1] + offsets[2] * offsets[2])
        )
        environment_ref[0, band, :] = smooth
        for field in range(3):
            environment_ref[1 + field, band, :] = smooth * offsets[field]
        kind_ref[band, :] = neighbour(3)

    group = 8

    def stacked(values):
        high, low = split(values)
        return jnp.concatenate([high, low, high], axis=0)

    def one_group(start):
        pieces = []
        for row in range(group):
            smooth = jnp.broadcast_to(environment_ref[0, pl.ds(start + row, 1), :], (32, 128))
            kind = jnp.broadcast_to(kind_ref[pl.ds(start + row, 1), :], (32, 128))
            pieces.append(
                jnp.tanh(smooth * ((1.0 - kind) * embed_zero + kind * embed_one))
            )
        first = jnp.concatenate(pieces, axis=1)
        second = jnp.tanh(multiply(second_weight, stacked(first), ((1,), (0,))))
        second = second + jnp.concatenate([first, first], axis=0)
        third = jnp.tanh(multiply(third_weight, stacked(second), ((1,), (0,))))
        third = third + jnp.concatenate([second, second], axis=0)
        third_pair = split(third)
        for half in range(group // 4):
            columns = slice(512 * half, 512 * half + 512)
            bands = []
            for part in range(4):
                bands.append(
                    jnp.concatenate(
                        [
                            jnp.where(
                                sub == row + jnp.where(lane < 64, 0, 4),
                                jnp.broadcast_to(
                                    environment_ref[part, pl.ds(start + 4 * half + row, 1), :],
                                    (8, 128),
                                ),
                                0.0,
                            )
                            for row in range(4)
                        ],
                        axis=1,
                    )
                )
            environment = split(jnp.concatenate(bands, axis=0))
            both = multiply(
                jnp.concatenate(environment, axis=0), third_pair[0][:, columns], LANES
            )
            sums = both[0:32] + both[32:64]
            sums = sums + multiply(environment[0], third_pair[1][:, columns], LANES)
            sums = sums * (1.0 / slots)
            for part in range(4):
                moments_ref[part, pl.ds(2 * start + 8 * half, 8), :] = sums[
                    8 * part : 8 * part + 8
                ]

    def body(step, carry):
        for part in range(unroll):
            one_group(pl.multiple_of(step * unroll * group + part * group, group))
        return carry

    unroll = rows // group
    lax.fori_loop(0, rows // (unroll * group), body, 0)

    chunks = (descriptor_ref.shape[1] + 127) // 128
    last = descriptor_ref.shape[1] - 128 * (chunks - 1)

    def describe_band(start):
        band = pl.ds(start, 8)
        moments = [moments_ref[part, band, :] for part in range(4)]
        axis_part = [lane_pick(moments[part], lane & 15) for part in range(4)]
        for chunk in range(chunks):
            spot = jnp.broadcast_to(spot_ref[chunk : chunk + 1, :], (8, 128))
            total = lane_pick(moments[0], spot) * axis_part[0]
            for part in range(1, 4):
                total = total + lane_pick(moments[part], spot) * axis_part[part]
            if chunk < chunks - 1:
                descriptor_ref[band, 128 * chunk : 128 * chunk + 128] = total
            else:
                descriptor_ref[band, 128 * chunk : 128 * chunk + last] = total[:, 0:last]

    bands = 8 if atoms % 64 == 0 else 1

    def describe(step, carry):
        for part in range(bands):
            describe_band(pl.multiple_of(step * 8 * bands + 8 * part, 8))
        return carry

    lax.fori_loop(0, atoms // (8 * bands), describe, 0)

    store = pltpu.make_async_copy(descriptor_ref, descriptor_hbm, semaphores.at[2])
    store.start()
    for fetch in fetches:
        fetch.wait()
    shift = fitting_rows(descriptor_ref, weight_in_ref, weight_hidden_ref, weight_out_ref)
    kind = types_ref[...].astype(jnp.float32)
    charge = (1.0 - kind) * charges_ref[0] + kind * charges_ref[1] + natural_order(shift)
    charge_ref[...] = charge
    fields = [
        cell_x_ref[...].astype(jnp.float32),
        (cell_y_ref[...] + base_ref[0]).astype(jnp.float32),
        cell_z_ref[...].astype(jnp.float32),
    ]
    fields = fields + [fraction_ref[axis] for axis in range(3)] + [charge]
    for place, field in enumerate(fields):
        row_ref[:, atoms * place : atoms * (place + 1)] = field
    for copy in range(copies_ref.shape[0]):
        copies_ref[copy] = row_ref[...]
    store.wait()


def spot_table(embed, desc):
    column = np.arange(desc) // AXIS
    quarter = embed // 4
    place = 32 * (column // quarter) + column % quarter
    chunks = (desc + 127) // 128
    table = np.zeros((chunks * 128,), np.int32)
    table[:desc] = place
    padded = np.zeros(((chunks + 7) // 8 * 8, 128), np.int32)
    padded[:chunks] = table.reshape(chunks, 128)
    return padded


def networks(
    copies,
    ghosts,
    base,
    charge_base,
    own,
    lower,
    upper,
    neighbours,
    types,
    cells,
    fraction,
    embed,
    weight_in,
    weight_hidden,
    weight_out,
):
    atoms = types.shape[1]
    desc, width = weight_in.shape
    spots = jnp.asarray(spot_table(embed[2].shape[1], desc))
    anywhere = pl.BlockSpec(memory_space=pl.ANY)
    scalars = pl.BlockSpec(memory_space=pltpu.SMEM)
    blocks = (own, lower, upper, neighbours[0].T, types, *cells, fraction, *embed, spots)
    weight_out = weight_out.reshape(1, -1)
    results = [
        jax.ShapeDtypeStruct((atoms, desc), jnp.float32),
        jax.ShapeDtypeStruct((1, atoms), jnp.float32),
        jax.ShapeDtypeStruct((copies, 1, FIELDS * atoms), jnp.float32),
    ]
    return pl.pallas_call(
        functools.partial(network_kernel, ghosts),
        grid=(1,),
        out_shape=results,
        in_specs=[scalars, scalars]
        + whole_specs(*blocks)
        + [anywhere, anywhere]
        + whole_specs(weight_out),
        out_specs=[anywhere] + whole_specs(*results[1:]),
        scratch_shapes=[
            pltpu.VMEM((atoms, desc), jnp.float32),
            pltpu.VMEM((4, atoms // 2, 128), jnp.float32),
            pltpu.VMEM((atoms // 2, 128), jnp.float32),
            pltpu.VMEM((4, atoms, 128), jnp.float32),
            pltpu.VMEM((3, 128, 128), jnp.float32),
            pltpu.VMEM((width, desc), jnp.float32),
            pltpu.VMEM(weight_hidden.shape, jnp.float32),
            pltpu.VMEM((1, FIELDS * atoms), jnp.float32),
            pltpu.SemaphoreType.DMA((3,)),
        ],
        compiler_params=pltpu.CompilerParams(vmem_limit_bytes=VMEM_BYTES),
        name="networks",
    )(base, charge_base, *blocks, weight_in.T, weight_hidden, weight_out)


def energy_kernel(descriptor_ref, weight_in_ref, weight_hidden_ref, weight_out_ref, energy_ref):
    energy_ref[...] = natural_order(
        fitting_rows(descriptor_ref, weight_in_ref, weight_hidden_ref, weight_out_ref)
    )


def energies(descriptor, weight_in, weight_hidden, weight_out):
    atoms, desc = descriptor.shape
    width = weight_in.shape[1]
    arrays = (descriptor, weight_in.T, weight_hidden, weight_out.reshape(1, -1))
    result = jax.ShapeDtypeStruct((1, atoms), jnp.float32)
    return pl.pallas_call(
        energy_kernel,
        grid=(1,),
        out_shape=result,
        in_specs=whole_specs(*arrays),
        out_specs=whole(result.shape),
        compiler_params=pltpu.CompilerParams(vmem_limit_bytes=VMEM_BYTES),
        cost_estimate=pl.CostEstimate(
            flops=6 * atoms * desc * width, bytes_accessed=4 * desc * width, transcendentals=0
        ),
        name="energies",
    )(*arrays)


def weight_rows(fraction):
    square = fraction * fraction
    cubed = square * fraction
    rest = 1.0 - fraction
    return [
        rest * rest * rest / 6.0,
        (3.0 * cubed - 6.0 * square + 4.0) / 6.0,
        (-3.0 * cubed + 3.0 * square + 3.0 * fraction + 1.0) / 6.0,
        cubed / 6.0,
    ]


def placed_weights(distance, weights):
    shape = distance.shape
    result = jnp.zeros(shape, jnp.float32)
    for step in range(4):
        result = jnp.where(
            distance == step, jnp.broadcast_to(weights[step], shape), result
        )
    return result


def third_factors(fields, waves_ref, cosine_ref):
    atoms = fields.shape[1]
    start = fields[2:3, :].astype(jnp.int32)
    along = weight_rows(fields[5:6, :])
    parts = waves_ref.shape[0]
    cosine = jnp.broadcast_to(cosine_ref[...], (parts, 128))
    wave = jnp.broadcast_to(waves_ref[:, 0:1], (parts, 128))
    shift = jnp.broadcast_to(waves_ref[:, 1:2], (parts, 128))
    pieces = []
    for chunk in range(atoms // 128):
        lanes = slice(128 * chunk, 128 * chunk + 128)
        total = jnp.zeros((parts, 128), jnp.float32)
        for step in range(4):
            place = jnp.broadcast_to(start[:, lanes] + step, (parts, 128))
            phase = (wave * place + shift) & (NG - 1)
            value = lane_pick(cosine, phase & 127)
            value = jnp.where(phase < 128, value, -value)
            total = total + value * jnp.broadcast_to(along[step][:, lanes], (parts, 128))
        pieces.append(total)
    return jnp.concatenate(pieces, axis=1)


def first_third_split(fields, waves_ref, cosine_ref, window, scale, high_ref, low_ref):
    atoms = fields.shape[1]
    third = third_factors(fields, waves_ref, cosine_ref) * scale
    rows = lax.broadcasted_iota(jnp.int32, (window, atoms), 0)
    first = placed_weights(
        rows - fields[0:1, :].astype(jnp.int32), weight_rows(fields[3:4, :])
    )
    for chunk in range(atoms // 128):
        lanes = slice(128 * chunk, 128 * (chunk + 1))
        for part in range(0, third.shape[0], 2):
            high, low = split(
                jnp.concatenate(
                    [first[:, lanes] * third[part + side : part + side + 1, lanes] for side in range(2)],
                    axis=0,
                )
            )
            place = slice(part * window, (part + 2) * window)
            high_ref[place, lanes] = high
            low_ref[place, lanes] = low
    return high_ref[...], low_ref[...]


def second_factors(fields, base, block_y, slabs, high_ref, low_ref):
    atoms = fields.shape[1]
    block = atoms // slabs
    reach = block_y + REACH
    start = fields[1:2, :].astype(jnp.int32) - base
    weights = weight_rows(fields[4:5, :])
    for chunk in range(atoms // 128):
        lanes = slice(128 * chunk, 128 * (chunk + 1))
        first = 128 * chunk // block
        last = (128 * chunk + 127) // block
        top = first * block_y
        rows = (last - first) * block_y + reach
        pieces = [(top, min(rows, NG - top))]
        if top + rows > NG:
            pieces.append((0, top + rows - NG))
        for row, count in pieces:
            index = row + lax.broadcasted_iota(jnp.int32, (count, 128), 0)
            table = split(
                placed_weights(
                    (index - start[:, lanes]) & (NG - 1), [weight[:, lanes] for weight in weights]
                )
            )
            high_ref[row : row + count, lanes] = table[0]
            low_ref[row : row + count, lanes] = table[1]
    return high_ref[...], low_ref[...]


def wave_of(index):
    return jnp.where(index <= NG // 2, index, index - NG // 2)


def damping(index):
    kappa = wave_of(index).astype(jnp.float32) * (2.0 * math.pi / NG)
    squared = kappa * kappa
    ends = (index == 0) | (index == NG // 2)
    return squared, jnp.exp(-0.5 * squared) * jnp.where(ends, 1.0 / NG, 2.0 / NG)


def transform(planes, kappa_ref, first_part, tables_ref, last_ref):
    count = len(planes)
    basis = tables_ref[0]
    turned = tables_ref[1]
    square_x, damp_x = damping(lax.broadcasted_iota(jnp.int32, (NG, 1), 0))
    square_y, damp_y = damping(lax.broadcasted_iota(jnp.int32, (1, NG), 1))
    square_xy = square_x + square_y
    damp_xy = damp_x * damp_y
    columns = [slice(NG * part, NG * (part + 1)) for part in range(count)]
    first = product(basis, jnp.concatenate(planes, axis=1))
    first = jnp.concatenate([first[:, column] for column in columns], axis=0)
    both = product(first, turned)
    scaled = []
    for part in range(count):
        squared = square_xy + kappa_ref[first_part + part, 0]
        root = jnp.where(squared == 0.0, 1.0, 0.0)
        green = (1.0 - root) * (damp_xy * kappa_ref[first_part + part, 1]) / (squared + root)
        scaled.append(both[columns[part]] * green)
    back = product(turned, jnp.concatenate(scaled, axis=1))
    back = jnp.concatenate([back[:, column] for column in columns], axis=0)
    return product(back, last_ref[...])


def send_blocks(full, block_x, block_y, put):
    low_lanes = lax.broadcasted_iota(jnp.int32, (NG, 128), 1) < block_y
    for pair in range(full.shape[0] // (2 * NG)):
        even = full[2 * NG * pair : 2 * NG * pair + NG, 0:128]
        odd = full[2 * NG * pair + NG : 2 * NG * (pair + 1), 0:128]
        blocks = [
            jnp.where(low_lanes, even, pltpu.roll(odd, block_y, 1)),
            jnp.where(low_lanes, pltpu.roll(even, block_y, 1), odd),
        ]
        for brick in range(NG // block_x):
            for side in range(2):
                for group in range(block_x // 8):
                    start = block_x * brick + 8 * group
                    put(pair, brick, side, group, blocks[side][start : start + 8])


def spread_kernel(
    block_x,
    block_y,
    window,
    kappa_ref,
    pair_ref,
    static_ref,
    waves_ref,
    cosine_ref,
    tables_hbm,
    last_hbm,
    short_hbm,
    sent_ref,
    full_ref,
    atoms_ref,
    later_hbm,
    grid_ref,
    tables_ref,
    last_ref,
    semaphores,
    *pair_refs,
):
    slabs = NG // block_y
    second_refs, first_refs = pair_refs[:4], pair_refs[4:]
    bricks = NG // block_x
    parts = waves_ref.shape[0]
    block = static_ref.shape[2] // FIELDS
    count = full_ref.shape[0]
    step = pl.program_id(0)
    later = later_hbm.shape[0]
    store = pltpu.make_async_copy(
        grid_ref.at[pl.ds(parts - later, later), pl.ds(0, NG)], later_hbm, semaphores.at[2]
    )

    @pl.when(step == 0)
    def _():
        fetches = [
            pltpu.make_async_copy(tables_hbm, tables_ref, semaphores.at[0]),
            pltpu.make_async_copy(last_hbm.at[pair_ref[0]], last_ref, semaphores.at[1]),
        ]
        for fetch in fetches:
            fetch.start()
        for slab in range(slabs):
            lanes = slice(block * slab, block * (slab + 1))
            for brick in range(bricks):
                for field in range(FIELDS):
                    atoms_ref[brick, field : field + 1, lanes] = static_ref[
                        slab * bricks + brick, :, block * field : block * (field + 1)
                    ]
        for ref in second_refs:
            ref[...] = jnp.zeros_like(ref)
        for brick in range(bricks):
            fields = atoms_ref[brick]
            table = first_third_split(
                fields,
                waves_ref,
                cosine_ref,
                window,
                fields[6:7, :],
                first_refs[2 * (brick % 2)],
                first_refs[2 * (brick % 2) + 1],
            )
            second = second_factors(
                fields, 0, block_y, slabs, second_refs[2 * (brick % 2)], second_refs[2 * (brick % 2) + 1]
            )
            spread = triple(table, second, LANES)
            start = block_x * brick
            extra = window - block_x
            for part in range(parts):
                shared = spread[part * window : part * window + extra]
                if brick > 0:
                    shared = shared + grid_ref[part, start : start + extra, :]
                grid_ref[part, start : start + extra, :] = shared
                grid_ref[part, start + extra : start + window, :] = spread[
                    part * window + extra : part * window + window
                ]
        for part in range(parts):
            grid_ref[part, 0:extra, :] += grid_ref[part, NG : NG + extra, :]
        store.start()
        for fetch in fetches:
            fetch.wait()

    planes = [grid_ref[count * step + part, 0:NG, :] for part in range(count)]
    full = transform(planes, kappa_ref, count * step, tables_ref, last_ref)
    for part in range(count):
        full_ref[part] = full[NG * part : NG * (part + 1)]

    def put(pair, brick, side, group, tile):
        sent_ref[2 * brick + side, group, pair] = tile

    send_blocks(full, block_x, block_y, put)

    @pl.when(step == pl.num_programs(0) - 1)
    def _():
        store.wait()


def early_pairs(parts):
    return parts // 4


def spread_and_solve(
    block_x, block_y, window, kappa, pair, static, waves, cosine_row, tables, last, short
):
    atoms = static.shape[2] // FIELDS
    slabs = NG // block_y
    bricks = NG // block_x
    parts = waves.shape[0]
    pairs = early_pairs(parts)
    count = 4
    anywhere = pl.BlockSpec(memory_space=pl.ANY)
    scalars = pl.BlockSpec(memory_space=pltpu.SMEM)
    sent_block = (2 * bricks, block_x // 8, count // 2, 8, 128)
    return pl.pallas_call(
        functools.partial(spread_kernel, block_x, block_y, window),
        grid=(2 * pairs // count,),
        out_shape=[
            jax.ShapeDtypeStruct((2 * bricks, block_x // 8, pairs, 8, 128), jnp.float32),
            jax.ShapeDtypeStruct((2 * pairs, NG, NG), jnp.float32),
            jax.ShapeDtypeStruct((bricks, 8, slabs * atoms), jnp.float32),
            jax.ShapeDtypeStruct((parts - 2 * pairs, NG, NG), jnp.float32),
        ],
        in_specs=[scalars, scalars]
        + whole_specs(static, waves, cosine_row)
        + [anywhere, anywhere, anywhere],
        out_specs=[
            pl.BlockSpec(sent_block, lambda step: (0, 0, step, 0, 0)),
            pl.BlockSpec((count, NG, NG), lambda step: (step, 0, 0)),
            whole((bricks, 8, slabs * atoms)),
            anywhere,
        ],
        scratch_shapes=[
            pltpu.VMEM((parts, NG + window - block_x, NG), jnp.float32),
            pltpu.VMEM(tables.shape, tables.dtype),
            pltpu.VMEM(last.shape[1:], last.dtype),
            pltpu.SemaphoreType.DMA((3,)),
        ]
        + [pltpu.VMEM((NG, slabs * atoms), jnp.bfloat16)] * 4
        + [pltpu.VMEM((parts * window, slabs * atoms), jnp.bfloat16)] * 4,
        compiler_params=pltpu.CompilerParams(vmem_limit_bytes=VMEM_BYTES),
        name="spread_and_solve",
    )(kappa, pair, static, waves, cosine_row, tables, last, short)


def sample_kernel(
    block_x,
    block_y,
    window,
    kappa_ref,
    pair_ref,
    atoms_ref,
    waves_ref,
    cosine_ref,
    tables_hbm,
    last_hbm,
    later_hbm,
    early_hbm,
    sent_ref,
    later_ref,
    full_ref,
    tables_ref,
    last_ref,
    semaphores,
    packed_ref,
):
    bricks = atoms_ref.shape[0]
    parts = waves_ref.shape[0]
    early = 2 * early_pairs(parts)
    block = atoms_ref.shape[2] * block_y // NG
    fetches = [
        pltpu.make_async_copy(tables_hbm, tables_ref, semaphores.at[0]),
        pltpu.make_async_copy(last_hbm.at[pair_ref[0]], last_ref, semaphores.at[1]),
        pltpu.make_async_copy(later_hbm, later_ref, semaphores.at[2]),
        pltpu.make_async_copy(early_hbm, full_ref.at[pl.ds(0, early)], semaphores.at[3]),
    ]
    for fetch in fetches:
        fetch.start()
    for fetch in fetches[:3]:
        fetch.wait()
    pairs = (parts - early) // 2
    planes = [later_ref[part] for part in range(parts - early)]
    full = transform(planes, kappa_ref, early, tables_ref, last_ref)
    for part in range(parts - early):
        full_ref[early + part] = full[NG * part : NG * (part + 1)]

    def put(pair, brick, side, group, tile):
        sent_ref[2 * brick + side, pairs * group + pair] = tile

    send_blocks(full, block_x, block_y, put)
    fetches[3].wait()

    reach = block_y + REACH
    lane = lax.broadcasted_iota(jnp.int32, (NG, 128), 1)
    for part in range(parts):
        for side in range(2):
            values = full_ref[part, :, 128 * side : 128 * (side + 1)]
            high = values.astype(jnp.bfloat16).astype(jnp.float32)
            again = pltpu.roll(high, reach, 1)
            low = pltpu.roll(values - high, 2 * reach - 128, 1)
            packed_ref[side, part, 0:NG, 0:128] = jnp.where(lane < reach, high, again)
            packed_ref[side, part, 0:NG, 128:NG] = jnp.where(
                lane < 2 * reach - 128, again, jnp.where(lane < 3 * reach - 128, low, 0.0)
            )
            packed_ref[side, part, NG : NG + window - block_x, :] = packed_ref[
                side, part, 0 : window - block_x, :
            ]
    extra = sent_ref.shape[1] - 1
    base = 2 * block_y * pair_ref[0]
    lanes = pl.ds(pl.multiple_of(2 * block * pair_ref[0], 128), 2 * block)
    for brick in range(bricks):
        fields = atoms_ref[brick, :, lanes]
        thirds = third_factors(fields, waves_ref, cosine_ref)
        rows = slice(block_x * brick, block_x * brick + window)
        for side in range(2):
            here = slice(block * side, block * (side + 1))
            third = thirds[:, here]
            ours = fields[:, here]
            index = lax.broadcasted_iota(jnp.int32, (window, block), 0)
            first = placed_weights(
                index - ours[0:1, :].astype(jnp.int32), weight_rows(ours[3:4, :])
            )
            index = lax.broadcasted_iota(jnp.int32, (reach, block), 0)
            start = ours[1:2, :].astype(jnp.int32) - (base + block_y * side)
            high, low = split(placed_weights(index - start, weight_rows(ours[4:5, :])))
            rest = jnp.zeros((NG - 3 * reach, block), jnp.bfloat16)
            second = jnp.concatenate([high, low, high, rest], axis=0)
            values = jnp.concatenate(
                [packed_ref[side, part, rows, :] for part in range(parts)], axis=0
            )
            along = multiply(values.astype(jnp.bfloat16), second, ((1,), (0,)))
            total = jnp.zeros((window, block), jnp.float32)
            for part in range(parts):
                total = total + along[window * part : window * (part + 1)] * third[part : part + 1]
            row = jnp.sum(total * first, axis=0, keepdims=True)
            sent_ref[2 * brick + side, extra] = jnp.zeros((8, 128), jnp.float32)
            sent_ref[2 * brick + side, extra, 0:1, :] = row[:, 0:128]
            sent_ref[2 * brick + side, extra, 1:2, 0 : block - 128] = row[:, 128:block]


def solve_and_sample(
    block_x, block_y, window, kappa, pair, atoms, waves, cosine_row, tables, last, later, early
):
    bricks = atoms.shape[0]
    parts = waves.shape[0]
    pairs = parts // 2 - early_pairs(parts)
    anywhere = pl.BlockSpec(memory_space=pl.ANY)
    scalars = pl.BlockSpec(memory_space=pltpu.SMEM)
    result = jax.ShapeDtypeStruct((2 * bricks, block_x // 8 * pairs + 1, 8, 128), jnp.float32)
    return pl.pallas_call(
        functools.partial(sample_kernel, block_x, block_y, window),
        grid=(1,),
        out_shape=result,
        in_specs=[scalars, scalars] + whole_specs(atoms, waves, cosine_row) + [anywhere] * 4,
        out_specs=whole(result.shape),
        scratch_shapes=[
            pltpu.VMEM((2 * pairs, NG, NG), jnp.float32),
            pltpu.VMEM((parts, NG, NG), jnp.float32),
            pltpu.VMEM(tables.shape, tables.dtype),
            pltpu.VMEM(last.shape[1:], last.dtype),
            pltpu.SemaphoreType.DMA((4,)),
        ]
        + [pltpu.VMEM((2, parts, NG + window - block_x, NG), jnp.float32)],
        compiler_params=pltpu.CompilerParams(vmem_limit_bytes=VMEM_BYTES),
        cost_estimate=pl.CostEstimate(
            flops=24 * parts * NG * NG * NG, bytes_accessed=4 * early.size, transcendentals=0
        ),
        name="solve_and_sample",
    )(kappa, pair, atoms, waves, cosine_row, tables, last, later, early)


def finish_kernel(
    block_y,
    early_ref,
    later_ref,
    sums_ref,
    short_hbm,
    charge_hbm,
    table_ref,
    out_ref,
    energy_ref,
    short_ref,
    charge_ref,
    semaphores,
):
    atoms = short_ref.shape[1]
    fetches = [
        pltpu.make_async_copy(short_hbm, short_ref, semaphores.at[0]),
        pltpu.make_async_copy(charge_hbm, charge_ref, semaphores.at[1]),
    ]

    @pl.when(pl.program_id(0) == 0)
    def _():
        for fetch in fetches:
            fetch.start()

    lines = early_ref.shape[3]
    sources, _, pairs = early_ref.shape[:3]
    early = early_ref.reshape(sources * pairs, lines, 128)
    later = later_ref.reshape(sources * later_ref.shape[1], lines, 128)
    pieces = []
    for line in range(lines):
        turned = jnp.concatenate([early[:, line, :], later[:, line, :]], axis=0).T
        pieces.append(jnp.concatenate([turned[0:block_y], turned[block_y:]], axis=1))
    result = product(jnp.concatenate(pieces, axis=0), table_ref[...])
    for line in range(lines):
        out_ref[line] = result[block_y * line : block_y * (line + 1)]

    @pl.when(pl.program_id(0) == 0)
    def _():
        for fetch in fetches:
            fetch.wait()
        total = jnp.sum(sums_ref[:, 0], axis=0)
        potential_at = jnp.concatenate([total[0:1, :], total[1:2, 0 : atoms - 128]], axis=1)
        energy_ref[...] = short_ref[...] + 0.5 * charge_ref[...] * potential_at


def finish(block_x, block_y, early, later, short, charge, table):
    bricks2, groups, pairs = early.shape[:3]
    rest = (later.shape[1] - 1) // groups
    atoms = short.shape[1]
    return pl.pallas_call(
        functools.partial(finish_kernel, block_y),
        grid=(groups,),
        out_shape=[
            jax.ShapeDtypeStruct((block_x, block_y, NG), jnp.float32),
            jax.ShapeDtypeStruct((1, atoms), jnp.float32),
        ],
        in_specs=[
            pl.BlockSpec((bricks2, 1, pairs, 8, 128), lambda index: (0, index, 0, 0, 0)),
            pl.BlockSpec((bricks2, rest, 8, 128), lambda index: (0, index, 0, 0)),
            pl.BlockSpec((bricks2, 1, 8, 128), lambda index: (0, groups * rest, 0, 0)),
            pl.BlockSpec(memory_space=pltpu.HBM),
            pl.BlockSpec(memory_space=pltpu.HBM),
            whole(table.shape),
        ],
        out_specs=[
            pl.BlockSpec((8, block_y, NG), lambda index: (index, 0, 0)),
            whole((1, atoms)),
        ],
        scratch_shapes=[
            pltpu.VMEM((1, atoms), jnp.float32),
            pltpu.VMEM((1, atoms), jnp.float32),
            pltpu.SemaphoreType.DMA((2,)),
        ],
        compiler_params=pltpu.CompilerParams(vmem_limit_bytes=32 * 2**20),
        name="finish",
    )(early, later, later, short, charge, table)


def real_basis():
    index = np.arange(NG)
    wave = np.where(index <= NG // 2, index, index - NG // 2)
    angle = (wave[:, None] * index[None, :] % NG) * (2.0 * math.pi / NG)
    return np.where((index <= NG // 2)[:, None], np.cos(angle), np.sin(angle))


def per_device(
    positions,
    types,
    neighbours,
    neighbour_count,
    send_index,
    cell_x,
    cell_y,
    cell_z,
    spline_fraction,
    embed_first,
    embed_second,
    embed_third,
    energy_in,
    energy_hidden,
    energy_out,
    wannier_in,
    wannier_hidden,
    wannier_out,
    charge_base,
):
    atoms = types.shape[1]
    ghosts = send_index.shape[1] // 2
    count_x = lax.axis_size("brick")
    count_y = lax.axis_size("slab")
    block_x = NG // count_x
    block_y = NG // count_y
    window = block_x + 8
    parts = NG // (2 * count_x)
    brick = lax.axis_index("brick")
    slab = lax.axis_index("slab")
    pair = (slab // 2).astype(jnp.int32).reshape(1)
    halves = [
        [b * count_y + 2 * p + side for b in range(count_x) for side in range(2)]
        for p in range(count_y // 2)
    ]

    def exchange(values, axes, groups=None):
        return lax.all_to_all(
            values, axes, split_axis=0, concat_axis=0, tiled=True, axis_index_groups=groups
        )

    own, outgoing = collect(positions, types, neighbour_count, send_index)
    up = [(i, (i + 1) % count_x) for i in range(count_x)]
    down = [((i + 1) % count_x, i) for i in range(count_x)]
    lower = lax.ppermute(outgoing, "brick", up)
    upper = lax.ppermute(outgoing, "brick", down)
    descriptor, charge, fields = networks(
        count_x * count_y,
        ghosts,
        (slab * block_y).astype(jnp.int32).reshape(1),
        charge_base,
        own,
        lower,
        upper,
        neighbours,
        types,
        (cell_x, cell_y, cell_z),
        spline_fraction,
        (embed_first, embed_second, embed_third),
        wannier_in,
        wannier_hidden,
        wannier_out,
    )
    every_field = exchange(fields, ("slab", "brick"))

    part = (2 * brick + slab % 2) * parts + jnp.arange(parts, dtype=jnp.int32)
    wave = wave_of(part)
    waves = jnp.stack([wave, jnp.where(part <= NG // 2, 0, 3 * NG // 4)], axis=1)
    kappa = wave.astype(jnp.float32) * (2.0 * math.pi / NG)
    squared = kappa * kappa
    ends = (part == 0) | (part == NG // 2)
    kappa = jnp.stack(
        [squared, jnp.exp(-0.5 * squared) * jnp.where(ends, 1.0 / NG, 2.0 / NG)], axis=1
    )
    basis = real_basis()
    tables = np.stack([basis, basis.T]).astype(np.float32)
    last = []
    for p in range(count_y // 2):
        points = np.concatenate(
            [np.arange(2 * block_y), block_y + np.arange(block_y + REACH)]
        )
        points = (2 * block_y * p + points) % NG
        columns = np.zeros((NG, NG))
        columns[:, : points.size] = basis[:, points]
        last.append(columns.astype(np.float32))
    cosine_row = np.cos(np.arange(128) * (2.0 * math.pi / NG)).astype(np.float32)[None]
    cosine_row = jnp.asarray(cosine_row)
    tables = jnp.asarray(tables)
    last = jnp.asarray(np.stack(last))
    energy_short = energies(descriptor, energy_in, energy_hidden, energy_out)
    early, full, every_atom, later = spread_and_solve(
        block_x,
        block_y,
        window,
        kappa,
        pair,
        every_field,
        waves,
        cosine_row,
        tables,
        last,
        energy_short,
    )

    def send(values):
        got = exchange(values.reshape(values.shape[0], -1, 128), ("brick", "slab"), halves)
        return got.reshape(values.shape)

    early = send(early)
    later = solve_and_sample(
        block_x,
        block_y,
        window,
        kappa,
        pair,
        every_atom,
        waves,
        cosine_row,
        tables,
        last,
        later,
        full,
    )
    later = send(later)
    source = np.arange(2 * count_x)[:, None] * parts
    pairs = 2 * np.arange(parts // 2)[None, :]
    order = np.concatenate(
        [
            (source + pairs[:, : early_pairs(parts)]).ravel(),
            (source + pairs[:, early_pairs(parts) :]).ravel(),
        ]
    )
    order = np.concatenate([order, order + 1])
    potential, atom_energy = finish(
        block_x,
        block_y,
        early,
        later,
        energy_short,
        charge,
        jnp.asarray(basis[order].astype(np.float32)),
    )
    return atom_energy, potential


def solution(mesh):
    placed = (
        P(None, "slab", "brick"),
        P("slab", "brick"),
        P("slab", "brick", None),
        P("slab", "brick"),
        P("slab", "brick"),
        P("slab", "brick"),
        P("slab", "brick"),
        P("slab", "brick"),
        P(None, "slab", "brick"),
    ) + (P(),) * 10
    bricks, slabs = mesh.shape["brick"], mesh.shape["slab"]
    fits = 2 * NG == 128 * slabs and NG % (32 * bricks) == 0
    return jax.shard_map(
        per_device if fits else per_device_general,
        mesh=mesh,
        in_specs=placed,
        out_specs=(P("slab", "brick"), P("brick", "slab", None)),
        check_vma=False,
    )
```

```python
import functools
import math

import jax
import jax.numpy as jnp
import numpy as np
from jax import lax
from jax.experimental import pallas as pl
from jax.experimental.pallas import tpu as pltpu
from jax.sharding import PartitionSpec as P

NG = 256
AXIS = 16
VMEM_BYTES = 60 * 2**20
REACH = 16
FIELDS = 7


HIGH = lax.Precision.HIGHEST


def with_halo(cells, sides, width):
    for axis, dim in sides:
        count = lax.axis_size(axis)
        head = lax.slice_in_dim(cells, 0, width, axis=dim)
        tail = lax.slice_in_dim(cells, cells.shape[dim] - width, cells.shape[dim], axis=dim)
        cells = jnp.concatenate(
            [
                lax.ppermute(tail, axis, [(i, (i + 1) % count) for i in range(count)]),
                cells,
                lax.ppermute(head, axis, [((i + 1) % count, i) for i in range(count)]),
            ],
            axis=dim,
        )
    return cells


def spline_weights(fraction):
    cubed = fraction * fraction * fraction
    square = fraction * fraction
    return jnp.stack(
        [
            (1.0 - fraction) * (1.0 - fraction) * (1.0 - fraction) / 6.0,
            (3.0 * cubed - 6.0 * square + 4.0) / 6.0,
            (-3.0 * cubed + 3.0 * square + 3.0 * fraction + 1.0) / 6.0,
            cubed / 6.0,
        ]
    )


def fitting(descriptor, weight_in, weight_hidden, weight_out):
    hidden = jnp.tanh(jnp.dot(descriptor, weight_in, precision=HIGH))
    for depth_index in range(weight_hidden.shape[0]):
        hidden = jnp.tanh(jnp.dot(hidden, weight_hidden[depth_index], precision=HIGH)) + hidden
    return jnp.dot(hidden, weight_out, precision=HIGH)


def atom_terms(
    extended,
    neighbour_rows,
    neighbour_total,
    embed_first,
    embed_second,
    embed_third,
    energy_in,
    energy_hidden,
    energy_out,
    wannier_in,
    wannier_hidden,
    wannier_out,
):
    atom_count, slots = neighbour_rows.shape
    ghost_rows = (extended.shape[1] - atom_count) // 2
    block_size = 64
    blocks = atom_count // block_size
    present = (jnp.arange(slots, dtype=jnp.int32)[None, :] < neighbour_total[:, None]).astype(
        jnp.float32
    )
    centre_ids = (ghost_rows + jnp.arange(atom_count, dtype=jnp.int32)).reshape(blocks, block_size)
    second_weight = embed_second.T
    third_weight = embed_third.T

    def one_block(pieces):
        centre_rows, rows_block, present_block = pieces
        centre_block = extended[:3, centre_rows]
        gathered = extended[:, rows_block]
        offsets = gathered[:3] - centre_block[:, :, None]
        smooth = present_block / (1.0 + jnp.sum(offsets * offsets, axis=0))
        environment = jnp.stack(
            [smooth, smooth * offsets[0], smooth * offsets[1], smooth * offsets[2]], axis=0
        )
        kind = gathered[3][None]
        mixing = (1.0 - kind) * embed_first[0][:, None, None] + kind * embed_first[1][:, None, None]
        first = jnp.tanh(smooth[None] * mixing).reshape(embed_first.shape[1], block_size * slots)
        second = jnp.tanh(jnp.dot(second_weight, first, precision=HIGH)) + jnp.concatenate(
            [first, first], axis=0
        )
        third = jnp.tanh(jnp.dot(third_weight, second, precision=HIGH)) + jnp.concatenate(
            [second, second], axis=0
        )
        third_blocks = third.reshape(third.shape[0], block_size, slots)
        moments = jnp.einsum("kan,can->akc", third_blocks, environment, precision=HIGH) / slots
        descriptor = jnp.einsum("amc,akc->amk", moments, moments[:, :AXIS], precision=HIGH).reshape(
            block_size, -1
        )
        return (
            fitting(descriptor, energy_in, energy_hidden, energy_out),
            fitting(descriptor, wannier_in, wannier_hidden, wannier_out),
        )

    energy_short, charge_shift = lax.map(
        one_block,
        (
            centre_ids,
            neighbour_rows.reshape(blocks, block_size, slots),
            present.reshape(blocks, block_size, slots),
        ),
    )
    return (energy_short.reshape(atom_count), charge_shift.reshape(atom_count))


def green_table(first, second, third, size):

    def folded(index):
        return jnp.where(index < size // 2, index, index - size).astype(jnp.float32) * (
            2.0 * math.pi / size
        )

    kappa_x = folded(first)[:, None, None]
    kappa_y = folded(second)[None, :, None]
    kappa_z = folded(third)[None, None, :]
    squared = kappa_x * kappa_x + kappa_y * kappa_y + kappa_z * kappa_z
    root = (
        (first[:, None, None] == 0) & (second[None, :, None] == 0) & (third[None, None, :] == 0)
    ).astype(jnp.float32)
    return (1.0 - root) * jnp.exp(-0.5 * squared) / (squared + root)


def dft_tables(size):
    index = jnp.arange(size, dtype=jnp.int32)
    phase = (index[:, None] * index[None, :] % size).astype(jnp.float32) * (2.0 * math.pi / size)
    return (jnp.cos(phase), jnp.sin(phase))


def along(values, table, axis_index):
    result = jnp.tensordot(values, table, axes=([axis_index], [0]), precision=HIGH)
    return jnp.moveaxis(result, -1, axis_index)


def complex_transform(paired, axis_index, cosine, sine, inverse):
    real_part = paired[0]
    imag_part = paired[1]
    inner = axis_index - 1
    real_cos = along(real_part, cosine, inner)
    real_sin = along(real_part, sine, inner)
    imag_cos = along(imag_part, cosine, inner)
    imag_sin = along(imag_part, sine, inner)
    if inverse:
        return jnp.stack([real_cos - imag_sin, imag_cos + real_sin])
    return jnp.stack([real_cos + imag_sin, imag_cos - real_sin])


def fold_windows(values, axis_index, block, count):
    front = jnp.moveaxis(values, axis_index, 0)
    rest = front.shape[1:]
    windows = front.reshape((count, block + 3) + rest)
    main_part = windows[:, :block]
    carried = jnp.roll(windows[:, block:], 1, axis=0)
    main_part = main_part.at[:, :3].add(carried)
    return jnp.moveaxis(main_part.reshape((count * block,) + rest), 0, axis_index)


def make_windows(values, axis_index, block, count):
    front = jnp.moveaxis(values, axis_index, 0)
    rest = front.shape[1:]
    pieces = front.reshape((count, block) + rest)
    trailing = jnp.roll(pieces, -1, axis=0)[:, :3]
    windows = jnp.concatenate([pieces, trailing], axis=1)
    return jnp.moveaxis(windows.reshape((count * (block + 3),) + rest), 0, axis_index)


def spread_matrix(start, weights, width, wrap_size):
    offsets = jnp.arange(4, dtype=jnp.int32)[:, None, None]
    target = start[None, :, None] + offsets
    if wrap_size > 0:
        target = target % wrap_size
    hits = (target == jnp.arange(width, dtype=jnp.int32)[None, None, :]).astype(jnp.float32)
    return jnp.sum(weights[:, :, None] * hits, axis=0)


def per_device_general(
    positions,
    types,
    neighbours,
    neighbour_count,
    send_index,
    cell_x,
    cell_y,
    cell_z,
    spline_fraction,
    embed_first,
    embed_second,
    embed_third,
    energy_in,
    energy_hidden,
    energy_out,
    wannier_in,
    wannier_hidden,
    wannier_out,
    charge_base,
):
    atom_count = types.shape[1]
    ghost_rows = send_index.shape[1] // 2
    kind_float = types[0].astype(jnp.float32)
    own_atoms = jnp.concatenate([positions[:, 0], kind_float[None]], axis=0)
    outgoing = own_atoms[:, send_index[0]]
    padded_ghosts = with_halo(outgoing, (("brick", 1),), ghost_rows)
    extended = jnp.concatenate(
        [padded_ghosts[:, :ghost_rows], own_atoms, padded_ghosts[:, 3 * ghost_rows :]], axis=1
    )
    energy_short, charge_shift = atom_terms(
        extended,
        neighbours[0],
        neighbour_count[0],
        embed_first,
        embed_second,
        embed_third,
        energy_in,
        energy_hidden,
        energy_out,
        wannier_in,
        wannier_hidden,
        wannier_out,
    )
    charge = (1.0 - kind_float) * charge_base[0] + kind_float * charge_base[1] + charge_shift
    count_x = lax.axis_size("brick")
    count_y = lax.axis_size("slab")
    block_x = NG // count_x
    block_y = NG // count_y
    wide_x = block_x + 3
    wide_y = block_y + 3
    spread_x = spread_matrix(cell_x[0], spline_weights(spline_fraction[0, 0]), wide_x, 0)
    spread_y = spread_matrix(cell_y[0], spline_weights(spline_fraction[1, 0]), wide_y, 0)
    spread_z = spread_matrix(cell_z[0], spline_weights(spline_fraction[2, 0]), NG, NG)
    spread_xy = (spread_x[:, :, None] * spread_y[:, None, :]).reshape(atom_count, wide_x * wide_y)
    charge_grid = jnp.einsum(
        "ap,az->pz", spread_xy, charge[:, None] * spread_z, precision=HIGH
    ).reshape(wide_x, wide_y, NG)
    cosine, sine = dft_tables(NG)
    scale = 1.0 / (NG * NG * NG)
    full_index = jnp.arange(NG, dtype=jnp.int32)
    paired = jnp.stack([along(charge_grid, cosine, 2), -along(charge_grid, sine, 2)])
    moved = lax.all_to_all(paired, "slab", split_axis=3, concat_axis=2, tiled=True)
    moved = complex_transform(fold_windows(moved, 2, block_y, count_y), 2, cosine, sine, False)
    moved = lax.all_to_all(moved, "brick", split_axis=2, concat_axis=1, tiled=True)
    moved = complex_transform(fold_windows(moved, 1, block_x, count_x), 1, cosine, sine, False)
    part_y = NG // count_x
    part_z = NG // count_y
    index_y = lax.axis_index("brick") * part_y + jnp.arange(part_y, dtype=jnp.int32)
    index_z = lax.axis_index("slab") * part_z + jnp.arange(part_z, dtype=jnp.int32)
    moved = moved * (green_table(full_index, index_y, index_z, NG) * scale)[None]
    moved = make_windows(complex_transform(moved, 1, cosine, sine, True), 1, block_x, count_x)
    moved = lax.all_to_all(moved, "brick", split_axis=1, concat_axis=2, tiled=True)
    moved = make_windows(complex_transform(moved, 2, cosine, sine, True), 2, block_y, count_y)
    moved = lax.all_to_all(moved, "slab", split_axis=2, concat_axis=3, tiled=True)
    potential_wide = along(moved[0], cosine, 2) - along(moved[1], sine, 2)
    sampled = jnp.einsum(
        "ap,pz->az", spread_xy, potential_wide.reshape(wide_x * wide_y, NG), precision=HIGH
    )
    potential_at = jnp.sum(sampled * spread_z, axis=1)
    atom_energy = energy_short + 0.5 * charge * potential_at
    return (atom_energy[None, :], potential_wide[:block_x, :block_y])


def split(values):
    high = values.astype(jnp.bfloat16)
    low = (values - high.astype(jnp.float32)).astype(jnp.bfloat16)
    return high, low


def multiply(left, right, dims):
    return lax.dot_general(left, right, (dims, ((), ())), preferred_element_type=jnp.float32)


def triple(left, right, dims=((1,), (0,))):
    (left_axis,), (right_axis,) = dims
    if left[0].shape[left_axis] % 128 == 0:
        return multiply(
            jnp.concatenate([left[0], left[0], left[1]], axis=left_axis),
            jnp.concatenate([right[0], right[1], right[0]], axis=right_axis),
            dims,
        )
    return (
        multiply(left[0], right[0], dims)
        + multiply(left[0], right[1], dims)
        + multiply(left[1], right[0], dims)
    )


LANES = ((1,), (1,))


def product(left, right, dims=((1,), (0,))):
    return lax.dot_general(
        left,
        right,
        (dims, ((), ())),
        precision=lax.Precision.HIGH,
        preferred_element_type=jnp.float32,
    )


def lane_pick(table, index):
    return jnp.take_along_axis(table, index, axis=1, mode="promise_in_bounds")


def whole(shape):
    return pl.BlockSpec(tuple(shape), lambda step: (0,) * len(shape))


def whole_specs(*arrays):
    return [whole(array.shape) for array in arrays]


def collect_kernel(
    positions_ref, types_ref, count_ref, send_ref, own_ref, outgoing_ref
):
    atoms = types_ref.shape[1]
    own_ref[...] = jnp.zeros_like(own_ref)
    for axis in range(3):
        own_ref[axis : axis + 1, 0:atoms] = positions_ref[axis]
    own_ref[3:4, 0:atoms] = types_ref[...].astype(jnp.float32)
    own_ref[4:5, 0:atoms] = count_ref[...].astype(jnp.float32)
    own_ref[5:6, 0:atoms] = send_ref[...].astype(jnp.float32)
    for chunk in range(2):
        lanes = slice(128 * chunk, 128 * chunk + 128)
        wanted = jnp.broadcast_to(own_ref[5:6, lanes], (8, 128)).astype(jnp.int32)
        within = wanted & 127
        outgoing_ref[:, lanes] = jnp.where(
            wanted < 128,
            lane_pick(own_ref[:, 0:128], within),
            lane_pick(own_ref[:, 128:256], within),
        )


def collect(positions, types, counts, send_index):
    arrays = (positions, types, counts, send_index)
    result = jax.ShapeDtypeStruct((8, 256), jnp.float32)
    return pl.pallas_call(
        collect_kernel,
        grid=(1,),
        out_shape=[result, result],
        in_specs=whole_specs(*arrays),
        out_specs=whole_specs(result, result),
        compiler_params=pltpu.CompilerParams(vmem_limit_bytes=VMEM_BYTES),
        name="collect_atoms",
    )(*arrays)


def fitting_rows(descriptor_ref, weight_in_ref, weight_hidden_ref, weight_out_ref):
    hidden = jnp.tanh(product(descriptor_ref[...], weight_in_ref[...], LANES))
    for layer in range(weight_hidden_ref.shape[0]):
        hidden = jnp.tanh(product(hidden, weight_hidden_ref[layer])) + hidden
    width = hidden.shape[1]
    return product(jnp.broadcast_to(weight_out_ref[...], (8, width)), hidden, LANES)


def natural_order(rows):
    atoms = rows.shape[1]
    padded = jnp.concatenate([rows, jnp.zeros((8, 256 - atoms), jnp.float32)], axis=1)
    pieces = []
    for chunk in range(2):
        atom = 128 * chunk + lax.broadcasted_iota(jnp.int32, (8, 128), 1)
        late = atom >= atoms // 2
        within = jnp.where(late, atom - atoms // 2, atom)
        place = 8 * (within >> 2) + (within & 3) + jnp.where(late, 4, 0)
        place = jnp.minimum(place, 255)
        pieces.append(
            jnp.where(
                place < 128,
                lane_pick(padded[:, 0:128], place & 127),
                lane_pick(padded[:, 128:256], place & 127),
            )
        )
    return jnp.concatenate(pieces, axis=1)[0:1, 0:atoms]


def network_kernel(
    ghosts,
    base_ref,
    charges_ref,
    own_ref,
    lower_ref,
    upper_ref,
    slots_ref,
    types_ref,
    cell_x_ref,
    cell_y_ref,
    cell_z_ref,
    fraction_ref,
    first_ref,
    second_ref,
    third_ref,
    spot_ref,
    weight_in_hbm,
    weight_hidden_hbm,
    weight_out_ref,
    descriptor_hbm,
    charge_ref,
    copies_ref,
    descriptor_ref,
    environment_ref,
    kind_ref,
    moments_ref,
    padded_ref,
    weight_in_ref,
    weight_hidden_ref,
    row_ref,
    semaphores,
):
    fetches = [
        pltpu.make_async_copy(weight_in_hbm, weight_in_ref, semaphores.at[0]),
        pltpu.make_async_copy(weight_hidden_hbm, weight_hidden_ref, semaphores.at[1]),
    ]
    for fetch in fetches:
        fetch.start()
    slots, atoms = slots_ref.shape
    rows = atoms // 2
    lane = lax.broadcasted_iota(jnp.int32, (8, 128), 1)
    sub = lax.broadcasted_iota(jnp.int32, (8, 128), 0)

    width = first_ref.shape[1]
    padded_ref[...] = jnp.zeros_like(padded_ref)
    padded_ref[0, 0:2, 0:width] = first_ref[...]
    for column in range(2):
        padded_ref[1, 0:width, 32 * column : 32 * column + width] = second_ref[
            :, width * column : width * (column + 1)
        ]
    for row in range(2):
        for column in range(4):
            padded_ref[2, 32 * row : 32 * row + width, 32 * column : 32 * column + width] = (
                third_ref[
                    width * row : width * (row + 1), width * column : width * (column + 1)
                ]
            )
    first_table = padded_ref[0].T
    embed_zero = jnp.broadcast_to(first_table[0:32, 0:1], (32, 128))
    embed_one = jnp.broadcast_to(first_table[0:32, 1:2], (32, 128))
    second_high, second_low = split(padded_ref[1].T[0:64, 0:32])
    second_weight = jnp.concatenate([second_high, second_high, second_low], axis=1)
    third_high, third_low = split(padded_ref[2].T[:, 0:64])
    third_weight = jnp.concatenate([third_high, third_high, third_low], axis=1)

    def spread(ref, field, chunk):
        return jnp.broadcast_to(ref[field : field + 1, 128 * chunk : 128 * chunk + 128], (8, 128))

    own = [[spread(own_ref, field, chunk) for chunk in range(2)] for field in range(5)]
    lower = [[spread(lower_ref, field, chunk) for chunk in range(2)] for field in range(4)]
    upper = [spread(upper_ref, field, 0) for field in range(4)]

    def pick_two(tables, index):
        within = index & 127
        return jnp.where(index < 128, lane_pick(tables[0], within), lane_pick(tables[1], within))

    pairs = jnp.concatenate([slots_ref[:, 0:rows], slots_ref[:, rows:atoms]], axis=0).T
    for tile in range(rows // 8):
        band = slice(8 * tile, 8 * tile + 8)
        index = pairs[band, :]
        centre = 8 * tile + sub + jnp.where(lane < 64, 0, rows)
        from_own = jnp.clip(index - ghosts, 0, atoms - 1)
        from_lower = jnp.minimum(index + (atoms - ghosts), 255)
        from_upper = jnp.clip(index - (ghosts + atoms), 0, 127)

        def neighbour(field):
            below = pick_two(lower[field], from_lower)
            inside = pick_two(own[field], from_own)
            above = lane_pick(upper[field], from_upper)
            return jnp.where(
                index < ghosts, below, jnp.where(index < ghosts + atoms, inside, above)
            )

        offsets = [neighbour(field) - pick_two(own[field], centre) for field in range(3)]
        live = pick_two(own[4], centre)
        present = jnp.where((lane & 63).astype(jnp.float32) < live, 1.0, 0.0)
        smooth = present / (
            1.0 + (offsets[0] * offsets[0] + offsets[1] * offsets[1] + offsets[2] * offsets[2])
        )
        environment_ref[0, band, :] = smooth
        for field in range(3):
            environment_ref[1 + field, band, :] = smooth * offsets[field]
        kind_ref[band, :] = neighbour(3)

    group = 8

    def stacked(values):
        high, low = split(values)
        return jnp.concatenate([high, low, high], axis=0)

    def one_group(start):
        pieces = []
        for row in range(group):
            smooth = jnp.broadcast_to(environment_ref[0, pl.ds(start + row, 1), :], (32, 128))
            kind = jnp.broadcast_to(kind_ref[pl.ds(start + row, 1), :], (32, 128))
            pieces.append(
                jnp.tanh(smooth * ((1.0 - kind) * embed_zero + kind * embed_one))
            )
        first = jnp.concatenate(pieces, axis=1)
        second = jnp.tanh(multiply(second_weight, stacked(first), ((1,), (0,))))
        second = second + jnp.concatenate([first, first], axis=0)
        third = jnp.tanh(multiply(third_weight, stacked(second), ((1,), (0,))))
        third = third + jnp.concatenate([second, second], axis=0)
        third_pair = split(third)
        for half in range(group // 4):
            columns = slice(512 * half, 512 * half + 512)
            bands = []
            for part in range(4):
                bands.append(
                    jnp.concatenate(
                        [
                            jnp.where(
                                sub == row + jnp.where(lane < 64, 0, 4),
                                jnp.broadcast_to(
                                    environment_ref[part, pl.ds(start + 4 * half + row, 1), :],
                                    (8, 128),
                                ),
                                0.0,
                            )
                            for row in range(4)
                        ],
                        axis=1,
                    )
                )
            environment = split(jnp.concatenate(bands, axis=0))
            both = multiply(
                jnp.concatenate(environment, axis=0), third_pair[0][:, columns], LANES
            )
            sums = both[0:32] + both[32:64]
            sums = sums + multiply(environment[0], third_pair[1][:, columns], LANES)
            sums = sums * (1.0 / slots)
            for part in range(4):
                moments_ref[part, pl.ds(2 * start + 8 * half, 8), :] = sums[
                    8 * part : 8 * part + 8
                ]

    def body(step, carry):
        for part in range(unroll):
            one_group(pl.multiple_of(step * unroll * group + part * group, group))
        return carry

    unroll = rows // group
    lax.fori_loop(0, rows // (unroll * group), body, 0)

    chunks = (descriptor_ref.shape[1] + 127) // 128
    last = descriptor_ref.shape[1] - 128 * (chunks - 1)

    def describe_band(start):
        band = pl.ds(start, 8)
        moments = [moments_ref[part, band, :] for part in range(4)]
        axis_part = [lane_pick(moments[part], lane & 15) for part in range(4)]
        for chunk in range(chunks):
            spot = jnp.broadcast_to(spot_ref[chunk : chunk + 1, :], (8, 128))
            total = lane_pick(moments[0], spot) * axis_part[0]
            for part in range(1, 4):
                total = total + lane_pick(moments[part], spot) * axis_part[part]
            if chunk < chunks - 1:
                descriptor_ref[band, 128 * chunk : 128 * chunk + 128] = total
            else:
                descriptor_ref[band, 128 * chunk : 128 * chunk + last] = total[:, 0:last]

    bands = 8 if atoms % 64 == 0 else 1

    def describe(step, carry):
        for part in range(bands):
            describe_band(pl.multiple_of(step * 8 * bands + 8 * part, 8))
        return carry

    lax.fori_loop(0, atoms // (8 * bands), describe, 0)

    store = pltpu.make_async_copy(descriptor_ref, descriptor_hbm, semaphores.at[2])
    store.start()
    for fetch in fetches:
        fetch.wait()
    shift = fitting_rows(descriptor_ref, weight_in_ref, weight_hidden_ref, weight_out_ref)
    kind = types_ref[...].astype(jnp.float32)
    charge = (1.0 - kind) * charges_ref[0] + kind * charges_ref[1] + natural_order(shift)
    charge_ref[...] = charge
    fields = [
        cell_x_ref[...].astype(jnp.float32),
        (cell_y_ref[...] + base_ref[0]).astype(jnp.float32),
        cell_z_ref[...].astype(jnp.float32),
    ]
    fields = fields + [fraction_ref[axis] for axis in range(3)] + [charge]
    for place, field in enumerate(fields):
        row_ref[:, atoms * place : atoms * (place + 1)] = field
    for copy in range(copies_ref.shape[0]):
        copies_ref[copy] = row_ref[...]
    store.wait()


def spot_table(embed, desc):
    column = np.arange(desc) // AXIS
    quarter = embed // 4
    place = 32 * (column // quarter) + column % quarter
    chunks = (desc + 127) // 128
    table = np.zeros((chunks * 128,), np.int32)
    table[:desc] = place
    padded = np.zeros(((chunks + 7) // 8 * 8, 128), np.int32)
    padded[:chunks] = table.reshape(chunks, 128)
    return padded


def networks(
    copies,
    ghosts,
    base,
    charge_base,
    own,
    lower,
    upper,
    neighbours,
    types,
    cells,
    fraction,
    embed,
    weight_in,
    weight_hidden,
    weight_out,
):
    atoms = types.shape[1]
    desc, width = weight_in.shape
    spots = jnp.asarray(spot_table(embed[2].shape[1], desc))
    anywhere = pl.BlockSpec(memory_space=pl.ANY)
    scalars = pl.BlockSpec(memory_space=pltpu.SMEM)
    blocks = (own, lower, upper, neighbours[0].T, types, *cells, fraction, *embed, spots)
    weight_out = weight_out.reshape(1, -1)
    results = [
        jax.ShapeDtypeStruct((atoms, desc), jnp.float32),
        jax.ShapeDtypeStruct((1, atoms), jnp.float32),
        jax.ShapeDtypeStruct((copies, 1, FIELDS * atoms), jnp.float32),
    ]
    return pl.pallas_call(
        functools.partial(network_kernel, ghosts),
        grid=(1,),
        out_shape=results,
        in_specs=[scalars, scalars]
        + whole_specs(*blocks)
        + [anywhere, anywhere]
        + whole_specs(weight_out),
        out_specs=[anywhere] + whole_specs(*results[1:]),
        scratch_shapes=[
            pltpu.VMEM((atoms, desc), jnp.float32),
            pltpu.VMEM((4, atoms // 2, 128), jnp.float32),
            pltpu.VMEM((atoms // 2, 128), jnp.float32),
            pltpu.VMEM((4, atoms, 128), jnp.float32),
            pltpu.VMEM((3, 128, 128), jnp.float32),
            pltpu.VMEM((width, desc), jnp.float32),
            pltpu.VMEM(weight_hidden.shape, jnp.float32),
            pltpu.VMEM((1, FIELDS * atoms), jnp.float32),
            pltpu.SemaphoreType.DMA((3,)),
        ],
        compiler_params=pltpu.CompilerParams(vmem_limit_bytes=VMEM_BYTES),
        name="networks",
    )(base, charge_base, *blocks, weight_in.T, weight_hidden, weight_out)


def energy_kernel(descriptor_ref, weight_in_ref, weight_hidden_ref, weight_out_ref, energy_ref):
    energy_ref[...] = natural_order(
        fitting_rows(descriptor_ref, weight_in_ref, weight_hidden_ref, weight_out_ref)
    )


def energies(descriptor, weight_in, weight_hidden, weight_out):
    atoms, desc = descriptor.shape
    width = weight_in.shape[1]
    arrays = (descriptor, weight_in.T, weight_hidden, weight_out.reshape(1, -1))
    result = jax.ShapeDtypeStruct((1, atoms), jnp.float32)
    return pl.pallas_call(
        energy_kernel,
        grid=(1,),
        out_shape=result,
        in_specs=whole_specs(*arrays),
        out_specs=whole(result.shape),
        compiler_params=pltpu.CompilerParams(vmem_limit_bytes=VMEM_BYTES),
        cost_estimate=pl.CostEstimate(
            flops=6 * atoms * desc * width, bytes_accessed=4 * desc * width, transcendentals=0
        ),
        name="energies",
    )(*arrays)


def weight_rows(fraction):
    square = fraction * fraction
    cubed = square * fraction
    rest = 1.0 - fraction
    return [
        rest * rest * rest / 6.0,
        (3.0 * cubed - 6.0 * square + 4.0) / 6.0,
        (-3.0 * cubed + 3.0 * square + 3.0 * fraction + 1.0) / 6.0,
        cubed / 6.0,
    ]


def placed_weights(distance, weights):
    shape = distance.shape
    result = jnp.zeros(shape, jnp.float32)
    for step in range(4):
        result = jnp.where(
            distance == step, jnp.broadcast_to(weights[step], shape), result
        )
    return result


def third_factors(fields, waves_ref, cosine_ref):
    atoms = fields.shape[1]
    start = fields[2:3, :].astype(jnp.int32)
    along = weight_rows(fields[5:6, :])
    parts = waves_ref.shape[0]
    cosine = jnp.broadcast_to(cosine_ref[...], (parts, 128))
    wave = jnp.broadcast_to(waves_ref[:, 0:1], (parts, 128))
    shift = jnp.broadcast_to(waves_ref[:, 1:2], (parts, 128))
    pieces = []
    for chunk in range(atoms // 128):
        lanes = slice(128 * chunk, 128 * chunk + 128)
        total = jnp.zeros((parts, 128), jnp.float32)
        for step in range(4):
            place = jnp.broadcast_to(start[:, lanes] + step, (parts, 128))
            phase = (wave * place + shift) & (NG - 1)
            value = lane_pick(cosine, phase & 127)
            value = jnp.where(phase < 128, value, -value)
            total = total + value * jnp.broadcast_to(along[step][:, lanes], (parts, 128))
        pieces.append(total)
    return jnp.concatenate(pieces, axis=1)


def first_third_split(fields, waves_ref, cosine_ref, window, scale, high_ref, low_ref):
    atoms = fields.shape[1]
    third = third_factors(fields, waves_ref, cosine_ref) * scale
    rows = lax.broadcasted_iota(jnp.int32, (window, atoms), 0)
    first = placed_weights(
        rows - fields[0:1, :].astype(jnp.int32), weight_rows(fields[3:4, :])
    )
    for chunk in range(atoms // 128):
        lanes = slice(128 * chunk, 128 * (chunk + 1))
        for part in range(0, third.shape[0], 2):
            high, low = split(
                jnp.concatenate(
                    [first[:, lanes] * third[part + side : part + side + 1, lanes] for side in range(2)],
                    axis=0,
                )
            )
            place = slice(part * window, (part + 2) * window)
            high_ref[place, lanes] = high
            low_ref[place, lanes] = low
    return high_ref[...], low_ref[...]


def second_factors(fields, base, block_y, slabs, high_ref, low_ref):
    atoms = fields.shape[1]
    block = atoms // slabs
    reach = block_y + REACH
    start = fields[1:2, :].astype(jnp.int32) - base
    weights = weight_rows(fields[4:5, :])
    for chunk in range(atoms // 128):
        lanes = slice(128 * chunk, 128 * (chunk + 1))
        first = 128 * chunk // block
        last = (128 * chunk + 127) // block
        top = first * block_y
        rows = (last - first) * block_y + reach
        pieces = [(top, min(rows, NG - top))]
        if top + rows > NG:
            pieces.append((0, top + rows - NG))
        for row, count in pieces:
            index = row + lax.broadcasted_iota(jnp.int32, (count, 128), 0)
            table = split(
                placed_weights(
                    (index - start[:, lanes]) & (NG - 1), [weight[:, lanes] for weight in weights]
                )
            )
            high_ref[row : row + count, lanes] = table[0]
            low_ref[row : row + count, lanes] = table[1]
    return high_ref[...], low_ref[...]


def wave_of(index):
    return jnp.where(index <= NG // 2, index, index - NG // 2)


def damping(index):
    kappa = wave_of(index).astype(jnp.float32) * (2.0 * math.pi / NG)
    squared = kappa * kappa
    ends = (index == 0) | (index == NG // 2)
    return squared, jnp.exp(-0.5 * squared) * jnp.where(ends, 1.0 / NG, 2.0 / NG)


def transform(planes, kappa_ref, first_part, tables_ref, last_ref):
    count = len(planes)
    basis = tables_ref[0]
    turned = tables_ref[1]
    square_x, damp_x = damping(lax.broadcasted_iota(jnp.int32, (NG, 1), 0))
    square_y, damp_y = damping(lax.broadcasted_iota(jnp.int32, (1, NG), 1))
    square_xy = square_x + square_y
    damp_xy = damp_x * damp_y
    columns = [slice(NG * part, NG * (part + 1)) for part in range(count)]
    first = product(basis, jnp.concatenate(planes, axis=1))
    first = jnp.concatenate([first[:, column] for column in columns], axis=0)
    both = product(first, turned)
    scaled = []
    for part in range(count):
        squared = square_xy + kappa_ref[first_part + part, 0]
        root = jnp.where(squared == 0.0, 1.0, 0.0)
        green = (1.0 - root) * (damp_xy * kappa_ref[first_part + part, 1]) / (squared + root)
        scaled.append(both[columns[part]] * green)
    back = product(turned, jnp.concatenate(scaled, axis=1))
    back = jnp.concatenate([back[:, column] for column in columns], axis=0)
    return product(back, last_ref[...])


def send_blocks(full, block_x, block_y, put):
    low_lanes = lax.broadcasted_iota(jnp.int32, (NG, 128), 1) < block_y
    for pair in range(full.shape[0] // (2 * NG)):
        even = full[2 * NG * pair : 2 * NG * pair + NG, 0:128]
        odd = full[2 * NG * pair + NG : 2 * NG * (pair + 1), 0:128]
        blocks = [
            jnp.where(low_lanes, even, pltpu.roll(odd, block_y, 1)),
            jnp.where(low_lanes, pltpu.roll(even, block_y, 1), odd),
        ]
        for brick in range(NG // block_x):
            for side in range(2):
                for group in range(block_x // 8):
                    start = block_x * brick + 8 * group
                    put(pair, brick, side, group, blocks[side][start : start + 8])


def spread_kernel(
    block_x,
    block_y,
    window,
    kappa_ref,
    pair_ref,
    static_ref,
    waves_ref,
    cosine_ref,
    tables_hbm,
    last_hbm,
    short_hbm,
    sent_ref,
    full_hbm,
    atoms_ref,
    later_hbm,
    full_ref,
    grid_ref,
    tables_ref,
    last_ref,
    semaphores,
    *pair_refs,
):
    slabs = NG // block_y
    second_refs, first_refs = pair_refs[:4], pair_refs[4:]
    bricks = NG // block_x
    parts = waves_ref.shape[0]
    block = static_ref.shape[2] // FIELDS
    later = later_hbm.shape[0]
    store = pltpu.make_async_copy(
        grid_ref.at[pl.ds(parts - later, later), pl.ds(0, NG)], later_hbm, semaphores.at[2]
    )
    fetches = [
        pltpu.make_async_copy(tables_hbm, tables_ref, semaphores.at[0]),
        pltpu.make_async_copy(last_hbm.at[pair_ref[0]], last_ref, semaphores.at[1]),
    ]
    for fetch in fetches:
        fetch.start()
    for slab in range(slabs):
        lanes = slice(block * slab, block * (slab + 1))
        for brick in range(bricks):
            for field in range(FIELDS):
                atoms_ref[brick, field : field + 1, lanes] = static_ref[
                    slab * bricks + brick, :, block * field : block * (field + 1)
                ]
    for ref in second_refs:
        ref[...] = jnp.zeros_like(ref)
    for brick in range(bricks):
        fields = atoms_ref[brick]
        table = first_third_split(
            fields,
            waves_ref,
            cosine_ref,
            window,
            fields[6:7, :],
            first_refs[2 * (brick % 2)],
            first_refs[2 * (brick % 2) + 1],
        )
        second = second_factors(
            fields, 0, block_y, slabs, second_refs[2 * (brick % 2)], second_refs[2 * (brick % 2) + 1]
        )
        spread = triple(table, second, LANES)
        start = block_x * brick
        extra = window - block_x
        for part in range(parts):
            shared = spread[part * window : part * window + extra]
            if brick > 0:
                shared = shared + grid_ref[part, start : start + extra, :]
            grid_ref[part, start : start + extra, :] = shared
            grid_ref[part, start + extra : start + window, :] = spread[
                part * window + extra : part * window + window
            ]
    for part in range(parts):
        grid_ref[part, 0:extra, :] += grid_ref[part, NG : NG + extra, :]
    store.start()
    for fetch in fetches:
        fetch.wait()

    count = 4
    outs = []
    for step in range(full_hbm.shape[0] // count):
        planes = [grid_ref[count * step + part, 0:NG, :] for part in range(count)]
        full = transform(planes, kappa_ref, count * step, tables_ref, last_ref)
        for part in range(count):
            full_ref[count * step + part] = full[NG * part : NG * (part + 1)]

        def put(pair, brick, side, group, tile):
            sent_ref[2 * brick + side, group, count // 2 * step + pair] = tile

        send_blocks(full, block_x, block_y, put)
        ours = pl.ds(count * step, count)
        outs.append(
            pltpu.make_async_copy(
                full_ref.at[ours], full_hbm.at[ours], semaphores.at[3 + step]
            )
        )
    for out in outs:
        out.start()
    for out in outs:
        out.wait()
    store.wait()


def early_pairs(parts):
    return parts // 4


def spread_and_solve(
    block_x, block_y, window, kappa, pair, static, waves, cosine_row, tables, last, short
):
    atoms = static.shape[2] // FIELDS
    slabs = NG // block_y
    bricks = NG // block_x
    parts = waves.shape[0]
    pairs = early_pairs(parts)
    anywhere = pl.BlockSpec(memory_space=pl.ANY)
    scalars = pl.BlockSpec(memory_space=pltpu.SMEM)
    sent_block = (2 * bricks, block_x // 8, pairs, 8, 128)
    return pl.pallas_call(
        functools.partial(spread_kernel, block_x, block_y, window),
        grid=(1,),
        out_shape=[
            jax.ShapeDtypeStruct((2 * bricks, block_x // 8, pairs, 8, 128), jnp.float32),
            jax.ShapeDtypeStruct((2 * pairs, NG, NG), jnp.float32),
            jax.ShapeDtypeStruct((bricks, 8, slabs * atoms), jnp.float32),
            jax.ShapeDtypeStruct((parts - 2 * pairs, NG, NG), jnp.float32),
        ],
        in_specs=[scalars, scalars]
        + whole_specs(static, waves, cosine_row)
        + [anywhere, anywhere, anywhere],
        out_specs=[
            whole(sent_block),
            anywhere,
            whole((bricks, 8, slabs * atoms)),
            anywhere,
        ],
        scratch_shapes=[
            pltpu.VMEM((2 * pairs, NG, NG), jnp.float32),
            pltpu.VMEM((parts, NG + window - block_x, NG), jnp.float32),
            pltpu.VMEM(tables.shape, tables.dtype),
            pltpu.VMEM(last.shape[1:], last.dtype),
            pltpu.SemaphoreType.DMA((3 + pairs // 2,)),
        ]
        + [pltpu.VMEM((NG, slabs * atoms), jnp.bfloat16)] * 4
        + [pltpu.VMEM((parts * window, slabs * atoms), jnp.bfloat16)] * 4,
        compiler_params=pltpu.CompilerParams(vmem_limit_bytes=VMEM_BYTES),
        name="spread_and_solve",
    )(kappa, pair, static, waves, cosine_row, tables, last, short)


def sample_kernel(
    block_x,
    block_y,
    window,
    kappa_ref,
    pair_ref,
    atoms_ref,
    waves_ref,
    cosine_ref,
    tables_hbm,
    last_hbm,
    later_hbm,
    early_hbm,
    sent_ref,
    later_ref,
    full_ref,
    tables_ref,
    last_ref,
    semaphores,
    packed_ref,
):
    bricks = atoms_ref.shape[0]
    parts = waves_ref.shape[0]
    early = 2 * early_pairs(parts)
    block = atoms_ref.shape[2] * block_y // NG
    fetches = [
        pltpu.make_async_copy(tables_hbm, tables_ref, semaphores.at[0]),
        pltpu.make_async_copy(last_hbm.at[pair_ref[0]], last_ref, semaphores.at[1]),
        pltpu.make_async_copy(later_hbm, later_ref, semaphores.at[2]),
        pltpu.make_async_copy(early_hbm, full_ref.at[pl.ds(0, early)], semaphores.at[3]),
    ]
    for fetch in fetches:
        fetch.start()
    for fetch in fetches[:3]:
        fetch.wait()
    pairs = (parts - early) // 2
    planes = [later_ref[part] for part in range(parts - early)]
    full = transform(planes, kappa_ref, early, tables_ref, last_ref)
    for part in range(parts - early):
        full_ref[early + part] = full[NG * part : NG * (part + 1)]

    def put(pair, brick, side, group, tile):
        sent_ref[2 * brick + side, pairs * group + pair] = tile

    send_blocks(full, block_x, block_y, put)
    fetches[3].wait()

    reach = block_y + REACH
    lane = lax.broadcasted_iota(jnp.int32, (NG, 128), 1)
    for part in range(parts):
        for side in range(2):
            values = full_ref[part, :, 128 * side : 128 * (side + 1)]
            high = values.astype(jnp.bfloat16).astype(jnp.float32)
            again = pltpu.roll(high, reach, 1)
            low = pltpu.roll(values - high, 2 * reach - 128, 1)
            packed_ref[side, part, 0:NG, 0:128] = jnp.where(lane < reach, high, again)
            packed_ref[side, part, 0:NG, 128:NG] = jnp.where(
                lane < 2 * reach - 128, again, jnp.where(lane < 3 * reach - 128, low, 0.0)
            )
            packed_ref[side, part, NG : NG + window - block_x, :] = packed_ref[
                side, part, 0 : window - block_x, :
            ]
    extra = sent_ref.shape[1] - 1
    base = 2 * block_y * pair_ref[0]
    lanes = pl.ds(pl.multiple_of(2 * block * pair_ref[0], 128), 2 * block)
    for brick in range(bricks):
        fields = atoms_ref[brick, :, lanes]
        thirds = third_factors(fields, waves_ref, cosine_ref)
        rows = slice(block_x * brick, block_x * brick + window)
        for side in range(2):
            here = slice(block * side, block * (side + 1))
            third = thirds[:, here]
            ours = fields[:, here]
            index = lax.broadcasted_iota(jnp.int32, (window, block), 0)
            first = placed_weights(
                index - ours[0:1, :].astype(jnp.int32), weight_rows(ours[3:4, :])
            )
            index = lax.broadcasted_iota(jnp.int32, (reach, block), 0)
            start = ours[1:2, :].astype(jnp.int32) - (base + block_y * side)
            high, low = split(placed_weights(index - start, weight_rows(ours[4:5, :])))
            rest = jnp.zeros((NG - 3 * reach, block), jnp.bfloat16)
            second = jnp.concatenate([high, low, high, rest], axis=0)
            values = jnp.concatenate(
                [packed_ref[side, part, rows, :] for part in range(parts)], axis=0
            )
            along = multiply(values.astype(jnp.bfloat16), second, ((1,), (0,)))
            total = jnp.zeros((window, block), jnp.float32)
            for part in range(parts):
                total = total + along[window * part : window * (part + 1)] * third[part : part + 1]
            row = jnp.sum(total * first, axis=0, keepdims=True)
            sent_ref[2 * brick + side, extra] = jnp.zeros((8, 128), jnp.float32)
            sent_ref[2 * brick + side, extra, 0:1, :] = row[:, 0:128]
            sent_ref[2 * brick + side, extra, 1:2, 0 : block - 128] = row[:, 128:block]


def solve_and_sample(
    block_x, block_y, window, kappa, pair, atoms, waves, cosine_row, tables, last, later, early
):
    bricks = atoms.shape[0]
    parts = waves.shape[0]
    pairs = parts // 2 - early_pairs(parts)
    anywhere = pl.BlockSpec(memory_space=pl.ANY)
    scalars = pl.BlockSpec(memory_space=pltpu.SMEM)
    result = jax.ShapeDtypeStruct((2 * bricks, block_x // 8 * pairs + 1, 8, 128), jnp.float32)
    return pl.pallas_call(
        functools.partial(sample_kernel, block_x, block_y, window),
        grid=(1,),
        out_shape=result,
        in_specs=[scalars, scalars] + whole_specs(atoms, waves, cosine_row) + [anywhere] * 4,
        out_specs=whole(result.shape),
        scratch_shapes=[
            pltpu.VMEM((2 * pairs, NG, NG), jnp.float32),
            pltpu.VMEM((parts, NG, NG), jnp.float32),
            pltpu.VMEM(tables.shape, tables.dtype),
            pltpu.VMEM(last.shape[1:], last.dtype),
            pltpu.SemaphoreType.DMA((4,)),
        ]
        + [pltpu.VMEM((2, parts, NG + window - block_x, NG), jnp.float32)],
        compiler_params=pltpu.CompilerParams(vmem_limit_bytes=VMEM_BYTES),
        cost_estimate=pl.CostEstimate(
            flops=24 * parts * NG * NG * NG, bytes_accessed=4 * early.size, transcendentals=0
        ),
        name="solve_and_sample",
    )(kappa, pair, atoms, waves, cosine_row, tables, last, later, early)


def finish_kernel(
    block_y,
    early_ref,
    later_ref,
    sums_ref,
    short_hbm,
    charge_hbm,
    table_ref,
    out_ref,
    energy_ref,
    short_ref,
    charge_ref,
    semaphores,
):
    atoms = short_ref.shape[1]
    fetches = [
        pltpu.make_async_copy(short_hbm, short_ref, semaphores.at[0]),
        pltpu.make_async_copy(charge_hbm, charge_ref, semaphores.at[1]),
    ]

    @pl.when(pl.program_id(0) == 0)
    def _():
        for fetch in fetches:
            fetch.start()

    lines = early_ref.shape[3]
    sources, _, pairs = early_ref.shape[:3]
    early = early_ref.reshape(sources * pairs, lines, 128)
    later = later_ref.reshape(sources * later_ref.shape[1], lines, 128)
    pieces = []
    for line in range(lines):
        turned = jnp.concatenate([early[:, line, :], later[:, line, :]], axis=0).T
        pieces.append(jnp.concatenate([turned[0:block_y], turned[block_y:]], axis=1))
    result = product(jnp.concatenate(pieces, axis=0), table_ref[...])
    for line in range(lines):
        out_ref[line] = result[block_y * line : block_y * (line + 1)]

    @pl.when(pl.program_id(0) == 0)
    def _():
        for fetch in fetches:
            fetch.wait()
        total = jnp.sum(sums_ref[:, 0], axis=0)
        potential_at = jnp.concatenate([total[0:1, :], total[1:2, 0 : atoms - 128]], axis=1)
        energy_ref[...] = short_ref[...] + 0.5 * charge_ref[...] * potential_at


def finish(block_x, block_y, early, later, short, charge, table):
    bricks2, groups, pairs = early.shape[:3]
    rest = (later.shape[1] - 1) // groups
    atoms = short.shape[1]
    return pl.pallas_call(
        functools.partial(finish_kernel, block_y),
        grid=(groups,),
        out_shape=[
            jax.ShapeDtypeStruct((block_x, block_y, NG), jnp.float32),
            jax.ShapeDtypeStruct((1, atoms), jnp.float32),
        ],
        in_specs=[
            pl.BlockSpec((bricks2, 1, pairs, 8, 128), lambda index: (0, index, 0, 0, 0)),
            pl.BlockSpec((bricks2, rest, 8, 128), lambda index: (0, index, 0, 0)),
            pl.BlockSpec((bricks2, 1, 8, 128), lambda index: (0, groups * rest, 0, 0)),
            pl.BlockSpec(memory_space=pltpu.HBM),
            pl.BlockSpec(memory_space=pltpu.HBM),
            whole(table.shape),
        ],
        out_specs=[
            pl.BlockSpec((8, block_y, NG), lambda index: (index, 0, 0)),
            whole((1, atoms)),
        ],
        scratch_shapes=[
            pltpu.VMEM((1, atoms), jnp.float32),
            pltpu.VMEM((1, atoms), jnp.float32),
            pltpu.SemaphoreType.DMA((2,)),
        ],
        compiler_params=pltpu.CompilerParams(vmem_limit_bytes=32 * 2**20),
        name="finish",
    )(early, later, later, short, charge, table)


def real_basis():
    index = np.arange(NG)
    wave = np.where(index <= NG // 2, index, index - NG // 2)
    angle = (wave[:, None] * index[None, :] % NG) * (2.0 * math.pi / NG)
    return np.where((index <= NG // 2)[:, None], np.cos(angle), np.sin(angle))


def per_device(
    positions,
    types,
    neighbours,
    neighbour_count,
    send_index,
    cell_x,
    cell_y,
    cell_z,
    spline_fraction,
    embed_first,
    embed_second,
    embed_third,
    energy_in,
    energy_hidden,
    energy_out,
    wannier_in,
    wannier_hidden,
    wannier_out,
    charge_base,
):
    atoms = types.shape[1]
    ghosts = send_index.shape[1] // 2
    count_x = lax.axis_size("brick")
    count_y = lax.axis_size("slab")
    block_x = NG // count_x
    block_y = NG // count_y
    window = block_x + 8
    parts = NG // (2 * count_x)
    brick = lax.axis_index("brick")
    slab = lax.axis_index("slab")
    pair = (slab // 2).astype(jnp.int32).reshape(1)
    halves = [
        [b * count_y + 2 * p + side for b in range(count_x) for side in range(2)]
        for p in range(count_y // 2)
    ]

    def exchange(values, axes, groups=None):
        return lax.all_to_all(
            values, axes, split_axis=0, concat_axis=0, tiled=True, axis_index_groups=groups
        )

    own, outgoing = collect(positions, types, neighbour_count, send_index)
    up = [(i, (i + 1) % count_x) for i in range(count_x)]
    down = [((i + 1) % count_x, i) for i in range(count_x)]
    lower = lax.ppermute(outgoing, "brick", up)
    upper = lax.ppermute(outgoing, "brick", down)
    descriptor, charge, fields = networks(
        count_x * count_y,
        ghosts,
        (slab * block_y).astype(jnp.int32).reshape(1),
        charge_base,
        own,
        lower,
        upper,
        neighbours,
        types,
        (cell_x, cell_y, cell_z),
        spline_fraction,
        (embed_first, embed_second, embed_third),
        wannier_in,
        wannier_hidden,
        wannier_out,
    )
    every_field = exchange(fields, ("slab", "brick"))

    part = (2 * brick + slab % 2) * parts + jnp.arange(parts, dtype=jnp.int32)
    wave = wave_of(part)
    waves = jnp.stack([wave, jnp.where(part <= NG // 2, 0, 3 * NG // 4)], axis=1)
    kappa = wave.astype(jnp.float32) * (2.0 * math.pi / NG)
    squared = kappa * kappa
    ends = (part == 0) | (part == NG // 2)
    kappa = jnp.stack(
        [squared, jnp.exp(-0.5 * squared) * jnp.where(ends, 1.0 / NG, 2.0 / NG)], axis=1
    )
    basis = real_basis()
    tables = np.stack([basis, basis.T]).astype(np.float32)
    last = []
    for p in range(count_y // 2):
        points = np.concatenate(
            [np.arange(2 * block_y), block_y + np.arange(block_y + REACH)]
        )
        points = (2 * block_y * p + points) % NG
        columns = np.zeros((NG, NG))
        columns[:, : points.size] = basis[:, points]
        last.append(columns.astype(np.float32))
    cosine_row = np.cos(np.arange(128) * (2.0 * math.pi / NG)).astype(np.float32)[None]
    cosine_row = jnp.asarray(cosine_row)
    tables = jnp.asarray(tables)
    last = jnp.asarray(np.stack(last))
    energy_short = energies(descriptor, energy_in, energy_hidden, energy_out)
    early, full, every_atom, later = spread_and_solve(
        block_x,
        block_y,
        window,
        kappa,
        pair,
        every_field,
        waves,
        cosine_row,
        tables,
        last,
        energy_short,
    )

    def send(values):
        got = exchange(values.reshape(values.shape[0], -1, 128), ("brick", "slab"), halves)
        return got.reshape(values.shape)

    early = send(early)
    later = solve_and_sample(
        block_x,
        block_y,
        window,
        kappa,
        pair,
        every_atom,
        waves,
        cosine_row,
        tables,
        last,
        later,
        full,
    )
    later = send(later)
    source = np.arange(2 * count_x)[:, None] * parts
    pairs = 2 * np.arange(parts // 2)[None, :]
    order = np.concatenate(
        [
            (source + pairs[:, : early_pairs(parts)]).ravel(),
            (source + pairs[:, early_pairs(parts) :]).ravel(),
        ]
    )
    order = np.concatenate([order, order + 1])
    potential, atom_energy = finish(
        block_x,
        block_y,
        early,
        later,
        energy_short,
        charge,
        jnp.asarray(basis[order].astype(np.float32)),
    )
    return atom_energy, potential


def solution(mesh):
    placed = (
        P(None, "slab", "brick"),
        P("slab", "brick"),
        P("slab", "brick", None),
        P("slab", "brick"),
        P("slab", "brick"),
        P("slab", "brick"),
        P("slab", "brick"),
        P("slab", "brick"),
        P(None, "slab", "brick"),
    ) + (P(),) * 10
    bricks, slabs = mesh.shape["brick"], mesh.shape["slab"]
    fits = 2 * NG == 128 * slabs and NG % (32 * bricks) == 0
    return jax.shard_map(
        per_device if fits else per_device_general,
        mesh=mesh,
        in_specs=placed,
        out_specs=(P("slab", "brick"), P("brick", "slab", None)),
        check_vma=False,
    )
```

```python
import functools
import math

import jax
import jax.numpy as jnp
import numpy as np
from jax import lax
from jax.experimental import pallas as pl
from jax.experimental.pallas import tpu as pltpu
from jax.sharding import PartitionSpec as P

NG = 256
AXIS = 16
VMEM_BYTES = 60 * 2**20
REACH = 16
FIELDS = 7


HIGH = lax.Precision.HIGHEST


def with_halo(cells, sides, width):
    for axis, dim in sides:
        count = lax.axis_size(axis)
        head = lax.slice_in_dim(cells, 0, width, axis=dim)
        tail = lax.slice_in_dim(cells, cells.shape[dim] - width, cells.shape[dim], axis=dim)
        cells = jnp.concatenate(
            [
                lax.ppermute(tail, axis, [(i, (i + 1) % count) for i in range(count)]),
                cells,
                lax.ppermute(head, axis, [((i + 1) % count, i) for i in range(count)]),
            ],
            axis=dim,
        )
    return cells


def spline_weights(fraction):
    cubed = fraction * fraction * fraction
    square = fraction * fraction
    return jnp.stack(
        [
            (1.0 - fraction) * (1.0 - fraction) * (1.0 - fraction) / 6.0,
            (3.0 * cubed - 6.0 * square + 4.0) / 6.0,
            (-3.0 * cubed + 3.0 * square + 3.0 * fraction + 1.0) / 6.0,
            cubed / 6.0,
        ]
    )


def fitting(descriptor, weight_in, weight_hidden, weight_out):
    hidden = jnp.tanh(jnp.dot(descriptor, weight_in, precision=HIGH))
    for depth_index in range(weight_hidden.shape[0]):
        hidden = jnp.tanh(jnp.dot(hidden, weight_hidden[depth_index], precision=HIGH)) + hidden
    return jnp.dot(hidden, weight_out, precision=HIGH)


def atom_terms(
    extended,
    neighbour_rows,
    neighbour_total,
    embed_first,
    embed_second,
    embed_third,
    energy_in,
    energy_hidden,
    energy_out,
    wannier_in,
    wannier_hidden,
    wannier_out,
):
    atom_count, slots = neighbour_rows.shape
    ghost_rows = (extended.shape[1] - atom_count) // 2
    block_size = 64
    blocks = atom_count // block_size
    present = (jnp.arange(slots, dtype=jnp.int32)[None, :] < neighbour_total[:, None]).astype(
        jnp.float32
    )
    centre_ids = (ghost_rows + jnp.arange(atom_count, dtype=jnp.int32)).reshape(blocks, block_size)
    second_weight = embed_second.T
    third_weight = embed_third.T

    def one_block(pieces):
        centre_rows, rows_block, present_block = pieces
        centre_block = extended[:3, centre_rows]
        gathered = extended[:, rows_block]
        offsets = gathered[:3] - centre_block[:, :, None]
        smooth = present_block / (1.0 + jnp.sum(offsets * offsets, axis=0))
        environment = jnp.stack(
            [smooth, smooth * offsets[0], smooth * offsets[1], smooth * offsets[2]], axis=0
        )
        kind = gathered[3][None]
        mixing = (1.0 - kind) * embed_first[0][:, None, None] + kind * embed_first[1][:, None, None]
        first = jnp.tanh(smooth[None] * mixing).reshape(embed_first.shape[1], block_size * slots)
        second = jnp.tanh(jnp.dot(second_weight, first, precision=HIGH)) + jnp.concatenate(
            [first, first], axis=0
        )
        third = jnp.tanh(jnp.dot(third_weight, second, precision=HIGH)) + jnp.concatenate(
            [second, second], axis=0
        )
        third_blocks = third.reshape(third.shape[0], block_size, slots)
        moments = jnp.einsum("kan,can->akc", third_blocks, environment, precision=HIGH) / slots
        descriptor = jnp.einsum("amc,akc->amk", moments, moments[:, :AXIS], precision=HIGH).reshape(
            block_size, -1
        )
        return (
            fitting(descriptor, energy_in, energy_hidden, energy_out),
            fitting(descriptor, wannier_in, wannier_hidden, wannier_out),
        )

    energy_short, charge_shift = lax.map(
        one_block,
        (
            centre_ids,
            neighbour_rows.reshape(blocks, block_size, slots),
            present.reshape(blocks, block_size, slots),
        ),
    )
    return (energy_short.reshape(atom_count), charge_shift.reshape(atom_count))


def green_table(first, second, third, size):

    def folded(index):
        return jnp.where(index < size // 2, index, index - size).astype(jnp.float32) * (
            2.0 * math.pi / size
        )

    kappa_x = folded(first)[:, None, None]
    kappa_y = folded(second)[None, :, None]
    kappa_z = folded(third)[None, None, :]
    squared = kappa_x * kappa_x + kappa_y * kappa_y + kappa_z * kappa_z
    root = (
        (first[:, None, None] == 0) & (second[None, :, None] == 0) & (third[None, None, :] == 0)
    ).astype(jnp.float32)
    return (1.0 - root) * jnp.exp(-0.5 * squared) / (squared + root)


def dft_tables(size):
    index = jnp.arange(size, dtype=jnp.int32)
    phase = (index[:, None] * index[None, :] % size).astype(jnp.float32) * (2.0 * math.pi / size)
    return (jnp.cos(phase), jnp.sin(phase))


def along(values, table, axis_index):
    result = jnp.tensordot(values, table, axes=([axis_index], [0]), precision=HIGH)
    return jnp.moveaxis(result, -1, axis_index)


def complex_transform(paired, axis_index, cosine, sine, inverse):
    real_part = paired[0]
    imag_part = paired[1]
    inner = axis_index - 1
    real_cos = along(real_part, cosine, inner)
    real_sin = along(real_part, sine, inner)
    imag_cos = along(imag_part, cosine, inner)
    imag_sin = along(imag_part, sine, inner)
    if inverse:
        return jnp.stack([real_cos - imag_sin, imag_cos + real_sin])
    return jnp.stack([real_cos + imag_sin, imag_cos - real_sin])


def fold_windows(values, axis_index, block, count):
    front = jnp.moveaxis(values, axis_index, 0)
    rest = front.shape[1:]
    windows = front.reshape((count, block + 3) + rest)
    main_part = windows[:, :block]
    carried = jnp.roll(windows[:, block:], 1, axis=0)
    main_part = main_part.at[:, :3].add(carried)
    return jnp.moveaxis(main_part.reshape((count * block,) + rest), 0, axis_index)


def make_windows(values, axis_index, block, count):
    front = jnp.moveaxis(values, axis_index, 0)
    rest = front.shape[1:]
    pieces = front.reshape((count, block) + rest)
    trailing = jnp.roll(pieces, -1, axis=0)[:, :3]
    windows = jnp.concatenate([pieces, trailing], axis=1)
    return jnp.moveaxis(windows.reshape((count * (block + 3),) + rest), 0, axis_index)


def spread_matrix(start, weights, width, wrap_size):
    offsets = jnp.arange(4, dtype=jnp.int32)[:, None, None]
    target = start[None, :, None] + offsets
    if wrap_size > 0:
        target = target % wrap_size
    hits = (target == jnp.arange(width, dtype=jnp.int32)[None, None, :]).astype(jnp.float32)
    return jnp.sum(weights[:, :, None] * hits, axis=0)


def per_device_general(
    positions,
    types,
    neighbours,
    neighbour_count,
    send_index,
    cell_x,
    cell_y,
    cell_z,
    spline_fraction,
    embed_first,
    embed_second,
    embed_third,
    energy_in,
    energy_hidden,
    energy_out,
    wannier_in,
    wannier_hidden,
    wannier_out,
    charge_base,
):
    atom_count = types.shape[1]
    ghost_rows = send_index.shape[1] // 2
    kind_float = types[0].astype(jnp.float32)
    own_atoms = jnp.concatenate([positions[:, 0], kind_float[None]], axis=0)
    outgoing = own_atoms[:, send_index[0]]
    padded_ghosts = with_halo(outgoing, (("brick", 1),), ghost_rows)
    extended = jnp.concatenate(
        [padded_ghosts[:, :ghost_rows], own_atoms, padded_ghosts[:, 3 * ghost_rows :]], axis=1
    )
    energy_short, charge_shift = atom_terms(
        extended,
        neighbours[0],
        neighbour_count[0],
        embed_first,
        embed_second,
        embed_third,
        energy_in,
        energy_hidden,
        energy_out,
        wannier_in,
        wannier_hidden,
        wannier_out,
    )
    charge = (1.0 - kind_float) * charge_base[0] + kind_float * charge_base[1] + charge_shift
    count_x = lax.axis_size("brick")
    count_y = lax.axis_size("slab")
    block_x = NG // count_x
    block_y = NG // count_y
    wide_x = block_x + 3
    wide_y = block_y + 3
    spread_x = spread_matrix(cell_x[0], spline_weights(spline_fraction[0, 0]), wide_x, 0)
    spread_y = spread_matrix(cell_y[0], spline_weights(spline_fraction[1, 0]), wide_y, 0)
    spread_z = spread_matrix(cell_z[0], spline_weights(spline_fraction[2, 0]), NG, NG)
    spread_xy = (spread_x[:, :, None] * spread_y[:, None, :]).reshape(atom_count, wide_x * wide_y)
    charge_grid = jnp.einsum(
        "ap,az->pz", spread_xy, charge[:, None] * spread_z, precision=HIGH
    ).reshape(wide_x, wide_y, NG)
    cosine, sine = dft_tables(NG)
    scale = 1.0 / (NG * NG * NG)
    full_index = jnp.arange(NG, dtype=jnp.int32)
    paired = jnp.stack([along(charge_grid, cosine, 2), -along(charge_grid, sine, 2)])
    moved = lax.all_to_all(paired, "slab", split_axis=3, concat_axis=2, tiled=True)
    moved = complex_transform(fold_windows(moved, 2, block_y, count_y), 2, cosine, sine, False)
    moved = lax.all_to_all(moved, "brick", split_axis=2, concat_axis=1, tiled=True)
    moved = complex_transform(fold_windows(moved, 1, block_x, count_x), 1, cosine, sine, False)
    part_y = NG // count_x
    part_z = NG // count_y
    index_y = lax.axis_index("brick") * part_y + jnp.arange(part_y, dtype=jnp.int32)
    index_z = lax.axis_index("slab") * part_z + jnp.arange(part_z, dtype=jnp.int32)
    moved = moved * (green_table(full_index, index_y, index_z, NG) * scale)[None]
    moved = make_windows(complex_transform(moved, 1, cosine, sine, True), 1, block_x, count_x)
    moved = lax.all_to_all(moved, "brick", split_axis=1, concat_axis=2, tiled=True)
    moved = make_windows(complex_transform(moved, 2, cosine, sine, True), 2, block_y, count_y)
    moved = lax.all_to_all(moved, "slab", split_axis=2, concat_axis=3, tiled=True)
    potential_wide = along(moved[0], cosine, 2) - along(moved[1], sine, 2)
    sampled = jnp.einsum(
        "ap,pz->az", spread_xy, potential_wide.reshape(wide_x * wide_y, NG), precision=HIGH
    )
    potential_at = jnp.sum(sampled * spread_z, axis=1)
    atom_energy = energy_short + 0.5 * charge * potential_at
    return (atom_energy[None, :], potential_wide[:block_x, :block_y])


def split(values):
    high = values.astype(jnp.bfloat16)
    low = (values - high.astype(jnp.float32)).astype(jnp.bfloat16)
    return high, low


def multiply(left, right, dims):
    return lax.dot_general(left, right, (dims, ((), ())), preferred_element_type=jnp.float32)


def triple(left, right, dims=((1,), (0,))):
    return (
        multiply(left[0], right[0], dims)
        + multiply(left[0], right[1], dims)
        + multiply(left[1], right[0], dims)
    )


LANES = ((1,), (1,))


def product(left, right, dims=((1,), (0,))):
    return lax.dot_general(
        left,
        right,
        (dims, ((), ())),
        precision=lax.Precision.HIGH,
        preferred_element_type=jnp.float32,
    )


def lane_pick(table, index):
    return jnp.take_along_axis(table, index, axis=1, mode="promise_in_bounds")


def whole(shape):
    return pl.BlockSpec(tuple(shape), lambda step: (0,) * len(shape))


def whole_specs(*arrays):
    return [whole(array.shape) for array in arrays]


def collect_kernel(
    positions_ref, types_ref, count_ref, send_ref, own_ref, outgoing_ref
):
    atoms = types_ref.shape[1]
    own_ref[...] = jnp.zeros_like(own_ref)
    for axis in range(3):
        own_ref[axis : axis + 1, 0:atoms] = positions_ref[axis]
    own_ref[3:4, 0:atoms] = types_ref[...].astype(jnp.float32)
    own_ref[4:5, 0:atoms] = count_ref[...].astype(jnp.float32)
    own_ref[5:6, 0:atoms] = send_ref[...].astype(jnp.float32)
    for chunk in range(2):
        lanes = slice(128 * chunk, 128 * chunk + 128)
        wanted = jnp.broadcast_to(own_ref[5:6, lanes], (8, 128)).astype(jnp.int32)
        within = wanted & 127
        outgoing_ref[:, lanes] = jnp.where(
            wanted < 128,
            lane_pick(own_ref[:, 0:128], within),
            lane_pick(own_ref[:, 128:256], within),
        )


def collect(positions, types, counts, send_index):
    arrays = (positions, types, counts, send_index)
    result = jax.ShapeDtypeStruct((8, 256), jnp.float32)
    return pl.pallas_call(
        collect_kernel,
        grid=(1,),
        out_shape=[result, result],
        in_specs=whole_specs(*arrays),
        out_specs=whole_specs(result, result),
        compiler_params=pltpu.CompilerParams(vmem_limit_bytes=VMEM_BYTES),
        name="collect_atoms",
    )(*arrays)


def fitting_rows(descriptor_ref, weight_in_ref, weight_hidden_ref, weight_out_ref):
    hidden = jnp.tanh(product(descriptor_ref[...], weight_in_ref[...], LANES))
    for layer in range(weight_hidden_ref.shape[0]):
        hidden = jnp.tanh(product(hidden, weight_hidden_ref[layer])) + hidden
    width = hidden.shape[1]
    return product(jnp.broadcast_to(weight_out_ref[...], (8, width)), hidden, LANES)


def natural_order(rows):
    atoms = rows.shape[1]
    padded = jnp.concatenate([rows, jnp.zeros((8, 256 - atoms), jnp.float32)], axis=1)
    pieces = []
    for chunk in range(2):
        atom = 128 * chunk + lax.broadcasted_iota(jnp.int32, (8, 128), 1)
        late = atom >= atoms // 2
        within = jnp.where(late, atom - atoms // 2, atom)
        place = 8 * (within >> 2) + (within & 3) + jnp.where(late, 4, 0)
        place = jnp.minimum(place, 255)
        pieces.append(
            jnp.where(
                place < 128,
                lane_pick(padded[:, 0:128], place & 127),
                lane_pick(padded[:, 128:256], place & 127),
            )
        )
    return jnp.concatenate(pieces, axis=1)[0:1, 0:atoms]


def network_kernel(
    ghosts,
    base_ref,
    charges_ref,
    own_ref,
    lower_ref,
    upper_ref,
    slots_ref,
    types_ref,
    cell_x_ref,
    cell_y_ref,
    cell_z_ref,
    fraction_ref,
    first_ref,
    second_ref,
    third_ref,
    spot_ref,
    weight_in_hbm,
    weight_hidden_hbm,
    weight_out_ref,
    descriptor_hbm,
    charge_ref,
    copies_ref,
    descriptor_ref,
    environment_ref,
    kind_ref,
    moments_ref,
    padded_ref,
    weight_in_ref,
    weight_hidden_ref,
    row_ref,
    semaphores,
):
    fetches = [
        pltpu.make_async_copy(weight_in_hbm, weight_in_ref, semaphores.at[0]),
        pltpu.make_async_copy(weight_hidden_hbm, weight_hidden_ref, semaphores.at[1]),
    ]
    for fetch in fetches:
        fetch.start()
    slots, atoms = slots_ref.shape
    rows = atoms // 2
    lane = lax.broadcasted_iota(jnp.int32, (8, 128), 1)
    sub = lax.broadcasted_iota(jnp.int32, (8, 128), 0)

    width = first_ref.shape[1]
    padded_ref[...] = jnp.zeros_like(padded_ref)
    padded_ref[0, 0:2, 0:width] = first_ref[...]
    for column in range(2):
        padded_ref[1, 0:width, 32 * column : 32 * column + width] = second_ref[
            :, width * column : width * (column + 1)
        ]
    for row in range(2):
        for column in range(4):
            padded_ref[2, 32 * row : 32 * row + width, 32 * column : 32 * column + width] = (
                third_ref[
                    width * row : width * (row + 1), width * column : width * (column + 1)
                ]
            )
    first_table = padded_ref[0].T
    embed_zero = jnp.broadcast_to(first_table[0:32, 0:1], (32, 128))
    embed_one = jnp.broadcast_to(first_table[0:32, 1:2], (32, 128))
    second_high, second_low = split(padded_ref[1].T[0:64, 0:32])
    second_weight = jnp.concatenate([second_high, second_high, second_low], axis=1)
    third_high, third_low = split(padded_ref[2].T[:, 0:64])
    third_weight = jnp.concatenate([third_high, third_high, third_low], axis=1)

    def spread(ref, field, chunk):
        return jnp.broadcast_to(ref[field : field + 1, 128 * chunk : 128 * chunk + 128], (8, 128))

    own = [[spread(own_ref, field, chunk) for chunk in range(2)] for field in range(5)]
    lower = [[spread(lower_ref, field, chunk) for chunk in range(2)] for field in range(4)]
    upper = [spread(upper_ref, field, 0) for field in range(4)]

    def pick_two(tables, index):
        within = index & 127
        return jnp.where(index < 128, lane_pick(tables[0], within), lane_pick(tables[1], within))

    pairs = jnp.concatenate([slots_ref[:, 0:rows], slots_ref[:, rows:atoms]], axis=0).T
    for tile in range(rows // 8):
        band = slice(8 * tile, 8 * tile + 8)
        index = pairs[band, :]
        centre = 8 * tile + sub + jnp.where(lane < 64, 0, rows)
        from_own = jnp.clip(index - ghosts, 0, atoms - 1)
        from_lower = jnp.minimum(index + (atoms - ghosts), 255)
        from_upper = jnp.clip(index - (ghosts + atoms), 0, 127)

        def neighbour(field):
            below = pick_two(lower[field], from_lower)
            inside = pick_two(own[field], from_own)
            above = lane_pick(upper[field], from_upper)
            return jnp.where(
                index < ghosts, below, jnp.where(index < ghosts + atoms, inside, above)
            )

        offsets = [neighbour(field) - pick_two(own[field], centre) for field in range(3)]
        live = pick_two(own[4], centre)
        present = jnp.where((lane & 63).astype(jnp.float32) < live, 1.0, 0.0)
        smooth = present / (
            1.0 + (offsets[0] * offsets[0] + offsets[1] * offsets[1] + offsets[2] * offsets[2])
        )
        environment_ref[0, band, :] = smooth
        for field in range(3):
            environment_ref[1 + field, band, :] = smooth * offsets[field]
        kind_ref[band, :] = neighbour(3)

    group = 8

    def stacked(values):
        high, low = split(values)
        return jnp.concatenate([high, low, high], axis=0)

    def one_group(start):
        pieces = []
        for row in range(group):
            smooth = jnp.broadcast_to(environment_ref[0, pl.ds(start + row, 1), :], (32, 128))
            kind = jnp.broadcast_to(kind_ref[pl.ds(start + row, 1), :], (32, 128))
            pieces.append(
                jnp.tanh(smooth * ((1.0 - kind) * embed_zero + kind * embed_one))
            )
        first = jnp.concatenate(pieces, axis=1)
        second = jnp.tanh(multiply(second_weight, stacked(first), ((1,), (0,))))
        second = second + jnp.concatenate([first, first], axis=0)
        third = jnp.tanh(multiply(third_weight, stacked(second), ((1,), (0,))))
        third = third + jnp.concatenate([second, second], axis=0)
        third_pair = jnp.concatenate(split(third), axis=0)
        for half in range(group // 4):
            columns = slice(512 * half, 512 * half + 512)
            bands = []
            for part in range(4):
                bands.append(
                    jnp.concatenate(
                        [
                            jnp.where(
                                sub == row + jnp.where(lane < 64, 0, 4),
                                jnp.broadcast_to(
                                    environment_ref[part, pl.ds(start + 4 * half + row, 1), :],
                                    (8, 128),
                                ),
                                0.0,
                            )
                            for row in range(4)
                        ],
                        axis=1,
                    )
                )
            environment = split(jnp.concatenate(bands, axis=0))
            both = multiply(
                jnp.concatenate(environment, axis=0), third_pair[:, columns], LANES
            )
            sums = both[0:32, 0:128] + both[32:64, 0:128] + both[0:32, 128:256]
            sums = sums * (1.0 / slots)
            for part in range(4):
                moments_ref[part, pl.ds(2 * start + 8 * half, 8), :] = sums[
                    8 * part : 8 * part + 8
                ]

    def body(step, carry):
        for part in range(unroll):
            one_group(pl.multiple_of(step * unroll * group + part * group, group))
        return carry

    unroll = rows // group
    lax.fori_loop(0, rows // (unroll * group), body, 0)

    chunks = (descriptor_ref.shape[1] + 127) // 128
    last = descriptor_ref.shape[1] - 128 * (chunks - 1)

    def describe_band(start):
        band = pl.ds(start, 8)
        moments = [moments_ref[part, band, :] for part in range(4)]
        axis_part = [lane_pick(moments[part], lane & 15) for part in range(4)]
        for chunk in range(chunks):
            spot = jnp.broadcast_to(spot_ref[chunk : chunk + 1, :], (8, 128))
            total = lane_pick(moments[0], spot) * axis_part[0]
            for part in range(1, 4):
                total = total + lane_pick(moments[part], spot) * axis_part[part]
            if chunk < chunks - 1:
                descriptor_ref[band, 128 * chunk : 128 * chunk + 128] = total
            else:
                descriptor_ref[band, 128 * chunk : 128 * chunk + last] = total[:, 0:last]

    bands = 8 if atoms % 64 == 0 else 1

    def describe(step, carry):
        for part in range(bands):
            describe_band(pl.multiple_of(step * 8 * bands + 8 * part, 8))
        return carry

    lax.fori_loop(0, atoms // (8 * bands), describe, 0)

    store = pltpu.make_async_copy(descriptor_ref, descriptor_hbm, semaphores.at[2])
    store.start()
    for fetch in fetches:
        fetch.wait()
    shift = fitting_rows(descriptor_ref, weight_in_ref, weight_hidden_ref, weight_out_ref)
    kind = types_ref[...].astype(jnp.float32)
    charge = (1.0 - kind) * charges_ref[0] + kind * charges_ref[1] + natural_order(shift)
    charge_ref[...] = charge
    fields = [
        cell_x_ref[...].astype(jnp.float32),
        (cell_y_ref[...] + base_ref[0]).astype(jnp.float32),
        cell_z_ref[...].astype(jnp.float32),
    ]
    fields = fields + [fraction_ref[axis] for axis in range(3)] + [charge]
    for place, field in enumerate(fields):
        row_ref[:, atoms * place : atoms * (place + 1)] = field
    for copy in range(copies_ref.shape[0]):
        copies_ref[copy] = row_ref[...]
    store.wait()


def spot_table(embed, desc):
    column = np.arange(desc) // AXIS
    quarter = embed // 4
    place = 32 * (column // quarter) + column % quarter
    chunks = (desc + 127) // 128
    table = np.zeros((chunks * 128,), np.int32)
    table[:desc] = place
    padded = np.zeros(((chunks + 7) // 8 * 8, 128), np.int32)
    padded[:chunks] = table.reshape(chunks, 128)
    return padded


def networks(
    copies,
    ghosts,
    base,
    charge_base,
    own,
    lower,
    upper,
    neighbours,
    types,
    cells,
    fraction,
    embed,
    weight_in,
    weight_hidden,
    weight_out,
):
    atoms = types.shape[1]
    desc, width = weight_in.shape
    spots = jnp.asarray(spot_table(embed[2].shape[1], desc))
    anywhere = pl.BlockSpec(memory_space=pl.ANY)
    scalars = pl.BlockSpec(memory_space=pltpu.SMEM)
    blocks = (own, lower, upper, neighbours[0].T, types, *cells, fraction, *embed, spots)
    weight_out = weight_out.reshape(1, -1)
    results = [
        jax.ShapeDtypeStruct((atoms, desc), jnp.float32),
        jax.ShapeDtypeStruct((1, atoms), jnp.float32),
        jax.ShapeDtypeStruct((copies, 1, FIELDS * atoms), jnp.float32),
    ]
    return pl.pallas_call(
        functools.partial(network_kernel, ghosts),
        grid=(1,),
        out_shape=results,
        in_specs=[scalars, scalars]
        + whole_specs(*blocks)
        + [anywhere, anywhere]
        + whole_specs(weight_out),
        out_specs=[anywhere] + whole_specs(*results[1:]),
        scratch_shapes=[
            pltpu.VMEM((atoms, desc), jnp.float32),
            pltpu.VMEM((4, atoms // 2, 128), jnp.float32),
            pltpu.VMEM((atoms // 2, 128), jnp.float32),
            pltpu.VMEM((4, atoms, 128), jnp.float32),
            pltpu.VMEM((3, 128, 128), jnp.float32),
            pltpu.VMEM((width, desc), jnp.float32),
            pltpu.VMEM(weight_hidden.shape, jnp.float32),
            pltpu.VMEM((1, FIELDS * atoms), jnp.float32),
            pltpu.SemaphoreType.DMA((3,)),
        ],
        compiler_params=pltpu.CompilerParams(vmem_limit_bytes=VMEM_BYTES),
        name="networks",
    )(base, charge_base, *blocks, weight_in.T, weight_hidden, weight_out)


def energy_kernel(descriptor_ref, weight_in_ref, weight_hidden_ref, weight_out_ref, energy_ref):
    energy_ref[...] = natural_order(
        fitting_rows(descriptor_ref, weight_in_ref, weight_hidden_ref, weight_out_ref)
    )


def energies(descriptor, weight_in, weight_hidden, weight_out):
    atoms, desc = descriptor.shape
    width = weight_in.shape[1]
    arrays = (descriptor, weight_in.T, weight_hidden, weight_out.reshape(1, -1))
    result = jax.ShapeDtypeStruct((1, atoms), jnp.float32)
    return pl.pallas_call(
        energy_kernel,
        grid=(1,),
        out_shape=result,
        in_specs=whole_specs(*arrays),
        out_specs=whole(result.shape),
        compiler_params=pltpu.CompilerParams(vmem_limit_bytes=VMEM_BYTES),
        cost_estimate=pl.CostEstimate(
            flops=6 * atoms * desc * width, bytes_accessed=4 * desc * width, transcendentals=0
        ),
        name="energies",
    )(*arrays)


def weight_rows(fraction):
    square = fraction * fraction
    cubed = square * fraction
    rest = 1.0 - fraction
    return [
        rest * rest * rest / 6.0,
        (3.0 * cubed - 6.0 * square + 4.0) / 6.0,
        (-3.0 * cubed + 3.0 * square + 3.0 * fraction + 1.0) / 6.0,
        cubed / 6.0,
    ]


def placed_weights(distance, weights):
    shape = distance.shape
    result = jnp.zeros(shape, jnp.float32)
    for step in range(4):
        result = jnp.where(
            distance == step, jnp.broadcast_to(weights[step], shape), result
        )
    return result


def third_factors(fields, waves_ref, cosine_ref):
    atoms = fields.shape[1]
    start = fields[2:3, :].astype(jnp.int32)
    along = weight_rows(fields[5:6, :])
    parts = waves_ref.shape[0]
    cosine = jnp.broadcast_to(cosine_ref[...], (parts, 128))
    wave = jnp.broadcast_to(waves_ref[:, 0:1], (parts, 128))
    shift = jnp.broadcast_to(waves_ref[:, 1:2], (parts, 128))
    pieces = []
    for chunk in range(atoms // 128):
        lanes = slice(128 * chunk, 128 * chunk + 128)
        total = jnp.zeros((parts, 128), jnp.float32)
        for step in range(4):
            place = jnp.broadcast_to(start[:, lanes] + step, (parts, 128))
            phase = (wave * place + shift) & (NG - 1)
            value = lane_pick(cosine, phase & 127)
            value = jnp.where(phase < 128, value, -value)
            total = total + value * jnp.broadcast_to(along[step][:, lanes], (parts, 128))
        pieces.append(total)
    return jnp.concatenate(pieces, axis=1)


def first_third_split(fields, waves_ref, cosine_ref, window, scale, high_ref, low_ref):
    atoms = fields.shape[1]
    third = third_factors(fields, waves_ref, cosine_ref) * scale
    rows = lax.broadcasted_iota(jnp.int32, (window, atoms), 0)
    first = placed_weights(
        rows - fields[0:1, :].astype(jnp.int32), weight_rows(fields[3:4, :])
    )
    for chunk in range(atoms // 128):
        lanes = slice(128 * chunk, 128 * (chunk + 1))
        for part in range(0, third.shape[0], 2):
            high, low = split(
                jnp.concatenate(
                    [first[:, lanes] * third[part + side : part + side + 1, lanes] for side in range(2)],
                    axis=0,
                )
            )
            place = slice(part * window, (part + 2) * window)
            high_ref[place, lanes] = high
            low_ref[place, lanes] = low
    return high_ref[...], low_ref[...]


def second_factors(fields, base, block_y, slabs, high_ref, low_ref):
    atoms = fields.shape[1]
    block = atoms // slabs
    reach = block_y + REACH
    start = fields[1:2, :].astype(jnp.int32) - base
    weights = weight_rows(fields[4:5, :])
    for chunk in range(atoms // 128):
        lanes = slice(128 * chunk, 128 * (chunk + 1))
        first = 128 * chunk // block
        last = (128 * chunk + 127) // block
        top = first * block_y
        rows = (last - first) * block_y + reach
        pieces = [(top, min(rows, NG - top))]
        if top + rows > NG:
            pieces.append((0, top + rows - NG))
        for row, count in pieces:
            index = row + lax.broadcasted_iota(jnp.int32, (count, 128), 0)
            table = split(
                placed_weights(
                    (index - start[:, lanes]) & (NG - 1), [weight[:, lanes] for weight in weights]
                )
            )
            high_ref[row : row + count, lanes] = table[0]
            low_ref[row : row + count, lanes] = table[1]
    return high_ref[...], low_ref[...]


def wave_of(index):
    return jnp.where(index <= NG // 2, index, index - NG // 2)


def damping(index):
    kappa = wave_of(index).astype(jnp.float32) * (2.0 * math.pi / NG)
    squared = kappa * kappa
    ends = (index == 0) | (index == NG // 2)
    return squared, jnp.exp(-0.5 * squared) * jnp.where(ends, 1.0 / NG, 2.0 / NG)


def transform(planes, kappa_ref, first_part, tables_ref, last_ref):
    count = len(planes)
    basis = tables_ref[0]
    turned = tables_ref[1]
    square_x, damp_x = damping(lax.broadcasted_iota(jnp.int32, (NG, 1), 0))
    square_y, damp_y = damping(lax.broadcasted_iota(jnp.int32, (1, NG), 1))
    square_xy = square_x + square_y
    damp_xy = damp_x * damp_y
    columns = [slice(NG * part, NG * (part + 1)) for part in range(count)]
    first = product(basis, jnp.concatenate(planes, axis=1))
    first = jnp.concatenate([first[:, column] for column in columns], axis=0)
    both = product(first, turned)
    scaled = []
    for part in range(count):
        squared = square_xy + kappa_ref[first_part + part, 0]
        root = jnp.where(squared == 0.0, 1.0, 0.0)
        green = (1.0 - root) * (damp_xy * kappa_ref[first_part + part, 1]) / (squared + root)
        scaled.append(both[columns[part]] * green)
    back = product(turned, jnp.concatenate(scaled, axis=1))
    back = jnp.concatenate([back[:, column] for column in columns], axis=0)
    return product(back, last_ref[...])


def send_blocks(full, block_x, block_y, put):
    low_lanes = lax.broadcasted_iota(jnp.int32, (NG, 128), 1) < block_y
    for pair in range(full.shape[0] // (2 * NG)):
        even = full[2 * NG * pair : 2 * NG * pair + NG, 0:128]
        odd = full[2 * NG * pair + NG : 2 * NG * (pair + 1), 0:128]
        blocks = [
            jnp.where(low_lanes, even, pltpu.roll(odd, block_y, 1)),
            jnp.where(low_lanes, pltpu.roll(even, block_y, 1), odd),
        ]
        for brick in range(NG // block_x):
            for side in range(2):
                for group in range(block_x // 8):
                    start = block_x * brick + 8 * group
                    put(pair, brick, side, group, blocks[side][start : start + 8])


def spread_kernel(
    block_x,
    block_y,
    window,
    kappa_ref,
    pair_ref,
    static_ref,
    waves_ref,
    cosine_ref,
    tables_hbm,
    last_hbm,
    short_hbm,
    sent_ref,
    full_ref,
    atoms_ref,
    later_hbm,
    grid_ref,
    tables_ref,
    last_ref,
    semaphores,
    *pair_refs,
):
    slabs = NG // block_y
    second_refs, first_refs = pair_refs[:4], pair_refs[4:]
    bricks = NG // block_x
    parts = waves_ref.shape[0]
    block = static_ref.shape[2] // FIELDS
    count = full_ref.shape[0]
    step = pl.program_id(0)
    later = later_hbm.shape[0]
    store = pltpu.make_async_copy(
        grid_ref.at[pl.ds(parts - later, later), pl.ds(0, NG)], later_hbm, semaphores.at[2]
    )

    @pl.when(step == 0)
    def _():
        fetches = [
            pltpu.make_async_copy(tables_hbm, tables_ref, semaphores.at[0]),
            pltpu.make_async_copy(last_hbm.at[pair_ref[0]], last_ref, semaphores.at[1]),
        ]
        for fetch in fetches:
            fetch.start()
        for slab in range(slabs):
            lanes = slice(block * slab, block * (slab + 1))
            for brick in range(bricks):
                for field in range(FIELDS):
                    atoms_ref[brick, field : field + 1, lanes] = static_ref[
                        slab * bricks + brick, :, block * field : block * (field + 1)
                    ]
        for ref in second_refs:
            ref[...] = jnp.zeros_like(ref)
        for brick in range(bricks):
            fields = atoms_ref[brick]
            table = first_third_split(
                fields,
                waves_ref,
                cosine_ref,
                window,
                fields[6:7, :],
                first_refs[2 * (brick % 2)],
                first_refs[2 * (brick % 2) + 1],
            )
            second = second_factors(
                fields, 0, block_y, slabs, second_refs[2 * (brick % 2)], second_refs[2 * (brick % 2) + 1]
            )
            spread = triple(table, second, LANES)
            start = block_x * brick
            extra = window - block_x
            for part in range(parts):
                shared = spread[part * window : part * window + extra]
                if brick > 0:
                    shared = shared + grid_ref[part, start : start + extra, :]
                grid_ref[part, start : start + extra, :] = shared
                grid_ref[part, start + extra : start + window, :] = spread[
                    part * window + extra : part * window + window
                ]
        for part in range(parts):
            grid_ref[part, 0:extra, :] += grid_ref[part, NG : NG + extra, :]
        store.start()
        for fetch in fetches:
            fetch.wait()

    planes = [grid_ref[count * step + part, 0:NG, :] for part in range(count)]
    full = transform(planes, kappa_ref, count * step, tables_ref, last_ref)
    for part in range(count):
        full_ref[part] = full[NG * part : NG * (part + 1)]

    def put(pair, brick, side, group, tile):
        sent_ref[2 * brick + side, group, pair] = tile

    send_blocks(full, block_x, block_y, put)

    @pl.when(step == pl.num_programs(0) - 1)
    def _():
        store.wait()


def early_pairs(parts):
    return parts // 4


def spread_and_solve(
    block_x, block_y, window, kappa, pair, static, waves, cosine_row, tables, last, short
):
    atoms = static.shape[2] // FIELDS
    slabs = NG // block_y
    bricks = NG // block_x
    parts = waves.shape[0]
    pairs = early_pairs(parts)
    count = 4
    anywhere = pl.BlockSpec(memory_space=pl.ANY)
    scalars = pl.BlockSpec(memory_space=pltpu.SMEM)
    sent_block = (2 * bricks, block_x // 8, count // 2, 8, 128)
    return pl.pallas_call(
        functools.partial(spread_kernel, block_x, block_y, window),
        grid=(2 * pairs // count,),
        out_shape=[
            jax.ShapeDtypeStruct((2 * bricks, block_x // 8, pairs, 8, 128), jnp.float32),
            jax.ShapeDtypeStruct((2 * pairs, NG, NG), jnp.float32),
            jax.ShapeDtypeStruct((bricks, 8, slabs * atoms), jnp.float32),
            jax.ShapeDtypeStruct((parts - 2 * pairs, NG, NG), jnp.float32),
        ],
        in_specs=[scalars, scalars]
        + whole_specs(static, waves, cosine_row)
        + [anywhere, anywhere, anywhere],
        out_specs=[
            pl.BlockSpec(sent_block, lambda step: (0, 0, step, 0, 0)),
            pl.BlockSpec((count, NG, NG), lambda step: (step, 0, 0)),
            whole((bricks, 8, slabs * atoms)),
            anywhere,
        ],
        scratch_shapes=[
            pltpu.VMEM((parts, NG + window - block_x, NG), jnp.float32),
            pltpu.VMEM(tables.shape, tables.dtype),
            pltpu.VMEM(last.shape[1:], last.dtype),
            pltpu.SemaphoreType.DMA((3,)),
        ]
        + [pltpu.VMEM((NG, slabs * atoms), jnp.bfloat16)] * 4
        + [pltpu.VMEM((parts * window, slabs * atoms), jnp.bfloat16)] * 4,
        compiler_params=pltpu.CompilerParams(vmem_limit_bytes=VMEM_BYTES),
        name="spread_and_solve",
    )(kappa, pair, static, waves, cosine_row, tables, last, short)


def sample_kernel(
    block_x,
    block_y,
    window,
    kappa_ref,
    pair_ref,
    atoms_ref,
    waves_ref,
    cosine_ref,
    tables_hbm,
    last_hbm,
    later_hbm,
    early_hbm,
    sent_ref,
    later_ref,
    full_ref,
    tables_ref,
    last_ref,
    semaphores,
    packed_ref,
):
    bricks = atoms_ref.shape[0]
    parts = waves_ref.shape[0]
    early = 2 * early_pairs(parts)
    block = atoms_ref.shape[2] * block_y // NG
    fetches = [
        pltpu.make_async_copy(tables_hbm, tables_ref, semaphores.at[0]),
        pltpu.make_async_copy(last_hbm.at[pair_ref[0]], last_ref, semaphores.at[1]),
        pltpu.make_async_copy(later_hbm, later_ref, semaphores.at[2]),
        pltpu.make_async_copy(early_hbm, full_ref.at[pl.ds(0, early)], semaphores.at[3]),
    ]
    for fetch in fetches:
        fetch.start()
    for fetch in fetches[:3]:
        fetch.wait()
    pairs = (parts - early) // 2
    planes = [later_ref[part] for part in range(parts - early)]
    full = transform(planes, kappa_ref, early, tables_ref, last_ref)
    for part in range(parts - early):
        full_ref[early + part] = full[NG * part : NG * (part + 1)]

    def put(pair, brick, side, group, tile):
        sent_ref[2 * brick + side, pairs * group + pair] = tile

    send_blocks(full, block_x, block_y, put)
    fetches[3].wait()

    reach = block_y + REACH
    lane = lax.broadcasted_iota(jnp.int32, (NG, 128), 1)
    for part in range(parts):
        for side in range(2):
            values = full_ref[part, :, 128 * side : 128 * (side + 1)]
            high = values.astype(jnp.bfloat16).astype(jnp.float32)
            again = pltpu.roll(high, reach, 1)
            low = pltpu.roll(values - high, 2 * reach - 128, 1)
            packed_ref[side, part, 0:NG, 0:128] = jnp.where(lane < reach, high, again)
            packed_ref[side, part, 0:NG, 128:NG] = jnp.where(
                lane < 2 * reach - 128, again, jnp.where(lane < 3 * reach - 128, low, 0.0)
            )
            packed_ref[side, part, NG : NG + window - block_x, :] = packed_ref[
                side, part, 0 : window - block_x, :
            ]
    extra = sent_ref.shape[1] - 1
    base = 2 * block_y * pair_ref[0]
    lanes = pl.ds(pl.multiple_of(2 * block * pair_ref[0], 128), 2 * block)
    for brick in range(bricks):
        fields = atoms_ref[brick, :, lanes]
        thirds = third_factors(fields, waves_ref, cosine_ref)
        rows = slice(block_x * brick, block_x * brick + window)
        for side in range(2):
            here = slice(block * side, block * (side + 1))
            third = thirds[:, here]
            ours = fields[:, here]
            index = lax.broadcasted_iota(jnp.int32, (window, block), 0)
            first = placed_weights(
                index - ours[0:1, :].astype(jnp.int32), weight_rows(ours[3:4, :])
            )
            index = lax.broadcasted_iota(jnp.int32, (reach, block), 0)
            start = ours[1:2, :].astype(jnp.int32) - (base + block_y * side)
            high, low = split(placed_weights(index - start, weight_rows(ours[4:5, :])))
            rest = jnp.zeros((NG - 3 * reach, block), jnp.bfloat16)
            second = jnp.concatenate([high, low, high, rest], axis=0)
            values = jnp.concatenate(
                [packed_ref[side, part, rows, :] for part in range(parts)], axis=0
            )
            along = multiply(values.astype(jnp.bfloat16), second, ((1,), (0,)))
            total = jnp.zeros((window, block), jnp.float32)
            for part in range(parts):
                total = total + along[window * part : window * (part + 1)] * third[part : part + 1]
            row = jnp.sum(total * first, axis=0, keepdims=True)
            sent_ref[2 * brick + side, extra] = jnp.zeros((8, 128), jnp.float32)
            sent_ref[2 * brick + side, extra, 0:1, :] = row[:, 0:128]
            sent_ref[2 * brick + side, extra, 1:2, 0 : block - 128] = row[:, 128:block]


def solve_and_sample(
    block_x, block_y, window, kappa, pair, atoms, waves, cosine_row, tables, last, later, early
):
    bricks = atoms.shape[0]
    parts = waves.shape[0]
    pairs = parts // 2 - early_pairs(parts)
    anywhere = pl.BlockSpec(memory_space=pl.ANY)
    scalars = pl.BlockSpec(memory_space=pltpu.SMEM)
    result = jax.ShapeDtypeStruct((2 * bricks, block_x // 8 * pairs + 1, 8, 128), jnp.float32)
    return pl.pallas_call(
        functools.partial(sample_kernel, block_x, block_y, window),
        grid=(1,),
        out_shape=result,
        in_specs=[scalars, scalars] + whole_specs(atoms, waves, cosine_row) + [anywhere] * 4,
        out_specs=whole(result.shape),
        scratch_shapes=[
            pltpu.VMEM((2 * pairs, NG, NG), jnp.float32),
            pltpu.VMEM((parts, NG, NG), jnp.float32),
            pltpu.VMEM(tables.shape, tables.dtype),
            pltpu.VMEM(last.shape[1:], last.dtype),
            pltpu.SemaphoreType.DMA((4,)),
        ]
        + [pltpu.VMEM((2, parts, NG + window - block_x, NG), jnp.float32)],
        compiler_params=pltpu.CompilerParams(vmem_limit_bytes=VMEM_BYTES),
        cost_estimate=pl.CostEstimate(
            flops=24 * parts * NG * NG * NG, bytes_accessed=4 * early.size, transcendentals=0
        ),
        name="solve_and_sample",
    )(kappa, pair, atoms, waves, cosine_row, tables, last, later, early)


def finish_kernel(
    block_y,
    early_ref,
    later_ref,
    sums_ref,
    short_hbm,
    charge_hbm,
    table_ref,
    out_ref,
    energy_ref,
    short_ref,
    charge_ref,
    semaphores,
):
    atoms = short_ref.shape[1]
    fetches = [
        pltpu.make_async_copy(short_hbm, short_ref, semaphores.at[0]),
        pltpu.make_async_copy(charge_hbm, charge_ref, semaphores.at[1]),
    ]

    @pl.when(pl.program_id(0) == 0)
    def _():
        for fetch in fetches:
            fetch.start()

    lines = early_ref.shape[3]
    sources, _, pairs = early_ref.shape[:3]
    early = early_ref.reshape(sources * pairs, lines, 128)
    later = later_ref.reshape(sources * later_ref.shape[1], lines, 128)
    pieces = []
    for line in range(lines):
        turned = jnp.concatenate([early[:, line, :], later[:, line, :]], axis=0).T
        pieces.append(jnp.concatenate([turned[0:block_y], turned[block_y:]], axis=1))
    result = product(jnp.concatenate(pieces, axis=0), table_ref[...])
    for line in range(lines):
        out_ref[line] = result[block_y * line : block_y * (line + 1)]

    @pl.when(pl.program_id(0) == 0)
    def _():
        for fetch in fetches:
            fetch.wait()
        total = jnp.sum(sums_ref[:, 0], axis=0)
        potential_at = jnp.concatenate([total[0:1, :], total[1:2, 0 : atoms - 128]], axis=1)
        energy_ref[...] = short_ref[...] + 0.5 * charge_ref[...] * potential_at


def finish(block_x, block_y, early, later, short, charge, table):
    bricks2, groups, pairs = early.shape[:3]
    rest = (later.shape[1] - 1) // groups
    atoms = short.shape[1]
    return pl.pallas_call(
        functools.partial(finish_kernel, block_y),
        grid=(groups,),
        out_shape=[
            jax.ShapeDtypeStruct((block_x, block_y, NG), jnp.float32),
            jax.ShapeDtypeStruct((1, atoms), jnp.float32),
        ],
        in_specs=[
            pl.BlockSpec((bricks2, 1, pairs, 8, 128), lambda index: (0, index, 0, 0, 0)),
            pl.BlockSpec((bricks2, rest, 8, 128), lambda index: (0, index, 0, 0)),
            pl.BlockSpec((bricks2, 1, 8, 128), lambda index: (0, groups * rest, 0, 0)),
            pl.BlockSpec(memory_space=pltpu.HBM),
            pl.BlockSpec(memory_space=pltpu.HBM),
            whole(table.shape),
        ],
        out_specs=[
            pl.BlockSpec((8, block_y, NG), lambda index: (index, 0, 0)),
            whole((1, atoms)),
        ],
        scratch_shapes=[
            pltpu.VMEM((1, atoms), jnp.float32),
            pltpu.VMEM((1, atoms), jnp.float32),
            pltpu.SemaphoreType.DMA((2,)),
        ],
        compiler_params=pltpu.CompilerParams(vmem_limit_bytes=32 * 2**20),
        name="finish",
    )(early, later, later, short, charge, table)


def real_basis():
    index = np.arange(NG)
    wave = np.where(index <= NG // 2, index, index - NG // 2)
    angle = (wave[:, None] * index[None, :] % NG) * (2.0 * math.pi / NG)
    return np.where((index <= NG // 2)[:, None], np.cos(angle), np.sin(angle))


def per_device(
    positions,
    types,
    neighbours,
    neighbour_count,
    send_index,
    cell_x,
    cell_y,
    cell_z,
    spline_fraction,
    embed_first,
    embed_second,
    embed_third,
    energy_in,
    energy_hidden,
    energy_out,
    wannier_in,
    wannier_hidden,
    wannier_out,
    charge_base,
):
    atoms = types.shape[1]
    ghosts = send_index.shape[1] // 2
    count_x = lax.axis_size("brick")
    count_y = lax.axis_size("slab")
    block_x = NG // count_x
    block_y = NG // count_y
    window = block_x + 8
    parts = NG // (2 * count_x)
    brick = lax.axis_index("brick")
    slab = lax.axis_index("slab")
    pair = (slab // 2).astype(jnp.int32).reshape(1)
    halves = [
        [b * count_y + 2 * p + side for b in range(count_x) for side in range(2)]
        for p in range(count_y // 2)
    ]

    def exchange(values, axes, groups=None):
        return lax.all_to_all(
            values, axes, split_axis=0, concat_axis=0, tiled=True, axis_index_groups=groups
        )

    own, outgoing = collect(positions, types, neighbour_count, send_index)
    up = [(i, (i + 1) % count_x) for i in range(count_x)]
    down = [((i + 1) % count_x, i) for i in range(count_x)]
    lower = lax.ppermute(outgoing, "brick", up)
    upper = lax.ppermute(outgoing, "brick", down)
    descriptor, charge, fields = networks(
        count_x * count_y,
        ghosts,
        (slab * block_y).astype(jnp.int32).reshape(1),
        charge_base,
        own,
        lower,
        upper,
        neighbours,
        types,
        (cell_x, cell_y, cell_z),
        spline_fraction,
        (embed_first, embed_second, embed_third),
        wannier_in,
        wannier_hidden,
        wannier_out,
    )
    every_field = exchange(fields, ("slab", "brick"))

    part = (2 * brick + slab % 2) * parts + jnp.arange(parts, dtype=jnp.int32)
    wave = wave_of(part)
    waves = jnp.stack([wave, jnp.where(part <= NG // 2, 0, 3 * NG // 4)], axis=1)
    kappa = wave.astype(jnp.float32) * (2.0 * math.pi / NG)
    squared = kappa * kappa
    ends = (part == 0) | (part == NG // 2)
    kappa = jnp.stack(
        [squared, jnp.exp(-0.5 * squared) * jnp.where(ends, 1.0 / NG, 2.0 / NG)], axis=1
    )
    basis = real_basis()
    tables = np.stack([basis, basis.T]).astype(np.float32)
    last = []
    for p in range(count_y // 2):
        points = np.concatenate(
            [np.arange(2 * block_y), block_y + np.arange(block_y + REACH)]
        )
        points = (2 * block_y * p + points) % NG
        columns = np.zeros((NG, NG))
        columns[:, : points.size] = basis[:, points]
        last.append(columns.astype(np.float32))
    cosine_row = np.cos(np.arange(128) * (2.0 * math.pi / NG)).astype(np.float32)[None]
    cosine_row = jnp.asarray(cosine_row)
    tables = jnp.asarray(tables)
    last = jnp.asarray(np.stack(last))
    energy_short = energies(descriptor, energy_in, energy_hidden, energy_out)
    early, full, every_atom, later = spread_and_solve(
        block_x,
        block_y,
        window,
        kappa,
        pair,
        every_field,
        waves,
        cosine_row,
        tables,
        last,
        energy_short,
    )

    def send(values):
        got = exchange(values.reshape(values.shape[0], -1, 128), ("brick", "slab"), halves)
        return got.reshape(values.shape)

    early = send(early)
    later = solve_and_sample(
        block_x,
        block_y,
        window,
        kappa,
        pair,
        every_atom,
        waves,
        cosine_row,
        tables,
        last,
        later,
        full,
    )
    later = send(later)
    source = np.arange(2 * count_x)[:, None] * parts
    pairs = 2 * np.arange(parts // 2)[None, :]
    order = np.concatenate(
        [
            (source + pairs[:, : early_pairs(parts)]).ravel(),
            (source + pairs[:, early_pairs(parts) :]).ravel(),
        ]
    )
    order = np.concatenate([order, order + 1])
    potential, atom_energy = finish(
        block_x,
        block_y,
        early,
        later,
        energy_short,
        charge,
        jnp.asarray(basis[order].astype(np.float32)),
    )
    return atom_energy, potential


def solution(mesh):
    placed = (
        P(None, "slab", "brick"),
        P("slab", "brick"),
        P("slab", "brick", None),
        P("slab", "brick"),
        P("slab", "brick"),
        P("slab", "brick"),
        P("slab", "brick"),
        P("slab", "brick"),
        P(None, "slab", "brick"),
    ) + (P(),) * 10
    bricks, slabs = mesh.shape["brick"], mesh.shape["slab"]
    fits = 2 * NG == 128 * slabs and NG % (32 * bricks) == 0
    return jax.shard_map(
        per_device if fits else per_device_general,
        mesh=mesh,
        in_specs=placed,
        out_specs=(P("slab", "brick"), P("brick", "slab", None)),
        check_vma=False,
    )
```

```python
import functools
import math

import jax
import jax.numpy as jnp
import numpy as np
from jax import lax
from jax.experimental import pallas as pl
from jax.experimental.pallas import tpu as pltpu
from jax.sharding import PartitionSpec as P

NG = 256
AXIS = 16
VMEM_BYTES = 60 * 2**20
REACH = 16
FIELDS = 7


HIGH = lax.Precision.HIGHEST


def with_halo(cells, sides, width):
    for axis, dim in sides:
        count = lax.axis_size(axis)
        head = lax.slice_in_dim(cells, 0, width, axis=dim)
        tail = lax.slice_in_dim(cells, cells.shape[dim] - width, cells.shape[dim], axis=dim)
        cells = jnp.concatenate(
            [
                lax.ppermute(tail, axis, [(i, (i + 1) % count) for i in range(count)]),
                cells,
                lax.ppermute(head, axis, [((i + 1) % count, i) for i in range(count)]),
            ],
            axis=dim,
        )
    return cells


def spline_weights(fraction):
    cubed = fraction * fraction * fraction
    square = fraction * fraction
    return jnp.stack(
        [
            (1.0 - fraction) * (1.0 - fraction) * (1.0 - fraction) / 6.0,
            (3.0 * cubed - 6.0 * square + 4.0) / 6.0,
            (-3.0 * cubed + 3.0 * square + 3.0 * fraction + 1.0) / 6.0,
            cubed / 6.0,
        ]
    )


def fitting(descriptor, weight_in, weight_hidden, weight_out):
    hidden = jnp.tanh(jnp.dot(descriptor, weight_in, precision=HIGH))
    for depth_index in range(weight_hidden.shape[0]):
        hidden = jnp.tanh(jnp.dot(hidden, weight_hidden[depth_index], precision=HIGH)) + hidden
    return jnp.dot(hidden, weight_out, precision=HIGH)


def atom_terms(
    extended,
    neighbour_rows,
    neighbour_total,
    embed_first,
    embed_second,
    embed_third,
    energy_in,
    energy_hidden,
    energy_out,
    wannier_in,
    wannier_hidden,
    wannier_out,
):
    atom_count, slots = neighbour_rows.shape
    ghost_rows = (extended.shape[1] - atom_count) // 2
    block_size = 64
    blocks = atom_count // block_size
    present = (jnp.arange(slots, dtype=jnp.int32)[None, :] < neighbour_total[:, None]).astype(
        jnp.float32
    )
    centre_ids = (ghost_rows + jnp.arange(atom_count, dtype=jnp.int32)).reshape(blocks, block_size)
    second_weight = embed_second.T
    third_weight = embed_third.T

    def one_block(pieces):
        centre_rows, rows_block, present_block = pieces
        centre_block = extended[:3, centre_rows]
        gathered = extended[:, rows_block]
        offsets = gathered[:3] - centre_block[:, :, None]
        smooth = present_block / (1.0 + jnp.sum(offsets * offsets, axis=0))
        environment = jnp.stack(
            [smooth, smooth * offsets[0], smooth * offsets[1], smooth * offsets[2]], axis=0
        )
        kind = gathered[3][None]
        mixing = (1.0 - kind) * embed_first[0][:, None, None] + kind * embed_first[1][:, None, None]
        first = jnp.tanh(smooth[None] * mixing).reshape(embed_first.shape[1], block_size * slots)
        second = jnp.tanh(jnp.dot(second_weight, first, precision=HIGH)) + jnp.concatenate(
            [first, first], axis=0
        )
        third = jnp.tanh(jnp.dot(third_weight, second, precision=HIGH)) + jnp.concatenate(
            [second, second], axis=0
        )
        third_blocks = third.reshape(third.shape[0], block_size, slots)
        moments = jnp.einsum("kan,can->akc", third_blocks, environment, precision=HIGH) / slots
        descriptor = jnp.einsum("amc,akc->amk", moments, moments[:, :AXIS], precision=HIGH).reshape(
            block_size, -1
        )
        return (
            fitting(descriptor, energy_in, energy_hidden, energy_out),
            fitting(descriptor, wannier_in, wannier_hidden, wannier_out),
        )

    energy_short, charge_shift = lax.map(
        one_block,
        (
            centre_ids,
            neighbour_rows.reshape(blocks, block_size, slots),
            present.reshape(blocks, block_size, slots),
        ),
    )
    return (energy_short.reshape(atom_count), charge_shift.reshape(atom_count))


def green_table(first, second, third, size):

    def folded(index):
        return jnp.where(index < size // 2, index, index - size).astype(jnp.float32) * (
            2.0 * math.pi / size
        )

    kappa_x = folded(first)[:, None, None]
    kappa_y = folded(second)[None, :, None]
    kappa_z = folded(third)[None, None, :]
    squared = kappa_x * kappa_x + kappa_y * kappa_y + kappa_z * kappa_z
    root = (
        (first[:, None, None] == 0) & (second[None, :, None] == 0) & (third[None, None, :] == 0)
    ).astype(jnp.float32)
    return (1.0 - root) * jnp.exp(-0.5 * squared) / (squared + root)


def dft_tables(size):
    index = jnp.arange(size, dtype=jnp.int32)
    phase = (index[:, None] * index[None, :] % size).astype(jnp.float32) * (2.0 * math.pi / size)
    return (jnp.cos(phase), jnp.sin(phase))


def along(values, table, axis_index):
    result = jnp.tensordot(values, table, axes=([axis_index], [0]), precision=HIGH)
    return jnp.moveaxis(result, -1, axis_index)


def complex_transform(paired, axis_index, cosine, sine, inverse):
    real_part = paired[0]
    imag_part = paired[1]
    inner = axis_index - 1
    real_cos = along(real_part, cosine, inner)
    real_sin = along(real_part, sine, inner)
    imag_cos = along(imag_part, cosine, inner)
    imag_sin = along(imag_part, sine, inner)
    if inverse:
        return jnp.stack([real_cos - imag_sin, imag_cos + real_sin])
    return jnp.stack([real_cos + imag_sin, imag_cos - real_sin])


def fold_windows(values, axis_index, block, count):
    front = jnp.moveaxis(values, axis_index, 0)
    rest = front.shape[1:]
    windows = front.reshape((count, block + 3) + rest)
    main_part = windows[:, :block]
    carried = jnp.roll(windows[:, block:], 1, axis=0)
    main_part = main_part.at[:, :3].add(carried)
    return jnp.moveaxis(main_part.reshape((count * block,) + rest), 0, axis_index)


def make_windows(values, axis_index, block, count):
    front = jnp.moveaxis(values, axis_index, 0)
    rest = front.shape[1:]
    pieces = front.reshape((count, block) + rest)
    trailing = jnp.roll(pieces, -1, axis=0)[:, :3]
    windows = jnp.concatenate([pieces, trailing], axis=1)
    return jnp.moveaxis(windows.reshape((count * (block + 3),) + rest), 0, axis_index)


def spread_matrix(start, weights, width, wrap_size):
    offsets = jnp.arange(4, dtype=jnp.int32)[:, None, None]
    target = start[None, :, None] + offsets
    if wrap_size > 0:
        target = target % wrap_size
    hits = (target == jnp.arange(width, dtype=jnp.int32)[None, None, :]).astype(jnp.float32)
    return jnp.sum(weights[:, :, None] * hits, axis=0)


def per_device_general(
    positions,
    types,
    neighbours,
    neighbour_count,
    send_index,
    cell_x,
    cell_y,
    cell_z,
    spline_fraction,
    embed_first,
    embed_second,
    embed_third,
    energy_in,
    energy_hidden,
    energy_out,
    wannier_in,
    wannier_hidden,
    wannier_out,
    charge_base,
):
    atom_count = types.shape[1]
    ghost_rows = send_index.shape[1] // 2
    kind_float = types[0].astype(jnp.float32)
    own_atoms = jnp.concatenate([positions[:, 0], kind_float[None]], axis=0)
    outgoing = own_atoms[:, send_index[0]]
    padded_ghosts = with_halo(outgoing, (("brick", 1),), ghost_rows)
    extended = jnp.concatenate(
        [padded_ghosts[:, :ghost_rows], own_atoms, padded_ghosts[:, 3 * ghost_rows :]], axis=1
    )
    energy_short, charge_shift = atom_terms(
        extended,
        neighbours[0],
        neighbour_count[0],
        embed_first,
        embed_second,
        embed_third,
        energy_in,
        energy_hidden,
        energy_out,
        wannier_in,
        wannier_hidden,
        wannier_out,
    )
    charge = (1.0 - kind_float) * charge_base[0] + kind_float * charge_base[1] + charge_shift
    count_x = lax.axis_size("brick")
    count_y = lax.axis_size("slab")
    block_x = NG // count_x
    block_y = NG // count_y
    wide_x = block_x + 3
    wide_y = block_y + 3
    spread_x = spread_matrix(cell_x[0], spline_weights(spline_fraction[0, 0]), wide_x, 0)
    spread_y = spread_matrix(cell_y[0], spline_weights(spline_fraction[1, 0]), wide_y, 0)
    spread_z = spread_matrix(cell_z[0], spline_weights(spline_fraction[2, 0]), NG, NG)
    spread_xy = (spread_x[:, :, None] * spread_y[:, None, :]).reshape(atom_count, wide_x * wide_y)
    charge_grid = jnp.einsum(
        "ap,az->pz", spread_xy, charge[:, None] * spread_z, precision=HIGH
    ).reshape(wide_x, wide_y, NG)
    cosine, sine = dft_tables(NG)
    scale = 1.0 / (NG * NG * NG)
    full_index = jnp.arange(NG, dtype=jnp.int32)
    paired = jnp.stack([along(charge_grid, cosine, 2), -along(charge_grid, sine, 2)])
    moved = lax.all_to_all(paired, "slab", split_axis=3, concat_axis=2, tiled=True)
    moved = complex_transform(fold_windows(moved, 2, block_y, count_y), 2, cosine, sine, False)
    moved = lax.all_to_all(moved, "brick", split_axis=2, concat_axis=1, tiled=True)
    moved = complex_transform(fold_windows(moved, 1, block_x, count_x), 1, cosine, sine, False)
    part_y = NG // count_x
    part_z = NG // count_y
    index_y = lax.axis_index("brick") * part_y + jnp.arange(part_y, dtype=jnp.int32)
    index_z = lax.axis_index("slab") * part_z + jnp.arange(part_z, dtype=jnp.int32)
    moved = moved * (green_table(full_index, index_y, index_z, NG) * scale)[None]
    moved = make_windows(complex_transform(moved, 1, cosine, sine, True), 1, block_x, count_x)
    moved = lax.all_to_all(moved, "brick", split_axis=1, concat_axis=2, tiled=True)
    moved = make_windows(complex_transform(moved, 2, cosine, sine, True), 2, block_y, count_y)
    moved = lax.all_to_all(moved, "slab", split_axis=2, concat_axis=3, tiled=True)
    potential_wide = along(moved[0], cosine, 2) - along(moved[1], sine, 2)
    sampled = jnp.einsum(
        "ap,pz->az", spread_xy, potential_wide.reshape(wide_x * wide_y, NG), precision=HIGH
    )
    potential_at = jnp.sum(sampled * spread_z, axis=1)
    atom_energy = energy_short + 0.5 * charge * potential_at
    return (atom_energy[None, :], potential_wide[:block_x, :block_y])


def split(values):
    high = values.astype(jnp.bfloat16)
    low = (values - high.astype(jnp.float32)).astype(jnp.bfloat16)
    return high, low


def multiply(left, right, dims):
    return lax.dot_general(left, right, (dims, ((), ())), preferred_element_type=jnp.float32)


def triple(left, right, dims=((1,), (0,))):
    (left_axis,), (right_axis,) = dims
    if left[0].shape[left_axis] % 128 == 0:
        return multiply(
            jnp.concatenate([left[0], left[0], left[1]], axis=left_axis),
            jnp.concatenate([right[0], right[1], right[0]], axis=right_axis),
            dims,
        )
    return (
        multiply(left[0], right[0], dims)
        + multiply(left[0], right[1], dims)
        + multiply(left[1], right[0], dims)
    )


LANES = ((1,), (1,))


def product(left, right, dims=((1,), (0,))):
    return lax.dot_general(
        left,
        right,
        (dims, ((), ())),
        precision=lax.Precision.HIGH,
        preferred_element_type=jnp.float32,
    )


def lane_pick(table, index):
    return jnp.take_along_axis(table, index, axis=1, mode="promise_in_bounds")


def whole(shape):
    return pl.BlockSpec(tuple(shape), lambda step: (0,) * len(shape))


def whole_specs(*arrays):
    return [whole(array.shape) for array in arrays]


def collect_kernel(
    positions_ref, types_ref, count_ref, send_ref, own_ref, outgoing_ref
):
    atoms = types_ref.shape[1]
    own_ref[...] = jnp.zeros_like(own_ref)
    for axis in range(3):
        own_ref[axis : axis + 1, 0:atoms] = positions_ref[axis]
    own_ref[3:4, 0:atoms] = types_ref[...].astype(jnp.float32)
    own_ref[4:5, 0:atoms] = count_ref[...].astype(jnp.float32)
    own_ref[5:6, 0:atoms] = send_ref[...].astype(jnp.float32)
    for chunk in range(2):
        lanes = slice(128 * chunk, 128 * chunk + 128)
        wanted = jnp.broadcast_to(own_ref[5:6, lanes], (8, 128)).astype(jnp.int32)
        within = wanted & 127
        outgoing_ref[:, lanes] = jnp.where(
            wanted < 128,
            lane_pick(own_ref[:, 0:128], within),
            lane_pick(own_ref[:, 128:256], within),
        )


def collect(positions, types, counts, send_index):
    arrays = (positions, types, counts, send_index)
    result = jax.ShapeDtypeStruct((8, 256), jnp.float32)
    return pl.pallas_call(
        collect_kernel,
        grid=(1,),
        out_shape=[result, result],
        in_specs=whole_specs(*arrays),
        out_specs=whole_specs(result, result),
        compiler_params=pltpu.CompilerParams(vmem_limit_bytes=VMEM_BYTES),
        name="collect_atoms",
    )(*arrays)


def fitting_rows(descriptor_ref, weight_in_ref, weight_hidden_ref, weight_out_ref):
    hidden = jnp.tanh(product(descriptor_ref[...], weight_in_ref[...], LANES))
    for layer in range(weight_hidden_ref.shape[0]):
        hidden = jnp.tanh(product(hidden, weight_hidden_ref[layer])) + hidden
    width = hidden.shape[1]
    return product(jnp.broadcast_to(weight_out_ref[...], (8, width)), hidden, LANES)


def natural_order(rows):
    atoms = rows.shape[1]
    padded = jnp.concatenate([rows, jnp.zeros((8, 256 - atoms), jnp.float32)], axis=1)
    pieces = []
    for chunk in range(2):
        atom = 128 * chunk + lax.broadcasted_iota(jnp.int32, (8, 128), 1)
        late = atom >= atoms // 2
        within = jnp.where(late, atom - atoms // 2, atom)
        place = 8 * (within >> 2) + (within & 3) + jnp.where(late, 4, 0)
        place = jnp.minimum(place, 255)
        pieces.append(
            jnp.where(
                place < 128,
                lane_pick(padded[:, 0:128], place & 127),
                lane_pick(padded[:, 128:256], place & 127),
            )
        )
    return jnp.concatenate(pieces, axis=1)[0:1, 0:atoms]


def network_kernel(
    ghosts,
    base_ref,
    charges_ref,
    own_ref,
    lower_ref,
    upper_ref,
    slots_ref,
    types_ref,
    cell_x_ref,
    cell_y_ref,
    cell_z_ref,
    fraction_ref,
    first_ref,
    second_ref,
    third_ref,
    spot_ref,
    weight_in_hbm,
    weight_hidden_hbm,
    weight_out_ref,
    descriptor_hbm,
    charge_ref,
    copies_ref,
    descriptor_ref,
    environment_ref,
    kind_ref,
    moments_ref,
    padded_ref,
    weight_in_ref,
    weight_hidden_ref,
    row_ref,
    semaphores,
):
    fetches = [
        pltpu.make_async_copy(weight_in_hbm, weight_in_ref, semaphores.at[0]),
        pltpu.make_async_copy(weight_hidden_hbm, weight_hidden_ref, semaphores.at[1]),
    ]
    for fetch in fetches:
        fetch.start()
    slots, atoms = slots_ref.shape
    rows = atoms // 2
    lane = lax.broadcasted_iota(jnp.int32, (8, 128), 1)
    sub = lax.broadcasted_iota(jnp.int32, (8, 128), 0)

    width = first_ref.shape[1]
    padded_ref[...] = jnp.zeros_like(padded_ref)
    padded_ref[0, 0:2, 0:width] = first_ref[...]
    for column in range(2):
        padded_ref[1, 0:width, 32 * column : 32 * column + width] = second_ref[
            :, width * column : width * (column + 1)
        ]
    for row in range(2):
        for column in range(4):
            padded_ref[2, 32 * row : 32 * row + width, 32 * column : 32 * column + width] = (
                third_ref[
                    width * row : width * (row + 1), width * column : width * (column + 1)
                ]
            )
    first_table = padded_ref[0].T
    embed_zero = jnp.broadcast_to(first_table[0:32, 0:1], (32, 128))
    embed_one = jnp.broadcast_to(first_table[0:32, 1:2], (32, 128))
    second_high, second_low = split(padded_ref[1].T[0:64, 0:32])
    second_weight = jnp.concatenate([second_high, second_high, second_low], axis=1)
    third_high, third_low = split(padded_ref[2].T[:, 0:64])
    third_weight = jnp.concatenate([third_high, third_high, third_low], axis=1)

    def spread(ref, field, chunk):
        return jnp.broadcast_to(ref[field : field + 1, 128 * chunk : 128 * chunk + 128], (8, 128))

    own = [[spread(own_ref, field, chunk) for chunk in range(2)] for field in range(5)]
    lower = [[spread(lower_ref, field, chunk) for chunk in range(2)] for field in range(4)]
    upper = [spread(upper_ref, field, 0) for field in range(4)]

    def pick_two(tables, index):
        within = index & 127
        return jnp.where(index < 128, lane_pick(tables[0], within), lane_pick(tables[1], within))

    pairs = jnp.concatenate([slots_ref[:, 0:rows], slots_ref[:, rows:atoms]], axis=0).T
    for tile in range(rows // 8):
        band = slice(8 * tile, 8 * tile + 8)
        index = pairs[band, :]
        centre = 8 * tile + sub + jnp.where(lane < 64, 0, rows)
        from_own = jnp.clip(index - ghosts, 0, atoms - 1)
        from_lower = jnp.minimum(index + (atoms - ghosts), 255)
        from_upper = jnp.clip(index - (ghosts + atoms), 0, 127)

        def neighbour(field):
            below = pick_two(lower[field], from_lower)
            inside = pick_two(own[field], from_own)
            above = lane_pick(upper[field], from_upper)
            return jnp.where(
                index < ghosts, below, jnp.where(index < ghosts + atoms, inside, above)
            )

        offsets = [neighbour(field) - pick_two(own[field], centre) for field in range(3)]
        live = pick_two(own[4], centre)
        present = jnp.where((lane & 63).astype(jnp.float32) < live, 1.0, 0.0)
        smooth = present / (
            1.0 + (offsets[0] * offsets[0] + offsets[1] * offsets[1] + offsets[2] * offsets[2])
        )
        environment_ref[0, band, :] = smooth
        for field in range(3):
            environment_ref[1 + field, band, :] = smooth * offsets[field]
        kind_ref[band, :] = neighbour(3)

    group = 8

    def stacked(values):
        high, low = split(values)
        return jnp.concatenate([high, low, high], axis=0)

    def one_group(start):
        pieces = []
        for row in range(group):
            smooth = jnp.broadcast_to(environment_ref[0, pl.ds(start + row, 1), :], (32, 128))
            kind = jnp.broadcast_to(kind_ref[pl.ds(start + row, 1), :], (32, 128))
            pieces.append(
                jnp.tanh(smooth * ((1.0 - kind) * embed_zero + kind * embed_one))
            )
        first = jnp.concatenate(pieces, axis=1)
        second = jnp.tanh(multiply(second_weight, stacked(first), ((1,), (0,))))
        second = second + jnp.concatenate([first, first], axis=0)
        third = jnp.tanh(multiply(third_weight, stacked(second), ((1,), (0,))))
        third = third + jnp.concatenate([second, second], axis=0)
        third_pair = split(third)
        for half in range(group // 4):
            columns = slice(512 * half, 512 * half + 512)
            bands = []
            for part in range(4):
                bands.append(
                    jnp.concatenate(
                        [
                            jnp.where(
                                sub == row + jnp.where(lane < 64, 0, 4),
                                jnp.broadcast_to(
                                    environment_ref[part, pl.ds(start + 4 * half + row, 1), :],
                                    (8, 128),
                                ),
                                0.0,
                            )
                            for row in range(4)
                        ],
                        axis=1,
                    )
                )
            environment = split(jnp.concatenate(bands, axis=0))
            both = multiply(
                jnp.concatenate(environment, axis=0), third_pair[0][:, columns], LANES
            )
            sums = both[0:32] + both[32:64]
            sums = sums + multiply(environment[0], third_pair[1][:, columns], LANES)
            sums = sums * (1.0 / slots)
            for part in range(4):
                moments_ref[part, pl.ds(2 * start + 8 * half, 8), :] = sums[
                    8 * part : 8 * part + 8
                ]

    chunks = (descriptor_ref.shape[1] + 127) // 128
    last = descriptor_ref.shape[1] - 128 * (chunks - 1)

    def describe_band(start):
        band = pl.ds(start, 8)
        moments = [moments_ref[part, band, :] for part in range(4)]
        axis_part = [lane_pick(moments[part], lane & 15) for part in range(4)]
        for chunk in range(chunks):
            spot = jnp.broadcast_to(spot_ref[chunk : chunk + 1, :], (8, 128))
            total = lane_pick(moments[0], spot) * axis_part[0]
            for part in range(1, 4):
                total = total + lane_pick(moments[part], spot) * axis_part[part]
            if chunk < chunks - 1:
                descriptor_ref[band, 128 * chunk : 128 * chunk + 128] = total
            else:
                descriptor_ref[band, 128 * chunk : 128 * chunk + last] = total[:, 0:last]

    for start in range(0, rows + group, group):
        if start < rows:
            one_group(start)
        if start > 0:
            for band in range(2 * (start - group), 2 * start, 8):
                describe_band(band)

    store = pltpu.make_async_copy(descriptor_ref, descriptor_hbm, semaphores.at[2])
    store.start()
    for fetch in fetches:
        fetch.wait()
    shift = fitting_rows(descriptor_ref, weight_in_ref, weight_hidden_ref, weight_out_ref)
    kind = types_ref[...].astype(jnp.float32)
    charge = (1.0 - kind) * charges_ref[0] + kind * charges_ref[1] + natural_order(shift)
    charge_ref[...] = charge
    fields = [
        cell_x_ref[...].astype(jnp.float32),
        (cell_y_ref[...] + base_ref[0]).astype(jnp.float32),
        cell_z_ref[...].astype(jnp.float32),
    ]
    fields = fields + [fraction_ref[axis] for axis in range(3)] + [charge]
    for place, field in enumerate(fields):
        row_ref[:, atoms * place : atoms * (place + 1)] = field
    for copy in range(copies_ref.shape[0]):
        copies_ref[copy] = row_ref[...]
    store.wait()


def spot_table(embed, desc):
    column = np.arange(desc) // AXIS
    quarter = embed // 4
    place = 32 * (column // quarter) + column % quarter
    chunks = (desc + 127) // 128
    table = np.zeros((chunks * 128,), np.int32)
    table[:desc] = place
    padded = np.zeros(((chunks + 7) // 8 * 8, 128), np.int32)
    padded[:chunks] = table.reshape(chunks, 128)
    return padded


def networks(
    copies,
    ghosts,
    base,
    charge_base,
    own,
    lower,
    upper,
    neighbours,
    types,
    cells,
    fraction,
    embed,
    weight_in,
    weight_hidden,
    weight_out,
):
    atoms = types.shape[1]
    desc, width = weight_in.shape
    spots = jnp.asarray(spot_table(embed[2].shape[1], desc))
    anywhere = pl.BlockSpec(memory_space=pl.ANY)
    scalars = pl.BlockSpec(memory_space=pltpu.SMEM)
    blocks = (own, lower, upper, neighbours[0].T, types, *cells, fraction, *embed, spots)
    weight_out = weight_out.reshape(1, -1)
    results = [
        jax.ShapeDtypeStruct((atoms, desc), jnp.float32),
        jax.ShapeDtypeStruct((1, atoms), jnp.float32),
        jax.ShapeDtypeStruct((copies, 1, FIELDS * atoms), jnp.float32),
    ]
    return pl.pallas_call(
        functools.partial(network_kernel, ghosts),
        grid=(1,),
        out_shape=results,
        in_specs=[scalars, scalars]
        + whole_specs(*blocks)
        + [anywhere, anywhere]
        + whole_specs(weight_out),
        out_specs=[anywhere] + whole_specs(*results[1:]),
        scratch_shapes=[
            pltpu.VMEM((atoms, desc), jnp.float32),
            pltpu.VMEM((4, atoms // 2, 128), jnp.float32),
            pltpu.VMEM((atoms // 2, 128), jnp.float32),
            pltpu.VMEM((4, atoms, 128), jnp.float32),
            pltpu.VMEM((3, 128, 128), jnp.float32),
            pltpu.VMEM((width, desc), jnp.float32),
            pltpu.VMEM(weight_hidden.shape, jnp.float32),
            pltpu.VMEM((1, FIELDS * atoms), jnp.float32),
            pltpu.SemaphoreType.DMA((3,)),
        ],
        compiler_params=pltpu.CompilerParams(vmem_limit_bytes=VMEM_BYTES),
        name="networks",
    )(base, charge_base, *blocks, weight_in.T, weight_hidden, weight_out)


def energy_kernel(descriptor_ref, weight_in_ref, weight_hidden_ref, weight_out_ref, energy_ref):
    energy_ref[...] = natural_order(
        fitting_rows(descriptor_ref, weight_in_ref, weight_hidden_ref, weight_out_ref)
    )


def energies(descriptor, weight_in, weight_hidden, weight_out):
    atoms, desc = descriptor.shape
    width = weight_in.shape[1]
    arrays = (descriptor, weight_in.T, weight_hidden, weight_out.reshape(1, -1))
    result = jax.ShapeDtypeStruct((1, atoms), jnp.float32)
    return pl.pallas_call(
        energy_kernel,
        grid=(1,),
        out_shape=result,
        in_specs=whole_specs(*arrays),
        out_specs=whole(result.shape),
        compiler_params=pltpu.CompilerParams(vmem_limit_bytes=VMEM_BYTES),
        cost_estimate=pl.CostEstimate(
            flops=6 * atoms * desc * width, bytes_accessed=4 * desc * width, transcendentals=0
        ),
        name="energies",
    )(*arrays)


def weight_rows(fraction):
    square = fraction * fraction
    cubed = square * fraction
    rest = 1.0 - fraction
    return [
        rest * rest * rest / 6.0,
        (3.0 * cubed - 6.0 * square + 4.0) / 6.0,
        (-3.0 * cubed + 3.0 * square + 3.0 * fraction + 1.0) / 6.0,
        cubed / 6.0,
    ]


def placed_weights(distance, weights):
    shape = distance.shape
    result = jnp.zeros(shape, jnp.float32)
    for step in range(4):
        result = jnp.where(
            distance == step, jnp.broadcast_to(weights[step], shape), result
        )
    return result


def third_factors(fields, waves_ref, cosine_ref):
    atoms = fields.shape[1]
    start = fields[2:3, :].astype(jnp.int32)
    along = weight_rows(fields[5:6, :])
    parts = waves_ref.shape[0]
    cosine = jnp.broadcast_to(cosine_ref[...], (parts, 128))
    wave = jnp.broadcast_to(waves_ref[:, 0:1], (parts, 128))
    shift = jnp.broadcast_to(waves_ref[:, 1:2], (parts, 128))
    pieces = []
    for chunk in range(atoms // 128):
        lanes = slice(128 * chunk, 128 * chunk + 128)
        total = jnp.zeros((parts, 128), jnp.float32)
        for step in range(4):
            place = jnp.broadcast_to(start[:, lanes] + step, (parts, 128))
            phase = (wave * place + shift) & (NG - 1)
            value = lane_pick(cosine, phase & 127)
            value = jnp.where(phase < 128, value, -value)
            total = total + value * jnp.broadcast_to(along[step][:, lanes], (parts, 128))
        pieces.append(total)
    return jnp.concatenate(pieces, axis=1)


def first_third_split(fields, waves_ref, cosine_ref, window, scale, high_ref, low_ref):
    atoms = fields.shape[1]
    third = third_factors(fields, waves_ref, cosine_ref) * scale
    rows = lax.broadcasted_iota(jnp.int32, (window, atoms), 0)
    first = placed_weights(
        rows - fields[0:1, :].astype(jnp.int32), weight_rows(fields[3:4, :])
    )
    for chunk in range(atoms // 128):
        lanes = slice(128 * chunk, 128 * (chunk + 1))
        for part in range(0, third.shape[0], 2):
            high, low = split(
                jnp.concatenate(
                    [first[:, lanes] * third[part + side : part + side + 1, lanes] for side in range(2)],
                    axis=0,
                )
            )
            place = slice(part * window, (part + 2) * window)
            high_ref[place, lanes] = high
            low_ref[place, lanes] = low
    return high_ref[...], low_ref[...]


def second_factors(fields, base, block_y, slabs, high_ref, low_ref):
    atoms = fields.shape[1]
    block = atoms // slabs
    reach = block_y + REACH
    start = fields[1:2, :].astype(jnp.int32) - base
    weights = weight_rows(fields[4:5, :])
    for chunk in range(atoms // 128):
        lanes = slice(128 * chunk, 128 * (chunk + 1))
        first = 128 * chunk // block
        last = (128 * chunk + 127) // block
        top = first * block_y
        rows = (last - first) * block_y + reach
        pieces = [(top, min(rows, NG - top))]
        if top + rows > NG:
            pieces.append((0, top + rows - NG))
        for row, count in pieces:
            index = row + lax.broadcasted_iota(jnp.int32, (count, 128), 0)
            table = split(
                placed_weights(
                    (index - start[:, lanes]) & (NG - 1), [weight[:, lanes] for weight in weights]
                )
            )
            high_ref[row : row + count, lanes] = table[0]
            low_ref[row : row + count, lanes] = table[1]
    return high_ref[...], low_ref[...]


def wave_of(index):
    return jnp.where(index <= NG // 2, index, index - NG // 2)


def damping(index):
    kappa = wave_of(index).astype(jnp.float32) * (2.0 * math.pi / NG)
    squared = kappa * kappa
    ends = (index == 0) | (index == NG // 2)
    return squared, jnp.exp(-0.5 * squared) * jnp.where(ends, 1.0 / NG, 2.0 / NG)


def transform(planes, kappa_ref, first_part, tables_ref, last_ref):
    count = len(planes)
    basis = tables_ref[0]
    turned = tables_ref[1]
    square_x, damp_x = damping(lax.broadcasted_iota(jnp.int32, (NG, 1), 0))
    square_y, damp_y = damping(lax.broadcasted_iota(jnp.int32, (1, NG), 1))
    square_xy = square_x + square_y
    damp_xy = damp_x * damp_y
    columns = [slice(NG * part, NG * (part + 1)) for part in range(count)]
    first = product(basis, jnp.concatenate(planes, axis=1))
    first = jnp.concatenate([first[:, column] for column in columns], axis=0)
    both = product(first, turned)
    scaled = []
    for part in range(count):
        squared = square_xy + kappa_ref[first_part + part, 0]
        root = jnp.where(squared == 0.0, 1.0, 0.0)
        green = (1.0 - root) * (damp_xy * kappa_ref[first_part + part, 1]) / (squared + root)
        scaled.append(both[columns[part]] * green)
    back = product(turned, jnp.concatenate(scaled, axis=1))
    back = jnp.concatenate([back[:, column] for column in columns], axis=0)
    return product(back, last_ref[...])


def send_blocks(full, block_x, block_y, put):
    low_lanes = lax.broadcasted_iota(jnp.int32, (NG, 128), 1) < block_y
    for pair in range(full.shape[0] // (2 * NG)):
        even = full[2 * NG * pair : 2 * NG * pair + NG, 0:128]
        odd = full[2 * NG * pair + NG : 2 * NG * (pair + 1), 0:128]
        blocks = [
            jnp.where(low_lanes, even, pltpu.roll(odd, block_y, 1)),
            jnp.where(low_lanes, pltpu.roll(even, block_y, 1), odd),
        ]
        for brick in range(NG // block_x):
            for side in range(2):
                for group in range(block_x // 8):
                    start = block_x * brick + 8 * group
                    put(pair, brick, side, group, blocks[side][start : start + 8])


def spread_kernel(
    block_x,
    block_y,
    window,
    kappa_ref,
    pair_ref,
    static_ref,
    waves_ref,
    cosine_ref,
    tables_hbm,
    last_hbm,
    short_hbm,
    sent_ref,
    full_ref,
    atoms_ref,
    later_hbm,
    grid_ref,
    tables_ref,
    last_ref,
    semaphores,
    *pair_refs,
):
    slabs = NG // block_y
    second_refs, first_refs = pair_refs[:4], pair_refs[4:]
    bricks = NG // block_x
    parts = waves_ref.shape[0]
    block = static_ref.shape[2] // FIELDS
    count = full_ref.shape[0]
    step = pl.program_id(0)
    later = later_hbm.shape[0]
    store = pltpu.make_async_copy(
        grid_ref.at[pl.ds(parts - later, later), pl.ds(0, NG)], later_hbm, semaphores.at[2]
    )

    @pl.when(step == 0)
    def _():
        fetches = [
            pltpu.make_async_copy(tables_hbm, tables_ref, semaphores.at[0]),
            pltpu.make_async_copy(last_hbm.at[pair_ref[0]], last_ref, semaphores.at[1]),
        ]
        for fetch in fetches:
            fetch.start()
        for slab in range(slabs):
            lanes = slice(block * slab, block * (slab + 1))
            for brick in range(bricks):
                for field in range(FIELDS):
                    atoms_ref[brick, field : field + 1, lanes] = static_ref[
                        slab * bricks + brick, :, block * field : block * (field + 1)
                    ]
        for ref in second_refs:
            ref[...] = jnp.zeros_like(ref)
        for brick in range(bricks):
            fields = atoms_ref[brick]
            table = first_third_split(
                fields,
                waves_ref,
                cosine_ref,
                window,
                fields[6:7, :],
                first_refs[2 * (brick % 2)],
                first_refs[2 * (brick % 2) + 1],
            )
            second = second_factors(
                fields, 0, block_y, slabs, second_refs[2 * (brick % 2)], second_refs[2 * (brick % 2) + 1]
            )
            spread = triple(table, second, LANES)
            start = block_x * brick
            extra = window - block_x
            for part in range(parts):
                shared = spread[part * window : part * window + extra]
                if brick > 0:
                    shared = shared + grid_ref[part, start : start + extra, :]
                grid_ref[part, start : start + extra, :] = shared
                grid_ref[part, start + extra : start + window, :] = spread[
                    part * window + extra : part * window + window
                ]
        for part in range(parts):
            grid_ref[part, 0:extra, :] += grid_ref[part, NG : NG + extra, :]
        store.start()
        for fetch in fetches:
            fetch.wait()

    planes = [grid_ref[count * step + part, 0:NG, :] for part in range(count)]
    full = transform(planes, kappa_ref, count * step, tables_ref, last_ref)
    for part in range(count):
        full_ref[part] = full[NG * part : NG * (part + 1)]

    def put(pair, brick, side, group, tile):
        sent_ref[2 * brick + side, group, pair] = tile

    send_blocks(full, block_x, block_y, put)

    @pl.when(step == pl.num_programs(0) - 1)
    def _():
        store.wait()


def early_pairs(parts):
    return parts // 4


def spread_and_solve(
    block_x, block_y, window, kappa, pair, static, waves, cosine_row, tables, last, short
):
    atoms = static.shape[2] // FIELDS
    slabs = NG // block_y
    bricks = NG // block_x
    parts = waves.shape[0]
    pairs = early_pairs(parts)
    count = 4
    anywhere = pl.BlockSpec(memory_space=pl.ANY)
    scalars = pl.BlockSpec(memory_space=pltpu.SMEM)
    sent_block = (2 * bricks, block_x // 8, count // 2, 8, 128)
    return pl.pallas_call(
        functools.partial(spread_kernel, block_x, block_y, window),
        grid=(2 * pairs // count,),
        out_shape=[
            jax.ShapeDtypeStruct((2 * bricks, block_x // 8, pairs, 8, 128), jnp.float32),
            jax.ShapeDtypeStruct((2 * pairs, NG, NG), jnp.float32),
            jax.ShapeDtypeStruct((bricks, 8, slabs * atoms), jnp.float32),
            jax.ShapeDtypeStruct((parts - 2 * pairs, NG, NG), jnp.float32),
        ],
        in_specs=[scalars, scalars]
        + whole_specs(static, waves, cosine_row)
        + [anywhere, anywhere, anywhere],
        out_specs=[
            pl.BlockSpec(sent_block, lambda step: (0, 0, step, 0, 0)),
            pl.BlockSpec((count, NG, NG), lambda step: (step, 0, 0)),
            whole((bricks, 8, slabs * atoms)),
            anywhere,
        ],
        scratch_shapes=[
            pltpu.VMEM((parts, NG + window - block_x, NG), jnp.float32),
            pltpu.VMEM(tables.shape, tables.dtype),
            pltpu.VMEM(last.shape[1:], last.dtype),
            pltpu.SemaphoreType.DMA((3,)),
        ]
        + [pltpu.VMEM((NG, slabs * atoms), jnp.bfloat16)] * 4
        + [pltpu.VMEM((parts * window, slabs * atoms), jnp.bfloat16)] * 4,
        compiler_params=pltpu.CompilerParams(vmem_limit_bytes=VMEM_BYTES),
        name="spread_and_solve",
    )(kappa, pair, static, waves, cosine_row, tables, last, short)


def sample_kernel(
    block_x,
    block_y,
    window,
    kappa_ref,
    pair_ref,
    atoms_ref,
    waves_ref,
    cosine_ref,
    tables_hbm,
    last_hbm,
    later_hbm,
    early_hbm,
    sent_ref,
    later_ref,
    full_ref,
    tables_ref,
    last_ref,
    semaphores,
    packed_ref,
):
    bricks = atoms_ref.shape[0]
    parts = waves_ref.shape[0]
    early = 2 * early_pairs(parts)
    block = atoms_ref.shape[2] * block_y // NG
    fetches = [
        pltpu.make_async_copy(tables_hbm, tables_ref, semaphores.at[0]),
        pltpu.make_async_copy(last_hbm.at[pair_ref[0]], last_ref, semaphores.at[1]),
        pltpu.make_async_copy(later_hbm, later_ref, semaphores.at[2]),
        pltpu.make_async_copy(early_hbm, full_ref.at[pl.ds(0, early)], semaphores.at[3]),
    ]
    for fetch in fetches:
        fetch.start()
    for fetch in fetches[:3]:
        fetch.wait()
    pairs = (parts - early) // 2
    planes = [later_ref[part] for part in range(parts - early)]
    full = transform(planes, kappa_ref, early, tables_ref, last_ref)
    for part in range(parts - early):
        full_ref[early + part] = full[NG * part : NG * (part + 1)]

    def put(pair, brick, side, group, tile):
        sent_ref[2 * brick + side, pairs * group + pair] = tile

    send_blocks(full, block_x, block_y, put)
    fetches[3].wait()

    reach = block_y + REACH
    lane = lax.broadcasted_iota(jnp.int32, (NG, 128), 1)
    for part in range(parts):
        for side in range(2):
            values = full_ref[part, :, 128 * side : 128 * (side + 1)]
            high = values.astype(jnp.bfloat16).astype(jnp.float32)
            again = pltpu.roll(high, reach, 1)
            low = pltpu.roll(values - high, 2 * reach - 128, 1)
            packed_ref[side, part, 0:NG, 0:128] = jnp.where(lane < reach, high, again)
            packed_ref[side, part, 0:NG, 128:NG] = jnp.where(
                lane < 2 * reach - 128, again, jnp.where(lane < 3 * reach - 128, low, 0.0)
            )
            packed_ref[side, part, NG : NG + window - block_x, :] = packed_ref[
                side, part, 0 : window - block_x, :
            ]
    extra = sent_ref.shape[1] - 1
    base = 2 * block_y * pair_ref[0]
    lanes = pl.ds(pl.multiple_of(2 * block * pair_ref[0], 128), 2 * block)
    for brick in range(bricks):
        fields = atoms_ref[brick, :, lanes]
        thirds = third_factors(fields, waves_ref, cosine_ref)
        rows = slice(block_x * brick, block_x * brick + window)
        for side in range(2):
            here = slice(block * side, block * (side + 1))
            third = thirds[:, here]
            ours = fields[:, here]
            index = lax.broadcasted_iota(jnp.int32, (window, block), 0)
            first = placed_weights(
                index - ours[0:1, :].astype(jnp.int32), weight_rows(ours[3:4, :])
            )
            index = lax.broadcasted_iota(jnp.int32, (reach, block), 0)
            start = ours[1:2, :].astype(jnp.int32) - (base + block_y * side)
            high, low = split(placed_weights(index - start, weight_rows(ours[4:5, :])))
            rest = jnp.zeros((NG - 3 * reach, block), jnp.bfloat16)
            second = jnp.concatenate([high, low, high, rest], axis=0)
            values = jnp.concatenate(
                [packed_ref[side, part, rows, :] for part in range(parts)], axis=0
            )
            along = multiply(values.astype(jnp.bfloat16), second, ((1,), (0,)))
            total = jnp.zeros((window, block), jnp.float32)
            for part in range(parts):
                total = total + along[window * part : window * (part + 1)] * third[part : part + 1]
            row = jnp.sum(total * first, axis=0, keepdims=True)
            sent_ref[2 * brick + side, extra] = jnp.zeros((8, 128), jnp.float32)
            sent_ref[2 * brick + side, extra, 0:1, :] = row[:, 0:128]
            sent_ref[2 * brick + side, extra, 1:2, 0 : block - 128] = row[:, 128:block]


def solve_and_sample(
    block_x, block_y, window, kappa, pair, atoms, waves, cosine_row, tables, last, later, early
):
    bricks = atoms.shape[0]
    parts = waves.shape[0]
    pairs = parts // 2 - early_pairs(parts)
    anywhere = pl.BlockSpec(memory_space=pl.ANY)
    scalars = pl.BlockSpec(memory_space=pltpu.SMEM)
    result = jax.ShapeDtypeStruct((2 * bricks, block_x // 8 * pairs + 1, 8, 128), jnp.float32)
    return pl.pallas_call(
        functools.partial(sample_kernel, block_x, block_y, window),
        grid=(1,),
        out_shape=result,
        in_specs=[scalars, scalars] + whole_specs(atoms, waves, cosine_row) + [anywhere] * 4,
        out_specs=whole(result.shape),
        scratch_shapes=[
            pltpu.VMEM((2 * pairs, NG, NG), jnp.float32),
            pltpu.VMEM((parts, NG, NG), jnp.float32),
            pltpu.VMEM(tables.shape, tables.dtype),
            pltpu.VMEM(last.shape[1:], last.dtype),
            pltpu.SemaphoreType.DMA((4,)),
        ]
        + [pltpu.VMEM((2, parts, NG + window - block_x, NG), jnp.float32)],
        compiler_params=pltpu.CompilerParams(vmem_limit_bytes=VMEM_BYTES),
        cost_estimate=pl.CostEstimate(
            flops=24 * parts * NG * NG * NG, bytes_accessed=4 * early.size, transcendentals=0
        ),
        name="solve_and_sample",
    )(kappa, pair, atoms, waves, cosine_row, tables, last, later, early)


def finish_kernel(
    block_y,
    early_ref,
    later_ref,
    sums_ref,
    short_hbm,
    charge_hbm,
    table_ref,
    out_ref,
    energy_ref,
    short_ref,
    charge_ref,
    semaphores,
):
    atoms = short_ref.shape[1]
    fetches = [
        pltpu.make_async_copy(short_hbm, short_ref, semaphores.at[0]),
        pltpu.make_async_copy(charge_hbm, charge_ref, semaphores.at[1]),
    ]

    @pl.when(pl.program_id(0) == 0)
    def _():
        for fetch in fetches:
            fetch.start()

    lines = early_ref.shape[3]
    sources, _, pairs = early_ref.shape[:3]
    early = early_ref.reshape(sources * pairs, lines, 128)
    later = later_ref.reshape(sources * later_ref.shape[1], lines, 128)
    pieces = []
    for line in range(lines):
        turned = jnp.concatenate([early[:, line, :], later[:, line, :]], axis=0).T
        pieces.append(jnp.concatenate([turned[0:block_y], turned[block_y:]], axis=1))
    result = product(jnp.concatenate(pieces, axis=0), table_ref[...])
    for line in range(lines):
        out_ref[line] = result[block_y * line : block_y * (line + 1)]

    @pl.when(pl.program_id(0) == 0)
    def _():
        for fetch in fetches:
            fetch.wait()
        total = jnp.sum(sums_ref[:, 0], axis=0)
        potential_at = jnp.concatenate([total[0:1, :], total[1:2, 0 : atoms - 128]], axis=1)
        energy_ref[...] = short_ref[...] + 0.5 * charge_ref[...] * potential_at


def finish(block_x, block_y, early, later, short, charge, table):
    bricks2, groups, pairs = early.shape[:3]
    rest = (later.shape[1] - 1) // groups
    atoms = short.shape[1]
    return pl.pallas_call(
        functools.partial(finish_kernel, block_y),
        grid=(groups,),
        out_shape=[
            jax.ShapeDtypeStruct((block_x, block_y, NG), jnp.float32),
            jax.ShapeDtypeStruct((1, atoms), jnp.float32),
        ],
        in_specs=[
            pl.BlockSpec((bricks2, 1, pairs, 8, 128), lambda index: (0, index, 0, 0, 0)),
            pl.BlockSpec((bricks2, rest, 8, 128), lambda index: (0, index, 0, 0)),
            pl.BlockSpec((bricks2, 1, 8, 128), lambda index: (0, groups * rest, 0, 0)),
            pl.BlockSpec(memory_space=pltpu.HBM),
            pl.BlockSpec(memory_space=pltpu.HBM),
            whole(table.shape),
        ],
        out_specs=[
            pl.BlockSpec((8, block_y, NG), lambda index: (index, 0, 0)),
            whole((1, atoms)),
        ],
        scratch_shapes=[
            pltpu.VMEM((1, atoms), jnp.float32),
            pltpu.VMEM((1, atoms), jnp.float32),
            pltpu.SemaphoreType.DMA((2,)),
        ],
        compiler_params=pltpu.CompilerParams(vmem_limit_bytes=32 * 2**20),
        name="finish",
    )(early, later, later, short, charge, table)


def real_basis():
    index = np.arange(NG)
    wave = np.where(index <= NG // 2, index, index - NG // 2)
    angle = (wave[:, None] * index[None, :] % NG) * (2.0 * math.pi / NG)
    return np.where((index <= NG // 2)[:, None], np.cos(angle), np.sin(angle))


def per_device(
    positions,
    types,
    neighbours,
    neighbour_count,
    send_index,
    cell_x,
    cell_y,
    cell_z,
    spline_fraction,
    embed_first,
    embed_second,
    embed_third,
    energy_in,
    energy_hidden,
    energy_out,
    wannier_in,
    wannier_hidden,
    wannier_out,
    charge_base,
):
    atoms = types.shape[1]
    ghosts = send_index.shape[1] // 2
    count_x = lax.axis_size("brick")
    count_y = lax.axis_size("slab")
    block_x = NG // count_x
    block_y = NG // count_y
    window = block_x + 8
    parts = NG // (2 * count_x)
    brick = lax.axis_index("brick")
    slab = lax.axis_index("slab")
    pair = (slab // 2).astype(jnp.int32).reshape(1)
    halves = [
        [b * count_y + 2 * p + side for b in range(count_x) for side in range(2)]
        for p in range(count_y // 2)
    ]

    def exchange(values, axes, groups=None):
        return lax.all_to_all(
            values, axes, split_axis=0, concat_axis=0, tiled=True, axis_index_groups=groups
        )

    own, outgoing = collect(positions, types, neighbour_count, send_index)
    up = [(i, (i + 1) % count_x) for i in range(count_x)]
    down = [((i + 1) % count_x, i) for i in range(count_x)]
    lower = lax.ppermute(outgoing, "brick", up)
    upper = lax.ppermute(outgoing, "brick", down)
    descriptor, charge, fields = networks(
        count_x * count_y,
        ghosts,
        (slab * block_y).astype(jnp.int32).reshape(1),
        charge_base,
        own,
        lower,
        upper,
        neighbours,
        types,
        (cell_x, cell_y, cell_z),
        spline_fraction,
        (embed_first, embed_second, embed_third),
        wannier_in,
        wannier_hidden,
        wannier_out,
    )
    every_field = exchange(fields, ("slab", "brick"))

    part = (2 * brick + slab % 2) * parts + jnp.arange(parts, dtype=jnp.int32)
    wave = wave_of(part)
    waves = jnp.stack([wave, jnp.where(part <= NG // 2, 0, 3 * NG // 4)], axis=1)
    kappa = wave.astype(jnp.float32) * (2.0 * math.pi / NG)
    squared = kappa * kappa
    ends = (part == 0) | (part == NG // 2)
    kappa = jnp.stack(
        [squared, jnp.exp(-0.5 * squared) * jnp.where(ends, 1.0 / NG, 2.0 / NG)], axis=1
    )
    basis = real_basis()
    tables = np.stack([basis, basis.T]).astype(np.float32)
    last = []
    for p in range(count_y // 2):
        points = np.concatenate(
            [np.arange(2 * block_y), block_y + np.arange(block_y + REACH)]
        )
        points = (2 * block_y * p + points) % NG
        columns = np.zeros((NG, NG))
        columns[:, : points.size] = basis[:, points]
        last.append(columns.astype(np.float32))
    cosine_row = np.cos(np.arange(128) * (2.0 * math.pi / NG)).astype(np.float32)[None]
    cosine_row = jnp.asarray(cosine_row)
    tables = jnp.asarray(tables)
    last = jnp.asarray(np.stack(last))
    energy_short = energies(descriptor, energy_in, energy_hidden, energy_out)
    early, full, every_atom, later = spread_and_solve(
        block_x,
        block_y,
        window,
        kappa,
        pair,
        every_field,
        waves,
        cosine_row,
        tables,
        last,
        energy_short,
    )

    def send(values):
        got = exchange(values.reshape(values.shape[0], -1, 128), ("brick", "slab"), halves)
        return got.reshape(values.shape)

    early = send(early)
    later = solve_and_sample(
        block_x,
        block_y,
        window,
        kappa,
        pair,
        every_atom,
        waves,
        cosine_row,
        tables,
        last,
        later,
        full,
    )
    later = send(later)
    source = np.arange(2 * count_x)[:, None] * parts
    pairs = 2 * np.arange(parts // 2)[None, :]
    order = np.concatenate(
        [
            (source + pairs[:, : early_pairs(parts)]).ravel(),
            (source + pairs[:, early_pairs(parts) :]).ravel(),
        ]
    )
    order = np.concatenate([order, order + 1])
    potential, atom_energy = finish(
        block_x,
        block_y,
        early,
        later,
        energy_short,
        charge,
        jnp.asarray(basis[order].astype(np.float32)),
    )
    return atom_energy, potential


def solution(mesh):
    placed = (
        P(None, "slab", "brick"),
        P("slab", "brick"),
        P("slab", "brick", None),
        P("slab", "brick"),
        P("slab", "brick"),
        P("slab", "brick"),
        P("slab", "brick"),
        P("slab", "brick"),
        P(None, "slab", "brick"),
    ) + (P(),) * 10
    bricks, slabs = mesh.shape["brick"], mesh.shape["slab"]
    fits = 2 * NG == 128 * slabs and NG % (32 * bricks) == 0
    return jax.shard_map(
        per_device if fits else per_device_general,
        mesh=mesh,
        in_specs=placed,
        out_specs=(P("slab", "brick"), P("brick", "slab", None)),
        check_vma=False,
    )
```

```python
import functools
import math

import jax
import jax.numpy as jnp
import numpy as np
from jax import lax
from jax.experimental import pallas as pl
from jax.experimental.pallas import tpu as pltpu
from jax.sharding import PartitionSpec as P

NG = 256
AXIS = 16
VMEM_BYTES = 60 * 2**20
REACH = 16
FIELDS = 7


HIGH = lax.Precision.HIGHEST


def with_halo(cells, sides, width):
    for axis, dim in sides:
        count = lax.axis_size(axis)
        head = lax.slice_in_dim(cells, 0, width, axis=dim)
        tail = lax.slice_in_dim(cells, cells.shape[dim] - width, cells.shape[dim], axis=dim)
        cells = jnp.concatenate(
            [
                lax.ppermute(tail, axis, [(i, (i + 1) % count) for i in range(count)]),
                cells,
                lax.ppermute(head, axis, [((i + 1) % count, i) for i in range(count)]),
            ],
            axis=dim,
        )
    return cells


def spline_weights(fraction):
    cubed = fraction * fraction * fraction
    square = fraction * fraction
    return jnp.stack(
        [
            (1.0 - fraction) * (1.0 - fraction) * (1.0 - fraction) / 6.0,
            (3.0 * cubed - 6.0 * square + 4.0) / 6.0,
            (-3.0 * cubed + 3.0 * square + 3.0 * fraction + 1.0) / 6.0,
            cubed / 6.0,
        ]
    )


def fitting(descriptor, weight_in, weight_hidden, weight_out):
    hidden = jnp.tanh(jnp.dot(descriptor, weight_in, precision=HIGH))
    for depth_index in range(weight_hidden.shape[0]):
        hidden = jnp.tanh(jnp.dot(hidden, weight_hidden[depth_index], precision=HIGH)) + hidden
    return jnp.dot(hidden, weight_out, precision=HIGH)


def atom_terms(
    extended,
    neighbour_rows,
    neighbour_total,
    embed_first,
    embed_second,
    embed_third,
    energy_in,
    energy_hidden,
    energy_out,
    wannier_in,
    wannier_hidden,
    wannier_out,
):
    atom_count, slots = neighbour_rows.shape
    ghost_rows = (extended.shape[1] - atom_count) // 2
    block_size = 64
    blocks = atom_count // block_size
    present = (jnp.arange(slots, dtype=jnp.int32)[None, :] < neighbour_total[:, None]).astype(
        jnp.float32
    )
    centre_ids = (ghost_rows + jnp.arange(atom_count, dtype=jnp.int32)).reshape(blocks, block_size)
    second_weight = embed_second.T
    third_weight = embed_third.T

    def one_block(pieces):
        centre_rows, rows_block, present_block = pieces
        centre_block = extended[:3, centre_rows]
        gathered = extended[:, rows_block]
        offsets = gathered[:3] - centre_block[:, :, None]
        smooth = present_block / (1.0 + jnp.sum(offsets * offsets, axis=0))
        environment = jnp.stack(
            [smooth, smooth * offsets[0], smooth * offsets[1], smooth * offsets[2]], axis=0
        )
        kind = gathered[3][None]
        mixing = (1.0 - kind) * embed_first[0][:, None, None] + kind * embed_first[1][:, None, None]
        first = jnp.tanh(smooth[None] * mixing).reshape(embed_first.shape[1], block_size * slots)
        second = jnp.tanh(jnp.dot(second_weight, first, precision=HIGH)) + jnp.concatenate(
            [first, first], axis=0
        )
        third = jnp.tanh(jnp.dot(third_weight, second, precision=HIGH)) + jnp.concatenate(
            [second, second], axis=0
        )
        third_blocks = third.reshape(third.shape[0], block_size, slots)
        moments = jnp.einsum("kan,can->akc", third_blocks, environment, precision=HIGH) / slots
        descriptor = jnp.einsum("amc,akc->amk", moments, moments[:, :AXIS], precision=HIGH).reshape(
            block_size, -1
        )
        return (
            fitting(descriptor, energy_in, energy_hidden, energy_out),
            fitting(descriptor, wannier_in, wannier_hidden, wannier_out),
        )

    energy_short, charge_shift = lax.map(
        one_block,
        (
            centre_ids,
            neighbour_rows.reshape(blocks, block_size, slots),
            present.reshape(blocks, block_size, slots),
        ),
    )
    return (energy_short.reshape(atom_count), charge_shift.reshape(atom_count))


def green_table(first, second, third, size):

    def folded(index):
        return jnp.where(index < size // 2, index, index - size).astype(jnp.float32) * (
            2.0 * math.pi / size
        )

    kappa_x = folded(first)[:, None, None]
    kappa_y = folded(second)[None, :, None]
    kappa_z = folded(third)[None, None, :]
    squared = kappa_x * kappa_x + kappa_y * kappa_y + kappa_z * kappa_z
    root = (
        (first[:, None, None] == 0) & (second[None, :, None] == 0) & (third[None, None, :] == 0)
    ).astype(jnp.float32)
    return (1.0 - root) * jnp.exp(-0.5 * squared) / (squared + root)


def dft_tables(size):
    index = jnp.arange(size, dtype=jnp.int32)
    phase = (index[:, None] * index[None, :] % size).astype(jnp.float32) * (2.0 * math.pi / size)
    return (jnp.cos(phase), jnp.sin(phase))


def along(values, table, axis_index):
    result = jnp.tensordot(values, table, axes=([axis_index], [0]), precision=HIGH)
    return jnp.moveaxis(result, -1, axis_index)


def complex_transform(paired, axis_index, cosine, sine, inverse):
    real_part = paired[0]
    imag_part = paired[1]
    inner = axis_index - 1
    real_cos = along(real_part, cosine, inner)
    real_sin = along(real_part, sine, inner)
    imag_cos = along(imag_part, cosine, inner)
    imag_sin = along(imag_part, sine, inner)
    if inverse:
        return jnp.stack([real_cos - imag_sin, imag_cos + real_sin])
    return jnp.stack([real_cos + imag_sin, imag_cos - real_sin])


def fold_windows(values, axis_index, block, count):
    front = jnp.moveaxis(values, axis_index, 0)
    rest = front.shape[1:]
    windows = front.reshape((count, block + 3) + rest)
    main_part = windows[:, :block]
    carried = jnp.roll(windows[:, block:], 1, axis=0)
    main_part = main_part.at[:, :3].add(carried)
    return jnp.moveaxis(main_part.reshape((count * block,) + rest), 0, axis_index)


def make_windows(values, axis_index, block, count):
    front = jnp.moveaxis(values, axis_index, 0)
    rest = front.shape[1:]
    pieces = front.reshape((count, block) + rest)
    trailing = jnp.roll(pieces, -1, axis=0)[:, :3]
    windows = jnp.concatenate([pieces, trailing], axis=1)
    return jnp.moveaxis(windows.reshape((count * (block + 3),) + rest), 0, axis_index)


def spread_matrix(start, weights, width, wrap_size):
    offsets = jnp.arange(4, dtype=jnp.int32)[:, None, None]
    target = start[None, :, None] + offsets
    if wrap_size > 0:
        target = target % wrap_size
    hits = (target == jnp.arange(width, dtype=jnp.int32)[None, None, :]).astype(jnp.float32)
    return jnp.sum(weights[:, :, None] * hits, axis=0)


def per_device_general(
    positions,
    types,
    neighbours,
    neighbour_count,
    send_index,
    cell_x,
    cell_y,
    cell_z,
    spline_fraction,
    embed_first,
    embed_second,
    embed_third,
    energy_in,
    energy_hidden,
    energy_out,
    wannier_in,
    wannier_hidden,
    wannier_out,
    charge_base,
):
    atom_count = types.shape[1]
    ghost_rows = send_index.shape[1] // 2
    kind_float = types[0].astype(jnp.float32)
    own_atoms = jnp.concatenate([positions[:, 0], kind_float[None]], axis=0)
    outgoing = own_atoms[:, send_index[0]]
    padded_ghosts = with_halo(outgoing, (("brick", 1),), ghost_rows)
    extended = jnp.concatenate(
        [padded_ghosts[:, :ghost_rows], own_atoms, padded_ghosts[:, 3 * ghost_rows :]], axis=1
    )
    energy_short, charge_shift = atom_terms(
        extended,
        neighbours[0],
        neighbour_count[0],
        embed_first,
        embed_second,
        embed_third,
        energy_in,
        energy_hidden,
        energy_out,
        wannier_in,
        wannier_hidden,
        wannier_out,
    )
    charge = (1.0 - kind_float) * charge_base[0] + kind_float * charge_base[1] + charge_shift
    count_x = lax.axis_size("brick")
    count_y = lax.axis_size("slab")
    block_x = NG // count_x
    block_y = NG // count_y
    wide_x = block_x + 3
    wide_y = block_y + 3
    spread_x = spread_matrix(cell_x[0], spline_weights(spline_fraction[0, 0]), wide_x, 0)
    spread_y = spread_matrix(cell_y[0], spline_weights(spline_fraction[1, 0]), wide_y, 0)
    spread_z = spread_matrix(cell_z[0], spline_weights(spline_fraction[2, 0]), NG, NG)
    spread_xy = (spread_x[:, :, None] * spread_y[:, None, :]).reshape(atom_count, wide_x * wide_y)
    charge_grid = jnp.einsum(
        "ap,az->pz", spread_xy, charge[:, None] * spread_z, precision=HIGH
    ).reshape(wide_x, wide_y, NG)
    cosine, sine = dft_tables(NG)
    scale = 1.0 / (NG * NG * NG)
    full_index = jnp.arange(NG, dtype=jnp.int32)
    paired = jnp.stack([along(charge_grid, cosine, 2), -along(charge_grid, sine, 2)])
    moved = lax.all_to_all(paired, "slab", split_axis=3, concat_axis=2, tiled=True)
    moved = complex_transform(fold_windows(moved, 2, block_y, count_y), 2, cosine, sine, False)
    moved = lax.all_to_all(moved, "brick", split_axis=2, concat_axis=1, tiled=True)
    moved = complex_transform(fold_windows(moved, 1, block_x, count_x), 1, cosine, sine, False)
    part_y = NG // count_x
    part_z = NG // count_y
    index_y = lax.axis_index("brick") * part_y + jnp.arange(part_y, dtype=jnp.int32)
    index_z = lax.axis_index("slab") * part_z + jnp.arange(part_z, dtype=jnp.int32)
    moved = moved * (green_table(full_index, index_y, index_z, NG) * scale)[None]
    moved = make_windows(complex_transform(moved, 1, cosine, sine, True), 1, block_x, count_x)
    moved = lax.all_to_all(moved, "brick", split_axis=1, concat_axis=2, tiled=True)
    moved = make_windows(complex_transform(moved, 2, cosine, sine, True), 2, block_y, count_y)
    moved = lax.all_to_all(moved, "slab", split_axis=2, concat_axis=3, tiled=True)
    potential_wide = along(moved[0], cosine, 2) - along(moved[1], sine, 2)
    sampled = jnp.einsum(
        "ap,pz->az", spread_xy, potential_wide.reshape(wide_x * wide_y, NG), precision=HIGH
    )
    potential_at = jnp.sum(sampled * spread_z, axis=1)
    atom_energy = energy_short + 0.5 * charge * potential_at
    return (atom_energy[None, :], potential_wide[:block_x, :block_y])


def split(values):
    high = values.astype(jnp.bfloat16)
    low = (values - high.astype(jnp.float32)).astype(jnp.bfloat16)
    return high, low


def multiply(left, right, dims):
    return lax.dot_general(left, right, (dims, ((), ())), preferred_element_type=jnp.float32)


def triple(left, right, dims=((1,), (0,))):
    (left_axis,), (right_axis,) = dims
    if left[0].shape[left_axis] % 128 == 0:
        return multiply(
            jnp.concatenate([left[0], left[0], left[1]], axis=left_axis),
            jnp.concatenate([right[0], right[1], right[0]], axis=right_axis),
            dims,
        )
    return (
        multiply(left[0], right[0], dims)
        + multiply(left[0], right[1], dims)
        + multiply(left[1], right[0], dims)
    )


LANES = ((1,), (1,))


def product(left, right, dims=((1,), (0,))):
    return lax.dot_general(
        left,
        right,
        (dims, ((), ())),
        precision=lax.Precision.HIGH,
        preferred_element_type=jnp.float32,
    )


def lane_pick(table, index):
    return jnp.take_along_axis(table, index, axis=1, mode="promise_in_bounds")


def whole(shape):
    return pl.BlockSpec(tuple(shape), lambda step: (0,) * len(shape))


def whole_specs(*arrays):
    return [whole(array.shape) for array in arrays]


def collect_kernel(
    positions_ref, types_ref, count_ref, send_ref, own_ref, outgoing_ref
):
    atoms = types_ref.shape[1]
    own_ref[...] = jnp.zeros_like(own_ref)
    for axis in range(3):
        own_ref[axis : axis + 1, 0:atoms] = positions_ref[axis]
    own_ref[3:4, 0:atoms] = types_ref[...].astype(jnp.float32)
    own_ref[4:5, 0:atoms] = count_ref[...].astype(jnp.float32)
    own_ref[5:6, 0:atoms] = send_ref[...].astype(jnp.float32)
    for chunk in range(2):
        lanes = slice(128 * chunk, 128 * chunk + 128)
        wanted = jnp.broadcast_to(own_ref[5:6, lanes], (8, 128)).astype(jnp.int32)
        within = wanted & 127
        outgoing_ref[:, lanes] = jnp.where(
            wanted < 128,
            lane_pick(own_ref[:, 0:128], within),
            lane_pick(own_ref[:, 128:256], within),
        )


def collect(positions, types, counts, send_index):
    arrays = (positions, types, counts, send_index)
    result = jax.ShapeDtypeStruct((8, 256), jnp.float32)
    return pl.pallas_call(
        collect_kernel,
        grid=(1,),
        out_shape=[result, result],
        in_specs=whole_specs(*arrays),
        out_specs=whole_specs(result, result),
        compiler_params=pltpu.CompilerParams(vmem_limit_bytes=VMEM_BYTES),
        name="collect_atoms",
    )(*arrays)


def fitting_rows(descriptor_ref, weight_in_ref, weight_hidden_ref, weight_out_ref):
    hidden = jnp.tanh(product(descriptor_ref[...], weight_in_ref[...], LANES))
    for layer in range(weight_hidden_ref.shape[0]):
        hidden = jnp.tanh(product(hidden, weight_hidden_ref[layer])) + hidden
    width = hidden.shape[1]
    return product(jnp.broadcast_to(weight_out_ref[...], (8, width)), hidden, LANES)


def natural_order(rows):
    atoms = rows.shape[1]
    padded = jnp.concatenate([rows, jnp.zeros((8, 256 - atoms), jnp.float32)], axis=1)
    pieces = []
    for chunk in range(2):
        atom = 128 * chunk + lax.broadcasted_iota(jnp.int32, (8, 128), 1)
        late = atom >= atoms // 2
        within = jnp.where(late, atom - atoms // 2, atom)
        place = 8 * (within >> 2) + (within & 3) + jnp.where(late, 4, 0)
        place = jnp.minimum(place, 255)
        pieces.append(
            jnp.where(
                place < 128,
                lane_pick(padded[:, 0:128], place & 127),
                lane_pick(padded[:, 128:256], place & 127),
            )
        )
    return jnp.concatenate(pieces, axis=1)[0:1, 0:atoms]


def network_kernel(
    ghosts,
    base_ref,
    charges_ref,
    own_ref,
    lower_ref,
    upper_ref,
    slots_ref,
    types_ref,
    cell_x_ref,
    cell_y_ref,
    cell_z_ref,
    fraction_ref,
    first_ref,
    second_ref,
    third_ref,
    spot_ref,
    weight_in_hbm,
    weight_hidden_hbm,
    weight_out_ref,
    descriptor_hbm,
    charge_ref,
    copies_ref,
    descriptor_ref,
    environment_ref,
    kind_ref,
    moments_ref,
    padded_ref,
    weight_in_ref,
    weight_hidden_ref,
    row_ref,
    semaphores,
):
    fetches = [
        pltpu.make_async_copy(weight_in_hbm, weight_in_ref, semaphores.at[0]),
        pltpu.make_async_copy(weight_hidden_hbm, weight_hidden_ref, semaphores.at[1]),
    ]
    for fetch in fetches:
        fetch.start()
    slots, atoms = slots_ref.shape
    rows = atoms // 2
    lane = lax.broadcasted_iota(jnp.int32, (8, 128), 1)
    sub = lax.broadcasted_iota(jnp.int32, (8, 128), 0)

    width = first_ref.shape[1]
    padded_ref[...] = jnp.zeros_like(padded_ref)
    padded_ref[0, 0:2, 0:width] = first_ref[...]
    for column in range(2):
        padded_ref[1, 0:width, 32 * column : 32 * column + width] = second_ref[
            :, width * column : width * (column + 1)
        ]
    for row in range(2):
        for column in range(4):
            padded_ref[2, 32 * row : 32 * row + width, 32 * column : 32 * column + width] = (
                third_ref[
                    width * row : width * (row + 1), width * column : width * (column + 1)
                ]
            )
    first_table = padded_ref[0].T
    embed_zero = jnp.broadcast_to(first_table[0:32, 0:1], (32, 128))
    embed_one = jnp.broadcast_to(first_table[0:32, 1:2], (32, 128))
    second_high, second_low = split(padded_ref[1].T[0:64, 0:32])
    second_weight = jnp.concatenate([second_high, second_high, second_low], axis=1)
    third_high, third_low = split(padded_ref[2].T[:, 0:64])
    third_weight = jnp.concatenate([third_high, third_high, third_low], axis=1)

    def spread(ref, field, chunk):
        return jnp.broadcast_to(ref[field : field + 1, 128 * chunk : 128 * chunk + 128], (8, 128))

    own = [[spread(own_ref, field, chunk) for chunk in range(2)] for field in range(5)]
    lower = [[spread(lower_ref, field, chunk) for chunk in range(2)] for field in range(4)]
    upper = [spread(upper_ref, field, 0) for field in range(4)]

    def pick_two(tables, index):
        within = index & 127
        return jnp.where(index < 128, lane_pick(tables[0], within), lane_pick(tables[1], within))

    pairs = jnp.concatenate([slots_ref[:, 0:rows], slots_ref[:, rows:atoms]], axis=0).T
    for tile in range(rows // 8):
        band = slice(8 * tile, 8 * tile + 8)
        index = pairs[band, :]
        centre = 8 * tile + sub + jnp.where(lane < 64, 0, rows)
        from_own = jnp.clip(index - ghosts, 0, atoms - 1)
        from_lower = jnp.minimum(index + (atoms - ghosts), 255)
        from_upper = jnp.clip(index - (ghosts + atoms), 0, 127)

        def neighbour(field):
            below = pick_two(lower[field], from_lower)
            inside = pick_two(own[field], from_own)
            above = lane_pick(upper[field], from_upper)
            return jnp.where(
                index < ghosts, below, jnp.where(index < ghosts + atoms, inside, above)
            )

        offsets = [neighbour(field) - pick_two(own[field], centre) for field in range(3)]
        live = pick_two(own[4], centre)
        present = jnp.where((lane & 63).astype(jnp.float32) < live, 1.0, 0.0)
        smooth = present / (
            1.0 + (offsets[0] * offsets[0] + offsets[1] * offsets[1] + offsets[2] * offsets[2])
        )
        environment_ref[0, band, :] = smooth
        for field in range(3):
            environment_ref[1 + field, band, :] = smooth * offsets[field]
        kind_ref[band, :] = neighbour(3)

    group = 8

    def stacked(values):
        high, low = split(values)
        return jnp.concatenate([high, low, high], axis=0)

    def one_group(start):
        pieces = []
        for row in range(group):
            smooth = jnp.broadcast_to(environment_ref[0, pl.ds(start + row, 1), :], (32, 128))
            kind = jnp.broadcast_to(kind_ref[pl.ds(start + row, 1), :], (32, 128))
            pieces.append(
                jnp.tanh(smooth * ((1.0 - kind) * embed_zero + kind * embed_one))
            )
        first = jnp.concatenate(pieces, axis=1)
        second = jnp.tanh(multiply(second_weight, stacked(first), ((1,), (0,))))
        second = second + jnp.concatenate([first, first], axis=0)
        third = jnp.tanh(multiply(third_weight, stacked(second), ((1,), (0,))))
        third = third + jnp.concatenate([second, second], axis=0)
        third_pair = split(third)
        for half in range(group // 4):
            columns = slice(512 * half, 512 * half + 512)
            bands = []
            for part in range(4):
                bands.append(
                    jnp.concatenate(
                        [
                            jnp.where(
                                sub == row + jnp.where(lane < 64, 0, 4),
                                jnp.broadcast_to(
                                    environment_ref[part, pl.ds(start + 4 * half + row, 1), :],
                                    (8, 128),
                                ),
                                0.0,
                            )
                            for row in range(4)
                        ],
                        axis=1,
                    )
                )
            environment = split(jnp.concatenate(bands, axis=0))
            both = multiply(
                jnp.concatenate(environment, axis=0), third_pair[0][:, columns], LANES
            )
            sums = both[0:32] + both[32:64]
            sums = sums + multiply(environment[0], third_pair[1][:, columns], LANES)
            sums = sums * (1.0 / slots)
            for part in range(4):
                moments_ref[part, pl.ds(2 * start + 8 * half, 8), :] = sums[
                    8 * part : 8 * part + 8
                ]

    chunks = (descriptor_ref.shape[1] + 127) // 128
    last = descriptor_ref.shape[1] - 128 * (chunks - 1)

    def describe_band(start):
        band = pl.ds(start, 8)
        moments = [moments_ref[part, band, :] for part in range(4)]
        axis_part = [lane_pick(moments[part], lane & 15) for part in range(4)]
        for chunk in range(chunks):
            spot = jnp.broadcast_to(spot_ref[chunk : chunk + 1, :], (8, 128))
            total = lane_pick(moments[0], spot) * axis_part[0]
            for part in range(1, 4):
                total = total + lane_pick(moments[part], spot) * axis_part[part]
            if chunk < chunks - 1:
                descriptor_ref[band, 128 * chunk : 128 * chunk + 128] = total
            else:
                descriptor_ref[band, 128 * chunk : 128 * chunk + last] = total[:, 0:last]

    for start in range(0, rows + group, group):
        if start < rows:
            one_group(start)
        if start > 0:
            for band in range(2 * (start - group), 2 * start, 8):
                describe_band(band)

    store = pltpu.make_async_copy(descriptor_ref, descriptor_hbm, semaphores.at[2])
    store.start()
    for fetch in fetches:
        fetch.wait()
    shift = fitting_rows(descriptor_ref, weight_in_ref, weight_hidden_ref, weight_out_ref)
    kind = types_ref[...].astype(jnp.float32)
    charge = (1.0 - kind) * charges_ref[0] + kind * charges_ref[1] + natural_order(shift)
    charge_ref[...] = charge
    fields = [
        cell_x_ref[...].astype(jnp.float32),
        (cell_y_ref[...] + base_ref[0]).astype(jnp.float32),
        cell_z_ref[...].astype(jnp.float32),
    ]
    fields = fields + [fraction_ref[axis] for axis in range(3)] + [charge]
    for place, field in enumerate(fields):
        row_ref[:, atoms * place : atoms * (place + 1)] = field
    for copy in range(copies_ref.shape[0]):
        copies_ref[copy] = row_ref[...]
    store.wait()


def spot_table(embed, desc):
    column = np.arange(desc) // AXIS
    quarter = embed // 4
    place = 32 * (column // quarter) + column % quarter
    chunks = (desc + 127) // 128
    table = np.zeros((chunks * 128,), np.int32)
    table[:desc] = place
    padded = np.zeros(((chunks + 7) // 8 * 8, 128), np.int32)
    padded[:chunks] = table.reshape(chunks, 128)
    return padded


def networks(
    copies,
    ghosts,
    base,
    charge_base,
    own,
    lower,
    upper,
    neighbours,
    types,
    cells,
    fraction,
    embed,
    weight_in,
    weight_hidden,
    weight_out,
):
    atoms = types.shape[1]
    desc, width = weight_in.shape
    spots = jnp.asarray(spot_table(embed[2].shape[1], desc))
    anywhere = pl.BlockSpec(memory_space=pl.ANY)
    scalars = pl.BlockSpec(memory_space=pltpu.SMEM)
    blocks = (own, lower, upper, neighbours[0].T, types, *cells, fraction, *embed, spots)
    weight_out = weight_out.reshape(1, -1)
    results = [
        jax.ShapeDtypeStruct((atoms, desc), jnp.float32),
        jax.ShapeDtypeStruct((1, atoms), jnp.float32),
        jax.ShapeDtypeStruct((copies, 1, FIELDS * atoms), jnp.float32),
    ]
    return pl.pallas_call(
        functools.partial(network_kernel, ghosts),
        grid=(1,),
        out_shape=results,
        in_specs=[scalars, scalars]
        + whole_specs(*blocks)
        + [anywhere, anywhere]
        + whole_specs(weight_out),
        out_specs=[anywhere] + whole_specs(*results[1:]),
        scratch_shapes=[
            pltpu.VMEM((atoms, desc), jnp.float32),
            pltpu.VMEM((4, atoms // 2, 128), jnp.float32),
            pltpu.VMEM((atoms // 2, 128), jnp.float32),
            pltpu.VMEM((4, atoms, 128), jnp.float32),
            pltpu.VMEM((3, 128, 128), jnp.float32),
            pltpu.VMEM((width, desc), jnp.float32),
            pltpu.VMEM(weight_hidden.shape, jnp.float32),
            pltpu.VMEM((1, FIELDS * atoms), jnp.float32),
            pltpu.SemaphoreType.DMA((3,)),
        ],
        compiler_params=pltpu.CompilerParams(vmem_limit_bytes=VMEM_BYTES),
        name="networks",
    )(base, charge_base, *blocks, weight_in.T, weight_hidden, weight_out)


def energy_kernel(descriptor_ref, weight_in_ref, weight_hidden_ref, weight_out_ref, energy_ref):
    energy_ref[...] = natural_order(
        fitting_rows(descriptor_ref, weight_in_ref, weight_hidden_ref, weight_out_ref)
    )


def energies(descriptor, weight_in, weight_hidden, weight_out):
    atoms, desc = descriptor.shape
    width = weight_in.shape[1]
    arrays = (descriptor, weight_in.T, weight_hidden, weight_out.reshape(1, -1))
    result = jax.ShapeDtypeStruct((1, atoms), jnp.float32)
    return pl.pallas_call(
        energy_kernel,
        grid=(1,),
        out_shape=result,
        in_specs=whole_specs(*arrays),
        out_specs=whole(result.shape),
        compiler_params=pltpu.CompilerParams(vmem_limit_bytes=VMEM_BYTES),
        cost_estimate=pl.CostEstimate(
            flops=6 * atoms * desc * width, bytes_accessed=4 * desc * width, transcendentals=0
        ),
        name="energies",
    )(*arrays)


def weight_rows(fraction):
    square = fraction * fraction
    cubed = square * fraction
    rest = 1.0 - fraction
    return [
        rest * rest * rest / 6.0,
        (3.0 * cubed - 6.0 * square + 4.0) / 6.0,
        (-3.0 * cubed + 3.0 * square + 3.0 * fraction + 1.0) / 6.0,
        cubed / 6.0,
    ]


def placed_weights(distance, weights):
    shape = distance.shape
    result = jnp.zeros(shape, jnp.float32)
    for step in range(4):
        result = jnp.where(
            distance == step, jnp.broadcast_to(weights[step], shape), result
        )
    return result


def third_factors(fields, waves_ref, cosine_ref):
    atoms = fields.shape[1]
    start = fields[2:3, :].astype(jnp.int32)
    along = weight_rows(fields[5:6, :])
    parts = waves_ref.shape[0]
    cosine = jnp.broadcast_to(cosine_ref[...], (parts, 128))
    wave = jnp.broadcast_to(waves_ref[:, 0:1], (parts, 128))
    shift = jnp.broadcast_to(waves_ref[:, 1:2], (parts, 128))
    pieces = []
    for chunk in range(atoms // 128):
        lanes = slice(128 * chunk, 128 * chunk + 128)
        total = jnp.zeros((parts, 128), jnp.float32)
        for step in range(4):
            place = jnp.broadcast_to(start[:, lanes] + step, (parts, 128))
            phase = (wave * place + shift) & (NG - 1)
            value = lane_pick(cosine, phase & 127)
            value = jnp.where(phase < 128, value, -value)
            total = total + value * jnp.broadcast_to(along[step][:, lanes], (parts, 128))
        pieces.append(total)
    return jnp.concatenate(pieces, axis=1)


def first_third_split(fields, waves_ref, cosine_ref, window, scale, high_ref, low_ref):
    atoms = fields.shape[1]
    third = third_factors(fields, waves_ref, cosine_ref) * scale
    rows = lax.broadcasted_iota(jnp.int32, (window, atoms), 0)
    first = placed_weights(
        rows - fields[0:1, :].astype(jnp.int32), weight_rows(fields[3:4, :])
    )
    for chunk in range(atoms // 128):
        lanes = slice(128 * chunk, 128 * (chunk + 1))
        for part in range(0, third.shape[0], 2):
            high, low = split(
                jnp.concatenate(
                    [first[:, lanes] * third[part + side : part + side + 1, lanes] for side in range(2)],
                    axis=0,
                )
            )
            place = slice(part * window, (part + 2) * window)
            high_ref[place, lanes] = high
            low_ref[place, lanes] = low
    return high_ref[...], low_ref[...]


def second_factors(fields, base, block_y, slabs, high_ref, low_ref):
    atoms = fields.shape[1]
    block = atoms // slabs
    reach = block_y + REACH
    start = fields[1:2, :].astype(jnp.int32) - base
    weights = weight_rows(fields[4:5, :])
    for chunk in range(atoms // 128):
        lanes = slice(128 * chunk, 128 * (chunk + 1))
        first = 128 * chunk // block
        last = (128 * chunk + 127) // block
        top = first * block_y
        rows = (last - first) * block_y + reach
        pieces = [(top, min(rows, NG - top))]
        if top + rows > NG:
            pieces.append((0, top + rows - NG))
        for row, count in pieces:
            index = row + lax.broadcasted_iota(jnp.int32, (count, 128), 0)
            table = split(
                placed_weights(
                    (index - start[:, lanes]) & (NG - 1), [weight[:, lanes] for weight in weights]
                )
            )
            high_ref[row : row + count, lanes] = table[0]
            low_ref[row : row + count, lanes] = table[1]
    return high_ref[...], low_ref[...]


def wave_of(index):
    return jnp.where(index <= NG // 2, index, index - NG // 2)


def damping(index):
    kappa = wave_of(index).astype(jnp.float32) * (2.0 * math.pi / NG)
    squared = kappa * kappa
    ends = (index == 0) | (index == NG // 2)
    return squared, jnp.exp(-0.5 * squared) * jnp.where(ends, 1.0 / NG, 2.0 / NG)


def transform(planes, kappa_ref, first_part, tables_ref, last_ref):
    count = len(planes)
    basis = tables_ref[0]
    turned = tables_ref[1]
    square_x, damp_x = damping(lax.broadcasted_iota(jnp.int32, (NG, 1), 0))
    square_y, damp_y = damping(lax.broadcasted_iota(jnp.int32, (1, NG), 1))
    square_xy = square_x + square_y
    damp_xy = damp_x * damp_y
    columns = [slice(NG * part, NG * (part + 1)) for part in range(count)]
    first = product(basis, jnp.concatenate(planes, axis=1))
    first = jnp.concatenate([first[:, column] for column in columns], axis=0)
    both = product(first, turned)
    scaled = []
    for part in range(count):
        squared = square_xy + kappa_ref[first_part + part, 0]
        root = jnp.where(squared == 0.0, 1.0, 0.0)
        green = (1.0 - root) * (damp_xy * kappa_ref[first_part + part, 1]) / (squared + root)
        scaled.append(both[columns[part]] * green)
    back = product(turned, jnp.concatenate(scaled, axis=1))
    back = jnp.concatenate([back[:, column] for column in columns], axis=0)
    return product(back, last_ref[...])


def send_blocks(full, block_x, block_y, put):
    low_lanes = lax.broadcasted_iota(jnp.int32, (NG, 128), 1) < block_y
    for pair in range(full.shape[0] // (2 * NG)):
        even = full[2 * NG * pair : 2 * NG * pair + NG, 0:128]
        odd = full[2 * NG * pair + NG : 2 * NG * (pair + 1), 0:128]
        blocks = [
            jnp.where(low_lanes, even, pltpu.roll(odd, block_y, 1)),
            jnp.where(low_lanes, pltpu.roll(even, block_y, 1), odd),
        ]
        for brick in range(NG // block_x):
            for side in range(2):
                for group in range(block_x // 8):
                    start = block_x * brick + 8 * group
                    put(pair, brick, side, group, blocks[side][start : start + 8])


def spread_kernel(
    block_x,
    block_y,
    window,
    kappa_ref,
    pair_ref,
    static_ref,
    waves_ref,
    cosine_ref,
    tables_hbm,
    last_hbm,
    short_hbm,
    sent_ref,
    full_ref,
    atoms_ref,
    later_hbm,
    grid_ref,
    tables_ref,
    last_ref,
    semaphores,
    *pair_refs,
):
    slabs = NG // block_y
    second_refs, first_refs = pair_refs[:4], pair_refs[4:]
    bricks = NG // block_x
    parts = waves_ref.shape[0]
    block = static_ref.shape[2] // FIELDS
    count = full_ref.shape[0]
    step = pl.program_id(0)
    later = later_hbm.shape[0]
    store = pltpu.make_async_copy(
        grid_ref.at[pl.ds(parts - later, later), pl.ds(0, NG)], later_hbm, semaphores.at[2]
    )

    @pl.when(step == 0)
    def _():
        fetches = [
            pltpu.make_async_copy(tables_hbm, tables_ref, semaphores.at[0]),
            pltpu.make_async_copy(last_hbm.at[pair_ref[0]], last_ref, semaphores.at[1]),
        ]
        for fetch in fetches:
            fetch.start()
        for slab in range(slabs):
            lanes = slice(block * slab, block * (slab + 1))
            for brick in range(bricks):
                for field in range(FIELDS):
                    atoms_ref[brick, field : field + 1, lanes] = static_ref[
                        slab * bricks + brick, :, block * field : block * (field + 1)
                    ]
        for ref in second_refs:
            ref[...] = jnp.zeros_like(ref)
        def tables_of(brick):
            fields = atoms_ref[brick]
            table = first_third_split(
                fields,
                waves_ref,
                cosine_ref,
                window,
                fields[6:7, :],
                first_refs[2 * (brick % 2)],
                first_refs[2 * (brick % 2) + 1],
            )
            second = second_factors(
                fields, 0, block_y, slabs, second_refs[2 * (brick % 2)], second_refs[2 * (brick % 2) + 1]
            )
            return table, second

        coming = tables_of(0)
        for brick in range(bricks):
            table, second = coming
            if brick + 1 < bricks:
                coming = tables_of(brick + 1)
            spread = triple(table, second, LANES)
            start = block_x * brick
            extra = window - block_x
            for part in range(parts):
                shared = spread[part * window : part * window + extra]
                if brick > 0:
                    shared = shared + grid_ref[part, start : start + extra, :]
                grid_ref[part, start : start + extra, :] = shared
                grid_ref[part, start + extra : start + window, :] = spread[
                    part * window + extra : part * window + window
                ]
        for part in range(parts):
            grid_ref[part, 0:extra, :] += grid_ref[part, NG : NG + extra, :]
        store.start()
        for fetch in fetches:
            fetch.wait()

    planes = [grid_ref[count * step + part, 0:NG, :] for part in range(count)]
    full = transform(planes, kappa_ref, count * step, tables_ref, last_ref)
    for part in range(count):
        full_ref[part] = full[NG * part : NG * (part + 1)]

    def put(pair, brick, side, group, tile):
        sent_ref[2 * brick + side, group, pair] = tile

    send_blocks(full, block_x, block_y, put)

    @pl.when(step == pl.num_programs(0) - 1)
    def _():
        store.wait()


def early_pairs(parts):
    return parts // 4


def spread_and_solve(
    block_x, block_y, window, kappa, pair, static, waves, cosine_row, tables, last, short
):
    atoms = static.shape[2] // FIELDS
    slabs = NG // block_y
    bricks = NG // block_x
    parts = waves.shape[0]
    pairs = early_pairs(parts)
    count = 4
    anywhere = pl.BlockSpec(memory_space=pl.ANY)
    scalars = pl.BlockSpec(memory_space=pltpu.SMEM)
    sent_block = (2 * bricks, block_x // 8, count // 2, 8, 128)
    return pl.pallas_call(
        functools.partial(spread_kernel, block_x, block_y, window),
        grid=(2 * pairs // count,),
        out_shape=[
            jax.ShapeDtypeStruct((2 * bricks, block_x // 8, pairs, 8, 128), jnp.float32),
            jax.ShapeDtypeStruct((2 * pairs, NG, NG), jnp.float32),
            jax.ShapeDtypeStruct((bricks, 8, slabs * atoms), jnp.float32),
            jax.ShapeDtypeStruct((parts - 2 * pairs, NG, NG), jnp.float32),
        ],
        in_specs=[scalars, scalars]
        + whole_specs(static, waves, cosine_row)
        + [anywhere, anywhere, anywhere],
        out_specs=[
            pl.BlockSpec(sent_block, lambda step: (0, 0, step, 0, 0)),
            pl.BlockSpec((count, NG, NG), lambda step: (step, 0, 0)),
            whole((bricks, 8, slabs * atoms)),
            anywhere,
        ],
        scratch_shapes=[
            pltpu.VMEM((parts, NG + window - block_x, NG), jnp.float32),
            pltpu.VMEM(tables.shape, tables.dtype),
            pltpu.VMEM(last.shape[1:], last.dtype),
            pltpu.SemaphoreType.DMA((3,)),
        ]
        + [pltpu.VMEM((NG, slabs * atoms), jnp.bfloat16)] * 4
        + [pltpu.VMEM((parts * window, slabs * atoms), jnp.bfloat16)] * 4,
        compiler_params=pltpu.CompilerParams(vmem_limit_bytes=VMEM_BYTES),
        name="spread_and_solve",
    )(kappa, pair, static, waves, cosine_row, tables, last, short)


def sample_kernel(
    block_x,
    block_y,
    window,
    kappa_ref,
    pair_ref,
    atoms_ref,
    waves_ref,
    cosine_ref,
    tables_hbm,
    last_hbm,
    later_hbm,
    early_hbm,
    sent_ref,
    later_ref,
    full_ref,
    tables_ref,
    last_ref,
    semaphores,
    packed_ref,
):
    bricks = atoms_ref.shape[0]
    parts = waves_ref.shape[0]
    early = 2 * early_pairs(parts)
    block = atoms_ref.shape[2] * block_y // NG
    fetches = [
        pltpu.make_async_copy(tables_hbm, tables_ref, semaphores.at[0]),
        pltpu.make_async_copy(last_hbm.at[pair_ref[0]], last_ref, semaphores.at[1]),
        pltpu.make_async_copy(later_hbm, later_ref, semaphores.at[2]),
        pltpu.make_async_copy(early_hbm, full_ref.at[pl.ds(0, early)], semaphores.at[3]),
    ]
    for fetch in fetches:
        fetch.start()
    for fetch in fetches[:3]:
        fetch.wait()
    pairs = (parts - early) // 2
    planes = [later_ref[part] for part in range(parts - early)]
    full = transform(planes, kappa_ref, early, tables_ref, last_ref)
    for part in range(parts - early):
        full_ref[early + part] = full[NG * part : NG * (part + 1)]

    def put(pair, brick, side, group, tile):
        sent_ref[2 * brick + side, pairs * group + pair] = tile

    send_blocks(full, block_x, block_y, put)
    fetches[3].wait()

    reach = block_y + REACH
    lane = lax.broadcasted_iota(jnp.int32, (NG, 128), 1)
    for part in range(parts):
        for side in range(2):
            values = full_ref[part, :, 128 * side : 128 * (side + 1)]
            high = values.astype(jnp.bfloat16).astype(jnp.float32)
            again = pltpu.roll(high, reach, 1)
            low = pltpu.roll(values - high, 2 * reach - 128, 1)
            packed_ref[side, part, 0:NG, 0:128] = jnp.where(lane < reach, high, again)
            packed_ref[side, part, 0:NG, 128:NG] = jnp.where(
                lane < 2 * reach - 128, again, jnp.where(lane < 3 * reach - 128, low, 0.0)
            )
            packed_ref[side, part, NG : NG + window - block_x, :] = packed_ref[
                side, part, 0 : window - block_x, :
            ]
    extra = sent_ref.shape[1] - 1
    base = 2 * block_y * pair_ref[0]
    lanes = pl.ds(pl.multiple_of(2 * block * pair_ref[0], 128), 2 * block)
    for brick in range(bricks):
        fields = atoms_ref[brick, :, lanes]
        thirds = third_factors(fields, waves_ref, cosine_ref)
        rows = slice(block_x * brick, block_x * brick + window)
        for side in range(2):
            here = slice(block * side, block * (side + 1))
            third = thirds[:, here]
            ours = fields[:, here]
            index = lax.broadcasted_iota(jnp.int32, (window, block), 0)
            first = placed_weights(
                index - ours[0:1, :].astype(jnp.int32), weight_rows(ours[3:4, :])
            )
            index = lax.broadcasted_iota(jnp.int32, (reach, block), 0)
            start = ours[1:2, :].astype(jnp.int32) - (base + block_y * side)
            high, low = split(placed_weights(index - start, weight_rows(ours[4:5, :])))
            rest = jnp.zeros((NG - 3 * reach, block), jnp.bfloat16)
            second = jnp.concatenate([high, low, high, rest], axis=0)
            values = jnp.concatenate(
                [packed_ref[side, part, rows, :] for part in range(parts)], axis=0
            )
            along = multiply(values.astype(jnp.bfloat16), second, ((1,), (0,)))
            total = jnp.zeros((window, block), jnp.float32)
            for part in range(parts):
                total = total + along[window * part : window * (part + 1)] * third[part : part + 1]
            row = jnp.sum(total * first, axis=0, keepdims=True)
            sent_ref[2 * brick + side, extra] = jnp.zeros((8, 128), jnp.float32)
            sent_ref[2 * brick + side, extra, 0:1, :] = row[:, 0:128]
            sent_ref[2 * brick + side, extra, 1:2, 0 : block - 128] = row[:, 128:block]


def solve_and_sample(
    block_x, block_y, window, kappa, pair, atoms, waves, cosine_row, tables, last, later, early
):
    bricks = atoms.shape[0]
    parts = waves.shape[0]
    pairs = parts // 2 - early_pairs(parts)
    anywhere = pl.BlockSpec(memory_space=pl.ANY)
    scalars = pl.BlockSpec(memory_space=pltpu.SMEM)
    result = jax.ShapeDtypeStruct((2 * bricks, block_x // 8 * pairs + 1, 8, 128), jnp.float32)
    return pl.pallas_call(
        functools.partial(sample_kernel, block_x, block_y, window),
        grid=(1,),
        out_shape=result,
        in_specs=[scalars, scalars] + whole_specs(atoms, waves, cosine_row) + [anywhere] * 4,
        out_specs=whole(result.shape),
        scratch_shapes=[
            pltpu.VMEM((2 * pairs, NG, NG), jnp.float32),
            pltpu.VMEM((parts, NG, NG), jnp.float32),
            pltpu.VMEM(tables.shape, tables.dtype),
            pltpu.VMEM(last.shape[1:], last.dtype),
            pltpu.SemaphoreType.DMA((4,)),
        ]
        + [pltpu.VMEM((2, parts, NG + window - block_x, NG), jnp.float32)],
        compiler_params=pltpu.CompilerParams(vmem_limit_bytes=VMEM_BYTES),
        cost_estimate=pl.CostEstimate(
            flops=24 * parts * NG * NG * NG, bytes_accessed=4 * early.size, transcendentals=0
        ),
        name="solve_and_sample",
    )(kappa, pair, atoms, waves, cosine_row, tables, last, later, early)


def finish_kernel(
    block_y,
    early_ref,
    later_ref,
    sums_ref,
    short_hbm,
    charge_hbm,
    table_ref,
    out_ref,
    energy_ref,
    short_ref,
    charge_ref,
    semaphores,
):
    atoms = short_ref.shape[1]
    fetches = [
        pltpu.make_async_copy(short_hbm, short_ref, semaphores.at[0]),
        pltpu.make_async_copy(charge_hbm, charge_ref, semaphores.at[1]),
    ]

    @pl.when(pl.program_id(0) == 0)
    def _():
        for fetch in fetches:
            fetch.start()

    lines = early_ref.shape[3]
    sources, _, pairs = early_ref.shape[:3]
    early = early_ref.reshape(sources * pairs, lines, 128)
    later = later_ref.reshape(sources * later_ref.shape[1], lines, 128)
    pieces = []
    for line in range(lines):
        turned = jnp.concatenate([early[:, line, :], later[:, line, :]], axis=0).T
        pieces.append(jnp.concatenate([turned[0:block_y], turned[block_y:]], axis=1))
    result = product(jnp.concatenate(pieces, axis=0), table_ref[...])
    for line in range(lines):
        out_ref[line] = result[block_y * line : block_y * (line + 1)]

    @pl.when(pl.program_id(0) == 0)
    def _():
        for fetch in fetches:
            fetch.wait()
        total = jnp.sum(sums_ref[:, 0], axis=0)
        potential_at = jnp.concatenate([total[0:1, :], total[1:2, 0 : atoms - 128]], axis=1)
        energy_ref[...] = short_ref[...] + 0.5 * charge_ref[...] * potential_at


def finish(block_x, block_y, early, later, short, charge, table):
    bricks2, groups, pairs = early.shape[:3]
    rest = (later.shape[1] - 1) // groups
    atoms = short.shape[1]
    return pl.pallas_call(
        functools.partial(finish_kernel, block_y),
        grid=(groups,),
        out_shape=[
            jax.ShapeDtypeStruct((block_x, block_y, NG), jnp.float32),
            jax.ShapeDtypeStruct((1, atoms), jnp.float32),
        ],
        in_specs=[
            pl.BlockSpec((bricks2, 1, pairs, 8, 128), lambda index: (0, index, 0, 0, 0)),
            pl.BlockSpec((bricks2, rest, 8, 128), lambda index: (0, index, 0, 0)),
            pl.BlockSpec((bricks2, 1, 8, 128), lambda index: (0, groups * rest, 0, 0)),
            pl.BlockSpec(memory_space=pltpu.HBM),
            pl.BlockSpec(memory_space=pltpu.HBM),
            whole(table.shape),
        ],
        out_specs=[
            pl.BlockSpec((8, block_y, NG), lambda index: (index, 0, 0)),
            whole((1, atoms)),
        ],
        scratch_shapes=[
            pltpu.VMEM((1, atoms), jnp.float32),
            pltpu.VMEM((1, atoms), jnp.float32),
            pltpu.SemaphoreType.DMA((2,)),
        ],
        compiler_params=pltpu.CompilerParams(vmem_limit_bytes=32 * 2**20),
        name="finish",
    )(early, later, later, short, charge, table)


def real_basis():
    index = np.arange(NG)
    wave = np.where(index <= NG // 2, index, index - NG // 2)
    angle = (wave[:, None] * index[None, :] % NG) * (2.0 * math.pi / NG)
    return np.where((index <= NG // 2)[:, None], np.cos(angle), np.sin(angle))


def per_device(
    positions,
    types,
    neighbours,
    neighbour_count,
    send_index,
    cell_x,
    cell_y,
    cell_z,
    spline_fraction,
    embed_first,
    embed_second,
    embed_third,
    energy_in,
    energy_hidden,
    energy_out,
    wannier_in,
    wannier_hidden,
    wannier_out,
    charge_base,
):
    atoms = types.shape[1]
    ghosts = send_index.shape[1] // 2
    count_x = lax.axis_size("brick")
    count_y = lax.axis_size("slab")
    block_x = NG // count_x
    block_y = NG // count_y
    window = block_x + 8
    parts = NG // (2 * count_x)
    brick = lax.axis_index("brick")
    slab = lax.axis_index("slab")
    pair = (slab // 2).astype(jnp.int32).reshape(1)
    halves = [
        [b * count_y + 2 * p + side for b in range(count_x) for side in range(2)]
        for p in range(count_y // 2)
    ]

    def exchange(values, axes, groups=None):
        return lax.all_to_all(
            values, axes, split_axis=0, concat_axis=0, tiled=True, axis_index_groups=groups
        )

    own, outgoing = collect(positions, types, neighbour_count, send_index)
    up = [(i, (i + 1) % count_x) for i in range(count_x)]
    down = [((i + 1) % count_x, i) for i in range(count_x)]
    lower = lax.ppermute(outgoing, "brick", up)
    upper = lax.ppermute(outgoing, "brick", down)
    descriptor, charge, fields = networks(
        count_x * count_y,
        ghosts,
        (slab * block_y).astype(jnp.int32).reshape(1),
        charge_base,
        own,
        lower,
        upper,
        neighbours,
        types,
        (cell_x, cell_y, cell_z),
        spline_fraction,
        (embed_first, embed_second, embed_third),
        wannier_in,
        wannier_hidden,
        wannier_out,
    )
    every_field = exchange(fields, ("slab", "brick"))

    part = (2 * brick + slab % 2) * parts + jnp.arange(parts, dtype=jnp.int32)
    wave = wave_of(part)
    waves = jnp.stack([wave, jnp.where(part <= NG // 2, 0, 3 * NG // 4)], axis=1)
    kappa = wave.astype(jnp.float32) * (2.0 * math.pi / NG)
    squared = kappa * kappa
    ends = (part == 0) | (part == NG // 2)
    kappa = jnp.stack(
        [squared, jnp.exp(-0.5 * squared) * jnp.where(ends, 1.0 / NG, 2.0 / NG)], axis=1
    )
    basis = real_basis()
    tables = np.stack([basis, basis.T]).astype(np.float32)
    last = []
    for p in range(count_y // 2):
        points = np.concatenate(
            [np.arange(2 * block_y), block_y + np.arange(block_y + REACH)]
        )
        points = (2 * block_y * p + points) % NG
        columns = np.zeros((NG, NG))
        columns[:, : points.size] = basis[:, points]
        last.append(columns.astype(np.float32))
    cosine_row = np.cos(np.arange(128) * (2.0 * math.pi / NG)).astype(np.float32)[None]
    cosine_row = jnp.asarray(cosine_row)
    tables = jnp.asarray(tables)
    last = jnp.asarray(np.stack(last))
    energy_short = energies(descriptor, energy_in, energy_hidden, energy_out)
    early, full, every_atom, later = spread_and_solve(
        block_x,
        block_y,
        window,
        kappa,
        pair,
        every_field,
        waves,
        cosine_row,
        tables,
        last,
        energy_short,
    )

    def send(values):
        got = exchange(values.reshape(values.shape[0], -1, 128), ("brick", "slab"), halves)
        return got.reshape(values.shape)

    early = send(early)
    later = solve_and_sample(
        block_x,
        block_y,
        window,
        kappa,
        pair,
        every_atom,
        waves,
        cosine_row,
        tables,
        last,
        later,
        full,
    )
    later = send(later)
    source = np.arange(2 * count_x)[:, None] * parts
    pairs = 2 * np.arange(parts // 2)[None, :]
    order = np.concatenate(
        [
            (source + pairs[:, : early_pairs(parts)]).ravel(),
            (source + pairs[:, early_pairs(parts) :]).ravel(),
        ]
    )
    order = np.concatenate([order, order + 1])
    potential, atom_energy = finish(
        block_x,
        block_y,
        early,
        later,
        energy_short,
        charge,
        jnp.asarray(basis[order].astype(np.float32)),
    )
    return atom_energy, potential


def solution(mesh):
    placed = (
        P(None, "slab", "brick"),
        P("slab", "brick"),
        P("slab", "brick", None),
        P("slab", "brick"),
        P("slab", "brick"),
        P("slab", "brick"),
        P("slab", "brick"),
        P("slab", "brick"),
        P(None, "slab", "brick"),
    ) + (P(),) * 10
    bricks, slabs = mesh.shape["brick"], mesh.shape["slab"]
    fits = 2 * NG == 128 * slabs and NG % (32 * bricks) == 0
    return jax.shard_map(
        per_device if fits else per_device_general,
        mesh=mesh,
        in_specs=placed,
        out_specs=(P("slab", "brick"), P("brick", "slab", None)),
        check_vma=False,
    )
```
